32 devices in a mesh: groups: 2 (over y), rows: 4 (over z), cols: 2 (over x), sub: 2 (over core).
Axes of the slice: x: 2, y: 2, z: 4, core: 2. Of those that a mesh axis runs over, the one named last changes fastest.
Arguments:
- homolog_activations: bfloat16 [32, 256, 256], P(('groups', 'rows'), ('cols', 'sub')), parts along dimension 0, may hold values from -6 to 6
- homolog_valid_flags: int32 [32], P('groups'), parts along dimension 0, may hold values 0 or 1
- position_valid_flags: int32 [512], P('groups'), parts along dimension 0, may hold values 0 or 1
- centering_factor: float32 [256], replicated, may hold values from 0.1 to 1.9
- centering_shift: float32 [256], replicated, may hold values from -3 to 3
- first_factor_matrix: bfloat16 [256, 32], replicated, may hold values from -0.375 to 0.375
- second_factor_matrix: bfloat16 [256, 32], replicated, may hold values from -0.375 to 0.375
- couple_weight_matrix: bfloat16 [1024, 128], replicated, may hold values from -1.5 to 1.5
- couple_shift_vector: float32 [128], replicated, may hold values from -3 to 3
- loss_sensitivity: bfloat16 [512, 256, 128], P(('groups', 'rows'), ('cols', 'sub')), parts along dimension 0, may hold values from -6 to 6
Outputs:
- pair_update_output: bfloat16 [512, 256, 128], P(('groups', 'rows'), ('cols', 'sub')), parts along dimension 0
- alignment_gradient: bfloat16 [32, 256, 256], P(('groups', 'rows'), ('cols', 'sub')), parts along dimension 0
The draws below stay inside these ranges and needn't reach their ends.
There are 2 independent parts, one for each index of `groups`. The reference program is written for one: setup_inputs(seed, part) draws one part's arguments, and reference() takes and returns one part's arrays. A program takes and returns all parts, laid end to end along the dimension named above; an argument that names none is the same for every part. Nothing has to cross between parts.
All inputs are finite; a program needn't handle non-finite values.
Results may differ from the reference program's by a relative error of at most 0.0076.
Values may be sent and summed in bfloat16 or wider, within the bound.
No kernel may reach another device: no remote copies, remote signals or barrier semaphores. Data moves between devices by JAX's collectives and lax.ppermute only.
A program may use at most 64 MiB of HBM per device.

```python
import math
import jax
import jax.numpy as jnp
from jax import lax

FEATURE_DEPTH = 256
PROJECTED_WIDTH = 32
CZ = 128
CHAIN_LENGTH = 256
HOMOLOG_TOTAL = 16


def place_ends(drawn, rng, low, largest):
    longest = drawn.shape.index(max(drawn.shape))
    spots = []
    for shift in (0, 1):
        where = [jax.random.randint(jax.random.fold_in(rng, axis), (), 0, length) for axis, length in enumerate(drawn.shape)]
        where[longest] = (where[longest] + shift) % drawn.shape[longest]
        spots.append(tuple(where))
    return drawn.at[spots[0]].set(low).at[spots[1]].set(largest)


def shard_levels(stream_key, extent, pieces, smallest, largest):
    level, own = 1.0, jax.random.fold_in(stream_key, 6)
    for position, blocks in pieces:
        heights = jnp.exp(jax.random.uniform(jax.random.fold_in(own, position), (blocks,), jnp.float32, smallest / len(pieces), largest / len(pieces)))
        level = level * jnp.repeat(heights, extent[position] // blocks).reshape([-1 if axis == position else 1 for axis in range(len(extent))])
    return level


def noise(rng, dims, deviation, limit, shards=(), held_as=jnp.bfloat16):
    drawn = deviation * jax.random.normal(rng, dims, jnp.float32)
    if shards:
        drawn = drawn * shard_levels(rng, dims, shards, -0.22, 0.18)
    return jnp.clip(drawn, -limit, limit).astype(held_as)


def setup_inputs(seed: int = 0, part: int = 0) -> dict:
    seeds = jax.random.split(jax.random.key(seed), 11)
    part_keys = jax.random.split(jax.random.fold_in(seeds[10], part), 11)
    homolog_activations = noise(part_keys[0], (HOMOLOG_TOTAL, CHAIN_LENGTH, FEATURE_DEPTH), 1.0, 6.0, ((0, 4), (1, 4)))
    homolog_valid_flags = place_ends((jax.random.randint(part_keys[1], (HOMOLOG_TOTAL,), 0, 4) < 3).astype(jnp.int32), jax.random.fold_in(part_keys[1], 1), 0, 1)
    position_valid_flags = place_ends((jax.random.randint(part_keys[2], (CHAIN_LENGTH,), 0, 8) < 7).astype(jnp.int32), jax.random.fold_in(part_keys[2], 1), 0, 1)
    centering_factor = jnp.clip(1.0 + 0.18 * jax.random.normal(seeds[3], (FEATURE_DEPTH,), jnp.float32), 0.1, 1.9)
    centering_shift = noise(seeds[4], (FEATURE_DEPTH,), 0.5, 3.0, (), jnp.float32)
    first_factor_matrix = noise(seeds[5], (FEATURE_DEPTH, PROJECTED_WIDTH), FEATURE_DEPTH ** -0.5, 0.375)
    second_factor_matrix = noise(seeds[6], (FEATURE_DEPTH, PROJECTED_WIDTH), FEATURE_DEPTH ** -0.5, 0.375)
    couple_weight_matrix = noise(seeds[7], (PROJECTED_WIDTH * PROJECTED_WIDTH, CZ), 16 ** -0.5, 1.5)
    couple_shift_vector = noise(seeds[8], (CZ,), 0.5, 3.0, (), jnp.float32)
    loss_sensitivity = noise(part_keys[9], (CHAIN_LENGTH, CHAIN_LENGTH, CZ), 1.0, 6.0, ((0, 4), (1, 4)))
    return dict(homolog_activations=homolog_activations, homolog_valid_flags=homolog_valid_flags, position_valid_flags=position_valid_flags, centering_factor=centering_factor, centering_shift=centering_shift, first_factor_matrix=first_factor_matrix, second_factor_matrix=second_factor_matrix, couple_weight_matrix=couple_weight_matrix, couple_shift_vector=couple_shift_vector, loss_sensitivity=loss_sensitivity)


def feature_standardize(x, norm_multiplier, norm_offset):
    mean_val = lax.optimization_barrier(jnp.mean(x, axis=-1, keepdims=True))
    mean_removed = x - mean_val
    variance = lax.optimization_barrier(jnp.mean(mean_removed * mean_removed, axis=-1, keepdims=True))
    reciprocal_spread = lax.rsqrt(variance + 1e-05)
    whitened_features = mean_removed * reciprocal_spread
    return (whitened_features * norm_multiplier + norm_offset, whitened_features, reciprocal_spread)

def reference(homolog_activations, homolog_valid_flags, position_valid_flags, centering_factor, centering_shift, first_factor_matrix, second_factor_matrix, couple_weight_matrix, couple_shift_vector, loss_sensitivity):
    thirty_two_real = jnp.float32
    brain_float_half = jnp.bfloat16
    centered_real, whitened_features, reciprocal_spread = feature_standardize(homolog_activations.astype(thirty_two_real), centering_factor, centering_shift)
    normed = centered_real.astype(brain_float_half).astype(thirty_two_real)
    seq_f = homolog_valid_flags.astype(thirty_two_real)
    res_f = position_valid_flags.astype(thirty_two_real)
    mask = seq_f[:, None] * res_f[None, :]
    left = (jnp.einsum('src,cp->srp', normed, first_factor_matrix.astype(thirty_two_real)) * mask[..., None]).astype(brain_float_half).astype(thirty_two_real)
    right = (jnp.einsum('src,cp->srp', normed, second_factor_matrix.astype(thirty_two_real)) * mask[..., None]).astype(brain_float_half).astype(thirty_two_real)
    count = jnp.maximum(jnp.sum(seq_f) * res_f[:, None] * res_f[None, :], 1.0)
    rows_blk = math.gcd(CHAIN_LENGTH, 32)
    steps_count = CHAIN_LENGTH // rows_blk

    def section(carry, index):
        start = (index * rows_blk).astype(jnp.int32)
        left_blk = lax.dynamic_slice_in_dim(left, start, rows_blk, 1)
        outer = jnp.einsum('sip,sjq->ijpq', left_blk, right).astype(brain_float_half)
        outer = outer.reshape(rows_blk * CHAIN_LENGTH, PROJECTED_WIDTH * PROJECTED_WIDTH)
        projected = jnp.dot(outer, couple_weight_matrix, preferred_element_type=thirty_two_real).reshape(rows_blk, CHAIN_LENGTH, CZ)
        counts = lax.dynamic_slice_in_dim(count, start, rows_blk, 0)[..., None]
        pair = ((projected + couple_shift_vector.astype(thirty_two_real)) / counts).astype(brain_float_half)
        grad_in = lax.dynamic_slice_in_dim(loss_sensitivity, start, rows_blk, 0).astype(thirty_two_real)
        scaled = (grad_in / counts).astype(brain_float_half).reshape(rows_blk * CHAIN_LENGTH, CZ)
        outer_grad = jnp.dot(scaled, couple_weight_matrix.T, preferred_element_type=thirty_two_real).astype(brain_float_half)
        outer_grad = outer_grad.astype(thirty_two_real).reshape(rows_blk, CHAIN_LENGTH, PROJECTED_WIDTH, PROJECTED_WIDTH)
        left_part = jnp.einsum('ijpq,sjq->sip', outer_grad, right)
        carry = carry + jnp.einsum('ijpq,sip->sjq', outer_grad, left_blk)
        return (carry, (pair, left_part))
    right_grad, (pairs, left_parts) = lax.scan(section, jnp.zeros((HOMOLOG_TOTAL, CHAIN_LENGTH, PROJECTED_WIDTH), thirty_two_real), jnp.arange(steps_count, dtype=jnp.int32))
    pair_update_output = pairs.reshape(CHAIN_LENGTH, CHAIN_LENGTH, CZ)
    left_grad = jnp.transpose(left_parts, (1, 0, 2, 3)).reshape(HOMOLOG_TOTAL, CHAIN_LENGTH, PROJECTED_WIDTH)
    masked_left = (left_grad * mask[..., None]).astype(brain_float_half).astype(thirty_two_real)
    masked_right = (right_grad * mask[..., None]).astype(brain_float_half).astype(thirty_two_real)
    normed_grad = jnp.einsum('srp,cp->src', masked_left, first_factor_matrix.astype(thirty_two_real)) + jnp.einsum('srp,cp->src', masked_right, second_factor_matrix.astype(thirty_two_real))
    gradient_scaled = normed_grad * centering_factor
    alignment_gradient = reciprocal_spread * (gradient_scaled - lax.optimization_barrier(jnp.mean(gradient_scaled, axis=-1, keepdims=True)) - whitened_features * lax.optimization_barrier(jnp.mean(gradient_scaled * whitened_features, axis=-1, keepdims=True)))
    return (pair_update_output, alignment_gradient.astype(brain_float_half))
```

```python
import jax
import jax.numpy as jnp
from jax import lax
from jax.experimental import pallas as pl
from jax.experimental.pallas import tpu as pltpu
from jax.sharding import PartitionSpec as P

F32 = jnp.float32
BF16 = jnp.bfloat16
PLACES = ("rows", "cols", "sub")
BUNCH = 16
VMEM_BYTES = 48 * 1024 * 1024


def dot(a, b):
    return lax.dot_general(a, b, (((1,), (0,)), ((), ())), preferred_element_type=F32)


def dot_t(a, b):
    return lax.dot_general(a, b, (((1,), (1,)), ((), ())), preferred_element_type=F32)


def place():
    blocks = lax.axis_size("cols") * lax.axis_size("sub")
    column = lax.axis_index("cols") * lax.axis_size("sub") + lax.axis_index("sub")
    return lax.axis_index("rows"), column, blocks


def flag_column(flags_ref, start, length):
    flags = flags_ref[...].astype(F32).reshape(1, -1)
    total = flags.shape[1]
    spot = lax.broadcasted_iota(jnp.int32, (length, total), 0) + start
    lane = lax.broadcasted_iota(jnp.int32, (length, total), 1)
    return jnp.sum(jnp.where(spot == lane, flags, 0.0), axis=1, keepdims=True)


def own_mask(seq_ref, res_ref, row_at, column_at, seqs, length, width):
    residues = flag_column(res_ref, column_at * length, length)
    lane = lax.broadcasted_iota(jnp.int32, (length, 2 * seqs * width), 1)
    which = (lane % (seqs * width)) // width
    flags = jnp.zeros((length, 2 * seqs * width), F32)
    for s in range(seqs):
        value = seq_ref[row_at * seqs + s].astype(F32)
        flags = jnp.where(which == s, value, flags)
    return flags * residues


def fill_block_diagonal(diag, first_ref, second_ref, seqs):
    width, channels = first_ref.shape
    diag[...] = jnp.zeros_like(diag)
    for s in range(seqs):
        lanes = slice(s * channels, (s + 1) * channels)
        diag[s * width : (s + 1) * width, lanes] = first_ref[...]
        diag[(seqs + s) * width : (seqs + s + 1) * width, lanes] = second_ref[...]


def whiten(x):
    mean = jnp.mean(x, axis=-1, keepdims=True)
    off = x - mean
    spread = lax.rsqrt(jnp.mean(off * off, axis=-1, keepdims=True) + 1e-05)
    return off * spread, spread


def project_kernel(seq_ref, x_ref, res_ref, gain_ref, bias_ref, first_ref, second_ref, out_ref, diag):
    row_at, column_at, _ = place()
    seqs, length, channels = x_ref.shape
    width = first_ref.shape[0]
    fill_block_diagonal(diag, first_ref, second_ref, seqs)
    gain = gain_ref[...].reshape(1, channels)
    bias = bias_ref[...].reshape(1, channels)
    total = jnp.zeros((length, 2 * seqs * width), F32)
    for s in range(seqs):
        hat, _ = whiten(x_ref[s].astype(F32))
        normed = (hat * gain + bias).astype(BF16)
        total += dot_t(normed, diag[:, s * channels : (s + 1) * channels])
    both = (total * own_mask(seq_ref, res_ref, row_at, column_at, seqs, length, width)).astype(BF16)
    for slot in range(out_ref.shape[0]):
        out_ref[slot] = both


def tile_kernel(
    seq_ref,
    resi_ref,
    res_ref,
    lr_ref,
    w_ref,
    shift_ref,
    loss_ref,
    pair_ref,
    slots_ref,
    wide,
    weight,
    swap,
    left_rows,
    left_grad,
    right_cols,
    right_t,
    scaled,
    t_buf,
    u_buf,
    right_acc,
):
    row_at, column_at, blocks = place()
    step = pl.program_id(0)
    rows_blk, length, cz = loss_ref.shape
    half = lr_ref.shape[2] // 2
    total_seq = seq_ref.shape[0]
    width = weight.shape[0]
    span = BUNCH * width
    bunches = total_seq // BUNCH
    per_bunch = span // half

    @pl.when(step == 0)
    def _():
        wide[...] = w_ref[...].astype(F32)
        for q in range(width):
            weight[:, q * cz : (q + 1) * cz] = wide[pl.ds(q, width, stride=width), :].astype(BF16)
        to = lax.broadcasted_iota(jnp.int32, (span, span), 0)
        at = lax.broadcasted_iota(jnp.int32, (span, span), 1)
        swap[...] = jnp.where((to // BUNCH == at % width) & (to % BUNCH == at // width), 1.0, 0.0).astype(BF16)
        for g in range(bunches):
            right = jnp.concatenate(
                [lr_ref[(g * per_bunch + k) * blocks + column_at, :, half:] for k in range(per_bunch)], axis=1
            )
            right_cols[:, g * span : (g + 1) * span] = dot_t(right, swap[...]).astype(BF16)
            right_t[g * span : (g + 1) * span, :] = dot_t(swap[...], right).astype(BF16)
            for k in range(per_bunch):
                left = lr_ref[(g * per_bunch + k) * blocks + row_at, :, :half].astype(F32)
                for s in range(half // width):
                    left_rows[g, pl.ds(k * (half // width) + s, length, stride=BUNCH), :] = left[
                        :, s * width : (s + 1) * width
                    ]
        right_acc[...] = jnp.zeros_like(right_acc)

    present = seq_ref[0].astype(F32)
    for s in range(1, total_seq):
        present = present + seq_ref[s].astype(F32)
    residues = flag_column(res_ref, column_at * length, length)
    inverse = jnp.broadcast_to(1.0 / jnp.maximum(present * residues, 1.0), (length, cz))
    shift = shift_ref[...].reshape(1, cz)
    factors = []
    for i in range(rows_blk):
        here = resi_ref[row_at * left_rows.shape[1] // BUNCH + step * rows_blk + i]
        factors.append(jnp.where(here > 0, inverse, 1.0))
        scaled[:, i * cz : (i + 1) * cz] = (loss_ref[i].astype(F32) * factors[i]).astype(BF16)

    rows = rows_blk * BUNCH
    for g in range(bunches):
        lefts = left_rows[g, pl.ds(pl.multiple_of(step * rows, rows), rows), :].astype(BF16)
        for n in range(width // 2):
            made = dot(lefts, weight[:, n * 2 * cz : (n + 1) * 2 * cz]).astype(BF16)
            for a in range(2):
                q = 2 * n + a
                for i in range(rows_blk):
                    t_buf[
                        g * span + q * BUNCH : g * span + (q + 1) * BUNCH, i * cz : (i + 1) * cz
                    ] = made[i * BUNCH : (i + 1) * BUNCH, a * cz : (a + 1) * cz]
    right_acc[...] += dot_t(t_buf[...], scaled[...])
    for n in range(rows_blk // 2):
        made = dot(right_cols[...], t_buf[:, n * 2 * cz : (n + 1) * 2 * cz])
        for a in range(2):
            pair_ref[2 * n + a] = ((made[:, a * cz : (a + 1) * cz] + shift) * factors[2 * n + a]).astype(BF16)
    for g in range(bunches):
        for n in range(rows_blk // 2):
            made = dot(
                right_t[g * span : (g + 1) * span, :], scaled[:, n * 2 * cz : (n + 1) * 2 * cz]
            ).astype(BF16)
            for a in range(2):
                i = 2 * n + a
                for q in range(width):
                    u_buf[i * BUNCH : (i + 1) * BUNCH, q * cz : (q + 1) * cz] = made[
                        q * BUNCH : (q + 1) * BUNCH, a * cz : (a + 1) * cz
                    ]
        left_grad[g, pl.ds(pl.multiple_of(step * rows, rows), rows), :] = dot_t(u_buf[...], weight[...])

    @pl.when(step == pl.num_programs(0) - 1)
    def _():
        for g in range(bunches):
            turned = jnp.transpose(right_acc[g * span : (g + 1) * span, :]).astype(BF16)
            right = dot(turned, swap[...]).astype(BF16)
            for k in range(per_bunch):
                left = jnp.concatenate(
                    [
                        left_grad[g, pl.ds(k * (half // width) + s, length, stride=BUNCH), :]
                        for s in range(half // width)
                    ],
                    axis=1,
                ).astype(BF16)
                for c in range(slots_ref.shape[0] // (bunches * per_bunch)):
                    slot = (g * per_bunch + k) * (slots_ref.shape[0] // (bunches * per_bunch)) + c
                    slots_ref[slot, :, :half] = left
                    slots_ref[slot, :, half:] = right[:, k * half : (k + 1) * half]


def finish_kernel(seq_ref, grads_ref, x_ref, res_ref, gain_ref, first_ref, second_ref, out_ref, diag):
    row_at, column_at, blocks = place()
    seqs, length, channels = x_ref.shape
    width = first_ref.shape[0]
    half = seqs * width
    fill_block_diagonal(diag, first_ref, second_ref, seqs)
    count = grads_ref.shape[0] // blocks
    left = grads_ref[column_at * blocks, :, :half].astype(F32)
    right = grads_ref[column_at, :, half:].astype(F32)
    for k in range(1, count):
        left += grads_ref[column_at * blocks + k, :, :half].astype(F32)
        right += grads_ref[k * blocks + column_at, :, half:].astype(F32)
    mask = own_mask(seq_ref, res_ref, row_at, column_at, seqs, length, width)
    both = (jnp.concatenate([left, right], axis=1) * mask).astype(BF16)
    gain = gain_ref[...].reshape(1, channels)
    for s in range(seqs):
        hat, spread = whiten(x_ref[s].astype(F32))
        grad = dot(both, diag[:, s * channels : (s + 1) * channels]) * gain
        out_ref[s] = (
            spread
            * (
                grad
                - jnp.mean(grad, axis=-1, keepdims=True)
                - hat * jnp.mean(grad * hat, axis=-1, keepdims=True)
            )
        ).astype(BF16)


def in_vmem():
    return pl.BlockSpec(memory_space=pltpu.VMEM)


def in_smem():
    return pl.BlockSpec(memory_space=pltpu.SMEM)


def per_device(
    homolog_activations,
    homolog_valid_flags,
    position_valid_flags,
    centering_factor,
    centering_shift,
    first_factor_matrix,
    second_factor_matrix,
    couple_weight_matrix,
    couple_shift_vector,
    loss_sensitivity,
):
    seqs, length, channels = homolog_activations.shape
    total_seq = homolog_valid_flags.shape[0]
    width = first_factor_matrix.shape[1]
    row_len, column_len, cz = loss_sensitivity.shape
    blocks = lax.axis_size("cols") * lax.axis_size("sub")
    devices = lax.axis_size("rows") * blocks
    bunches = total_seq // BUNCH
    span = BUNCH * width
    rows_blk = 16
    first = first_factor_matrix.T
    second = second_factor_matrix.T
    params = pltpu.CompilerParams(vmem_limit_bytes=VMEM_BYTES)
    slots = jax.ShapeDtypeStruct((devices, length, 2 * seqs * width), BF16)
    diag = pltpu.VMEM((2 * seqs * width, seqs * channels), BF16)

    both = pl.pallas_call(
        project_kernel,
        out_shape=slots,
        in_specs=[in_smem()] + [in_vmem()] * 6,
        out_specs=in_vmem(),
        scratch_shapes=[diag],
        compiler_params=params,
        name="project",
    )(
        homolog_valid_flags,
        homolog_activations,
        position_valid_flags,
        centering_factor,
        centering_shift,
        first,
        second,
    )
    both = lax.all_to_all(both, PLACES, split_axis=0, concat_axis=0, tiled=True)

    pair, grads = pl.pallas_call(
        tile_kernel,
        grid=(row_len // rows_blk,),
        out_shape=(jax.ShapeDtypeStruct(loss_sensitivity.shape, BF16), slots),
        in_specs=[in_smem()] * 2
        + [in_vmem()] * 4
        + [pl.BlockSpec((rows_blk, column_len, cz), lambda n: (n, 0, 0))],
        out_specs=(
            pl.BlockSpec((rows_blk, column_len, cz), lambda n: (n, 0, 0)),
            pl.BlockSpec(slots.shape, lambda n: (0, 0, 0)),
        ),
        scratch_shapes=[
            pltpu.VMEM((width * width, cz), F32),
            pltpu.VMEM((width, width * cz), BF16),
            pltpu.VMEM((span, span), BF16),
            pltpu.VMEM((bunches, row_len * BUNCH, width), F32),
            pltpu.VMEM((bunches, row_len * BUNCH, width), F32),
            pltpu.VMEM((column_len, bunches * span), BF16),
            pltpu.VMEM((bunches * span, column_len), BF16),
            pltpu.VMEM((column_len, rows_blk * cz), BF16),
            pltpu.VMEM((bunches * span, rows_blk * cz), BF16),
            pltpu.VMEM((rows_blk * BUNCH, width * cz), BF16),
            pltpu.VMEM((bunches * span, column_len), F32),
        ],
        compiler_params=params,
        name="tile",
    )(
        homolog_valid_flags,
        position_valid_flags,
        position_valid_flags,
        both,
        couple_weight_matrix,
        couple_shift_vector,
        loss_sensitivity,
    )
    grads = lax.all_to_all(grads, PLACES, split_axis=0, concat_axis=0, tiled=True)

    alignment = pl.pallas_call(
        finish_kernel,
        out_shape=jax.ShapeDtypeStruct(homolog_activations.shape, BF16),
        in_specs=[in_smem()] + [in_vmem()] * 6,
        out_specs=in_vmem(),
        scratch_shapes=[diag],
        compiler_params=params,
        name="finish",
    )(
        homolog_valid_flags,
        grads,
        homolog_activations,
        position_valid_flags,
        centering_factor,
        first,
        second,
    )
    return pair, alignment


def solution(mesh):
    split = P(("groups", "rows"), ("cols", "sub"), None)
    return jax.shard_map(
        per_device,
        mesh=mesh,
        in_specs=(split, P("groups"), P("groups"), P(), P(), P(), P(), P(), P(), split),
        out_specs=(split, split),
        check_vma=False,
    )
```

```python
import functools

import jax
import jax.numpy as jnp
from jax import lax
from jax.experimental import pallas as pl
from jax.experimental.pallas import tpu as pltpu
from jax.sharding import PartitionSpec as P

F32 = jnp.float32
BF16 = jnp.bfloat16
PLACES = ("rows", "cols", "sub")
BUNCH = 16
CHUNK = 16


def dot(a, b):
    return lax.dot_general(a, b, (((1,), (0,)), ((), ())), preferred_element_type=F32)


def dot_t(a, b):
    return lax.dot_general(a, b, (((1,), (1,)), ((), ())), preferred_element_type=F32)


def place():
    blocks = lax.axis_size("cols") * lax.axis_size("sub")
    column = lax.axis_index("cols") * lax.axis_size("sub") + lax.axis_index("sub")
    return lax.axis_index("rows"), column, blocks


def flag_column(flags_ref, start, length):
    flags = flags_ref[...].astype(F32).reshape(1, -1)
    total = flags.shape[1]
    spot = lax.broadcasted_iota(jnp.int32, (length, total), 0) + start
    lane = lax.broadcasted_iota(jnp.int32, (length, total), 1)
    return jnp.sum(jnp.where(spot == lane, flags, 0.0), axis=1, keepdims=True)


def own_mask(seq_ref, res_ref, row_at, column_at, seqs, length, width):
    residues = flag_column(res_ref, column_at * length, length)
    lane = lax.broadcasted_iota(jnp.int32, (length, 2 * seqs * width), 1)
    which = (lane % (seqs * width)) // width
    flags = jnp.zeros((length, 2 * seqs * width), F32)
    for s in range(seqs):
        value = seq_ref[row_at * seqs + s].astype(F32)
        flags = jnp.where(which == s, value, flags)
    return flags * residues


def fill_block_diagonal(diag, first_ref, second_ref, seqs):
    width, channels = first_ref.shape
    diag[...] = jnp.zeros_like(diag)
    for s in range(seqs):
        lanes = slice(s * channels, (s + 1) * channels)
        diag[s * width : (s + 1) * width, lanes] = first_ref[...]
        diag[(seqs + s) * width : (seqs + s + 1) * width, lanes] = second_ref[...]


def whiten(x):
    mean = jnp.mean(x, axis=-1, keepdims=True)
    off = x - mean
    spread = lax.rsqrt(jnp.mean(off * off, axis=-1, keepdims=True) + 1e-05)
    return off * spread, spread


def load_all(pairs, sems):
    copies = [pltpu.make_async_copy(src, dst, sems.at[n]) for n, (src, dst) in enumerate(pairs)]
    for copy in copies:
        copy.start()
    for copy in copies:
        copy.wait()


def project_kernel(*refs):
    sources, (left_ref, right_ref), held, (diag, sems) = refs[:7], refs[7:9], refs[9:16], refs[16:]
    load_all(list(zip(sources, held)), sems)
    seq_ref, x_ref, res_ref, gain_ref, bias_ref, first_ref, second_ref = held
    row_at, column_at, _ = place()
    seqs, length, channels = x_ref.shape
    width = first_ref.shape[0]
    half = seqs * width
    fill_block_diagonal(diag, first_ref, second_ref, seqs)
    gain = gain_ref[...].reshape(1, channels)
    bias = bias_ref[...].reshape(1, channels)
    total = jnp.zeros((length, 2 * half), F32)
    for s in range(seqs):
        hat, _ = whiten(x_ref[s].astype(F32))
        normed = (hat * gain + bias).astype(BF16)
        total += dot_t(normed, diag[:, s * channels : (s + 1) * channels])
    both = (total * own_mask(seq_ref, res_ref, row_at, column_at, seqs, length, width)).astype(BF16)
    left_ref[...] = both[:, :half]
    right_ref[...] = both[:, half:]


def prepare_kernel(
    seq_ref,
    resi_ref,
    res_ref,
    w_ref,
    loss_ref,
    x_ref,
    first_ref,
    second_ref,
    weight,
    swap,
    scaled,
    inverse_ref,
    diag,
    mask_ref,
    hat_ref,
    spread_ref,
    wide,
):
    row_at, column_at, _ = place()
    rows, length, cz = loss_ref.shape
    seqs, _, _ = x_ref.shape
    width = first_ref.shape[0]
    fill_block_diagonal(diag, first_ref, second_ref, seqs)
    mask_ref[...] = own_mask(seq_ref, res_ref, row_at, column_at, seqs, length, width)
    for s in range(seqs):
        hat, spread = whiten(x_ref[s].astype(F32))
        hat_ref[s] = hat
        spread_ref[s] = jnp.broadcast_to(spread, spread_ref.shape[1:])
    wide[...] = w_ref[...].astype(F32)
    for q in range(width):
        weight[:, q * cz : (q + 1) * cz] = wide[pl.ds(q, width, stride=width), :].astype(BF16)
    span = swap.shape[0]
    to = lax.broadcasted_iota(jnp.int32, (span, span), 0)
    at = lax.broadcasted_iota(jnp.int32, (span, span), 1)
    swap[...] = jnp.where((to // BUNCH == at % width) & (to % BUNCH == at // width), 1.0, 0.0).astype(BF16)
    present = seq_ref[0].astype(F32)
    for s in range(1, seq_ref.shape[0]):
        present = present + seq_ref[s].astype(F32)
    residues = flag_column(res_ref, column_at * length, length)
    inverse = jnp.broadcast_to(1.0 / jnp.maximum(present * residues, 1.0), (length, cz))
    inverse_ref[...] = inverse
    for i in range(rows):
        factor = jnp.where(resi_ref[row_at * rows + i] > 0, inverse, 1.0)
        scaled[:, i * cz : (i + 1) * cz] = (loss_ref[i].astype(F32) * factor).astype(BF16)


def left_kernel(blocks, *refs):
    rights, (swap, scaled, weight) = refs[:blocks], refs[blocks : blocks + 3]
    right_cols = refs[blocks + 3]
    outs = refs[blocks + 4 : 2 * blocks + 4]
    ordered, right_t, u_buf, left_grad, parts = refs[2 * blocks + 4 :]
    row_at, column_at, _ = place()
    length, half = rights[0].shape
    span = swap.shape[0]
    width = weight.shape[0]
    cz = weight.shape[1] // width
    per_bunch = span // half
    bunches = blocks // per_bunch
    rows = CHUNK * BUNCH
    for k in range(blocks):
        ordered[lax.rem(row_at + k, blocks)] = rights[k][...]
    for g in range(bunches):
        right = jnp.concatenate([ordered[g * per_bunch + k] for k in range(per_bunch)], axis=1)
        right_cols[:, g * span : (g + 1) * span] = dot_t(right, swap[...]).astype(BF16)
        right_t[g * span : (g + 1) * span, :] = dot_t(swap[...], right).astype(BF16)

    def section(step, _):
        for g in range(bunches):
            for n in range(CHUNK // 2):
                lanes = pl.ds(pl.multiple_of((step * CHUNK + 2 * n) * cz, 2 * cz), 2 * cz)
                made = dot(right_t[g * span : (g + 1) * span, :], scaled[:, lanes]).astype(BF16)
                for a in range(2):
                    i = 2 * n + a
                    for q in range(width):
                        u_buf[i * BUNCH : (i + 1) * BUNCH, q * cz : (q + 1) * cz] = made[
                            q * BUNCH : (q + 1) * BUNCH, a * cz : (a + 1) * cz
                        ]
            left_grad[g, pl.ds(pl.multiple_of(step * rows, rows), rows), :] = dot_t(u_buf[...], weight[...])
        return 0

    lax.fori_loop(0, scaled.shape[1] // cz // CHUNK, section, 0)
    for g in range(bunches):
        for k in range(per_bunch):
            parts[g * per_bunch + k] = jnp.concatenate(
                [
                    left_grad[g, pl.ds(k * (half // width) + s, length, stride=BUNCH), :]
                    for s in range(half // width)
                ],
                axis=1,
            ).astype(BF16)
    for k in range(blocks):
        outs[k][...] = parts[lax.rem(column_at - k + blocks, blocks)]


def right_kernel(blocks, *refs):
    lefts, (swap, scaled, weight) = refs[:blocks], refs[blocks : blocks + 3]
    t_ref = refs[blocks + 3]
    outs = refs[blocks + 4 : 2 * blocks + 4]
    left_rows, right_acc, parts = refs[2 * blocks + 4 :]
    row_at, column_at, _ = place()
    length, half = lefts[0].shape
    span = swap.shape[0]
    width = weight.shape[0]
    cz = weight.shape[1] // width
    per_bunch = span // half
    bunches = blocks // per_bunch
    rows = CHUNK * BUNCH
    for k in range(blocks):
        source = lax.rem(column_at + k, blocks)
        left = lefts[k][...].astype(F32)
        for s in range(half // width):
            spot = lax.rem(source, per_bunch) * (half // width) + s
            left_rows[source // per_bunch, pl.ds(spot, length, stride=BUNCH), :] = left[
                :, s * width : (s + 1) * width
            ]
    right_acc[...] = jnp.zeros_like(right_acc)

    def section(step, _):
        for g in range(bunches):
            taken = left_rows[g, pl.ds(pl.multiple_of(step * rows, rows), rows), :].astype(BF16)
            for n in range(width // 2):
                made = dot(taken, weight[:, n * 2 * cz : (n + 1) * 2 * cz]).astype(BF16)
                for a in range(2):
                    q = 2 * n + a
                    for i in range(CHUNK):
                        lanes = pl.ds(pl.multiple_of((step * CHUNK + i) * cz, cz), cz)
                        t_ref[g * span + q * BUNCH : g * span + (q + 1) * BUNCH, lanes] = made[
                            i * BUNCH : (i + 1) * BUNCH, a * cz : (a + 1) * cz
                        ]
        lanes = pl.ds(pl.multiple_of(step * CHUNK * cz, CHUNK * cz), CHUNK * cz)
        right_acc[...] += dot_t(t_ref[:, lanes], scaled[:, lanes])
        return 0

    lax.fori_loop(0, scaled.shape[1] // cz // CHUNK, section, 0)
    for g in range(bunches):
        turned = jnp.transpose(right_acc[g * span : (g + 1) * span, :]).astype(BF16)
        right = dot(turned, swap[...]).astype(BF16)
        for k in range(per_bunch):
            parts[g * per_bunch + k] = right[:, k * half : (k + 1) * half]
    for k in range(blocks):
        outs[k][...] = parts[lax.rem(row_at - k + blocks, blocks)]


def pair_kernel(resi_ref, right_cols, t_ref, shift_ref, inverse_ref, out_ref, held, sems):
    row_at, _, _ = place()
    rows, length, cz = held.shape
    shift = shift_ref[...].reshape(1, cz)
    steps = rows // CHUNK

    def copy(step):
        spot = pl.ds(step * CHUNK, CHUNK)
        return pltpu.make_async_copy(held.at[spot], out_ref.at[spot], sems.at[step])

    def section(step, _):
        for n in range(CHUNK // 2):
            lanes = pl.ds(pl.multiple_of((step * CHUNK + 2 * n) * cz, 2 * cz), 2 * cz)
            made = dot(right_cols[...], t_ref[:, lanes])
            for a in range(2):
                i = step * CHUNK + 2 * n + a
                factor = jnp.where(resi_ref[row_at * rows + i] > 0, inverse_ref[...], 1.0)
                held[i] = ((made[:, a * cz : (a + 1) * cz] + shift) * factor).astype(BF16)
        copy(step).start()
        return 0

    lax.fori_loop(0, steps, section, 0)
    for step in range(steps):
        copy(step).wait()


def finish_kernel(blocks, *refs):
    lefts, rights = refs[:blocks], refs[blocks : 2 * blocks]
    mask_ref, diag, gain_ref, hat_ref, spread_ref, out_ref = refs[2 * blocks :]
    seqs, _, channels = hat_ref.shape
    left = lefts[0][...].astype(F32)
    right = rights[0][...].astype(F32)
    for k in range(1, blocks):
        left += lefts[k][...].astype(F32)
        right += rights[k][...].astype(F32)
    both = (jnp.concatenate([left, right], axis=1) * mask_ref[...]).astype(BF16)
    gain = gain_ref[...].reshape(1, channels)
    for s in range(seqs):
        hat = hat_ref[s]
        grad = dot(both, diag[:, s * channels : (s + 1) * channels]) * gain
        out_ref[s] = (
            spread_ref[s][:, :1]
            * (
                grad
                - jnp.mean(grad, axis=-1, keepdims=True)
                - hat * jnp.mean(grad * hat, axis=-1, keepdims=True)
            )
        ).astype(BF16)


def in_vmem():
    return pl.BlockSpec(memory_space=pltpu.VMEM)


def in_smem():
    return pl.BlockSpec(memory_space=pltpu.SMEM)


def in_hbm():
    return pl.BlockSpec(memory_space=pltpu.HBM)


def call(kernel, name, out_shape, in_specs, out_specs, scratch, flops, traffic, limit=24):
    return pl.pallas_call(
        kernel,
        out_shape=out_shape,
        in_specs=in_specs,
        out_specs=out_specs,
        scratch_shapes=scratch,
        compiler_params=pltpu.CompilerParams(vmem_limit_bytes=limit * 1024 * 1024),
        cost_estimate=pl.CostEstimate(flops=int(flops), bytes_accessed=int(traffic), transcendentals=0),
        name=name,
    )


def left_moves(blocks, shift):
    return [
        (z * blocks + c, c * blocks + (z - shift) % blocks) for z in range(blocks) for c in range(blocks)
    ]


def right_moves(blocks, shift):
    return [
        (z * blocks + c, (z - shift) % blocks * blocks + c) for z in range(blocks) for c in range(blocks)
    ]


def left_back(blocks, shift):
    return [
        (z * blocks + c, (c - shift) % blocks * blocks + z) for z in range(blocks) for c in range(blocks)
    ]


def per_device(
    homolog_activations,
    homolog_valid_flags,
    position_valid_flags,
    centering_factor,
    centering_shift,
    first_factor_matrix,
    second_factor_matrix,
    couple_weight_matrix,
    couple_shift_vector,
    loss_sensitivity,
):
    seqs, length, channels = homolog_activations.shape
    total_seq = homolog_valid_flags.shape[0]
    total_res = position_valid_flags.shape[0]
    width = first_factor_matrix.shape[1]
    rows, columns, cz = loss_sensitivity.shape
    blocks = lax.axis_size("cols") * lax.axis_size("sub")
    half = seqs * width
    span = BUNCH * width
    deep = total_seq * width
    bunches = total_seq // BUNCH
    first = first_factor_matrix.T
    second = second_factor_matrix.T
    shape = jax.ShapeDtypeStruct
    block = shape((length, half), BF16)
    work = 2 * rows * columns * width * width * cz

    left, right = call(
        project_kernel,
        "project",
        (block, block),
        [in_hbm()] * 7,
        (in_vmem(), in_vmem()),
        [
            pltpu.SMEM((total_seq,), jnp.int32),
            pltpu.VMEM((seqs, length, channels), BF16),
            pltpu.VMEM((total_res,), jnp.int32),
            pltpu.VMEM((channels,), F32),
            pltpu.VMEM((channels,), F32),
            pltpu.VMEM((width, channels), BF16),
            pltpu.VMEM((width, channels), BF16),
            pltpu.VMEM((2 * half, seqs * channels), BF16),
            pltpu.SemaphoreType.DMA((7,)),
        ],
        1e7,
        1e6,
    )(
        homolog_valid_flags,
        homolog_activations,
        position_valid_flags,
        centering_factor,
        centering_shift,
        first,
        second,
    )
    rights = [right] + [lax.ppermute(right, PLACES, right_moves(blocks, k)) for k in range(1, blocks)]
    lefts = [lax.ppermute(left, PLACES, left_moves(blocks, k)) for k in range(blocks)]

    weight, swap, scaled, inverse, diag, mask, hat, spread = call(
        prepare_kernel,
        "prepare",
        (
            shape((width, width * cz), BF16),
            shape((span, span), BF16),
            shape((columns, rows * cz), BF16),
            shape((columns, cz), F32),
            shape((2 * half, seqs * channels), BF16),
            shape((length, 2 * half), F32),
            shape((seqs, length, channels), F32),
            shape((seqs, length, cz), F32),
        ),
        [in_smem()] * 2 + [in_vmem()] * 6,
        tuple([in_vmem()] * 8),
        [pltpu.VMEM((width * width, cz), F32)],
        1e7,
        8e6,
    )(
        homolog_valid_flags,
        position_valid_flags,
        position_valid_flags,
        couple_weight_matrix,
        loss_sensitivity,
        homolog_activations,
        first,
        second,
    )

    outcome = call(
        functools.partial(left_kernel, blocks),
        "left_gradient",
        tuple([shape((columns, deep), BF16)] + [block] * blocks),
        [in_vmem()] * (blocks + 3),
        tuple([in_vmem()] * (blocks + 1)),
        [
            pltpu.VMEM((blocks, length, half), BF16),
            pltpu.VMEM((deep, columns), BF16),
            pltpu.VMEM((CHUNK * BUNCH, width * cz), BF16),
            pltpu.VMEM((bunches, rows * BUNCH, width), F32),
            pltpu.VMEM((blocks, length, half), BF16),
        ],
        2 * work,
        1e7,
    )(*rights, swap, scaled, weight)
    right_cols = outcome[0]
    left_parts = [
        lax.ppermute(part, PLACES, left_back(blocks, k)) for k, part in enumerate(outcome[1:])
    ]

    outcome = call(
        functools.partial(right_kernel, blocks),
        "right_gradient",
        tuple([shape((deep, rows * cz), BF16)] + [block] * blocks),
        [in_vmem()] * (blocks + 3),
        tuple([in_vmem()] * (blocks + 1)),
        [
            pltpu.VMEM((bunches, rows * BUNCH, width), F32),
            pltpu.VMEM((deep, columns), F32),
            pltpu.VMEM((blocks, length, half), BF16),
        ],
        2 * work,
        1e7,
        limit=16 + deep * rows * cz * 2 // 2**20,
    )(*lefts, swap, scaled, weight)
    t_all = outcome[0]
    right_parts = [outcome[1]] + [
        lax.ppermute(outcome[1 + k], PLACES, right_moves(blocks, k)) for k in range(1, blocks)
    ]

    pair = call(
        pair_kernel,
        "pair",
        shape(loss_sensitivity.shape, BF16),
        [in_smem()] + [in_vmem()] * 4,
        in_hbm(),
        [pltpu.VMEM(loss_sensitivity.shape, BF16), pltpu.SemaphoreType.DMA((rows // CHUNK,))],
        work,
        1e7,
        limit=16 + deep * rows * cz * 2 // 2**20,
    )(position_valid_flags, right_cols, t_all, couple_shift_vector, inverse)

    alignment = call(
        functools.partial(finish_kernel, blocks),
        "finish",
        shape(homolog_activations.shape, BF16),
        [in_vmem()] * (2 * blocks + 5),
        in_vmem(),
        [],
        1e7,
        1e6,
    )(*left_parts, *right_parts, mask, diag, centering_factor, hat, spread)
    return pair, alignment


def solution(mesh):
    split = P(("groups", "rows"), ("cols", "sub"), None)
    return jax.shard_map(
        per_device,
        mesh=mesh,
        in_specs=(split, P("groups"), P("groups"), P(), P(), P(), P(), P(), P(), split),
        out_specs=(split, split),
        check_vma=False,
    )
```

```python
import functools

import jax
import jax.numpy as jnp
from jax import lax
from jax.experimental import pallas as pl
from jax.experimental.pallas import tpu as pltpu
from jax.sharding import PartitionSpec as P

F32 = jnp.float32
BF16 = jnp.bfloat16
PLACES = ("rows", "cols", "sub")
BUNCH = 16
CHUNK = 16


def dot(a, b):
    return lax.dot_general(a, b, (((1,), (0,)), ((), ())), preferred_element_type=F32)


def dot_t(a, b):
    return lax.dot_general(a, b, (((1,), (1,)), ((), ())), preferred_element_type=F32)


def place():
    column = lax.axis_index("cols") * lax.axis_size("sub") + lax.axis_index("sub")
    return lax.axis_index("rows"), column


def lanes_at(start, size):
    return pl.ds(pl.multiple_of(start, size), size)


def flag_row(flags_ref):
    return flags_ref[...].astype(F32).reshape(1, -1)


def flag_column(flags_ref, start, length):
    flags = flag_row(flags_ref)
    total = flags.shape[1]
    spot = lax.broadcasted_iota(jnp.int32, (length, total), 0) + start
    lane = lax.broadcasted_iota(jnp.int32, (length, total), 1)
    return jnp.sum(jnp.where(spot == lane, flags, 0.0), axis=1, keepdims=True)


def load_all(pairs, sems):
    copies = [pltpu.make_async_copy(src, dst, sems.at[n]) for n, (src, dst) in enumerate(pairs)]
    for copy in copies:
        copy.start()
    return copies


def project_kernel(*refs):
    sources, outs, held, sems = refs[:7], refs[7:13], refs[13:20], refs[20]
    out_ref, diag, mask_ref, hat_ref, spread_ref, gain_out = outs
    copies = load_all(list(zip(sources, held)), sems)
    seq_ref, x_ref, res_ref, gain_ref, bias_ref, first_ref, second_ref = held
    row_at, column_at = place()
    seqs, length, channels = x_ref.shape
    width = first_ref.shape[0]
    half = seqs * width
    diag[...] = jnp.zeros_like(diag)
    for copy in copies:
        copy.wait()
    for s in range(seqs):
        lanes = slice(s * channels, (s + 1) * channels)
        diag[s * width : (s + 1) * width, lanes] = first_ref[...]
        diag[(seqs + s) * width : (seqs + s + 1) * width, lanes] = second_ref[...]
    flags = flag_row(seq_ref)
    spot = lax.broadcasted_iota(jnp.int32, flags.shape, 1)
    which = lax.broadcasted_iota(jnp.int32, (1, 2 * half), 1) % half // width
    own = jnp.zeros((1, 2 * half), F32)
    for s in range(seqs):
        value = jnp.sum(jnp.where(spot == row_at * seqs + s, flags, 0.0), axis=1, keepdims=True)
        own = jnp.where(which == s, value, own)
    mask = flag_column(res_ref, column_at * length, length) * own
    mask_ref[...] = mask
    gain = gain_ref[...].reshape(1, channels)
    bias = bias_ref[...].reshape(1, channels)
    gain_out[...] = jnp.broadcast_to(gain, gain_out.shape)
    total = jnp.zeros((length, 2 * half), F32)
    for s in range(seqs):
        x = x_ref[s].astype(F32)
        off = x - jnp.mean(x, axis=-1, keepdims=True)
        spread = lax.rsqrt(jnp.mean(off * off, axis=-1, keepdims=True) + 1e-05)
        hat = off * spread
        hat_ref[s] = hat
        spread_ref[s] = jnp.broadcast_to(spread, spread_ref.shape[1:])
        normed = (hat * gain + bias).astype(BF16)
        total += dot_t(normed, diag[:, s * channels : (s + 1) * channels])
    out_ref[0] = (total * mask).astype(BF16)


def weights_kernel(w_hbm, by_left, by_right, swap, held, wide, sem):
    (copy,) = load_all([(w_hbm, held)], sem)
    width = by_left.shape[0]
    cz = held.shape[1]
    span = swap.shape[0]
    to = lax.broadcasted_iota(jnp.int32, (span, span), 0)
    at = lax.broadcasted_iota(jnp.int32, (span, span), 1)
    swap[...] = jnp.where((to // BUNCH == at % width) & (to % BUNCH == at // width), 1.0, 0.0).astype(BF16)
    copy.wait()
    wide[...] = held[...].astype(F32)
    for n in range(width):
        by_left[:, n * cz : (n + 1) * cz] = wide[pl.ds(n, width, stride=width), :].astype(BF16)
        by_right[:, n * cz : (n + 1) * cz] = held[n * width : (n + 1) * width, :]


def scale_kernel(*refs):
    sources, outs, held, (wide, sems) = refs[:4], refs[4:9], refs[9:13], refs[13:]
    scaled, turned, inverse_ref, row_ref, shift_out = outs
    seq_ref, res_ref, shift_ref, loss_ref = held
    copies = load_all(list(zip(sources, held)), sems)
    row_at, column_at = place()
    rows, length, cz = loss_ref.shape
    for copy in copies[:3]:
        copy.wait()
    present = jnp.sum(flag_row(seq_ref), axis=1, keepdims=True)
    columns = flag_column(res_ref, column_at * length, length)
    inverse = jnp.broadcast_to(1.0 / jnp.maximum(present * columns, 1.0), (length, cz))
    inverse_ref[...] = inverse
    row_ref[...] = jnp.broadcast_to(flag_column(res_ref, row_at * rows, rows), (rows, cz))
    shift_out[...] = jnp.broadcast_to(shift_ref[...].reshape(1, cz), shift_out.shape)
    copies[3].wait()
    for i in range(rows):
        factor = jnp.where(row_ref[i : i + 1, :] > 0.0, inverse, 1.0)
        made = loss_ref[i].astype(F32) * factor
        wide[i * length : (i + 1) * length, :] = made
        scaled[:, i * cz : (i + 1) * cz] = made.astype(BF16)
    for j in range(length):
        turned[:, j * cz : (j + 1) * cz] = wide[pl.ds(j, rows, stride=length), :].astype(BF16)


def stack_kernel(own, got, out):
    count = own.shape[0]
    out[:count] = own[...]
    out[count:] = got[...]


def lefts_kernel(own, got, out):
    count, _, half = out.shape
    for n in range(count // 2):
        out[n] = own[n, :, :half]
        out[count // 2 + n] = got[n, :, :half]


def select_kernel(bit, own, got, out):
    row_at, column_at = place()
    other = (row_at ^ column_at) >> bit & 1

    @pl.when(other == 1)
    def _():
        out[...] = got[...]

    @pl.when(other == 0)
    def _():
        out[...] = own[...]


def add_kernel(own, got, out):
    out[...] = (own[...].astype(F32) + got[...].astype(F32)).astype(BF16)


def source_of(n, count):
    mask, bit, step = 0, count // 2, 0
    while bit:
        mask |= (n >> step & 1) * bit
        bit //= 2
        step += 1
    return mask


def spread_rows(rows, source, block, width):
    length, half = block.shape
    seqs = half // width
    per_bunch = BUNCH // seqs
    wide = block.astype(F32)
    for s in range(seqs):
        spot = source % per_bunch * seqs + s
        rows[source // per_bunch, pl.ds(spot, length, stride=BUNCH), :] = wide[:, s * width : (s + 1) * width]


def produce(out, start, rows, step, weight):
    width = weight.shape[0]
    cz = weight.shape[1] // width
    span = BUNCH * width
    size = CHUNK * BUNCH
    for g in range(rows.shape[0]):
        taken = rows[g, lanes_at(step * size, size), :].astype(BF16)
        for n in range(width // 2):
            made = dot(taken, weight[:, n * 2 * cz : (n + 1) * 2 * cz]).astype(BF16)
            for a in range(2):
                top = g * span + (2 * n + a) * BUNCH
                for i in range(CHUNK):
                    out[top : top + BUNCH, lanes_at(start + i * cz, cz)] = made[
                        i * BUNCH : (i + 1) * BUNCH, a * cz : (a + 1) * cz
                    ]


def ungroup(out, acc, swap):
    span = swap.shape[0]
    half = out.shape[2]
    per_bunch = span // half
    for g in range(acc.shape[1] // span):
        made = dot(acc[:, g * span : (g + 1) * span].astype(BF16), swap[...]).astype(BF16)
        for k in range(per_bunch):
            out[g * per_bunch + k] = made[:, k * half : (k + 1) * half]


def left_kernel(own, got, swap, turned, weight, right_cols, out, ordered, rows, v_buf, acc):
    row_at, _ = place()
    count, length, half = out.shape
    span = swap.shape[0]
    width = weight.shape[0]
    cz = weight.shape[1] // width
    per_bunch = span // half
    for n in range(count):
        block = (own if n < count // 2 else got)[n % (count // 2), :, half:]
        source = row_at ^ source_of(n, count)
        ordered[source] = block
        spread_rows(rows, source, block, width)
    for g in range(count // per_bunch):
        right = jnp.concatenate([ordered[g * per_bunch + k] for k in range(per_bunch)], axis=1)
        right_cols[:, g * span : (g + 1) * span] = dot_t(right, swap[...]).astype(BF16)
    acc[...] = jnp.zeros_like(acc)

    def section(step, _):
        produce(v_buf, 0, rows, step, weight)
        acc[...] += dot_t(turned[:, lanes_at(step * CHUNK * cz, CHUNK * cz)], v_buf[...])
        return 0

    lax.fori_loop(0, turned.shape[1] // cz // CHUNK, section, 0)
    ungroup(out, acc, swap)


def t_kernel(bit, own, got, weight, t_ref, rows):
    row_at, column_at = place()
    count = own.shape[0]
    width = weight.shape[0]
    cz = weight.shape[1] // width
    other = (row_at ^ column_at) >> bit & 1
    for n in range(count):
        block = jnp.where(other == 1, got[n].astype(F32), own[n].astype(F32))
        spread_rows(rows, row_at ^ source_of(n, count), block, width)

    def section(step, _):
        produce(t_ref, step * CHUNK * cz, rows, step, weight)
        return 0

    lax.fori_loop(0, t_ref.shape[1] // cz // CHUNK, section, 0)


def right_kernel(t_ref, scaled, swap, own, got, keep, send, acc, blocks):
    row_at, column_at = place()
    count, length, half = blocks.shape
    size = CHUNK * (scaled.shape[1] // length)
    acc[...] = jnp.zeros_like(acc)

    def section(step, _):
        lanes = lanes_at(step * size, size)
        acc[...] += dot_t(t_ref[:, lanes], scaled[:, lanes])
        return 0

    lax.fori_loop(0, scaled.shape[1] // size, section, 0)
    ungroup(blocks, jnp.transpose(acc[...]), swap)
    mine = jnp.where(row_at == column_at, 1.0, 0.0)
    low = row_at & 1
    for n in range(count // 2):
        for ref, spot in ((keep, 2 * n + low), (send, 2 * n + 1 - low)):
            ref[n, :, :half] = ((own[spot].astype(F32) + got[spot].astype(F32)) * mine).astype(BF16)
            ref[n, :, half:] = blocks[spot]


def halve_kernel(bit, own, got, keep, send):
    row_at, _ = place()
    low = row_at >> bit & 1
    for n in range(keep.shape[0]):
        for ref, spot in ((keep, 2 * n + low), (send, 2 * n + 1 - low)):
            ref[n] = (own[spot].astype(F32) + got[spot].astype(F32)).astype(BF16)


def pair_kernel(first, right_cols, t_ref, shift_ref, inverse_ref, row_ref, *refs):
    out_ref, held, sems = refs[-3:]
    rows, length, cz = held.shape
    steps = rows // CHUNK

    def copy(step):
        return pltpu.make_async_copy(
            held.at[pl.ds(step * CHUNK, CHUNK)],
            out_ref.at[pl.ds(first + step * CHUNK, CHUNK)],
            sems.at[step],
        )

    def section(step, _):
        flags = row_ref[pl.ds(pl.multiple_of(first + step * CHUNK, CHUNK), CHUNK), :]
        for n in range(CHUNK // 2):
            made = dot(right_cols[...], t_ref[:, lanes_at((first + step * CHUNK + 2 * n) * cz, 2 * cz)])
            for a in range(2):
                i = 2 * n + a
                factor = jnp.where(flags[i : i + 1, :] > 0.0, inverse_ref[...], 1.0)
                held[step * CHUNK + i] = (
                    (made[:, a * cz : (a + 1) * cz] + shift_ref[:1, :]) * factor
                ).astype(BF16)
        copy(step).start()
        return 0

    lax.fori_loop(0, steps, section, 0)
    for step in range(steps):
        copy(step).wait()


def finish_kernel(own, got, mask_ref, diag, gain_ref, hat_ref, spread_ref, out_ref):
    seqs, _, channels = hat_ref.shape
    both = ((own[0].astype(F32) + got[0].astype(F32)) * mask_ref[...]).astype(BF16)
    gain = gain_ref[:1, :]
    for s in range(seqs):
        hat = hat_ref[s]
        grad = dot(both, diag[:, s * channels : (s + 1) * channels]) * gain
        out_ref[s] = (
            spread_ref[s][:, :1]
            * (
                grad
                - jnp.mean(grad, axis=-1, keepdims=True)
                - hat * jnp.mean(grad * hat, axis=-1, keepdims=True)
            )
        ).astype(BF16)


VMEM = pl.BlockSpec(memory_space=pltpu.VMEM)
HBM = pl.BlockSpec(memory_space=pltpu.HBM)


def call(kernel, name, out_shape, scratch, micros, in_specs=None, out_specs=None, limit=24, aliases=None):
    def run(*args):
        specs = [VMEM] * len(args) if in_specs is None else in_specs
        outs = jax.tree.map(lambda _: VMEM, out_shape) if out_specs is None else out_specs
        return pl.pallas_call(
            kernel,
            out_shape=out_shape,
            in_specs=specs,
            out_specs=outs,
            scratch_shapes=scratch,
            input_output_aliases=aliases or {},
            compiler_params=pltpu.CompilerParams(vmem_limit_bytes=limit * 1024 * 1024),
            cost_estimate=pl.CostEstimate(flops=int(micros * 1e9), bytes_accessed=0, transcendentals=0),
            name=name,
        )(*args)

    return run


def swap_rows(x, blocks, bit):
    moves = [(z * blocks + c, (z ^ bit) * blocks + c) for z in range(blocks) for c in range(blocks)]
    return lax.ppermute(x, PLACES, moves)


def swap_columns(x, blocks, bit):
    moves = [(z * blocks + c, z * blocks + (c ^ bit)) for z in range(blocks) for c in range(blocks)]
    return lax.ppermute(x, PLACES, moves)


def per_device(
    homolog_activations,
    homolog_valid_flags,
    position_valid_flags,
    centering_factor,
    centering_shift,
    first_factor_matrix,
    second_factor_matrix,
    couple_weight_matrix,
    couple_shift_vector,
    loss_sensitivity,
):
    seqs, length, channels = homolog_activations.shape
    total_seq = homolog_valid_flags.shape[0]
    total_res = position_valid_flags.shape[0]
    width = first_factor_matrix.shape[1]
    rows, columns, cz = loss_sensitivity.shape
    blocks = lax.axis_size("cols") * lax.axis_size("sub")
    steps = blocks.bit_length() - 1
    assert blocks == 1 << steps == lax.axis_size("rows") and steps > 0
    half = seqs * width
    span = BUNCH * width
    deep = total_seq * width
    bunches = total_seq // BUNCH
    shape = jax.ShapeDtypeStruct

    def far(x):
        return pltpu.with_memory_space_constraint(x, pltpu.HBM)

    seq_flags, res_flags = far(homolog_valid_flags), far(position_valid_flags)

    stack, diag, mask, hat, spread, gain = call(
        project_kernel,
        "project",
        (
            shape((1, length, 2 * half), BF16),
            shape((2 * half, seqs * channels), BF16),
            shape((length, 2 * half), F32),
            shape((seqs, length, channels), F32),
            shape((seqs, length, cz), F32),
            shape((8, channels), F32),
        ),
        [
            pltpu.VMEM((total_seq,), jnp.int32),
            pltpu.VMEM((seqs, length, channels), BF16),
            pltpu.VMEM((total_res,), jnp.int32),
            pltpu.VMEM((channels,), F32),
            pltpu.VMEM((channels,), F32),
            pltpu.VMEM((width, channels), BF16),
            pltpu.VMEM((width, channels), BF16),
            pltpu.SemaphoreType.DMA((7,)),
        ],
        2,
        in_specs=[HBM] * 7,
    )(
        seq_flags,
        far(homolog_activations),
        res_flags,
        far(centering_factor),
        far(centering_shift),
        far(first_factor_matrix.T),
        far(second_factor_matrix.T),
    )

    by_left, by_right, swap = call(
        weights_kernel,
        "weights",
        (shape((width, width * cz), BF16), shape((width, width * cz), BF16), shape((span, span), BF16)),
        [
            pltpu.VMEM((width * width, cz), BF16),
            pltpu.VMEM((width * width, cz), F32),
            pltpu.SemaphoreType.DMA((1,)),
        ],
        1.5,
        in_specs=[HBM],
    )(far(couple_weight_matrix))

    scaled, turned, inverse, row_flags, shift = call(
        scale_kernel,
        "scale",
        (
            shape((columns, rows * cz), BF16),
            shape((rows, columns * cz), BF16),
            shape((columns, cz), F32),
            shape((rows, cz), F32),
            shape((8, cz), F32),
        ),
        [
            pltpu.VMEM((total_seq,), jnp.int32),
            pltpu.VMEM((total_res,), jnp.int32),
            pltpu.VMEM((cz,), F32),
            pltpu.VMEM((rows, columns, cz), BF16),
            pltpu.VMEM((rows * columns, cz), F32),
            pltpu.SemaphoreType.DMA((4,)),
        ],
        2,
        in_specs=[HBM] * 4,
    )(seq_flags, res_flags, far(couple_shift_vector), far(loss_sensitivity))

    for step in range(steps):
        got = swap_rows(stack, blocks, blocks >> (step + 1))
        if step < steps - 1:
            stack = call(stack_kernel, "stack", shape((2 << step, length, 2 * half), BF16), [], 0.3)(stack, got)
    own_stack, got_stack = stack, got

    all_blocks = shape((blocks, length, half), BF16)
    lefts = call(lefts_kernel, "lefts", all_blocks, [], 0.3)(own_stack, got_stack)
    for step in range(steps):
        got = swap_columns(lefts, blocks, 1 << step)
        if step < steps - 1:
            lefts = call(functools.partial(select_kernel, step), "select", all_blocks, [], 0.3)(lefts, got)
    got_lefts = got

    right_cols, left_sum = call(
        left_kernel,
        "left_gradient",
        (shape((columns, deep), BF16), all_blocks),
        [
            pltpu.VMEM((blocks, length, half), BF16),
            pltpu.VMEM((bunches, columns * BUNCH, width), F32),
            pltpu.VMEM((deep, CHUNK * cz), BF16),
            pltpu.VMEM((rows, deep), F32),
        ],
        6,
    )(own_stack, got_stack, swap, turned, by_right)
    for step in reversed(range(steps)):
        got = swap_columns(left_sum, blocks, 1 << step)
        if step > 0:
            left_sum = call(add_kernel, "add", all_blocks, [], 0.3)(left_sum, got)
    got_sum = got

    t_limit = 16 + deep * rows * cz * 2 // 2**20
    t_all = call(
        functools.partial(t_kernel, steps - 1),
        "expand",
        shape((deep, rows * cz), BF16),
        [pltpu.VMEM((bunches, rows * BUNCH, width), F32)],
        3,
        limit=t_limit,
    )(lefts, got_lefts, by_left)

    some = shape((blocks // 2, length, 2 * half), BF16)
    keep, send = call(
        right_kernel,
        "right_gradient",
        (some, some),
        [pltpu.VMEM((deep, columns), F32), pltpu.VMEM((blocks, length, half), BF16)],
        3,
        limit=t_limit,
    )(t_all, scaled, swap, left_sum, got_sum)
    for step in range(steps):
        got = swap_rows(send, blocks, 1 << step)
        if step < steps - 1:
            some = shape((blocks >> (step + 2), length, 2 * half), BF16)
            keep, send = call(functools.partial(halve_kernel, step + 1), "halve", (some, some), [], 0.3)(
                keep, got
            )

    pair = None
    for part in range(2):
        some = () if pair is None else (pair,)
        pair = call(
            functools.partial(pair_kernel, part * rows // 2),
            "pair",
            shape(loss_sensitivity.shape, BF16),
            [
                pltpu.VMEM((rows // 2, columns, cz), BF16),
                pltpu.SemaphoreType.DMA((rows // 2 // CHUNK,)),
            ],
            2,
            in_specs=[VMEM] * 5 + [HBM] * len(some),
            out_specs=HBM,
            limit=t_limit,
            aliases={5: 0} if some else None,
        )(right_cols, t_all, shift, inverse, row_flags, *some)

    alignment = call(finish_kernel, "finish", shape(homolog_activations.shape, BF16), [], 1)(
        keep, got, mask, diag, gain, hat, spread
    )
    return pair, alignment


def solution(mesh):
    split = P(("groups", "rows"), ("cols", "sub"), None)
    return jax.shard_map(
        per_device,
        mesh=mesh,
        in_specs=(split, P("groups"), P("groups"), P(), P(), P(), P(), P(), P(), split),
        out_specs=(split, split),
        check_vma=False,
    )
```

```python
import functools

import jax
import jax.numpy as jnp
from jax import lax
from jax.experimental import pallas as pl
from jax.experimental.pallas import tpu as pltpu
from jax.sharding import PartitionSpec as P

F32 = jnp.float32
BF16 = jnp.bfloat16
PLACES = ("rows", "cols", "sub")
CHUNK = 32
PASS = 16


def dot(a, b):
    return lax.dot_general(a, b, (((1,), (0,)), ((), ())), preferred_element_type=F32)


def dot_t(a, b):
    return lax.dot_general(a, b, (((1,), (1,)), ((), ())), preferred_element_type=F32)


def place():
    column = lax.axis_index("cols") * lax.axis_size("sub") + lax.axis_index("sub")
    return lax.axis_index("rows"), column


def lanes_at(start, size):
    return pl.ds(pl.multiple_of(start, size), size)


def flag_row(flags_ref):
    return flags_ref[...].astype(F32).reshape(1, -1)


def flag_column(flags_ref, start, length):
    flags = flag_row(flags_ref)
    total = flags.shape[1]
    spot = lax.broadcasted_iota(jnp.int32, (length, total), 0) + start
    lane = lax.broadcasted_iota(jnp.int32, (length, total), 1)
    return jnp.sum(jnp.where(spot == lane, flags, 0.0), axis=1, keepdims=True)


def load_all(pairs, sems):
    copies = [pltpu.make_async_copy(src, dst, sems.at[n]) for n, (src, dst) in enumerate(pairs)]
    for copy in copies:
        copy.start()
    return copies


def project_kernel(*refs):
    sources, outs, (loss_ref, w_ref), held, sems = refs[:9], refs[9:15], refs[15:17], refs[17:24], refs[24]
    out_ref, diag, mask_ref, hat_ref, spread_ref, gain_out = outs
    copies = load_all(list(zip(sources, held + (w_ref, loss_ref))), sems)
    seq_ref, x_ref, res_ref, gain_ref, bias_ref, first_ref, second_ref = held
    row_at, column_at = place()
    seqs, length, channels = x_ref.shape
    width = first_ref.shape[0]
    half = seqs * width
    diag[...] = jnp.zeros_like(diag)
    for copy in copies[:7]:
        copy.wait()
    for s in range(seqs):
        lanes = slice(s * channels, (s + 1) * channels)
        diag[s * width : (s + 1) * width, lanes] = first_ref[...]
        diag[(seqs + s) * width : (seqs + s + 1) * width, lanes] = second_ref[...]
    flags = flag_row(seq_ref)
    spot = lax.broadcasted_iota(jnp.int32, flags.shape, 1)
    which = lax.broadcasted_iota(jnp.int32, (1, 2 * half), 1) % half // width
    own = jnp.zeros((1, 2 * half), F32)
    for s in range(seqs):
        value = jnp.sum(jnp.where(spot == row_at * seqs + s, flags, 0.0), axis=1, keepdims=True)
        own = jnp.where(which == s, value, own)
    mask = flag_column(res_ref, column_at * length, length) * own
    mask_ref[...] = mask
    gain = gain_ref[...].reshape(1, channels)
    bias = bias_ref[...].reshape(1, channels)
    gain_out[...] = jnp.broadcast_to(gain, gain_out.shape)
    total = jnp.zeros((length, 2 * half), F32)
    for s in range(seqs):
        x = x_ref[s].astype(F32)
        off = x - jnp.mean(x, axis=-1, keepdims=True)
        spread = lax.rsqrt(jnp.mean(off * off, axis=-1, keepdims=True) + 1e-05)
        hat = off * spread
        hat_ref[s] = hat
        spread_ref[s] = jnp.broadcast_to(spread, spread_ref.shape[1:])
        normed = (hat * gain + bias).astype(BF16)
        total += dot_t(normed, diag[:, s * channels : (s + 1) * channels])
    out_ref[0] = (total * mask).astype(BF16)
    for copy in copies[7:]:
        copy.wait()


def prepare_kernel(*refs):
    sources, (loss_ref, w_ref), outs, held, (wide_w, wide, sems) = (
        refs[:3],
        refs[3:5],
        refs[5:13],
        refs[13:16],
        refs[16:],
    )
    by_left, by_right, swap, scaled, turned, inverse_ref, row_ref, shift_out = outs
    seq_ref, res_ref, shift_ref = held
    copies = load_all(list(zip(sources, held)), sems)
    row_at, column_at = place()
    rows, length, cz = loss_ref.shape
    width = by_left.shape[0]
    span = swap.shape[0]
    deep = span // width
    wide_w[...] = w_ref[...].astype(F32)
    for n in range(width):
        by_left[:, n * cz : (n + 1) * cz] = wide_w[pl.ds(n, width, stride=width), :].astype(BF16)
        by_right[:, n * cz : (n + 1) * cz] = w_ref[n * width : (n + 1) * width, :]
    to = lax.broadcasted_iota(jnp.int32, (span, span), 0)
    at = lax.broadcasted_iota(jnp.int32, (span, span), 1)
    swap[...] = jnp.where((to // deep == at % width) & (to % deep == at // width), 1.0, 0.0).astype(BF16)
    for copy in copies:
        copy.wait()
    present = jnp.sum(flag_row(seq_ref), axis=1, keepdims=True)
    columns = flag_column(res_ref, column_at * length, length)
    inverse = jnp.broadcast_to(1.0 / jnp.maximum(present * columns, 1.0), (length, cz))
    inverse_ref[...] = inverse
    row_ref[...] = jnp.broadcast_to(flag_column(res_ref, row_at * rows, rows), (rows, cz))
    shift_out[...] = jnp.broadcast_to(shift_ref[...].reshape(1, cz), shift_out.shape)
    for i in range(rows):
        factor = jnp.where(row_ref[i : i + 1, :] > 0.0, inverse, 1.0)
        made = loss_ref[i].astype(F32) * factor
        wide[i * length : (i + 1) * length, :] = made
        scaled[:, i * cz : (i + 1) * cz] = made.astype(BF16)
    for j in range(length):
        turned[:, j * cz : (j + 1) * cz] = wide[pl.ds(j, rows, stride=length), :].astype(BF16)


def stack_kernel(own, got, *refs):
    out = refs[-1]
    count = own.shape[0]
    out[:count] = own[...]
    out[count:] = got[...]


def lefts_kernel(own, got, *refs):
    out = refs[-1]
    count, _, half = out.shape
    for n in range(count // 2):
        out[n] = own[n, :, :half]
        out[count // 2 + n] = got[n, :, :half]


def select_kernel(bit, own, got, *refs):
    out = refs[-1]
    row_at, column_at = place()
    other = (row_at ^ column_at) >> bit & 1

    @pl.when(other == 1)
    def _():
        out[...] = got[...]

    @pl.when(other == 0)
    def _():
        out[...] = own[...]


def add_kernel(own, got, *refs):
    out = refs[-1]
    out[...] = (own[...].astype(F32) + got[...].astype(F32)).astype(BF16)


def spread_rows(rows, n, block, width, deep):
    length, half = block.shape
    seqs = half // width
    wide = block.astype(F32)
    for s in range(seqs):
        rows[pl.ds(n * seqs + s, length, stride=deep), :] = wide[:, s * width : (s + 1) * width]


def produce(out, top, start, rows, step, weight, deep):
    width = weight.shape[0]
    cz = weight.shape[1] // width
    size = CHUNK * deep
    taken = rows[lanes_at(step * size, size), :].astype(BF16)
    for n in range(width // 2):
        made = dot(taken, weight[:, n * 2 * cz : (n + 1) * 2 * cz])
        for i in range(CHUNK):
            both = jnp.concatenate(
                [made[i * deep : (i + 1) * deep, a * cz : (a + 1) * cz] for a in range(2)], axis=0
            )
            low = top + n * 2 * deep
            out[low : low + 2 * deep, lanes_at(start + i * cz, cz)] = both.astype(BF16)


def ungroup(out, acc, swap):
    half = out.shape[2]
    made = dot(acc.astype(BF16), swap[...]).astype(BF16)
    for k in range(out.shape[0]):
        out[k] = made[:, k * half : (k + 1) * half]


def left_kernel(first, last, ends, *refs):
    stack, swap, turned, weight = refs[:4]
    right_cols, out, rows, v_buf, acc = refs[-5:]
    count, _, both = stack.shape
    width = weight.shape[0]
    cz = weight.shape[1] // width
    deep = swap.shape[0] // width
    for n in range(count):
        spread_rows(rows, n, stack[n, :, both // 2 :], width, deep)
    if first > 0:
        acc[...] = refs[4][...]
    else:
        acc[...] = jnp.zeros_like(acc)

    def section(step, _):
        produce(v_buf, 0, 0, rows, step, weight, deep)
        acc[...] += dot_t(turned[:, lanes_at(step * CHUNK * cz, CHUNK * cz)], v_buf[...])
        return 0

    lax.fori_loop(first, last, section, 0)
    if ends:
        right = jnp.concatenate([stack[n, :, both // 2 :] for n in range(count)], axis=1)
        right_cols[...] = dot_t(right, swap[...]).astype(BF16)
        ungroup(out, acc[...], swap)
    else:
        out[...] = acc[...]


def t_kernel(bit, own, got, weight, *refs):
    t_ref, rows = refs[-2:]
    row_at, column_at = place()
    count = own.shape[0]
    width = weight.shape[0]
    cz = weight.shape[1] // width
    span = t_ref.shape[0] // 2
    deep = span // width
    other = (row_at ^ column_at) >> bit & 1
    for h in range(2):
        for n in range(count // 2):
            k = h * count // 2 + n
            block = jnp.where(other == 1, got[k].astype(F32), own[k].astype(F32))
            spread_rows(rows.at[h], n, block, width, deep)

    def section(step, _):
        for h in range(2):
            produce(t_ref, h * span, step * CHUNK * cz, rows.at[h], step, weight, deep)
        return 0

    lax.fori_loop(0, t_ref.shape[1] // cz // CHUNK, section, 0)


def right_kernel(part, t_ref, scaled, swap, *refs):
    out = refs[-1]
    span = swap.shape[0]
    ungroup(out, dot_t(scaled[...], t_ref[part * span : (part + 1) * span, :]), swap)


def join_kernel(part, right, own, got, out):
    row_at, column_at = place()
    mine = jnp.where(row_at == column_at, 1.0, 0.0)
    half = right.shape[2]
    count = right.shape[0]
    for n in range(count):
        k = part * count + n
        out[n, :, :half] = ((own[k].astype(F32) + got[k].astype(F32)) * mine).astype(BF16)
    out[:, :, half:] = right[...]


def halve_kernel(own, got, *refs):
    keep, send = refs[-2:]
    count = keep.shape[0]
    keep[...] = (own[:count].astype(F32) + got[:count].astype(F32)).astype(BF16)
    send[...] = (own[count:].astype(F32) + got[count:].astype(F32)).astype(BF16)


def pair_kernel(first, low_cols, high_cols, t_ref, shift_ref, inverse_ref, row_ref, *refs):
    out_ref, done_ref, held, sems = refs[-4:]
    rows, length, cz = held.shape
    steps = rows // PASS
    done_ref[...] = jnp.zeros_like(done_ref)
    span = low_cols.shape[1]

    def copy(step):
        return pltpu.make_async_copy(
            held.at[pl.ds(step * PASS, PASS)],
            out_ref.at[pl.ds(first + step * PASS, PASS)],
            sems.at[step],
        )

    def section(step, _):
        flags = row_ref[pl.ds(pl.multiple_of(first + step * PASS, PASS), PASS), :]
        right = jnp.concatenate([low_cols[...], high_cols[...]], axis=1)
        for n in range(PASS // 2):
            made = dot(right, t_ref[:, lanes_at((first + step * PASS + 2 * n) * cz, 2 * cz)])
            for a in range(2):
                i = 2 * n + a
                factor = jnp.where(flags[i : i + 1, :] > 0.0, inverse_ref[...], 1.0)
                held[step * PASS + i] = (
                    (made[:, a * cz : (a + 1) * cz] + shift_ref[:1, :]) * factor
                ).astype(BF16)
        copy(step).start()
        return 0

    lax.fori_loop(0, steps, section, 0)
    for step in range(steps):
        copy(step).wait()


def finish_kernel(own, got, mask_ref, diag, gain_ref, hat_ref, spread_ref, out_ref):
    seqs, _, channels = hat_ref.shape
    both = ((own[0].astype(F32) + got[0].astype(F32)) * mask_ref[...]).astype(BF16)
    gain = gain_ref[:1, :]
    for s in range(seqs):
        hat = hat_ref[s]
        grad = dot(both, diag[:, s * channels : (s + 1) * channels]) * gain
        out_ref[s] = (
            spread_ref[s][:, :1]
            * (
                grad
                - jnp.mean(grad, axis=-1, keepdims=True)
                - hat * jnp.mean(grad * hat, axis=-1, keepdims=True)
            )
        ).astype(BF16)


VMEM = pl.BlockSpec(memory_space=pltpu.VMEM)
HBM = pl.BlockSpec(memory_space=pltpu.HBM)


def call(kernel, name, out_shape, scratch, micros, in_specs=None, out_specs=None, limit=24, aliases=None, after=()):
    def run(*args):
        specs = [VMEM] * len(args) if in_specs is None else in_specs
        specs, args = specs + [pl.BlockSpec(memory_space=pl.ANY)] * len(after), args + tuple(after)
        outs = jax.tree.map(lambda _: VMEM, out_shape) if out_specs is None else out_specs
        return pl.pallas_call(
            kernel,
            out_shape=out_shape,
            in_specs=specs,
            out_specs=outs,
            scratch_shapes=scratch,
            input_output_aliases=aliases or {},
            compiler_params=pltpu.CompilerParams(vmem_limit_bytes=limit * 1024 * 1024),
            cost_estimate=pl.CostEstimate(flops=int(micros * 1e8), bytes_accessed=0, transcendentals=0),
            name=name,
        )(*args)

    return run


def swap_rows(x, blocks, bit):
    moves = [(z * blocks + c, (z ^ bit) * blocks + c) for z in range(blocks) for c in range(blocks)]
    return lax.ppermute(x, PLACES, moves)


def swap_columns(x, blocks, bit):
    moves = [(z * blocks + c, z * blocks + (c ^ bit)) for z in range(blocks) for c in range(blocks)]
    return lax.ppermute(x, PLACES, moves)


def per_device(
    homolog_activations,
    homolog_valid_flags,
    position_valid_flags,
    centering_factor,
    centering_shift,
    first_factor_matrix,
    second_factor_matrix,
    couple_weight_matrix,
    couple_shift_vector,
    loss_sensitivity,
):
    seqs, length, channels = homolog_activations.shape
    total_seq = homolog_valid_flags.shape[0]
    total_res = position_valid_flags.shape[0]
    width = first_factor_matrix.shape[1]
    rows, columns, cz = loss_sensitivity.shape
    blocks = lax.axis_size("cols") * lax.axis_size("sub")
    steps = blocks.bit_length() - 1
    assert blocks == 1 << steps == lax.axis_size("rows") and steps > 0
    half = seqs * width
    deep = total_seq // 2
    span = deep * width
    shape = jax.ShapeDtypeStruct

    def far(x):
        return pltpu.with_memory_space_constraint(x, pltpu.HBM)

    seq_flags, res_flags = far(homolog_valid_flags), far(position_valid_flags)

    stack, diag, mask, hat, spread, gain, loss, weights = call(
        project_kernel,
        "project",
        (
            shape((1, length, 2 * half), BF16),
            shape((2 * half, seqs * channels), BF16),
            shape((length, 2 * half), F32),
            shape((seqs, length, channels), F32),
            shape((seqs, length, cz), F32),
            shape((8, channels), F32),
            shape(loss_sensitivity.shape, BF16),
            shape(couple_weight_matrix.shape, BF16),
        ),
        [
            pltpu.VMEM((total_seq,), jnp.int32),
            pltpu.VMEM((seqs, length, channels), BF16),
            pltpu.VMEM((total_res,), jnp.int32),
            pltpu.VMEM((channels,), F32),
            pltpu.VMEM((channels,), F32),
            pltpu.VMEM((width, channels), BF16),
            pltpu.VMEM((width, channels), BF16),
            pltpu.SemaphoreType.DMA((9,)),
        ],
        2,
        in_specs=[HBM] * 9,
    )(
        seq_flags,
        far(homolog_activations),
        res_flags,
        far(centering_factor),
        far(centering_shift),
        far(first_factor_matrix.T),
        far(second_factor_matrix.T),
        far(couple_weight_matrix),
        far(loss_sensitivity),
    )

    by_left, by_right, swap, scaled, turned, inverse, row_flags, shift = call(
        prepare_kernel,
        "prepare",
        (
            shape((width, width * cz), BF16),
            shape((width, width * cz), BF16),
            shape((span, span), BF16),
            shape((columns, rows * cz), BF16),
            shape((rows, columns * cz), BF16),
            shape((columns, cz), F32),
            shape((rows, cz), F32),
            shape((8, cz), F32),
        ),
        [
            pltpu.VMEM((total_seq,), jnp.int32),
            pltpu.VMEM((total_res,), jnp.int32),
            pltpu.VMEM((cz,), F32),
            pltpu.VMEM((width * width, cz), F32),
            pltpu.VMEM((rows * columns, cz), F32),
            pltpu.SemaphoreType.DMA((3,)),
        ],
        3,
        in_specs=[HBM] * 3 + [VMEM] * 2,
    )(seq_flags, res_flags, far(couple_shift_vector), loss, weights)

    for step in range(steps):
        got = swap_rows(stack, blocks, blocks >> (step + 1))
        if step < steps - 1:
            stack = call(
                stack_kernel, "stack", shape((2 << step, length, 2 * half), BF16), [], 0.1, after=(shift,)
            )(stack, got)
    low_stack, high_stack = stack, got

    half_blocks = shape((blocks // 2, length, half), BF16)
    all_blocks = shape((blocks, length, half), BF16)
    cols_shape = shape((columns, span), BF16)

    def left_part(stack, first, last, *more, after=()):
        ends = last == columns // CHUNK
        return call(
            functools.partial(left_kernel, first, last, ends),
            "left_gradient",
            (cols_shape, half_blocks if ends else shape((rows, span), F32)),
            [
                pltpu.VMEM((columns * deep, width), F32),
                pltpu.VMEM((span, CHUNK * cz), BF16),
                pltpu.VMEM((rows, span), F32),
            ],
            3 * (last - first) * CHUNK / columns,
            after=after,
        )(stack, swap, turned, by_right, *more)

    low_cols, low_sum = left_part(low_stack, 0, columns // CHUNK)
    lefts = call(lefts_kernel, "lefts", all_blocks, [], 0.1, after=(low_sum,))(low_stack, high_stack)
    got = swap_columns(lefts, blocks, 1)
    _, partial_sum = left_part(high_stack, 0, 1, after=(lefts,))
    for step in range(1, steps):
        lefts = call(
            functools.partial(select_kernel, step - 1), "select", all_blocks, [], 0.1, after=(partial_sum,)
        )(lefts, got)
        got = swap_columns(lefts, blocks, 1 << step)
    got_lefts = got
    high_cols, high_sum = left_part(high_stack, 1, columns // CHUNK, partial_sum, after=(lefts,))
    sums = call(stack_kernel, "stack", all_blocks, [], 0.1)(low_sum, high_sum)

    for step in reversed(range(1, steps)):
        got = swap_columns(sums, blocks, 1 << step)
        if step > 1:
            sums = call(add_kernel, "add", all_blocks, [], 0.1)(sums, got)
    t_limit = 16 + 2 * span * rows * cz * 2 // 2**20
    t_all = call(
        functools.partial(t_kernel, steps - 1),
        "expand",
        shape((2 * span, rows * cz), BF16),
        [pltpu.VMEM((2, rows * deep, width), F32)],
        3,
        limit=t_limit,
        after=(sums,),
    )(lefts, got_lefts, by_left)
    sums = call(add_kernel, "add", all_blocks, [], 0.1, after=(t_all,))(sums, got)
    got = swap_columns(sums, blocks, 1)

    def right_part(part, *after):
        return call(
            functools.partial(right_kernel, part),
            "right_gradient",
            half_blocks,
            [],
            1.5,
            limit=t_limit,
            after=after,
        )(t_all, scaled, swap)

    def join(part, right):
        return call(
            functools.partial(join_kernel, part),
            "join",
            shape((blocks // 2, length, 2 * half), BF16),
            [],
            0.1,
        )(right, sums, got)

    send = join(1, right_part(1, sums))
    got_send = swap_rows(send, blocks, 1)
    keep = join(0, right_part(0, send))

    def pair_part(start, stop, before, *after):
        some = () if before is None else (before,)
        return call(
            functools.partial(pair_kernel, start),
            "pair",
            (shape(loss_sensitivity.shape, BF16), shape((8, cz), F32)),
            [
                pltpu.VMEM((stop - start, columns, cz), BF16),
                pltpu.SemaphoreType.DMA(((stop - start) // PASS,)),
            ],
            3.5 * (stop - start) / rows,
            in_specs=[VMEM] * 6 + [HBM] * len(some),
            out_specs=(HBM, VMEM),
            limit=t_limit,
            aliases={6: 0} if some else None,
            after=after,
        )(low_cols, high_cols, t_all, shift, inverse, row_flags, *some)

    pair, paired = pair_part(0, rows // 4, None, keep)
    for step in range(1, steps):
        some = shape((blocks >> (step + 1), length, 2 * half), BF16)
        keep, send = call(halve_kernel, "halve", (some, some), [], 0.1, after=(paired,))(keep, got_send)
        got_send = swap_rows(send, blocks, 1 << step)
    pair, _ = pair_part(rows // 4, rows, pair, send)

    alignment = call(finish_kernel, "finish", shape(homolog_activations.shape, BF16), [], 1)(
        keep, got_send, mask, diag, gain, hat, spread
    )
    return pair, alignment


def solution(mesh):
    split = P(("groups", "rows"), ("cols", "sub"), None)
    return jax.shard_map(
        per_device,
        mesh=mesh,
        in_specs=(split, P("groups"), P("groups"), P(), P(), P(), P(), P(), P(), split),
        out_specs=(split, split),
        check_vma=False,
    )
```

```python
import functools

import jax
import jax.numpy as jnp
from jax import lax
from jax.experimental import pallas as pl
from jax.experimental.pallas import tpu as pltpu
from jax.sharding import PartitionSpec as P

F32 = jnp.float32
BF16 = jnp.bfloat16
PLACES = ("rows", "cols", "sub")
PRODUCED = 256


def dot(a, b):
    return lax.dot_general(a, b, (((1,), (0,)), ((), ())), preferred_element_type=F32)


def dot_t(a, b):
    return lax.dot_general(a, b, (((1,), (1,)), ((), ())), preferred_element_type=F32)


def place():
    column = lax.axis_index("cols") * lax.axis_size("sub") + lax.axis_index("sub")
    return lax.axis_index("rows"), column


def lanes_at(start, size):
    return pl.ds(pl.multiple_of(start, size), size)


def flag_row(flags_ref):
    return flags_ref[...].astype(F32).reshape(1, -1)


def flag_column(flags_ref, start, length):
    flags = flag_row(flags_ref)
    total = flags.shape[1]
    spot = lax.broadcasted_iota(jnp.int32, (length, total), 0) + start
    lane = lax.broadcasted_iota(jnp.int32, (length, total), 1)
    return jnp.sum(jnp.where(spot == lane, flags, 0.0), axis=1, keepdims=True)


def load_all(pairs, sems):
    copies = [pltpu.make_async_copy(src, dst, sems.at[n]) for n, (src, dst) in enumerate(pairs)]
    for copy in copies:
        copy.start()
    return copies


def project_kernel(*refs):
    sources, outs, (loss_ref, w_ref), held, sems = refs[:9], refs[9:15], refs[15:17], refs[17:24], refs[24]
    out_ref, diag, mask_ref, hat_ref, spread_ref, gain_out = outs
    copies = load_all(list(zip(sources, held + (w_ref, loss_ref))), sems)
    seq_ref, x_ref, res_ref, gain_ref, bias_ref, first_ref, second_ref = held
    row_at, column_at = place()
    seqs, length, channels = x_ref.shape
    width = first_ref.shape[0]
    half = seqs * width
    diag[...] = jnp.zeros_like(diag)
    for copy in copies[:7]:
        copy.wait()
    for s in range(seqs):
        lanes = slice(s * channels, (s + 1) * channels)
        diag[s * width : (s + 1) * width, lanes] = first_ref[...]
        diag[(seqs + s) * width : (seqs + s + 1) * width, lanes] = second_ref[...]
    flags = flag_row(seq_ref)
    spot = lax.broadcasted_iota(jnp.int32, flags.shape, 1)
    which = lax.broadcasted_iota(jnp.int32, (1, 2 * half), 1) % half // width
    own = jnp.zeros((1, 2 * half), F32)
    for s in range(seqs):
        value = jnp.sum(jnp.where(spot == row_at * seqs + s, flags, 0.0), axis=1, keepdims=True)
        own = jnp.where(which == s, value, own)
    mask = flag_column(res_ref, column_at * length, length) * own
    mask_ref[...] = mask
    gain = gain_ref[...].reshape(1, channels)
    bias = bias_ref[...].reshape(1, channels)
    gain_out[...] = jnp.broadcast_to(gain, gain_out.shape)
    total = jnp.zeros((length, 2 * half), F32)
    for s in range(seqs):
        x = x_ref[s].astype(F32)
        off = x - jnp.mean(x, axis=-1, keepdims=True)
        spread = lax.rsqrt(jnp.mean(off * off, axis=-1, keepdims=True) + 1e-05)
        hat = off * spread
        hat_ref[s] = hat
        spread_ref[s] = jnp.broadcast_to(spread, spread_ref.shape[1:])
        normed = (hat * gain + bias).astype(BF16)
        total += dot_t(normed, diag[:, s * channels : (s + 1) * channels])
    out_ref[0] = (total * mask).astype(BF16)
    for copy in copies[7:]:
        copy.wait()


def prepare_kernel(*refs):
    sources, (loss_ref, w_ref), outs, held, (wide_w, wide, sems) = (
        refs[:3],
        refs[3:5],
        refs[5:13],
        refs[13:16],
        refs[16:],
    )
    by_left, by_right, swap, scaled, turned, inverse_ref, row_ref, shift_out = outs
    seq_ref, res_ref, shift_ref = held
    copies = load_all(list(zip(sources, held)), sems)
    row_at, column_at = place()
    rows, length, cz = loss_ref.shape
    width = by_left.shape[0]
    span = swap.shape[0]
    deep = span // width
    wide_w[...] = w_ref[...].astype(F32)
    for n in range(width):
        by_left[:, n * cz : (n + 1) * cz] = wide_w[pl.ds(n, width, stride=width), :].astype(BF16)
        by_right[:, n * cz : (n + 1) * cz] = w_ref[n * width : (n + 1) * width, :]
    to = lax.broadcasted_iota(jnp.int32, (span, span), 0)
    at = lax.broadcasted_iota(jnp.int32, (span, span), 1)
    swap[...] = jnp.where((to // deep == at % width) & (to % deep == at // width), 1.0, 0.0).astype(BF16)
    for copy in copies:
        copy.wait()
    present = jnp.sum(flag_row(seq_ref), axis=1, keepdims=True)
    columns = flag_column(res_ref, column_at * length, length)
    inverse = jnp.broadcast_to(1.0 / jnp.maximum(present * columns, 1.0), (length, cz))
    inverse_ref[...] = inverse
    row_ref[...] = jnp.broadcast_to(flag_column(res_ref, row_at * rows, rows), (rows, cz))
    shift_out[...] = jnp.broadcast_to(shift_ref[...].reshape(1, cz), shift_out.shape)
    for i in range(rows):
        factor = jnp.where(row_ref[i : i + 1, :] > 0.0, inverse, 1.0)
        made = loss_ref[i].astype(F32) * factor
        wide[i * length : (i + 1) * length, :] = made
        scaled[:, i * cz : (i + 1) * cz] = made.astype(BF16)
    for j in range(length):
        turned[:, j * cz : (j + 1) * cz] = wide[pl.ds(j, rows, stride=length), :].astype(BF16)


def stack_kernel(own, got, *refs):
    out = refs[-1]
    count = own.shape[0]
    out[:count] = own[...]
    out[count:] = got[...]


def lefts_kernel(own, got, *refs):
    out = refs[-1]
    count, _, half = out.shape
    for n in range(count // 2):
        out[n] = own[n, :, :half]
        out[count // 2 + n] = got[n, :, :half]


def select_kernel(bit, own, got, *refs):
    out = refs[-1]
    row_at, column_at = place()
    other = (row_at ^ column_at) >> bit & 1

    @pl.when(other == 1)
    def _():
        out[...] = got[...]

    @pl.when(other == 0)
    def _():
        out[...] = own[...]


def add_kernel(own, got, *refs):
    out = refs[-1]
    out[...] = (own[...].astype(F32) + got[...].astype(F32)).astype(BF16)


def spread_rows(rows, n, block, width, deep):
    length, half = block.shape
    seqs = half // width
    wide = block.astype(F32)
    for s in range(seqs):
        rows[pl.ds(n * seqs + s, length, stride=deep), :] = wide[:, s * width : (s + 1) * width]


def produce(out, top, rows, weight, deep):
    width = weight.shape[0]
    cz = weight.shape[1] // width
    chunk = PRODUCED // deep

    def section(step, _):
        taken = rows[lanes_at(step * chunk * deep, chunk * deep), :].astype(BF16)
        for n in range(width // 2):
            made = dot(taken, weight[:, n * 2 * cz : (n + 1) * 2 * cz])
            for i in range(chunk):
                both = jnp.concatenate(
                    [made[i * deep : (i + 1) * deep, a * cz : (a + 1) * cz] for a in range(2)], axis=0
                )
                low = top + n * 2 * deep
                out[low : low + 2 * deep, lanes_at((step * chunk + i) * cz, cz)] = both.astype(BF16)
        return 0

    lax.fori_loop(0, rows.shape[0] // (chunk * deep), section, 0)


def v_kernel(stack, swap, weight, *refs):
    right_cols, v_ref, rows = refs[-3:]
    count, _, both = stack.shape
    width = weight.shape[0]
    deep = swap.shape[0] // width
    for n in range(count):
        spread_rows(rows, n, stack[n, :, both // 2 :], width, deep)
    right = jnp.concatenate([stack[n, :, both // 2 :] for n in range(count)], axis=1)
    right_cols[...] = dot_t(right, swap[...]).astype(BF16)
    produce(v_ref, 0, rows, weight, deep)


def t_kernel(bit, own, got, weight, *refs):
    t_ref, rows = refs[-2:]
    row_at, column_at = place()
    count = own.shape[0]
    width = weight.shape[0]
    span = t_ref.shape[0] // 2
    deep = span // width
    other = (row_at ^ column_at) >> bit & 1
    for h in range(2):
        for n in range(count // 2):
            k = h * count // 2 + n
            block = jnp.where(other == 1, got[k].astype(F32), own[k].astype(F32))
            spread_rows(rows.at[h], n, block, width, deep)
    for h in range(2):
        produce(t_ref, h * span, rows.at[h], weight, deep)


def contract_kernel(part, full_ref, scaled, swap, *refs):
    out = refs[-1]
    span = swap.shape[0]
    half = out.shape[2]
    size = scaled.shape[1] * PRODUCED // span

    def section(step, acc):
        lanes = lanes_at(step * size, size)
        return acc + dot_t(scaled[:, lanes], full_ref[part * span : (part + 1) * span, lanes])

    acc = dot_t(scaled[:, :size], full_ref[part * span : (part + 1) * span, :size])
    acc = lax.fori_loop(1, span // PRODUCED, section, acc)
    made = dot(acc.astype(BF16), swap[...]).astype(BF16)
    for k in range(out.shape[0]):
        out[k] = made[:, k * half : (k + 1) * half]


def join_kernel(part, right, own, got, out):
    row_at, column_at = place()
    mine = jnp.where(row_at == column_at, 1.0, 0.0)
    half = right.shape[2]
    count = right.shape[0]
    for n in range(count):
        k = part * count + n
        out[n, :, :half] = ((own[k].astype(F32) + got[k].astype(F32)) * mine).astype(BF16)
    out[:, :, half:] = right[...]


def halve_kernel(own, got, *refs):
    keep, send = refs[-2:]
    count = keep.shape[0]
    keep[...] = (own[:count].astype(F32) + got[:count].astype(F32)).astype(BF16)
    send[...] = (own[count:].astype(F32) + got[count:].astype(F32)).astype(BF16)


def pair_kernel(first, low_cols, high_cols, t_ref, shift_ref, inverse_ref, row_ref, *refs):
    out_ref, done_ref, held, sems = refs[-4:]
    rows, length, cz = held.shape
    steps = sems.shape[0]
    step_rows = rows // steps
    done_ref[...] = jnp.zeros_like(done_ref)
    span = low_cols.shape[1]

    def copy(step):
        return pltpu.make_async_copy(
            held.at[pl.ds(step * step_rows, step_rows)],
            out_ref.at[pl.ds(first + step * step_rows, step_rows)],
            sems.at[step],
        )

    def section(step, _):
        flags = row_ref[pl.ds(pl.multiple_of(first + step * step_rows, step_rows), step_rows), :]
        right = jnp.concatenate([low_cols[...], high_cols[...]], axis=1)
        for n in range(step_rows // 2):
            made = dot(right, t_ref[:, lanes_at((first + step * step_rows + 2 * n) * cz, 2 * cz)])
            for a in range(2):
                i = 2 * n + a
                factor = jnp.where(flags[i : i + 1, :] > 0.0, inverse_ref[...], 1.0)
                held[step * step_rows + i] = (
                    (made[:, a * cz : (a + 1) * cz] + shift_ref[:1, :]) * factor
                ).astype(BF16)
        copy(step).start()
        return 0

    lax.fori_loop(0, steps, section, 0)
    for step in range(steps):
        copy(step).wait()


def finish_kernel(own, got, mask_ref, diag, gain_ref, hat_ref, spread_ref, out_ref):
    seqs, _, channels = hat_ref.shape
    both = ((own[0].astype(F32) + got[0].astype(F32)) * mask_ref[...]).astype(BF16)
    gain = gain_ref[:1, :]
    for s in range(seqs):
        hat = hat_ref[s]
        grad = dot(both, diag[:, s * channels : (s + 1) * channels]) * gain
        out_ref[s] = (
            spread_ref[s][:, :1]
            * (
                grad
                - jnp.mean(grad, axis=-1, keepdims=True)
                - hat * jnp.mean(grad * hat, axis=-1, keepdims=True)
            )
        ).astype(BF16)


VMEM = pl.BlockSpec(memory_space=pltpu.VMEM)
HBM = pl.BlockSpec(memory_space=pltpu.HBM)


def call(kernel, name, out_shape, scratch, micros, in_specs=None, out_specs=None, limit=24, aliases=None, after=()):
    def run(*args):
        specs = [VMEM] * len(args) if in_specs is None else in_specs
        specs, args = specs + [pl.BlockSpec(memory_space=pl.ANY)] * len(after), args + tuple(after)
        outs = jax.tree.map(lambda _: VMEM, out_shape) if out_specs is None else out_specs
        return pl.pallas_call(
            kernel,
            out_shape=out_shape,
            in_specs=specs,
            out_specs=outs,
            scratch_shapes=scratch,
            input_output_aliases=aliases or {},
            compiler_params=pltpu.CompilerParams(vmem_limit_bytes=limit * 1024 * 1024),
            cost_estimate=pl.CostEstimate(flops=int(micros * 1e8), bytes_accessed=0, transcendentals=0),
            name=name,
        )(*args)

    return run


def swap_rows(x, blocks, bit):
    moves = [(z * blocks + c, (z ^ bit) * blocks + c) for z in range(blocks) for c in range(blocks)]
    return lax.ppermute(x, PLACES, moves)


def swap_columns(x, blocks, bit):
    moves = [(z * blocks + c, z * blocks + (c ^ bit)) for z in range(blocks) for c in range(blocks)]
    return lax.ppermute(x, PLACES, moves)


def per_device(
    homolog_activations,
    homolog_valid_flags,
    position_valid_flags,
    centering_factor,
    centering_shift,
    first_factor_matrix,
    second_factor_matrix,
    couple_weight_matrix,
    couple_shift_vector,
    loss_sensitivity,
):
    seqs, length, channels = homolog_activations.shape
    total_seq = homolog_valid_flags.shape[0]
    total_res = position_valid_flags.shape[0]
    width = first_factor_matrix.shape[1]
    rows, columns, cz = loss_sensitivity.shape
    blocks = lax.axis_size("cols") * lax.axis_size("sub")
    steps = blocks.bit_length() - 1
    assert blocks == 1 << steps == lax.axis_size("rows") and steps > 0
    half = seqs * width
    deep = total_seq // 2
    span = deep * width
    shape = jax.ShapeDtypeStruct

    def far(x):
        return pltpu.with_memory_space_constraint(x, pltpu.HBM)

    seq_flags, res_flags = far(homolog_valid_flags), far(position_valid_flags)

    stack, diag, mask, hat, spread, gain, loss, weights = call(
        project_kernel,
        "project",
        (
            shape((1, length, 2 * half), BF16),
            shape((2 * half, seqs * channels), BF16),
            shape((length, 2 * half), F32),
            shape((seqs, length, channels), F32),
            shape((seqs, length, cz), F32),
            shape((8, channels), F32),
            shape(loss_sensitivity.shape, BF16),
            shape(couple_weight_matrix.shape, BF16),
        ),
        [
            pltpu.VMEM((total_seq,), jnp.int32),
            pltpu.VMEM((seqs, length, channels), BF16),
            pltpu.VMEM((total_res,), jnp.int32),
            pltpu.VMEM((channels,), F32),
            pltpu.VMEM((channels,), F32),
            pltpu.VMEM((width, channels), BF16),
            pltpu.VMEM((width, channels), BF16),
            pltpu.SemaphoreType.DMA((9,)),
        ],
        2,
        in_specs=[HBM] * 9,
    )(
        seq_flags,
        far(homolog_activations),
        res_flags,
        far(centering_factor),
        far(centering_shift),
        far(first_factor_matrix.T),
        far(second_factor_matrix.T),
        far(couple_weight_matrix),
        far(loss_sensitivity),
    )

    by_left, by_right, swap, scaled, turned, inverse, row_flags, shift = call(
        prepare_kernel,
        "prepare",
        (
            shape((width, width * cz), BF16),
            shape((width, width * cz), BF16),
            shape((span, span), BF16),
            shape((columns, rows * cz), BF16),
            shape((rows, columns * cz), BF16),
            shape((columns, cz), F32),
            shape((rows, cz), F32),
            shape((8, cz), F32),
        ),
        [
            pltpu.VMEM((total_seq,), jnp.int32),
            pltpu.VMEM((total_res,), jnp.int32),
            pltpu.VMEM((cz,), F32),
            pltpu.VMEM((width * width, cz), F32),
            pltpu.VMEM((rows * columns, cz), F32),
            pltpu.SemaphoreType.DMA((3,)),
        ],
        3,
        in_specs=[HBM] * 3 + [VMEM] * 2,
    )(seq_flags, res_flags, far(couple_shift_vector), loss, weights)

    for step in range(steps):
        got = swap_rows(stack, blocks, blocks >> (step + 1))
        if step < steps - 1:
            stack = call(
                stack_kernel, "stack", shape((2 << step, length, 2 * half), BF16), [], 0.1, after=(shift,)
            )(stack, got)
    low_stack, high_stack = stack, got

    half_blocks = shape((blocks // 2, length, half), BF16)
    all_blocks = shape((blocks, length, half), BF16)
    cols_shape = shape((columns, span), BF16)
    t_limit = 16 + 2 * span * rows * cz * 2 // 2**20

    def make_v(stack, *after):
        return call(
            v_kernel,
            "expand_right",
            (cols_shape, shape((span, columns * cz), BF16)),
            [pltpu.VMEM((columns * deep, width), F32)],
            1.5,
            limit=t_limit,
            after=after,
        )(stack, swap, by_right)

    def contract(part, full, side, *after):
        return call(
            functools.partial(contract_kernel, part), "contract", half_blocks, [], 1.5, limit=t_limit, after=after
        )(full, side, swap)

    low_cols, v_low = make_v(low_stack)
    low_sum = contract(0, v_low, turned)
    lefts = call(lefts_kernel, "lefts", all_blocks, [], 0.1, after=(low_sum,))(low_stack, high_stack)
    got = swap_columns(lefts, blocks, 1)
    high_cols, v_high = make_v(high_stack, lefts)
    for step in range(1, steps):
        lefts = call(
            functools.partial(select_kernel, step - 1), "select", all_blocks, [], 0.1, after=(high_cols,)
        )(lefts, got)
        got = swap_columns(lefts, blocks, 1 << step)
    got_lefts = got
    high_sum = contract(0, v_high, turned, lefts)
    sums = call(stack_kernel, "stack", all_blocks, [], 0.1)(low_sum, high_sum)

    for step in reversed(range(1, steps)):
        got = swap_columns(sums, blocks, 1 << step)
        if step > 1:
            sums = call(add_kernel, "add", all_blocks, [], 0.1)(sums, got)
    t_all = call(
        functools.partial(t_kernel, steps - 1),
        "expand",
        shape((2 * span, rows * cz), BF16),
        [pltpu.VMEM((2, rows * deep, width), F32)],
        3,
        limit=t_limit,
        after=(sums,),
    )(lefts, got_lefts, by_left)
    sums = call(add_kernel, "add", all_blocks, [], 0.1, after=(t_all,))(sums, got)
    got = swap_columns(sums, blocks, 1)

    def join(part, right):
        return call(
            functools.partial(join_kernel, part),
            "join",
            shape((blocks // 2, length, 2 * half), BF16),
            [],
            0.1,
        )(right, sums, got)

    send = join(1, contract(1, t_all, scaled, sums))
    got_send = swap_rows(send, blocks, 1)
    keep = join(0, contract(0, t_all, scaled, send))

    def pair_part(start, stop, before, *after):
        some = () if before is None else (before,)
        return call(
            functools.partial(pair_kernel, start),
            "pair",
            (shape(loss_sensitivity.shape, BF16), shape((8, cz), F32)),
            [
                pltpu.VMEM((stop - start, columns, cz), BF16),
                pltpu.SemaphoreType.DMA(((stop - start) * span // (16 * PRODUCED),)),
            ],
            3.5 * (stop - start) / rows,
            in_specs=[VMEM] * 6 + [HBM] * len(some),
            out_specs=(HBM, VMEM),
            limit=t_limit,
            aliases={6: 0} if some else None,
            after=after,
        )(low_cols, high_cols, t_all, shift, inverse, row_flags, *some)

    pair, paired = pair_part(0, rows // 4, None, keep)
    for step in range(1, steps):
        some = shape((blocks >> (step + 1), length, 2 * half), BF16)
        keep, send = call(halve_kernel, "halve", (some, some), [], 0.1, after=(paired,))(keep, got_send)
        got_send = swap_rows(send, blocks, 1 << step)
    pair, _ = pair_part(rows // 4, rows, pair, send)

    alignment = call(finish_kernel, "finish", shape(homolog_activations.shape, BF16), [], 1)(
        keep, got_send, mask, diag, gain, hat, spread
    )
    return pair, alignment


def solution(mesh):
    split = P(("groups", "rows"), ("cols", "sub"), None)
    return jax.shard_map(
        per_device,
        mesh=mesh,
        in_specs=(split, P("groups"), P("groups"), P(), P(), P(), P(), P(), P(), split),
        out_specs=(split, split),
        check_vma=False,
    )
```

```python
import functools

import jax
import jax.numpy as jnp
from jax import lax
from jax.experimental import pallas as pl
from jax.experimental.pallas import tpu as pltpu
from jax.sharding import PartitionSpec as P

F32 = jnp.float32
BF16 = jnp.bfloat16
PLACES = ("rows", "cols", "sub")
PRODUCED = 256
TILE = 16


def dot(a, b):
    return lax.dot_general(a, b, (((1,), (0,)), ((), ())), preferred_element_type=F32)


def dot_t(a, b):
    return lax.dot_general(a, b, (((1,), (1,)), ((), ())), preferred_element_type=F32)


def place():
    column = lax.axis_index("cols") * lax.axis_size("sub") + lax.axis_index("sub")
    return lax.axis_index("rows"), column


def lanes_at(start, size):
    return pl.ds(pl.multiple_of(start, size), size)


def flag_row(flags_ref):
    return flags_ref[...].astype(F32).reshape(1, -1)


def flag_column(flags_ref, start, length):
    flags = flag_row(flags_ref)
    total = flags.shape[1]
    spot = lax.broadcasted_iota(jnp.int32, (length, total), 0) + start
    lane = lax.broadcasted_iota(jnp.int32, (length, total), 1)
    return jnp.sum(jnp.where(spot == lane, flags, 0.0), axis=1, keepdims=True)


def load_all(pairs, sems):
    copies = [pltpu.make_async_copy(src, dst, sems.at[n]) for n, (src, dst) in enumerate(pairs)]
    for copy in copies:
        copy.start()
    return copies


def project_kernel(*refs):
    sources, outs, (loss_ref, w_ref), held, sems = refs[:9], refs[9:15], refs[15:17], refs[17:24], refs[24]
    out_ref, diag, mask_ref, hat_ref, spread_ref, gain_out = outs
    copies = load_all(list(zip(sources, held + (w_ref, loss_ref))), sems)
    seq_ref, x_ref, res_ref, gain_ref, bias_ref, first_ref, second_ref = held
    row_at, column_at = place()
    seqs, length, channels = x_ref.shape
    width = first_ref.shape[0]
    half = seqs * width
    diag[...] = jnp.zeros_like(diag)
    for copy in copies[:7]:
        copy.wait()
    for s in range(seqs):
        lanes = slice(s * channels, (s + 1) * channels)
        diag[s * width : (s + 1) * width, lanes] = first_ref[...]
        diag[(seqs + s) * width : (seqs + s + 1) * width, lanes] = second_ref[...]
    flags = flag_row(seq_ref)
    spot = lax.broadcasted_iota(jnp.int32, flags.shape, 1)
    which = lax.broadcasted_iota(jnp.int32, (1, 2 * half), 1) % half // width
    own = jnp.zeros((1, 2 * half), F32)
    for s in range(seqs):
        value = jnp.sum(jnp.where(spot == row_at * seqs + s, flags, 0.0), axis=1, keepdims=True)
        own = jnp.where(which == s, value, own)
    mask = flag_column(res_ref, column_at * length, length) * own
    mask_ref[...] = mask
    gain = gain_ref[...].reshape(1, channels)
    bias = bias_ref[...].reshape(1, channels)
    gain_out[...] = jnp.broadcast_to(gain, gain_out.shape)
    total = jnp.zeros((length, 2 * half), F32)
    for s in range(seqs):
        x = x_ref[s].astype(F32)
        off = x - jnp.mean(x, axis=-1, keepdims=True)
        spread = lax.rsqrt(jnp.mean(off * off, axis=-1, keepdims=True) + 1e-05)
        hat = off * spread
        hat_ref[s] = hat
        spread_ref[s] = jnp.broadcast_to(spread, spread_ref.shape[1:])
        normed = (hat * gain + bias).astype(BF16)
        total += dot_t(normed, diag[:, s * channels : (s + 1) * channels])
    out_ref[0] = (total * mask).astype(BF16)
    for copy in copies[7:]:
        copy.wait()


def prepare_kernel(*refs):
    sources, (loss_ref, w_ref), outs, held, (wide_w, sems) = (
        refs[:3],
        refs[3:5],
        refs[5:13],
        refs[13:16],
        refs[16:],
    )
    by_left, by_right, swap, scaled, turned, inverse_ref, row_ref, shift_out = outs
    seq_ref, res_ref, shift_ref = held
    copies = load_all(list(zip(sources, held)), sems)
    row_at, column_at = place()
    rows, length, cz = loss_ref.shape
    width = by_left.shape[0]
    span = swap.shape[0]
    deep = span // width
    wide_w[...] = w_ref[...].astype(F32)
    for n in range(width):
        by_left[:, n * cz : (n + 1) * cz] = wide_w[pl.ds(n, width, stride=width), :].astype(BF16)
        by_right[:, n * cz : (n + 1) * cz] = w_ref[n * width : (n + 1) * width, :]
    to = lax.broadcasted_iota(jnp.int32, (span, span), 0)
    at = lax.broadcasted_iota(jnp.int32, (span, span), 1)
    swap[...] = jnp.where((to // deep == at % width) & (to % deep == at // width), 1.0, 0.0).astype(BF16)
    for copy in copies:
        copy.wait()
    present = jnp.sum(flag_row(seq_ref), axis=1, keepdims=True)
    columns = flag_column(res_ref, column_at * length, length)
    inverse = jnp.broadcast_to(1.0 / jnp.maximum(present * columns, 1.0), (length, cz))
    inverse_ref[...] = inverse
    row_ref[...] = jnp.broadcast_to(flag_column(res_ref, row_at * rows, rows), (rows, cz))
    shift_out[...] = jnp.broadcast_to(shift_ref[...].reshape(1, cz), shift_out.shape)
    for i in range(rows):
        factor = jnp.where(row_ref[i : i + 1, :] > 0.0, inverse, 1.0)
        scaled[:, i * cz : (i + 1) * cz] = (loss_ref[i].astype(F32) * factor).astype(BF16)
    to = lax.broadcasted_iota(jnp.int32, (TILE * TILE, TILE * TILE), 0)
    at = lax.broadcasted_iota(jnp.int32, (TILE * TILE, TILE * TILE), 1)
    turn = jnp.where((to // TILE == at % TILE) & (to % TILE == at // TILE), 1.0, 0.0).astype(BF16)
    for i in range(0, rows, TILE):
        for j in range(0, length, 2 * TILE):
            taken = [
                jnp.concatenate(
                    [scaled[b : b + TILE, (i + k) * cz : (i + k + 1) * cz] for k in range(TILE)], axis=0
                )
                for b in (j, j + TILE)
            ]
            made = dot(turn, jnp.concatenate(taken, axis=1)).astype(BF16)
            for a in range(2):
                for k in range(TILE):
                    low = (j + a * TILE + k) * cz
                    turned[i : i + TILE, low : low + cz] = made[
                        k * TILE : (k + 1) * TILE, a * cz : (a + 1) * cz
                    ]


def stack_kernel(own, got, *refs):
    out = refs[-1]
    count = own.shape[0]
    out[:count] = own[...]
    out[count:] = got[...]


def lefts_kernel(own, got, *refs):
    out = refs[-1]
    count, _, half = out.shape
    for n in range(count // 2):
        out[n] = own[n, :, :half]
        out[count // 2 + n] = got[n, :, :half]


def select_kernel(bit, own, got, *refs):
    out = refs[-1]
    row_at, column_at = place()
    other = (row_at ^ column_at) >> bit & 1

    @pl.when(other == 1)
    def _():
        out[...] = got[...]

    @pl.when(other == 0)
    def _():
        out[...] = own[...]


def add_kernel(own, got, *refs):
    out = refs[-1]
    out[...] = (own[...].astype(F32) + got[...].astype(F32)).astype(BF16)


def spread_rows(rows, n, block, width, deep):
    length, half = block.shape
    seqs = half // width
    wide = block.astype(F32)
    for s in range(seqs):
        rows[pl.ds(n * seqs + s, length, stride=deep), :] = wide[:, s * width : (s + 1) * width]


def produce(out, top, rows, weight, deep):
    width = weight.shape[0]
    cz = weight.shape[1] // width
    chunk = PRODUCED // deep

    def section(step, _):
        taken = rows[lanes_at(step * chunk * deep, chunk * deep), :].astype(BF16)
        for n in range(width // 2):
            made = dot(taken, weight[:, n * 2 * cz : (n + 1) * 2 * cz])
            for i in range(chunk):
                both = jnp.concatenate(
                    [made[i * deep : (i + 1) * deep, a * cz : (a + 1) * cz] for a in range(2)], axis=0
                )
                low = top + n * 2 * deep
                out[low : low + 2 * deep, lanes_at((step * chunk + i) * cz, cz)] = both.astype(BF16)
        return 0

    lax.fori_loop(0, rows.shape[0] // (chunk * deep), section, 0)


def v_kernel(stack, swap, weight, *refs):
    right_cols, v_ref, rows = refs[-3:]
    count, _, both = stack.shape
    width = weight.shape[0]
    deep = swap.shape[0] // width
    for n in range(count):
        spread_rows(rows, n, stack[n, :, both // 2 :], width, deep)
    right = jnp.concatenate([stack[n, :, both // 2 :] for n in range(count)], axis=1)
    right_cols[...] = dot_t(right, swap[...]).astype(BF16)
    produce(v_ref, 0, rows, weight, deep)


def t_kernel(bit, own, got, weight, *refs):
    t_ref, rows = refs[-2:]
    row_at, column_at = place()
    count = own.shape[0]
    width = weight.shape[0]
    span = t_ref.shape[0] // 2
    deep = span // width
    other = (row_at ^ column_at) >> bit & 1
    for h in range(2):
        for n in range(count // 2):
            k = h * count // 2 + n
            block = jnp.where(other == 1, got[k].astype(F32), own[k].astype(F32))
            spread_rows(rows.at[h], n, block, width, deep)
    for h in range(2):
        produce(t_ref, h * span, rows.at[h], weight, deep)


def contract_kernel(part, full_ref, scaled, swap, *refs):
    out = refs[-1]
    span = swap.shape[0]
    half = out.shape[2]
    size = scaled.shape[1] * PRODUCED // span

    def section(step, acc):
        lanes = lanes_at(step * size, size)
        return acc + dot_t(scaled[:, lanes], full_ref[part * span : (part + 1) * span, lanes])

    acc = dot_t(scaled[:, :size], full_ref[part * span : (part + 1) * span, :size])
    acc = lax.fori_loop(1, span // PRODUCED, section, acc)
    made = dot(acc.astype(BF16), swap[...]).astype(BF16)
    for k in range(out.shape[0]):
        out[k] = made[:, k * half : (k + 1) * half]


def join_kernel(part, right, own, got, out):
    row_at, column_at = place()
    mine = jnp.where(row_at == column_at, 1.0, 0.0)
    half = right.shape[2]
    count = right.shape[0]
    for n in range(count):
        k = part * count + n
        out[n, :, :half] = ((own[k].astype(F32) + got[k].astype(F32)) * mine).astype(BF16)
    out[:, :, half:] = right[...]


def halve_kernel(own, got, *refs):
    keep, send = refs[-2:]
    count = keep.shape[0]
    keep[...] = (own[:count].astype(F32) + got[:count].astype(F32)).astype(BF16)
    send[...] = (own[count:].astype(F32) + got[count:].astype(F32)).astype(BF16)


def pair_kernel(first, low_cols, high_cols, t_ref, shift_ref, inverse_ref, row_ref, *refs):
    out_ref, done_ref = refs[-2:]
    rows, length, cz = out_ref.shape
    step_rows = 8 * PRODUCED // low_cols.shape[1]
    done_ref[...] = jnp.zeros_like(done_ref)

    def section(step, _):
        right = jnp.concatenate([low_cols[...], high_cols[...]], axis=1)
        for n in range(step_rows // 2):
            made = dot(right, t_ref[:, lanes_at((first + step * step_rows + 2 * n) * cz, 2 * cz)])
            for a in range(2):
                i = step * step_rows + 2 * n + a
                factor = jnp.where(row_ref[pl.ds(first + i, 1), :] > 0.0, inverse_ref[...], 1.0)
                out_ref[i] = ((made[:, a * cz : (a + 1) * cz] + shift_ref[:1, :]) * factor).astype(BF16)
        return 0

    lax.fori_loop(0, rows // step_rows, section, 0)


def finish_kernel(own, got, mask_ref, diag, gain_ref, hat_ref, spread_ref, upper, lower, pair_ref, out_ref, sems):
    seqs, _, channels = hat_ref.shape
    split = upper.shape[0]
    copies = load_all([(upper, pair_ref.at[:split]), (lower, pair_ref.at[split:])], sems)
    both = ((own[0].astype(F32) + got[0].astype(F32)) * mask_ref[...]).astype(BF16)
    gain = gain_ref[:1, :]
    for s in range(seqs):
        hat = hat_ref[s]
        grad = dot(both, diag[:, s * channels : (s + 1) * channels]) * gain
        out_ref[s] = (
            spread_ref[s][:, :1]
            * (
                grad
                - jnp.mean(grad, axis=-1, keepdims=True)
                - hat * jnp.mean(grad * hat, axis=-1, keepdims=True)
            )
        ).astype(BF16)
    for copy in copies:
        copy.wait()


VMEM = pl.BlockSpec(memory_space=pltpu.VMEM)
HBM = pl.BlockSpec(memory_space=pltpu.HBM)


def call(kernel, name, out_shape, scratch, micros, in_specs=None, out_specs=None, limit=24, after=()):
    def run(*args):
        specs = [VMEM] * len(args) if in_specs is None else in_specs
        specs, args = specs + [pl.BlockSpec(memory_space=pl.ANY)] * len(after), args + tuple(after)
        outs = jax.tree.map(lambda _: VMEM, out_shape) if out_specs is None else out_specs
        return pl.pallas_call(
            kernel,
            out_shape=out_shape,
            in_specs=specs,
            out_specs=outs,
            scratch_shapes=scratch,
            compiler_params=pltpu.CompilerParams(vmem_limit_bytes=limit * 1024 * 1024),
            cost_estimate=pl.CostEstimate(flops=int(micros * 1e8), bytes_accessed=0, transcendentals=0),
            name=name,
        )(*args)

    return run


def swap_rows(x, blocks, bit):
    moves = [(z * blocks + c, (z ^ bit) * blocks + c) for z in range(blocks) for c in range(blocks)]
    return lax.ppermute(x, PLACES, moves)


def swap_columns(x, blocks, bit):
    moves = [(z * blocks + c, z * blocks + (c ^ bit)) for z in range(blocks) for c in range(blocks)]
    return lax.ppermute(x, PLACES, moves)


def per_device(
    homolog_activations,
    homolog_valid_flags,
    position_valid_flags,
    centering_factor,
    centering_shift,
    first_factor_matrix,
    second_factor_matrix,
    couple_weight_matrix,
    couple_shift_vector,
    loss_sensitivity,
):
    seqs, length, channels = homolog_activations.shape
    total_seq = homolog_valid_flags.shape[0]
    total_res = position_valid_flags.shape[0]
    width = first_factor_matrix.shape[1]
    rows, columns, cz = loss_sensitivity.shape
    blocks = lax.axis_size("cols") * lax.axis_size("sub")
    steps = blocks.bit_length() - 1
    assert blocks == 1 << steps == lax.axis_size("rows") and steps > 0
    half = seqs * width
    deep = total_seq // 2
    span = deep * width
    shape = jax.ShapeDtypeStruct

    def far(x):
        return pltpu.with_memory_space_constraint(x, pltpu.HBM)

    seq_flags, res_flags = far(homolog_valid_flags), far(position_valid_flags)

    stack, diag, mask, hat, spread, gain, loss, weights = call(
        project_kernel,
        "project",
        (
            shape((1, length, 2 * half), BF16),
            shape((2 * half, seqs * channels), BF16),
            shape((length, 2 * half), F32),
            shape((seqs, length, channels), F32),
            shape((seqs, length, cz), F32),
            shape((8, channels), F32),
            shape(loss_sensitivity.shape, BF16),
            shape(couple_weight_matrix.shape, BF16),
        ),
        [
            pltpu.VMEM((total_seq,), jnp.int32),
            pltpu.VMEM((seqs, length, channels), BF16),
            pltpu.VMEM((total_res,), jnp.int32),
            pltpu.VMEM((channels,), F32),
            pltpu.VMEM((channels,), F32),
            pltpu.VMEM((width, channels), BF16),
            pltpu.VMEM((width, channels), BF16),
            pltpu.SemaphoreType.DMA((9,)),
        ],
        2,
        in_specs=[HBM] * 9,
    )(
        seq_flags,
        far(homolog_activations),
        res_flags,
        far(centering_factor),
        far(centering_shift),
        far(first_factor_matrix.T),
        far(second_factor_matrix.T),
        far(couple_weight_matrix),
        far(loss_sensitivity),
    )

    by_left, by_right, swap, scaled, turned, inverse, row_flags, shift = call(
        prepare_kernel,
        "prepare",
        (
            shape((width, width * cz), BF16),
            shape((width, width * cz), BF16),
            shape((span, span), BF16),
            shape((columns, rows * cz), BF16),
            shape((rows, columns * cz), BF16),
            shape((columns, cz), F32),
            shape((rows, cz), F32),
            shape((8, cz), F32),
        ),
        [
            pltpu.VMEM((total_seq,), jnp.int32),
            pltpu.VMEM((total_res,), jnp.int32),
            pltpu.VMEM((cz,), F32),
            pltpu.VMEM((width * width, cz), F32),
            pltpu.SemaphoreType.DMA((3,)),
        ],
        3,
        in_specs=[HBM] * 3 + [VMEM] * 2,
    )(seq_flags, res_flags, far(couple_shift_vector), loss, weights)

    for step in range(steps):
        got = swap_rows(stack, blocks, blocks >> (step + 1))
        if step < steps - 1:
            stack = call(
                stack_kernel, "stack", shape((2 << step, length, 2 * half), BF16), [], 0.1, after=(shift,)
            )(stack, got)
    low_stack, high_stack = stack, got

    half_blocks = shape((blocks // 2, length, half), BF16)
    all_blocks = shape((blocks, length, half), BF16)
    cols_shape = shape((columns, span), BF16)
    t_limit = 16 + 2 * span * rows * cz * 2 // 2**20

    def make_v(stack, *after):
        return call(
            v_kernel,
            "expand_right",
            (cols_shape, shape((span, columns * cz), BF16)),
            [pltpu.VMEM((columns * deep, width), F32)],
            1.5,
            limit=t_limit,
            after=after,
        )(stack, swap, by_right)

    def contract(part, full, side, *after):
        return call(
            functools.partial(contract_kernel, part), "contract", half_blocks, [], 1.5, limit=t_limit, after=after
        )(full, side, swap)

    low_cols, v_low = make_v(low_stack)
    low_sum = contract(0, v_low, turned)
    lefts = call(lefts_kernel, "lefts", all_blocks, [], 0.1, after=(low_sum,))(low_stack, high_stack)
    got = swap_columns(lefts, blocks, 1)
    high_cols, v_high = make_v(high_stack, lefts)
    for step in range(1, steps):
        lefts = call(
            functools.partial(select_kernel, step - 1), "select", all_blocks, [], 0.1, after=(high_cols,)
        )(lefts, got)
        got = swap_columns(lefts, blocks, 1 << step)
    got_lefts = got
    high_sum = contract(0, v_high, turned, lefts)
    sums = call(stack_kernel, "stack", all_blocks, [], 0.1)(low_sum, high_sum)

    for step in reversed(range(1, steps)):
        got = swap_columns(sums, blocks, 1 << step)
        if step > 1:
            sums = call(add_kernel, "add", all_blocks, [], 0.1)(sums, got)
    t_all = call(
        functools.partial(t_kernel, steps - 1),
        "expand",
        shape((2 * span, rows * cz), BF16),
        [pltpu.VMEM((2, rows * deep, width), F32)],
        3,
        limit=t_limit,
        after=(sums,),
    )(lefts, got_lefts, by_left)
    sums = call(add_kernel, "add", all_blocks, [], 0.1, after=(t_all,))(sums, got)
    got = swap_columns(sums, blocks, 1)

    def join(part, right):
        return call(
            functools.partial(join_kernel, part),
            "join",
            shape((blocks // 2, length, 2 * half), BF16),
            [],
            0.1,
        )(right, sums, got)

    send = join(1, contract(1, t_all, scaled, sums))
    got_send = swap_rows(send, blocks, 1)
    keep = join(0, contract(0, t_all, scaled, send))

    def pair_part(start, stop, *after):
        return call(
            functools.partial(pair_kernel, start),
            "pair",
            (shape((stop - start, columns, cz), BF16), shape((8, cz), F32)),
            [],
            3.5 * (stop - start) / rows,
            limit=t_limit,
            after=after,
        )(low_cols, high_cols, t_all, shift, inverse, row_flags)

    split = rows * 3 // 8
    upper, paired = pair_part(0, split, keep)
    for step in range(1, steps):
        some = shape((blocks >> (step + 1), length, 2 * half), BF16)
        keep, send = call(halve_kernel, "halve", (some, some), [], 0.1, after=(paired,))(keep, got_send)
        got_send = swap_rows(send, blocks, 1 << step)
    lower, _ = pair_part(split, rows, send)

    return call(
        finish_kernel,
        "finish",
        (shape(loss_sensitivity.shape, BF16), shape(homolog_activations.shape, BF16)),
        [pltpu.SemaphoreType.DMA((2,))],
        1,
        out_specs=(HBM, VMEM),
    )(keep, got_send, mask, diag, gain, hat, spread, upper, lower)


def solution(mesh):
    split = P(("groups", "rows"), ("cols", "sub"), None)
    return jax.shard_map(
        per_device,
        mesh=mesh,
        in_specs=(split, P("groups"), P("groups"), P(), P(), P(), P(), P(), P(), split),
        out_specs=(split, split),
        check_vma=False,
    )
```

```python
import functools

import jax
import jax.numpy as jnp
from jax import lax
from jax.experimental import pallas as pl
from jax.experimental.pallas import tpu as pltpu
from jax.sharding import PartitionSpec as P

F32 = jnp.float32
BF16 = jnp.bfloat16
PLACES = ("rows", "cols", "sub")
PRODUCED = 256
TILE = 16


def dot(a, b):
    return lax.dot_general(a, b, (((1,), (0,)), ((), ())), preferred_element_type=F32)


def dot_t(a, b):
    return lax.dot_general(a, b, (((1,), (1,)), ((), ())), preferred_element_type=F32)


def place():
    column = lax.axis_index("cols") * lax.axis_size("sub") + lax.axis_index("sub")
    return lax.axis_index("rows"), column


def lanes_at(start, size):
    return pl.ds(pl.multiple_of(start, size), size)


def flag_row(flags_ref):
    return flags_ref[...].astype(F32).reshape(1, -1)


def flag_column(flags_ref, start, length):
    flags = flag_row(flags_ref)
    total = flags.shape[1]
    spot = lax.broadcasted_iota(jnp.int32, (length, total), 0) + start
    lane = lax.broadcasted_iota(jnp.int32, (length, total), 1)
    return jnp.sum(jnp.where(spot == lane, flags, 0.0), axis=1, keepdims=True)


def load_all(pairs, sems):
    copies = [pltpu.make_async_copy(src, dst, sems.at[n]) for n, (src, dst) in enumerate(pairs)]
    for copy in copies:
        copy.start()
    return copies


def project_kernel(*refs):
    sources, outs, (loss_ref, w_ref), held, sems = refs[:9], refs[9:15], refs[15:17], refs[17:24], refs[24]
    out_ref, diag, mask_ref, hat_ref, spread_ref, gain_out = outs
    copies = load_all(list(zip(sources, held + (w_ref, loss_ref))), sems)
    seq_ref, x_ref, res_ref, gain_ref, bias_ref, first_ref, second_ref = held
    row_at, column_at = place()
    seqs, length, channels = x_ref.shape
    width = first_ref.shape[0]
    half = seqs * width
    diag[...] = jnp.zeros_like(diag)
    for copy in copies[:7]:
        copy.wait()
    for s in range(seqs):
        lanes = slice(s * channels, (s + 1) * channels)
        diag[s * width : (s + 1) * width, lanes] = first_ref[...]
        diag[(seqs + s) * width : (seqs + s + 1) * width, lanes] = second_ref[...]
    flags = flag_row(seq_ref)
    spot = lax.broadcasted_iota(jnp.int32, flags.shape, 1)
    which = lax.broadcasted_iota(jnp.int32, (1, 2 * half), 1) % half // width
    own = jnp.zeros((1, 2 * half), F32)
    for s in range(seqs):
        value = jnp.sum(jnp.where(spot == row_at * seqs + s, flags, 0.0), axis=1, keepdims=True)
        own = jnp.where(which == s, value, own)
    mask = flag_column(res_ref, column_at * length, length) * own
    mask_ref[...] = mask
    gain = gain_ref[...].reshape(1, channels)
    bias = bias_ref[...].reshape(1, channels)
    gain_out[...] = jnp.broadcast_to(gain, gain_out.shape)
    total = jnp.zeros((length, 2 * half), F32)
    for s in range(seqs):
        x = x_ref[s].astype(F32)
        off = x - jnp.mean(x, axis=-1, keepdims=True)
        spread = lax.rsqrt(jnp.mean(off * off, axis=-1, keepdims=True) + 1e-05)
        hat = off * spread
        hat_ref[s] = hat
        spread_ref[s] = jnp.broadcast_to(spread, spread_ref.shape[1:])
        normed = (hat * gain + bias).astype(BF16)
        total += dot_t(normed, diag[:, s * channels : (s + 1) * channels])
    out_ref[0] = (total * mask).astype(BF16)
    for copy in copies[7:]:
        copy.wait()


def prepare_kernel(*refs):
    sources, (loss_ref, w_ref), outs, held, (wide_w, sems) = (
        refs[:3],
        refs[3:5],
        refs[5:13],
        refs[13:16],
        refs[16:],
    )
    by_left, by_right, swap, scaled, turned, inverse_ref, row_ref, shift_out = outs
    seq_ref, res_ref, shift_ref = held
    copies = load_all(list(zip(sources, held)), sems)
    row_at, column_at = place()
    rows, length, cz = loss_ref.shape
    width = by_left.shape[0]
    span = swap.shape[0]
    deep = span // width
    wide_w[...] = w_ref[...].astype(F32)
    for n in range(width):
        by_left[:, n * cz : (n + 1) * cz] = wide_w[pl.ds(n, width, stride=width), :].astype(BF16)
        by_right[:, n * cz : (n + 1) * cz] = w_ref[n * width : (n + 1) * width, :]
    to = lax.broadcasted_iota(jnp.int32, (span, span), 0)
    at = lax.broadcasted_iota(jnp.int32, (span, span), 1)
    swap[...] = jnp.where((to // deep == at % width) & (to % deep == at // width), 1.0, 0.0).astype(BF16)
    for copy in copies:
        copy.wait()
    present = jnp.sum(flag_row(seq_ref), axis=1, keepdims=True)
    columns = flag_column(res_ref, column_at * length, length)
    inverse = jnp.broadcast_to(1.0 / jnp.maximum(present * columns, 1.0), (length, cz))
    inverse_ref[...] = inverse
    row_ref[...] = jnp.broadcast_to(flag_column(res_ref, row_at * rows, rows), (rows, cz))
    shift_out[...] = jnp.broadcast_to(shift_ref[...].reshape(1, cz), shift_out.shape)
    for i in range(rows):
        factor = jnp.where(row_ref[i : i + 1, :] > 0.0, inverse, 1.0)
        scaled[:, i * cz : (i + 1) * cz] = (loss_ref[i].astype(F32) * factor).astype(BF16)
    to = lax.broadcasted_iota(jnp.int32, (TILE * TILE, TILE * TILE), 0)
    at = lax.broadcasted_iota(jnp.int32, (TILE * TILE, TILE * TILE), 1)
    turn = jnp.where((to // TILE == at % TILE) & (to % TILE == at // TILE), 1.0, 0.0).astype(BF16)
    for i in range(0, rows, TILE):
        for j in range(0, length, 2 * TILE):
            taken = [
                jnp.concatenate(
                    [scaled[b : b + TILE, (i + k) * cz : (i + k + 1) * cz] for k in range(TILE)], axis=0
                )
                for b in (j, j + TILE)
            ]
            made = dot(turn, jnp.concatenate(taken, axis=1)).astype(BF16)
            for a in range(2):
                for k in range(TILE):
                    low = (j + a * TILE + k) * cz
                    turned[i : i + TILE, low : low + cz] = made[
                        k * TILE : (k + 1) * TILE, a * cz : (a + 1) * cz
                    ]


def stack_kernel(own, got, *refs):
    out = refs[-1]
    count = own.shape[0]
    out[:count] = own[...]
    out[count:] = got[...]


def lefts_kernel(own, got, *refs):
    out = refs[-1]
    count, _, half = out.shape
    for n in range(count // 2):
        out[n] = own[n, :, :half]
        out[count // 2 + n] = got[n, :, :half]


def select_kernel(bit, own, got, *refs):
    out = refs[-1]
    row_at, column_at = place()
    other = (row_at ^ column_at) >> bit & 1

    @pl.when(other == 1)
    def _():
        out[...] = got[...]

    @pl.when(other == 0)
    def _():
        out[...] = own[...]


def add_kernel(own, got, *refs):
    out = refs[-1]
    out[...] = (own[...].astype(F32) + got[...].astype(F32)).astype(BF16)


def spread_rows(rows, n, block, width, deep):
    length, half = block.shape
    seqs = half // width
    wide = block.astype(F32)
    for s in range(seqs):
        rows[pl.ds(n * seqs + s, length, stride=deep), :] = wide[:, s * width : (s + 1) * width]


def produce(out, top, rows, weight, deep, size):
    width = weight.shape[0]
    cz = weight.shape[1] // width
    chunk = size // deep

    def section(step, _):
        taken = rows[lanes_at(step * chunk * deep, chunk * deep), :].astype(BF16)
        for n in range(width // 2):
            made = dot(taken, weight[:, n * 2 * cz : (n + 1) * 2 * cz])
            for i in range(chunk):
                both = jnp.concatenate(
                    [made[i * deep : (i + 1) * deep, a * cz : (a + 1) * cz] for a in range(2)], axis=0
                )
                low = top + n * 2 * deep
                out[low : low + 2 * deep, lanes_at((step * chunk + i) * cz, cz)] = both.astype(BF16)
        return 0

    lax.fori_loop(0, rows.shape[0] // (chunk * deep), section, 0)


def v_kernel(first, stack, swap, weight, *refs):
    right_cols, v_ref, rows = refs[-3:]
    count, _, both = stack.shape
    width = weight.shape[0]
    deep = swap.shape[0] // width
    length = rows.shape[0] // deep
    for n in range(count):
        spread_rows(rows, n, stack[n, first : first + length, both // 2 :], width, deep)
    if first == 0:
        right = jnp.concatenate([stack[n, :, both // 2 :] for n in range(count)], axis=1)
        right_cols[...] = dot_t(right, swap[...]).astype(BF16)
    else:
        right_cols[...] = jnp.zeros_like(right_cols)
    produce(v_ref, 0, rows, weight, deep, PRODUCED)


def t_kernel(bit, own, got, weight, *refs):
    t_ref, rows = refs[-2:]
    row_at, column_at = place()
    count = own.shape[0]
    width = weight.shape[0]
    span = t_ref.shape[0] // 2
    deep = span // width
    other = (row_at ^ column_at) >> bit & 1
    for h in range(2):
        for n in range(count // 2):
            k = h * count // 2 + n
            block = jnp.where(other == 1, got[k].astype(F32), own[k].astype(F32))
            spread_rows(rows.at[h], n, block, width, deep)
    for h in range(2):
        produce(t_ref, h * span, rows.at[h], weight, deep, 2 * PRODUCED)


def ungroup(out, acc, swap):
    half = out.shape[2]
    made = dot(acc.astype(BF16), swap[...]).astype(BF16)
    for k in range(out.shape[0]):
        out[k] = made[:, k * half : (k + 1) * half]


def left_kernel(count, *refs):
    parts, turned, swap, out = refs[:count], refs[count], refs[count + 1], refs[-1]
    span = swap.shape[0]
    whole = parts[0].shape[1]
    size = min(whole, turned.shape[1] * PRODUCED // span)
    acc = jnp.zeros((turned.shape[0], span), F32)
    for n in range(count):

        def section(step, acc):
            lanes = lanes_at(step * size, size)
            return acc + dot_t(turned[:, lanes_at(n * whole + step * size, size)], parts[n][:, lanes])

        if whole == size:
            acc += dot_t(turned[:, n * whole : (n + 1) * whole], parts[n][...])
        else:
            acc = lax.fori_loop(0, whole // size, section, acc)
    ungroup(out, acc, swap)


def right_kernel(part, t_ref, scaled, swap, *refs):
    out = refs[-1]
    span = swap.shape[0]
    size = scaled.shape[1] * PRODUCED // span

    def section(step, acc):
        lanes = lanes_at(step * size, size)
        return acc + dot_t(t_ref[part * span : (part + 1) * span, lanes], scaled[:, lanes])

    acc = dot_t(t_ref[part * span : (part + 1) * span, :size], scaled[:, :size])
    acc = lax.fori_loop(1, span // PRODUCED, section, acc)
    ungroup(out, jnp.transpose(acc), swap)


def join_kernel(part, right, own, got, out):
    row_at, column_at = place()
    mine = jnp.where(row_at == column_at, 1.0, 0.0)
    half = right.shape[2]
    count = right.shape[0]
    for n in range(count):
        k = part * count + n
        out[n, :, :half] = ((own[k].astype(F32) + got[k].astype(F32)) * mine).astype(BF16)
    out[:, :, half:] = right[...]


def halve_kernel(own, got, *refs):
    keep, send = refs[-2:]
    count = keep.shape[0]
    keep[...] = (own[:count].astype(F32) + got[:count].astype(F32)).astype(BF16)
    send[...] = (own[count:].astype(F32) + got[count:].astype(F32)).astype(BF16)


def pair_rows(out_ref, first, step, step_rows, low_cols, high_cols, t_ref, shift_ref, inverse_ref, row_ref):
    cz = out_ref.shape[2]
    right = jnp.concatenate([low_cols[...], high_cols[...]], axis=1)
    for n in range(step_rows // 2):
        made = dot(right, t_ref[:, lanes_at((first + step * step_rows + 2 * n) * cz, 2 * cz)])
        for a in range(2):
            i = step * step_rows + 2 * n + a
            factor = jnp.where(row_ref[pl.ds(first + i, 1), :] > 0.0, inverse_ref[...], 1.0)
            out_ref[i] = ((made[:, a * cz : (a + 1) * cz] + shift_ref[:1, :]) * factor).astype(BF16)


def upper_pair_kernel(*refs):
    sources, (out_ref, done_ref) = refs[:6], refs[-2:]
    step_rows = 8 * PRODUCED // sources[0].shape[1]
    done_ref[...] = jnp.zeros_like(done_ref)

    def section(step, _):
        pair_rows(out_ref, 0, step, step_rows, *sources)
        return 0

    lax.fori_loop(0, out_ref.shape[0] // step_rows, section, 0)


def lower_pair_kernel(last, *refs):
    sources, upper, (pair_ref, last_ref, held, sems) = refs[:6], refs[6], refs[-4:]
    step_rows = 8 * PRODUCED // sources[0].shape[1]
    first = upper.shape[0]
    rows = held.shape[0]
    steps = rows // step_rows

    def copy(step):
        spot = pl.ds(step * step_rows, step_rows)
        return pltpu.make_async_copy(
            held.at[spot], pair_ref.at[pl.ds(first + step * step_rows, step_rows)], sems.at[1 + step]
        )

    above = pltpu.make_async_copy(upper, pair_ref.at[:first], sems.at[0])
    above.start()

    def section(step, _):
        pair_rows(held, first, step, step_rows, *sources)
        copy(step).start()
        return 0

    lax.fori_loop(0, steps, section, 0)

    def last_section(step, _):
        pair_rows(last_ref, first + rows, step, step_rows, *sources)
        return 0

    lax.fori_loop(0, last // step_rows, last_section, 0)
    above.wait()
    for step in range(steps):
        copy(step).wait()


def finish_kernel(own, got, mask_ref, diag, gain_ref, hat_ref, spread_ref, last, *refs):
    pair_ref, out_ref, sems = refs[-3:]
    seqs, _, channels = hat_ref.shape
    copies = load_all([(last, pair_ref.at[pair_ref.shape[0] - last.shape[0] :])], sems)
    both = ((own[0].astype(F32) + got[0].astype(F32)) * mask_ref[...]).astype(BF16)
    gain = gain_ref[:1, :]
    for s in range(seqs):
        hat = hat_ref[s]
        grad = dot(both, diag[:, s * channels : (s + 1) * channels]) * gain
        out_ref[s] = (
            spread_ref[s][:, :1]
            * (
                grad
                - jnp.mean(grad, axis=-1, keepdims=True)
                - hat * jnp.mean(grad * hat, axis=-1, keepdims=True)
            )
        ).astype(BF16)
    for copy in copies:
        copy.wait()


VMEM = pl.BlockSpec(memory_space=pltpu.VMEM)
HBM = pl.BlockSpec(memory_space=pltpu.HBM)


def call(kernel, name, out_shape, scratch, micros, in_specs=None, out_specs=None, limit=24, aliases=None, after=()):
    def run(*args):
        specs = [VMEM] * len(args) if in_specs is None else in_specs
        specs, args = specs + [pl.BlockSpec(memory_space=pl.ANY)] * len(after), args + tuple(after)
        outs = jax.tree.map(lambda _: VMEM, out_shape) if out_specs is None else out_specs
        return pl.pallas_call(
            kernel,
            out_shape=out_shape,
            in_specs=specs,
            out_specs=outs,
            scratch_shapes=scratch,
            input_output_aliases=aliases or {},
            compiler_params=pltpu.CompilerParams(vmem_limit_bytes=limit * 1024 * 1024),
            cost_estimate=pl.CostEstimate(flops=int(micros * 1e8), bytes_accessed=0, transcendentals=0),
            name=name,
        )(*args)

    return run


def swap_rows(x, blocks, bit):
    moves = [(z * blocks + c, (z ^ bit) * blocks + c) for z in range(blocks) for c in range(blocks)]
    return lax.ppermute(x, PLACES, moves)


def swap_columns(x, blocks, bit):
    moves = [(z * blocks + c, z * blocks + (c ^ bit)) for z in range(blocks) for c in range(blocks)]
    return lax.ppermute(x, PLACES, moves)


def per_device(
    homolog_activations,
    homolog_valid_flags,
    position_valid_flags,
    centering_factor,
    centering_shift,
    first_factor_matrix,
    second_factor_matrix,
    couple_weight_matrix,
    couple_shift_vector,
    loss_sensitivity,
):
    seqs, length, channels = homolog_activations.shape
    total_seq = homolog_valid_flags.shape[0]
    total_res = position_valid_flags.shape[0]
    width = first_factor_matrix.shape[1]
    rows, columns, cz = loss_sensitivity.shape
    blocks = lax.axis_size("cols") * lax.axis_size("sub")
    steps = blocks.bit_length() - 1
    assert blocks == 1 << steps == lax.axis_size("rows") and steps > 0
    half = seqs * width
    deep = total_seq // 2
    span = deep * width
    shape = jax.ShapeDtypeStruct

    def far(x):
        return pltpu.with_memory_space_constraint(x, pltpu.HBM)

    seq_flags, res_flags = far(homolog_valid_flags), far(position_valid_flags)

    stack, diag, mask, hat, spread, gain, loss, weights = call(
        project_kernel,
        "project",
        (
            shape((1, length, 2 * half), BF16),
            shape((2 * half, seqs * channels), BF16),
            shape((length, 2 * half), F32),
            shape((seqs, length, channels), F32),
            shape((seqs, length, cz), F32),
            shape((8, channels), F32),
            shape(loss_sensitivity.shape, BF16),
            shape(couple_weight_matrix.shape, BF16),
        ),
        [
            pltpu.VMEM((total_seq,), jnp.int32),
            pltpu.VMEM((seqs, length, channels), BF16),
            pltpu.VMEM((total_res,), jnp.int32),
            pltpu.VMEM((channels,), F32),
            pltpu.VMEM((channels,), F32),
            pltpu.VMEM((width, channels), BF16),
            pltpu.VMEM((width, channels), BF16),
            pltpu.SemaphoreType.DMA((9,)),
        ],
        2,
        in_specs=[HBM] * 9,
    )(
        seq_flags,
        far(homolog_activations),
        res_flags,
        far(centering_factor),
        far(centering_shift),
        far(first_factor_matrix.T),
        far(second_factor_matrix.T),
        far(couple_weight_matrix),
        far(loss_sensitivity),
    )

    by_left, by_right, swap, scaled, turned, inverse, row_flags, shift = call(
        prepare_kernel,
        "prepare",
        (
            shape((width, width * cz), BF16),
            shape((width, width * cz), BF16),
            shape((span, span), BF16),
            shape((columns, rows * cz), BF16),
            shape((rows, columns * cz), BF16),
            shape((columns, cz), F32),
            shape((rows, cz), F32),
            shape((8, cz), F32),
        ),
        [
            pltpu.VMEM((total_seq,), jnp.int32),
            pltpu.VMEM((total_res,), jnp.int32),
            pltpu.VMEM((cz,), F32),
            pltpu.VMEM((width * width, cz), F32),
            pltpu.SemaphoreType.DMA((3,)),
        ],
        3,
        in_specs=[HBM] * 3 + [VMEM] * 2,
    )(seq_flags, res_flags, far(couple_shift_vector), loss, weights)

    for step in range(steps):
        got = swap_rows(stack, blocks, blocks >> (step + 1))
        if step < steps - 1:
            stack = call(
                stack_kernel, "stack", shape((2 << step, length, 2 * half), BF16), [], 0.1, after=(shift,)
            )(stack, got)
    low_stack, high_stack = stack, got

    half_blocks = shape((blocks // 2, length, half), BF16)
    all_blocks = shape((blocks, length, half), BF16)
    cols_shape = shape((columns, span), BF16)
    t_limit = 16 + 2 * span * rows * cz * 2 // 2**20

    def make_v(stack, first, size, *after):
        return call(
            functools.partial(v_kernel, first),
            "expand_right",
            (cols_shape, shape((span, size * cz), BF16)),
            [pltpu.VMEM((size * deep, width), F32)],
            1.5 * size / columns,
            limit=t_limit,
            after=after,
        )(stack, swap, by_right)

    def left_part(parts, *after):
        return call(
            functools.partial(left_kernel, len(parts)),
            "left_gradient",
            half_blocks,
            [],
            1.5,
            limit=t_limit,
            after=after,
        )(*parts, turned, swap)

    def right_part(part, *after):
        return call(
            functools.partial(right_kernel, part),
            "right_gradient",
            half_blocks,
            [],
            1.5,
            limit=t_limit,
            after=after,
        )(t_all, scaled, swap)

    low_cols, v_low = make_v(low_stack, 0, columns)
    low_sum = left_part([v_low])
    lefts = call(lefts_kernel, "lefts", all_blocks, [], 0.1, after=(low_sum,))(low_stack, high_stack)
    got = swap_columns(lefts, blocks, 1)
    high_cols, v_high = make_v(high_stack, 0, columns // 2, lefts)
    for step in range(1, steps):
        lefts = call(
            functools.partial(select_kernel, step - 1), "select", all_blocks, [], 0.1, after=(high_cols,)
        )(lefts, got)
        got = swap_columns(lefts, blocks, 1 << step)
    got_lefts = got
    _, v_more = make_v(high_stack, columns // 2, columns // 2, lefts)
    high_sum = left_part([v_high, v_more])
    sums = call(stack_kernel, "stack", all_blocks, [], 0.1)(low_sum, high_sum)

    for step in reversed(range(1, steps)):
        got = swap_columns(sums, blocks, 1 << step)
        if step > 1:
            sums = call(add_kernel, "add", all_blocks, [], 0.1)(sums, got)
    t_all = call(
        functools.partial(t_kernel, steps - 1),
        "expand",
        shape((2 * span, rows * cz), BF16),
        [pltpu.VMEM((2, rows * deep, width), F32)],
        3,
        limit=t_limit,
        after=(sums,),
    )(lefts, got_lefts, by_left)
    sums = call(add_kernel, "add", all_blocks, [], 0.1, after=(t_all,))(sums, got)
    got = swap_columns(sums, blocks, 1)

    def join(part, right):
        return call(
            functools.partial(join_kernel, part),
            "join",
            shape((blocks // 2, length, 2 * half), BF16),
            [],
            0.1,
        )(right, sums, got)

    send = join(1, right_part(1, sums))
    got_send = swap_rows(send, blocks, 1)
    keep = join(0, right_part(0, send))

    pair_sources = (low_cols, high_cols, t_all, shift, inverse, row_flags)
    upper_rows, last_rows = rows * 3 // 8, rows // 4
    held_rows = rows - upper_rows - last_rows
    upper, paired = call(
        upper_pair_kernel,
        "pair",
        (shape((upper_rows, columns, cz), BF16), shape((8, cz), F32)),
        [],
        1,
        limit=t_limit,
        after=(keep,),
    )(*pair_sources)
    for step in range(1, steps):
        some = shape((blocks >> (step + 1), length, 2 * half), BF16)
        keep, send = call(halve_kernel, "halve", (some, some), [], 0.1, after=(paired,))(keep, got_send)
        got_send = swap_rows(send, blocks, 1 << step)
    pair, last = call(
        functools.partial(lower_pair_kernel, last_rows),
        "pair",
        (shape(loss_sensitivity.shape, BF16), shape((last_rows, columns, cz), BF16)),
        [
            pltpu.VMEM((held_rows, columns, cz), BF16),
            pltpu.SemaphoreType.DMA((1 + held_rows * span // (8 * PRODUCED),)),
        ],
        2,
        out_specs=(HBM, VMEM),
        limit=t_limit,
        after=(send,),
    )(*pair_sources, upper)

    return call(
        finish_kernel,
        "finish",
        (shape(loss_sensitivity.shape, BF16), shape(homolog_activations.shape, BF16)),
        [pltpu.SemaphoreType.DMA((1,))],
        1,
        in_specs=[VMEM] * 8 + [HBM],
        out_specs=(HBM, VMEM),
        aliases={8: 0},
    )(keep, got_send, mask, diag, gain, hat, spread, last, pair)


def solution(mesh):
    split = P(("groups", "rows"), ("cols", "sub"), None)
    return jax.shard_map(
        per_device,
        mesh=mesh,
        in_specs=(split, P("groups"), P("groups"), P(), P(), P(), P(), P(), P(), split),
        out_specs=(split, split),
        check_vma=False,
    )
```

```python
import functools

import jax
import jax.numpy as jnp
from jax import lax
from jax.experimental import pallas as pl
from jax.experimental.pallas import tpu as pltpu
from jax.sharding import PartitionSpec as P

F32 = jnp.float32
BF16 = jnp.bfloat16
PLACES = ("rows", "cols", "sub")
PRODUCED = 256
TILE = 16


def dot(a, b):
    return lax.dot_general(a, b, (((1,), (0,)), ((), ())), preferred_element_type=F32)


def dot_t(a, b):
    return lax.dot_general(a, b, (((1,), (1,)), ((), ())), preferred_element_type=F32)


def place():
    column = lax.axis_index("cols") * lax.axis_size("sub") + lax.axis_index("sub")
    return lax.axis_index("rows"), column


def lanes_at(start, size):
    return pl.ds(pl.multiple_of(start, size), size)


def flag_row(flags_ref):
    return flags_ref[...].astype(F32).reshape(1, -1)


def flag_column(flags_ref, start, length):
    flags = flag_row(flags_ref)
    total = flags.shape[1]
    spot = lax.broadcasted_iota(jnp.int32, (length, total), 0) + start
    lane = lax.broadcasted_iota(jnp.int32, (length, total), 1)
    return jnp.sum(jnp.where(spot == lane, flags, 0.0), axis=1, keepdims=True)


def load_all(pairs, sems):
    copies = [pltpu.make_async_copy(src, dst, sems.at[n]) for n, (src, dst) in enumerate(pairs)]
    for copy in copies:
        copy.start()
    return copies


def project_kernel(*refs):
    sources, outs, (loss_ref, w_ref), held, sems = refs[:9], refs[9:15], refs[15:17], refs[17:24], refs[24]
    out_ref, diag, mask_ref, hat_ref, spread_ref, gain_out = outs
    copies = load_all(list(zip(sources, held + (w_ref, loss_ref))), sems)
    seq_ref, x_ref, res_ref, gain_ref, bias_ref, first_ref, second_ref = held
    row_at, column_at = place()
    seqs, length, channels = x_ref.shape
    width = first_ref.shape[0]
    half = seqs * width
    diag[...] = jnp.zeros_like(diag)
    for copy in copies[:7]:
        copy.wait()
    for s in range(seqs):
        lanes = slice(s * channels, (s + 1) * channels)
        diag[s * width : (s + 1) * width, lanes] = first_ref[...]
        diag[(seqs + s) * width : (seqs + s + 1) * width, lanes] = second_ref[...]
    flags = flag_row(seq_ref)
    spot = lax.broadcasted_iota(jnp.int32, flags.shape, 1)
    which = lax.broadcasted_iota(jnp.int32, (1, 2 * half), 1) % half // width
    own = jnp.zeros((1, 2 * half), F32)
    for s in range(seqs):
        value = jnp.sum(jnp.where(spot == row_at * seqs + s, flags, 0.0), axis=1, keepdims=True)
        own = jnp.where(which == s, value, own)
    mask = flag_column(res_ref, column_at * length, length) * own
    mask_ref[...] = mask
    gain = gain_ref[...].reshape(1, channels)
    bias = bias_ref[...].reshape(1, channels)
    gain_out[...] = jnp.broadcast_to(gain, gain_out.shape)
    total = jnp.zeros((length, 2 * half), F32)
    for s in range(seqs):
        x = x_ref[s].astype(F32)
        off = x - jnp.mean(x, axis=-1, keepdims=True)
        spread = lax.rsqrt(jnp.mean(off * off, axis=-1, keepdims=True) + 1e-05)
        hat = off * spread
        hat_ref[s] = hat
        spread_ref[s] = jnp.broadcast_to(spread, spread_ref.shape[1:])
        normed = (hat * gain + bias).astype(BF16)
        total += dot_t(normed, diag[:, s * channels : (s + 1) * channels])
    out_ref[0] = (total * mask).astype(BF16)
    for copy in copies[7:]:
        copy.wait()


def prepare_kernel(*refs):
    sources, (loss_ref, w_ref), outs, held, (wide_w, sems) = (
        refs[:3],
        refs[3:5],
        refs[5:13],
        refs[13:16],
        refs[16:],
    )
    by_left, by_right, swap, scaled, turned, inverse_ref, row_ref, shift_out = outs
    seq_ref, res_ref, shift_ref = held
    copies = load_all(list(zip(sources, held)), sems)
    row_at, column_at = place()
    rows, length, cz = loss_ref.shape
    width = by_left.shape[0]
    span = swap.shape[0]
    deep = span // width
    wide_w[...] = w_ref[...].astype(F32)
    for n in range(width):
        by_left[:, n * cz : (n + 1) * cz] = wide_w[pl.ds(n, width, stride=width), :].astype(BF16)
        by_right[:, n * cz : (n + 1) * cz] = w_ref[n * width : (n + 1) * width, :]
    to = lax.broadcasted_iota(jnp.int32, (span, span), 0)
    at = lax.broadcasted_iota(jnp.int32, (span, span), 1)
    swap[...] = jnp.where((to // deep == at % width) & (to % deep == at // width), 1.0, 0.0).astype(BF16)
    for copy in copies:
        copy.wait()
    present = jnp.sum(flag_row(seq_ref), axis=1, keepdims=True)
    columns = flag_column(res_ref, column_at * length, length)
    inverse = jnp.broadcast_to(1.0 / jnp.maximum(present * columns, 1.0), (length, cz))
    inverse_ref[...] = inverse
    row_ref[...] = jnp.broadcast_to(flag_column(res_ref, row_at * rows, rows), (rows, cz))
    shift_out[...] = jnp.broadcast_to(shift_ref[...].reshape(1, cz), shift_out.shape)
    for i in range(rows):
        factor = jnp.where(row_ref[i : i + 1, :] > 0.0, inverse, 1.0)
        scaled[:, i * cz : (i + 1) * cz] = (loss_ref[i].astype(F32) * factor).astype(BF16)
    to = lax.broadcasted_iota(jnp.int32, (TILE * TILE, TILE * TILE), 0)
    at = lax.broadcasted_iota(jnp.int32, (TILE * TILE, TILE * TILE), 1)
    turn = jnp.where((to // TILE == at % TILE) & (to % TILE == at // TILE), 1.0, 0.0).astype(BF16)
    for i in range(0, rows, TILE):
        for j in range(0, length, 2 * TILE):
            taken = [
                jnp.concatenate(
                    [scaled[b : b + TILE, (i + k) * cz : (i + k + 1) * cz] for k in range(TILE)], axis=0
                )
                for b in (j, j + TILE)
            ]
            made = dot(turn, jnp.concatenate(taken, axis=1)).astype(BF16)
            for a in range(2):
                for k in range(TILE):
                    low = (j + a * TILE + k) * cz
                    turned[i : i + TILE, low : low + cz] = made[
                        k * TILE : (k + 1) * TILE, a * cz : (a + 1) * cz
                    ]


def stack_kernel(own, got, *refs):
    out = refs[-1]
    count = own.shape[0]
    out[:count] = own[...]
    out[count:] = got[...]


def lefts_kernel(own, got, *refs):
    out = refs[-1]
    count, _, half = out.shape
    for n in range(count // 2):
        out[n] = own[n, :, :half]
        out[count // 2 + n] = got[n, :, :half]


def select_kernel(bit, own, got, *refs):
    out = refs[-1]
    row_at, column_at = place()
    other = (row_at ^ column_at) >> bit & 1

    @pl.when(other == 1)
    def _():
        out[...] = got[...]

    @pl.when(other == 0)
    def _():
        out[...] = own[...]


def add_kernel(own, got, *refs):
    out = refs[-1]
    out[...] = (own[...].astype(F32) + got[...].astype(F32)).astype(BF16)


def spread_rows(rows, n, block, width, deep):
    length, half = block.shape
    seqs = half // width
    wide = block.astype(F32)
    for s in range(seqs):
        rows[pl.ds(n * seqs + s, length, stride=deep), :] = wide[:, s * width : (s + 1) * width]


def produce(out, rows, weight, deep):
    width = weight.shape[0]
    cz = weight.shape[1] // width
    chunk = min(2 * PRODUCED, rows.shape[0]) // deep

    def section(step, _):
        taken = rows[lanes_at(step * chunk * deep, chunk * deep), :].astype(BF16)
        for n in range(width // 2):
            made = dot(taken, weight[:, n * 2 * cz : (n + 1) * 2 * cz])
            for i in range(chunk):
                both = jnp.concatenate(
                    [made[i * deep : (i + 1) * deep, a * cz : (a + 1) * cz] for a in range(2)], axis=0
                )
                low = n * 2 * deep
                out[low : low + 2 * deep, lanes_at((step * chunk + i) * cz, cz)] = both.astype(BF16)
        return 0

    lax.fori_loop(0, rows.shape[0] // (chunk * deep), section, 0)


def v_kernel(first, stack, swap, weight, *refs):
    right_cols, v_ref, rows = refs[-3:]
    count, _, both = stack.shape
    width = weight.shape[0]
    deep = swap.shape[0] // width
    length = rows.shape[0] // deep
    for n in range(count):
        spread_rows(rows, n, stack[n, first : first + length, both // 2 :], width, deep)
    if first == 0:
        right = jnp.concatenate([stack[n, :, both // 2 :] for n in range(count)], axis=1)
        right_cols[...] = dot_t(right, swap[...]).astype(BF16)
    else:
        right_cols[...] = jnp.zeros_like(right_cols)
    produce(v_ref, rows, weight, deep)


def t_kernel(bit, part, own, got, weight, *refs):
    t_ref, rows = refs[-2:]
    row_at, column_at = place()
    count = own.shape[0] // 2
    width = weight.shape[0]
    deep = t_ref.shape[0] // width
    other = (row_at ^ column_at) >> bit & 1
    for n in range(count):
        k = part * count + n
        block = jnp.where(other == 1, got[k].astype(F32), own[k].astype(F32))
        spread_rows(rows, n, block, width, deep)
    produce(t_ref, rows, weight, deep)


def ungroup(out, acc, swap):
    half = out.shape[2]
    made = dot(acc.astype(BF16), swap[...]).astype(BF16)
    for k in range(out.shape[0]):
        out[k] = made[:, k * half : (k + 1) * half]


def gradient_kernel(count, *refs):
    parts, side, swap, out = refs[:count], refs[count], refs[count + 1], refs[-1]
    span = swap.shape[0]
    whole = parts[0].shape[1]
    size = min(whole, side.shape[1] * PRODUCED // span)
    acc = jnp.zeros((span, side.shape[0]), F32)
    for n in range(count):

        def section(step, acc):
            lanes = lanes_at(step * size, size)
            return acc + dot_t(parts[n][:, lanes], side[:, lanes_at(n * whole + step * size, size)])

        if whole == size:
            acc += dot_t(parts[n][...], side[:, n * whole : (n + 1) * whole])
        else:
            acc = lax.fori_loop(0, whole // size, section, acc)
    ungroup(out, jnp.transpose(acc), swap)


def join_kernel(part, right, own, got, out):
    row_at, column_at = place()
    mine = jnp.where(row_at == column_at, 1.0, 0.0)
    half = right.shape[2]
    count = right.shape[0]
    for n in range(count):
        k = part * count + n
        out[n, :, :half] = ((own[k].astype(F32) + got[k].astype(F32)) * mine).astype(BF16)
    out[:, :, half:] = right[...]


def halve_kernel(own, got, *refs):
    keep, send = refs[-2:]
    count = keep.shape[0]
    keep[...] = (own[:count].astype(F32) + got[:count].astype(F32)).astype(BF16)
    send[...] = (own[count:].astype(F32) + got[count:].astype(F32)).astype(BF16)


def rows_of_pass(span):
    return max(2, 4 * PRODUCED // span)


def pair_rows(out_ref, first, step, step_rows, low_cols, high_cols, t_low, t_high, shift_ref, inverse_ref, row_ref):
    cz = out_ref.shape[2]
    for n in range(step_rows // 2):
        lanes = lanes_at((first + step * step_rows + 2 * n) * cz, 2 * cz)
        made = dot(low_cols[...], t_low[:, lanes]) + dot(high_cols[...], t_high[:, lanes])
        for a in range(2):
            i = step * step_rows + 2 * n + a
            factor = jnp.where(row_ref[pl.ds(first + i, 1), :] > 0.0, inverse_ref[...], 1.0)
            out_ref[i] = ((made[:, a * cz : (a + 1) * cz] + shift_ref[:1, :]) * factor).astype(BF16)


def upper_pair_kernel(*refs):
    sources, (out_ref, done_ref) = refs[:7], refs[-2:]
    step_rows = rows_of_pass(sources[0].shape[1])
    done_ref[...] = jnp.zeros_like(done_ref)

    def section(step, _):
        pair_rows(out_ref, 0, step, step_rows, *sources)
        return 0

    lax.fori_loop(0, out_ref.shape[0] // step_rows, section, 0)


def lower_pair_kernel(*refs):
    sources, upper, (pair_ref, held, sems) = refs[:7], refs[7], refs[-3:]
    step_rows = rows_of_pass(sources[0].shape[1])
    first = upper.shape[0]
    steps = held.shape[0] // step_rows

    def copy(step):
        spot = pl.ds(step * step_rows, step_rows)
        return pltpu.make_async_copy(
            held.at[spot], pair_ref.at[pl.ds(first + step * step_rows, step_rows)], sems.at[1 + step]
        )

    above = pltpu.make_async_copy(upper, pair_ref.at[:first], sems.at[0])
    above.start()

    def section(step, _):
        pair_rows(held, first, step, step_rows, *sources)
        copy(step).start()
        return 0

    lax.fori_loop(0, steps, section, 0)
    above.wait()
    for step in range(steps):
        copy(step).wait()


def finish_kernel(own, got, mask_ref, diag, gain_ref, hat_ref, spread_ref, out_ref, held, sems):
    seqs, _, channels = hat_ref.shape
    both = ((own[0].astype(F32) + got[0].astype(F32)) * mask_ref[...]).astype(BF16)
    gain = gain_ref[:1, :]
    copies = []
    for s in range(seqs):
        hat = hat_ref[s]
        grad = dot(both, diag[:, s * channels : (s + 1) * channels]) * gain
        held[s] = (
            spread_ref[s][:, :1]
            * (
                grad
                - jnp.mean(grad, axis=-1, keepdims=True)
                - hat * jnp.mean(grad * hat, axis=-1, keepdims=True)
            )
        ).astype(BF16)
        copies.append(pltpu.make_async_copy(held.at[s], out_ref.at[s], sems.at[s]))
        copies[s].start()
    for copy in copies:
        copy.wait()


VMEM = pl.BlockSpec(memory_space=pltpu.VMEM)
HBM = pl.BlockSpec(memory_space=pltpu.HBM)


def call(kernel, name, out_shape, scratch, micros, in_specs=None, out_specs=None, limit=24, aliases=None, after=()):
    def run(*args):
        specs = [VMEM] * len(args) if in_specs is None else in_specs
        specs, args = specs + [pl.BlockSpec(memory_space=pl.ANY)] * len(after), args + tuple(after)
        outs = jax.tree.map(lambda _: VMEM, out_shape) if out_specs is None else out_specs
        return pl.pallas_call(
            kernel,
            out_shape=out_shape,
            in_specs=specs,
            out_specs=outs,
            scratch_shapes=scratch,
            input_output_aliases=aliases or {},
            compiler_params=pltpu.CompilerParams(vmem_limit_bytes=limit * 1024 * 1024),
            cost_estimate=pl.CostEstimate(flops=int(micros * 1e8), bytes_accessed=0, transcendentals=0),
            name=name,
        )(*args)

    return run


def swap_rows(x, blocks, bit):
    moves = [(z * blocks + c, (z ^ bit) * blocks + c) for z in range(blocks) for c in range(blocks)]
    return lax.ppermute(x, PLACES, moves)


def swap_columns(x, blocks, bit):
    moves = [(z * blocks + c, z * blocks + (c ^ bit)) for z in range(blocks) for c in range(blocks)]
    return lax.ppermute(x, PLACES, moves)


def per_device(
    homolog_activations,
    homolog_valid_flags,
    position_valid_flags,
    centering_factor,
    centering_shift,
    first_factor_matrix,
    second_factor_matrix,
    couple_weight_matrix,
    couple_shift_vector,
    loss_sensitivity,
):
    seqs, length, channels = homolog_activations.shape
    total_seq = homolog_valid_flags.shape[0]
    total_res = position_valid_flags.shape[0]
    width = first_factor_matrix.shape[1]
    rows, columns, cz = loss_sensitivity.shape
    blocks = lax.axis_size("cols") * lax.axis_size("sub")
    steps = blocks.bit_length() - 1
    assert blocks == 1 << steps == lax.axis_size("rows") and steps > 0
    half = seqs * width
    deep = total_seq // 2
    span = deep * width
    shape = jax.ShapeDtypeStruct

    def far(x):
        return pltpu.with_memory_space_constraint(x, pltpu.HBM)

    seq_flags, res_flags = far(homolog_valid_flags), far(position_valid_flags)

    stack, diag, mask, hat, spread, gain, loss, weights = call(
        project_kernel,
        "project",
        (
            shape((1, length, 2 * half), BF16),
            shape((2 * half, seqs * channels), BF16),
            shape((length, 2 * half), F32),
            shape((seqs, length, channels), F32),
            shape((seqs, length, cz), F32),
            shape((8, channels), F32),
            shape(loss_sensitivity.shape, BF16),
            shape(couple_weight_matrix.shape, BF16),
        ),
        [
            pltpu.VMEM((total_seq,), jnp.int32),
            pltpu.VMEM((seqs, length, channels), BF16),
            pltpu.VMEM((total_res,), jnp.int32),
            pltpu.VMEM((channels,), F32),
            pltpu.VMEM((channels,), F32),
            pltpu.VMEM((width, channels), BF16),
            pltpu.VMEM((width, channels), BF16),
            pltpu.SemaphoreType.DMA((9,)),
        ],
        2,
        in_specs=[HBM] * 9,
    )(
        seq_flags,
        far(homolog_activations),
        res_flags,
        far(centering_factor),
        far(centering_shift),
        far(first_factor_matrix.T),
        far(second_factor_matrix.T),
        far(couple_weight_matrix),
        far(loss_sensitivity),
    )

    by_left, by_right, swap, scaled, turned, inverse, row_flags, shift = call(
        prepare_kernel,
        "prepare",
        (
            shape((width, width * cz), BF16),
            shape((width, width * cz), BF16),
            shape((span, span), BF16),
            shape((columns, rows * cz), BF16),
            shape((rows, columns * cz), BF16),
            shape((columns, cz), F32),
            shape((rows, cz), F32),
            shape((8, cz), F32),
        ),
        [
            pltpu.VMEM((total_seq,), jnp.int32),
            pltpu.VMEM((total_res,), jnp.int32),
            pltpu.VMEM((cz,), F32),
            pltpu.VMEM((width * width, cz), F32),
            pltpu.SemaphoreType.DMA((3,)),
        ],
        3,
        in_specs=[HBM] * 3 + [VMEM] * 2,
    )(seq_flags, res_flags, far(couple_shift_vector), loss, weights)

    for step in range(steps):
        got = swap_rows(stack, blocks, blocks >> (step + 1))
        if step < steps - 1:
            stack = call(
                stack_kernel, "stack", shape((2 << step, length, 2 * half), BF16), [], 0.1, after=(shift,)
            )(stack, got)
    low_stack, high_stack = stack, got

    half_blocks = shape((blocks // 2, length, half), BF16)
    all_blocks = shape((blocks, length, half), BF16)
    cols_shape = shape((columns, span), BF16)
    t_limit = 16 + 2 * span * rows * cz * 2 // 2**20

    def make_v(stack, first, size, *after):
        return call(
            functools.partial(v_kernel, first),
            "expand_right",
            (cols_shape, shape((span, size * cz), BF16)),
            [pltpu.VMEM((size * deep, width), F32)],
            1.5 * size / columns,
            limit=t_limit,
            after=after,
        )(stack, swap, by_right)

    def gradient(parts, side, *after):
        return call(
            functools.partial(gradient_kernel, len(parts)),
            "gradient",
            half_blocks,
            [],
            1.5,
            limit=t_limit,
            after=after,
        )(*parts, side, swap)

    low_cols, v_low = make_v(low_stack, 0, columns)
    low_sum = gradient([v_low], turned)
    lefts = call(lefts_kernel, "lefts", all_blocks, [], 0.1, after=(low_sum,))(low_stack, high_stack)
    got = swap_columns(lefts, blocks, 1)
    high_cols, v_high = make_v(high_stack, 0, columns // 2, lefts)
    for step in range(1, steps):
        lefts = call(
            functools.partial(select_kernel, step - 1), "select", all_blocks, [], 0.1, after=(high_cols,)
        )(lefts, got)
        got = swap_columns(lefts, blocks, 1 << step)
    got_lefts = got
    _, v_more = make_v(high_stack, columns // 2, columns // 2, lefts)
    high_sum = gradient([v_high, v_more], turned)
    sums = call(stack_kernel, "stack", all_blocks, [], 0.1)(low_sum, high_sum)

    def make_t(part, *after):
        return call(
            functools.partial(t_kernel, steps - 1, part),
            "expand_left",
            shape((span, rows * cz), BF16),
            [pltpu.VMEM((rows * deep, width), F32)],
            1.2,
            limit=t_limit,
            after=after,
        )(lefts, got_lefts, by_left)

    for step in range(steps - 1):
        got = swap_columns(sums, blocks, 1 << step)
        if step == 0:
            t_low = make_t(0, sums)
        sums = call(add_kernel, "add", all_blocks, [], 0.1, after=(t_low,))(sums, got)
    got = swap_columns(sums, blocks, 1 << (steps - 1))
    t_high = make_t(1, sums)

    def join(part, right):
        return call(
            functools.partial(join_kernel, part),
            "join",
            shape((blocks // 2, length, 2 * half), BF16),
            [],
            0.1,
        )(right, sums, got)

    send = join(1, gradient([t_high], scaled, sums))
    got_send = swap_rows(send, blocks, 1)
    keep = join(0, gradient([t_low], scaled, send))

    pair_sources = (low_cols, high_cols, t_low, t_high, shift, inverse, row_flags)
    upper_rows = rows // 2
    upper, paired = call(
        upper_pair_kernel,
        "pair",
        (shape((upper_rows, columns, cz), BF16), shape((8, cz), F32)),
        [],
        1,
        limit=t_limit,
        after=(keep,),
    )(*pair_sources)
    for step in range(1, steps):
        some = shape((blocks >> (step + 1), length, 2 * half), BF16)
        keep, send = call(halve_kernel, "halve", (some, some), [], 0.1, after=(paired,))(keep, got_send)
        got_send = swap_rows(send, blocks, 1 << step)
    pair = call(
        lower_pair_kernel,
        "pair",
        shape(loss_sensitivity.shape, BF16),
        [
            pltpu.VMEM((rows - upper_rows, columns, cz), BF16),
            pltpu.SemaphoreType.DMA((1 + (rows - upper_rows) // rows_of_pass(span),)),
        ],
        2,
        out_specs=HBM,
        limit=t_limit,
        after=(send,),
    )(*pair_sources, upper)

    alignment = call(
        finish_kernel,
        "finish",
        shape(homolog_activations.shape, BF16),
        [pltpu.VMEM(homolog_activations.shape, BF16), pltpu.SemaphoreType.DMA((seqs,))],
        1,
        out_specs=HBM,
    )(keep, got_send, mask, diag, gain, hat, spread)
    return pair, alignment


def solution(mesh):
    split = P(("groups", "rows"), ("cols", "sub"), None)
    return jax.shard_map(
        per_device,
        mesh=mesh,
        in_specs=(split, P("groups"), P("groups"), P(), P(), P(), P(), P(), P(), split),
        out_specs=(split, split),
        check_vma=False,
    )
```

```python
import functools

import jax
import jax.numpy as jnp
from jax import lax
from jax.experimental import pallas as pl
from jax.experimental.pallas import tpu as pltpu
from jax.sharding import PartitionSpec as P

F32 = jnp.float32
BF16 = jnp.bfloat16
PLACES = ("rows", "cols", "sub")
PRODUCED = 256
TILE = 16


def dot(a, b):
    return lax.dot_general(a, b, (((1,), (0,)), ((), ())), preferred_element_type=F32)


def dot_t(a, b):
    return lax.dot_general(a, b, (((1,), (1,)), ((), ())), preferred_element_type=F32)


def place():
    column = lax.axis_index("cols") * lax.axis_size("sub") + lax.axis_index("sub")
    return lax.axis_index("rows"), column


def lanes_at(start, size):
    return pl.ds(pl.multiple_of(start, size), size)


def flag_row(flags_ref):
    return flags_ref[...].astype(F32).reshape(1, -1)


def flag_column(flags_ref, start, length):
    flags = flag_row(flags_ref)
    total = flags.shape[1]
    spot = lax.broadcasted_iota(jnp.int32, (length, total), 0) + start
    lane = lax.broadcasted_iota(jnp.int32, (length, total), 1)
    return jnp.sum(jnp.where(spot == lane, flags, 0.0), axis=1, keepdims=True)


def load_all(pairs, sems):
    copies = [pltpu.make_async_copy(src, dst, sems.at[n]) for n, (src, dst) in enumerate(pairs)]
    for copy in copies:
        copy.start()
    return copies


def project_kernel(*refs):
    sources, outs, (loss_ref, w_ref), held, sems = refs[:9], refs[9:15], refs[15:17], refs[17:24], refs[24]
    out_ref, diag, mask_ref, hat_ref, spread_ref, gain_out = outs
    copies = load_all(list(zip(sources, held + (w_ref, loss_ref))), sems)
    seq_ref, x_ref, res_ref, gain_ref, bias_ref, first_ref, second_ref = held
    row_at, column_at = place()
    seqs, length, channels = x_ref.shape
    width = first_ref.shape[0]
    half = seqs * width
    diag[...] = jnp.zeros_like(diag)
    for copy in copies[:7]:
        copy.wait()
    for s in range(seqs):
        lanes = slice(s * channels, (s + 1) * channels)
        diag[s * width : (s + 1) * width, lanes] = first_ref[...]
        diag[(seqs + s) * width : (seqs + s + 1) * width, lanes] = second_ref[...]
    flags = flag_row(seq_ref)
    spot = lax.broadcasted_iota(jnp.int32, flags.shape, 1)
    which = lax.broadcasted_iota(jnp.int32, (1, 2 * half), 1) % half // width
    own = jnp.zeros((1, 2 * half), F32)
    for s in range(seqs):
        value = jnp.sum(jnp.where(spot == row_at * seqs + s, flags, 0.0), axis=1, keepdims=True)
        own = jnp.where(which == s, value, own)
    mask = flag_column(res_ref, column_at * length, length) * own
    mask_ref[...] = mask
    gain = gain_ref[...].reshape(1, channels)
    bias = bias_ref[...].reshape(1, channels)
    gain_out[...] = jnp.broadcast_to(gain, gain_out.shape)
    total = jnp.zeros((length, 2 * half), F32)
    for s in range(seqs):
        x = x_ref[s].astype(F32)
        off = x - jnp.mean(x, axis=-1, keepdims=True)
        spread = lax.rsqrt(jnp.mean(off * off, axis=-1, keepdims=True) + 1e-05)
        hat = off * spread
        hat_ref[s] = hat
        spread_ref[s] = jnp.broadcast_to(spread, spread_ref.shape[1:])
        normed = (hat * gain + bias).astype(BF16)
        total += dot_t(normed, diag[:, s * channels : (s + 1) * channels])
    out_ref[0] = (total * mask).astype(BF16)
    for copy in copies[7:]:
        copy.wait()


def prepare_kernel(*refs):
    sources, (loss_ref, w_ref), outs, held, (wide_w, sems) = (
        refs[:3],
        refs[3:5],
        refs[5:13],
        refs[13:16],
        refs[16:],
    )
    by_left, by_right, swap, scaled, turned, inverse_ref, row_ref, shift_out = outs
    seq_ref, res_ref, shift_ref = held
    copies = load_all(list(zip(sources, held)), sems)
    row_at, column_at = place()
    rows, length, cz = loss_ref.shape
    width = by_left.shape[0]
    span = swap.shape[0]
    deep = span // width
    wide_w[...] = w_ref[...].astype(F32)
    for n in range(width):
        by_left[:, n * cz : (n + 1) * cz] = wide_w[pl.ds(n, width, stride=width), :].astype(BF16)
        by_right[:, n * cz : (n + 1) * cz] = w_ref[n * width : (n + 1) * width, :]
    to = lax.broadcasted_iota(jnp.int32, (span, span), 0)
    at = lax.broadcasted_iota(jnp.int32, (span, span), 1)
    swap[...] = jnp.where((to // deep == at % width) & (to % deep == at // width), 1.0, 0.0).astype(BF16)
    for copy in copies:
        copy.wait()
    present = jnp.sum(flag_row(seq_ref), axis=1, keepdims=True)
    columns = flag_column(res_ref, column_at * length, length)
    inverse = jnp.broadcast_to(1.0 / jnp.maximum(present * columns, 1.0), (length, cz))
    inverse_ref[...] = inverse
    row_ref[...] = jnp.broadcast_to(flag_column(res_ref, row_at * rows, rows), (rows, cz))
    shift_out[...] = jnp.broadcast_to(shift_ref[...].reshape(1, cz), shift_out.shape)
    for i in range(rows):
        factor = jnp.where(row_ref[i : i + 1, :] > 0.0, inverse, 1.0)
        scaled[:, i * cz : (i + 1) * cz] = (loss_ref[i].astype(F32) * factor).astype(BF16)
    to = lax.broadcasted_iota(jnp.int32, (TILE * TILE, TILE * TILE), 0)
    at = lax.broadcasted_iota(jnp.int32, (TILE * TILE, TILE * TILE), 1)
    turn = jnp.where((to // TILE == at % TILE) & (to % TILE == at // TILE), 1.0, 0.0).astype(BF16)
    for i in range(0, rows, TILE):
        for j in range(0, length, 2 * TILE):
            taken = [
                jnp.concatenate(
                    [scaled[b : b + TILE, (i + k) * cz : (i + k + 1) * cz] for k in range(TILE)], axis=0
                )
                for b in (j, j + TILE)
            ]
            made = dot(turn, jnp.concatenate(taken, axis=1)).astype(BF16)
            for a in range(2):
                for k in range(TILE):
                    low = (j + a * TILE + k) * cz
                    turned[i : i + TILE, low : low + cz] = made[
                        k * TILE : (k + 1) * TILE, a * cz : (a + 1) * cz
                    ]


def stack_kernel(own, got, *refs):
    out = refs[-1]
    count = own.shape[0]
    out[:count] = own[...]
    out[count:] = got[...]


def lefts_kernel(own, got, *refs):
    out = refs[-1]
    count, _, half = out.shape
    for n in range(count // 2):
        out[n] = own[n, :, :half]
        out[count // 2 + n] = got[n, :, :half]


def select_kernel(bit, own, got, *refs):
    out = refs[-1]
    row_at, column_at = place()
    other = (row_at ^ column_at) >> bit & 1

    @pl.when(other == 1)
    def _():
        out[...] = got[...]

    @pl.when(other == 0)
    def _():
        out[...] = own[...]


def add_kernel(own, got, *refs):
    out = refs[-1]
    out[...] = (own[...].astype(F32) + got[...].astype(F32)).astype(BF16)


def spread_rows(rows, n, block, width, deep):
    length, half = block.shape
    seqs = half // width
    wide = block.astype(F32)
    for s in range(seqs):
        rows[pl.ds(n * seqs + s, length, stride=deep), :] = wide[:, s * width : (s + 1) * width]


def produce(out, rows, weight, deep):
    width = weight.shape[0]
    cz = weight.shape[1] // width
    chunk = min(2 * PRODUCED, rows.shape[0]) // deep

    def section(step, _):
        taken = rows[lanes_at(step * chunk * deep, chunk * deep), :].astype(BF16)
        for n in range(width // 2):
            made = dot(taken, weight[:, n * 2 * cz : (n + 1) * 2 * cz])
            for i in range(chunk):
                both = jnp.concatenate(
                    [made[i * deep : (i + 1) * deep, a * cz : (a + 1) * cz] for a in range(2)], axis=0
                )
                low = n * 2 * deep
                out[low : low + 2 * deep, lanes_at((step * chunk + i) * cz, cz)] = both.astype(BF16)
        return 0

    lax.fori_loop(0, rows.shape[0] // (chunk * deep), section, 0)


def v_kernel(stack, swap, weight, *refs):
    right_cols, v_ref, rows = refs[-3:]
    count, _, both = stack.shape
    width = weight.shape[0]
    deep = swap.shape[0] // width
    for n in range(count):
        spread_rows(rows, n, stack[n, :, both // 2 :], width, deep)
    right = jnp.concatenate([stack[n, :, both // 2 :] for n in range(count)], axis=1)
    right_cols[...] = dot_t(right, swap[...]).astype(BF16)
    produce(v_ref, rows, weight, deep)


def t_kernel(bit, part, own, got, weight, *refs):
    t_ref, rows = refs[-2:]
    row_at, column_at = place()
    count = own.shape[0] // 2
    width = weight.shape[0]
    deep = t_ref.shape[0] // width
    other = (row_at ^ column_at) >> bit & 1
    for n in range(count):
        k = part * count + n
        block = jnp.where(other == 1, got[k].astype(F32), own[k].astype(F32))
        spread_rows(rows, n, block, width, deep)
    produce(t_ref, rows, weight, deep)


def ungroup(out, acc, swap):
    half = out.shape[2]
    made = dot(acc.astype(BF16), swap[...]).astype(BF16)
    for k in range(out.shape[0]):
        out[k] = made[:, k * half : (k + 1) * half]


def gradient_kernel(full_ref, side, swap, *refs):
    out = refs[-1]
    span = swap.shape[0]
    size = side.shape[1] * PRODUCED // span

    def section(step, acc):
        lanes = lanes_at(step * size, size)
        return acc + dot_t(full_ref[:, lanes], side[:, lanes])

    acc = dot_t(full_ref[:, :size], side[:, :size])
    acc = lax.fori_loop(1, span // PRODUCED, section, acc)
    ungroup(out, jnp.transpose(acc), swap)


def join_kernel(part, right, own, got, out):
    row_at, column_at = place()
    mine = jnp.where(row_at == column_at, 1.0, 0.0)
    half = right.shape[2]
    count = right.shape[0]
    for n in range(count):
        k = part * count + n
        out[n, :, :half] = ((own[k].astype(F32) + got[k].astype(F32)) * mine).astype(BF16)
    out[:, :, half:] = right[...]


def halve_kernel(own, got, *refs):
    keep, send = refs[-2:]
    count = keep.shape[0]
    keep[...] = (own[:count].astype(F32) + got[:count].astype(F32)).astype(BF16)
    send[...] = (own[count:].astype(F32) + got[count:].astype(F32)).astype(BF16)


def rows_of_pass(span):
    return max(2, 8 * PRODUCED // span)


def pair_rows(out_ref, first, step, step_rows, low_cols, high_cols, t_low, t_high, shift_ref, inverse_ref, row_ref):
    cz = out_ref.shape[2]
    for n in range(step_rows // 2):
        lanes = lanes_at((first + step * step_rows + 2 * n) * cz, 2 * cz)
        made = dot(low_cols[...], t_low[:, lanes]) + dot(high_cols[...], t_high[:, lanes])
        for a in range(2):
            i = step * step_rows + 2 * n + a
            factor = jnp.where(row_ref[pl.ds(first + i, 1), :] > 0.0, inverse_ref[...], 1.0)
            out_ref[i] = ((made[:, a * cz : (a + 1) * cz] + shift_ref[:1, :]) * factor).astype(BF16)


def upper_pair_kernel(*refs):
    sources, (out_ref, done_ref) = refs[:7], refs[-2:]
    step_rows = rows_of_pass(sources[0].shape[1])
    done_ref[...] = jnp.zeros_like(done_ref)

    def section(step, _):
        pair_rows(out_ref, 0, step, step_rows, *sources)
        return 0

    lax.fori_loop(0, out_ref.shape[0] // step_rows, section, 0)


def lower_pair_kernel(*refs):
    sources, upper, (pair_ref, held, sems) = refs[:7], refs[7], refs[-3:]
    step_rows = rows_of_pass(sources[0].shape[1])
    first = upper.shape[0]
    steps = held.shape[0] // step_rows

    def copy(step):
        spot = pl.ds(step * step_rows, step_rows)
        return pltpu.make_async_copy(
            held.at[spot], pair_ref.at[pl.ds(first + step * step_rows, step_rows)], sems.at[1 + step]
        )

    above = pltpu.make_async_copy(upper, pair_ref.at[:first], sems.at[0])
    above.start()

    def section(step, _):
        pair_rows(held, first, step, step_rows, *sources)
        copy(step).start()
        return 0

    lax.fori_loop(0, steps, section, 0)
    above.wait()
    for step in range(steps):
        copy(step).wait()


def finish_kernel(own, got, mask_ref, diag, gain_ref, hat_ref, spread_ref, out_ref, held, sems):
    seqs, _, channels = hat_ref.shape
    both = ((own[0].astype(F32) + got[0].astype(F32)) * mask_ref[...]).astype(BF16)
    gain = gain_ref[:1, :]
    copies = []
    for s in range(seqs):
        hat = hat_ref[s]
        grad = dot(both, diag[:, s * channels : (s + 1) * channels]) * gain
        held[s] = (
            spread_ref[s][:, :1]
            * (
                grad
                - jnp.mean(grad, axis=-1, keepdims=True)
                - hat * jnp.mean(grad * hat, axis=-1, keepdims=True)
            )
        ).astype(BF16)
        copies.append(pltpu.make_async_copy(held.at[s], out_ref.at[s], sems.at[s]))
        copies[s].start()
    for copy in copies:
        copy.wait()


VMEM = pl.BlockSpec(memory_space=pltpu.VMEM)
HBM = pl.BlockSpec(memory_space=pltpu.HBM)


def call(kernel, name, out_shape, scratch, micros, in_specs=None, out_specs=None, limit=24, aliases=None, after=()):
    def run(*args):
        specs = [VMEM] * len(args) if in_specs is None else in_specs
        specs, args = specs + [pl.BlockSpec(memory_space=pl.ANY)] * len(after), args + tuple(after)
        outs = jax.tree.map(lambda _: VMEM, out_shape) if out_specs is None else out_specs
        return pl.pallas_call(
            kernel,
            out_shape=out_shape,
            in_specs=specs,
            out_specs=outs,
            scratch_shapes=scratch,
            input_output_aliases=aliases or {},
            compiler_params=pltpu.CompilerParams(vmem_limit_bytes=limit * 1024 * 1024),
            cost_estimate=pl.CostEstimate(flops=int(micros * 1e8), bytes_accessed=0, transcendentals=0),
            name=name,
        )(*args)

    return run


def swap_rows(x, blocks, bit):
    moves = [(z * blocks + c, (z ^ bit) * blocks + c) for z in range(blocks) for c in range(blocks)]
    return lax.ppermute(x, PLACES, moves)


def swap_columns(x, blocks, bit):
    moves = [(z * blocks + c, z * blocks + (c ^ bit)) for z in range(blocks) for c in range(blocks)]
    return lax.ppermute(x, PLACES, moves)


def per_device(
    homolog_activations,
    homolog_valid_flags,
    position_valid_flags,
    centering_factor,
    centering_shift,
    first_factor_matrix,
    second_factor_matrix,
    couple_weight_matrix,
    couple_shift_vector,
    loss_sensitivity,
):
    seqs, length, channels = homolog_activations.shape
    total_seq = homolog_valid_flags.shape[0]
    total_res = position_valid_flags.shape[0]
    width = first_factor_matrix.shape[1]
    rows, columns, cz = loss_sensitivity.shape
    blocks = lax.axis_size("cols") * lax.axis_size("sub")
    steps = blocks.bit_length() - 1
    assert blocks == 1 << steps == lax.axis_size("rows") and steps > 0
    half = seqs * width
    deep = total_seq // 2
    span = deep * width
    shape = jax.ShapeDtypeStruct

    def far(x):
        return pltpu.with_memory_space_constraint(x, pltpu.HBM)

    seq_flags, res_flags = far(homolog_valid_flags), far(position_valid_flags)

    stack, diag, mask, hat, spread, gain, loss, weights = call(
        project_kernel,
        "project",
        (
            shape((1, length, 2 * half), BF16),
            shape((2 * half, seqs * channels), BF16),
            shape((length, 2 * half), F32),
            shape((seqs, length, channels), F32),
            shape((seqs, length, cz), F32),
            shape((8, channels), F32),
            shape(loss_sensitivity.shape, BF16),
            shape(couple_weight_matrix.shape, BF16),
        ),
        [
            pltpu.VMEM((total_seq,), jnp.int32),
            pltpu.VMEM((seqs, length, channels), BF16),
            pltpu.VMEM((total_res,), jnp.int32),
            pltpu.VMEM((channels,), F32),
            pltpu.VMEM((channels,), F32),
            pltpu.VMEM((width, channels), BF16),
            pltpu.VMEM((width, channels), BF16),
            pltpu.SemaphoreType.DMA((9,)),
        ],
        2,
        in_specs=[HBM] * 9,
    )(
        seq_flags,
        far(homolog_activations),
        res_flags,
        far(centering_factor),
        far(centering_shift),
        far(first_factor_matrix.T),
        far(second_factor_matrix.T),
        far(couple_weight_matrix),
        far(loss_sensitivity),
    )

    by_left, by_right, swap, scaled, turned, inverse, row_flags, shift = call(
        prepare_kernel,
        "prepare",
        (
            shape((width, width * cz), BF16),
            shape((width, width * cz), BF16),
            shape((span, span), BF16),
            shape((columns, rows * cz), BF16),
            shape((rows, columns * cz), BF16),
            shape((columns, cz), F32),
            shape((rows, cz), F32),
            shape((8, cz), F32),
        ),
        [
            pltpu.VMEM((total_seq,), jnp.int32),
            pltpu.VMEM((total_res,), jnp.int32),
            pltpu.VMEM((cz,), F32),
            pltpu.VMEM((width * width, cz), F32),
            pltpu.SemaphoreType.DMA((3,)),
        ],
        3,
        in_specs=[HBM] * 3 + [VMEM] * 2,
    )(seq_flags, res_flags, far(couple_shift_vector), loss, weights)

    for step in range(steps):
        got = swap_rows(stack, blocks, blocks >> (step + 1))
        if step < steps - 1:
            stack = call(
                stack_kernel, "stack", shape((2 << step, length, 2 * half), BF16), [], 0.1, after=(shift,)
            )(stack, got)
    low_stack, high_stack = stack, got

    half_blocks = shape((blocks // 2, length, half), BF16)
    all_blocks = shape((blocks, length, half), BF16)
    cols_shape = shape((columns, span), BF16)
    t_limit = 16 + 2 * span * rows * cz * 2 // 2**20

    def make_v(stack, *after):
        return call(
            v_kernel,
            "expand_right",
            (cols_shape, shape((span, columns * cz), BF16)),
            [pltpu.VMEM((columns * deep, width), F32)],
            1.3,
            limit=t_limit,
            after=after,
        )(stack, swap, by_right)

    def gradient(full, side, *after):
        return call(gradient_kernel, "gradient", half_blocks, [], 1.5, limit=t_limit, after=after)(full, side, swap)

    low_cols, v_low = make_v(low_stack)
    low_sum = gradient(v_low, turned)
    lefts = call(lefts_kernel, "lefts", all_blocks, [], 0.1, after=(low_sum,))(low_stack, high_stack)
    got = swap_columns(lefts, blocks, 1)
    high_cols, v_high = make_v(high_stack, lefts)
    for step in range(1, steps):
        lefts = call(
            functools.partial(select_kernel, step - 1), "select", all_blocks, [], 0.1, after=(high_cols,)
        )(lefts, got)
        got = swap_columns(lefts, blocks, 1 << step)
    got_lefts = got
    high_sum = gradient(v_high, turned, lefts)
    sums = call(stack_kernel, "stack", all_blocks, [], 0.1)(low_sum, high_sum)

    def make_t(part, *after):
        return call(
            functools.partial(t_kernel, steps - 1, part),
            "expand_left",
            shape((span, rows * cz), BF16),
            [pltpu.VMEM((rows * deep, width), F32)],
            1.2,
            limit=t_limit,
            after=after,
        )(lefts, got_lefts, by_left)

    def make_t(part, *after):
        return call(
            functools.partial(t_kernel, steps - 1, part),
            "expand_left",
            shape((span, rows * cz), BF16),
            [pltpu.VMEM((rows * deep, width), F32)],
            1.3,
            limit=t_limit,
            after=after,
        )(lefts, got_lefts, by_left)

    for step in range(steps - 1):
        got = swap_columns(sums, blocks, 1 << step)
        sums = call(add_kernel, "add", all_blocks, [], 0.1, after=(got_lefts,))(sums, got)
    got = swap_columns(sums, blocks, 1 << (steps - 1))
    t_high = make_t(1, sums)

    def join(part, right):
        return call(
            functools.partial(join_kernel, part),
            "join",
            shape((blocks // 2, length, 2 * half), BF16),
            [],
            0.1,
        )(right, sums, got)

    send = join(1, gradient(t_high, scaled, sums))
    got_send = swap_rows(send, blocks, 1)
    t_low = make_t(0, send)
    keep = join(0, gradient(t_low, scaled, send))

    pair_sources = (low_cols, high_cols, t_low, t_high, shift, inverse, row_flags)
    upper_rows = rows // 4
    upper, paired = call(
        upper_pair_kernel,
        "pair",
        (shape((upper_rows, columns, cz), BF16), shape((8, cz), F32)),
        [],
        1,
        limit=t_limit,
        after=(keep,),
    )(*pair_sources)
    for step in range(1, steps):
        some = shape((blocks >> (step + 1), length, 2 * half), BF16)
        keep, send = call(halve_kernel, "halve", (some, some), [], 0.1, after=(paired,))(keep, got_send)
        got_send = swap_rows(send, blocks, 1 << step)
    pair = call(
        lower_pair_kernel,
        "pair",
        shape(loss_sensitivity.shape, BF16),
        [
            pltpu.VMEM((rows - upper_rows, columns, cz), BF16),
            pltpu.SemaphoreType.DMA((1 + (rows - upper_rows) // rows_of_pass(span),)),
        ],
        2,
        out_specs=HBM,
        limit=t_limit,
        after=(send,),
    )(*pair_sources, upper)

    alignment = call(
        finish_kernel,
        "finish",
        shape(homolog_activations.shape, BF16),
        [pltpu.VMEM(homolog_activations.shape, BF16), pltpu.SemaphoreType.DMA((seqs,))],
        1,
        out_specs=HBM,
    )(keep, got_send, mask, diag, gain, hat, spread)
    return pair, alignment


def solution(mesh):
    split = P(("groups", "rows"), ("cols", "sub"), None)
    return jax.shard_map(
        per_device,
        mesh=mesh,
        in_specs=(split, P("groups"), P("groups"), P(), P(), P(), P(), P(), P(), split),
        out_specs=(split, split),
        check_vma=False,
    )
```

```python
import functools

import jax
import jax.numpy as jnp
from jax import lax
from jax.experimental import pallas as pl
from jax.experimental.pallas import tpu as pltpu
from jax.sharding import PartitionSpec as P

F32 = jnp.float32
BF16 = jnp.bfloat16
PLACES = ("rows", "cols", "sub")
PRODUCED = 256
TILE = 16
LOSS_COPIES = 8
PASS_COPIES = 4


def dot(a, b):
    return lax.dot_general(a, b, (((1,), (0,)), ((), ())), preferred_element_type=F32)


def dot_t(a, b):
    return lax.dot_general(a, b, (((1,), (1,)), ((), ())), preferred_element_type=F32)


def place():
    column = lax.axis_index("cols") * lax.axis_size("sub") + lax.axis_index("sub")
    return lax.axis_index("rows"), column


def lanes_at(start, size):
    return pl.ds(pl.multiple_of(start, size), size)


def flag_row(flags_ref):
    return flags_ref[...].astype(F32).reshape(1, -1)


def flag_column(flags_ref, start, length):
    flags = flag_row(flags_ref)
    total = flags.shape[1]
    spot = lax.broadcasted_iota(jnp.int32, (length, total), 0) + start
    lane = lax.broadcasted_iota(jnp.int32, (length, total), 1)
    return jnp.sum(jnp.where(spot == lane, flags, 0.0), axis=1, keepdims=True)


def load_all(pairs, sems):
    copies = [pltpu.make_async_copy(src, dst, sems.at[n]) for n, (src, dst) in enumerate(pairs)]
    for copy in copies:
        copy.start()
    return copies


def pieces(src, dst, count):
    size = src.shape[0] // count
    return [(src.at[pl.ds(n * size, size)], dst.at[pl.ds(n * size, size)]) for n in range(count)]


def project_kernel(*refs):
    sources, outs, (loss_ref, w_ref), held, sems = refs[:9], refs[9:15], refs[15:17], refs[17:24], refs[24]
    out_ref, diag, mask_ref, hat_ref, spread_ref, gain_out = outs
    seq_ref, x_ref, res_ref, gain_ref, bias_ref, first_ref, second_ref = held
    row_at, column_at = place()
    seqs, length, channels = x_ref.shape
    near = [(sources[n], held[n]) for n in (0, 2, 3, 4, 5, 6)]
    copies = load_all(
        pieces(sources[1], x_ref, seqs)
        + near
        + pieces(sources[7], w_ref, 4)
        + pieces(sources[8], loss_ref, LOSS_COPIES),
        sems,
    )
    width = first_ref.shape[0]
    half = seqs * width
    diag[...] = jnp.zeros_like(diag)
    for copy in copies[seqs : seqs + 6]:
        copy.wait()
    for s in range(seqs):
        lanes = slice(s * channels, (s + 1) * channels)
        diag[s * width : (s + 1) * width, lanes] = first_ref[...]
        diag[(seqs + s) * width : (seqs + s + 1) * width, lanes] = second_ref[...]
    flags = flag_row(seq_ref)
    spot = lax.broadcasted_iota(jnp.int32, flags.shape, 1)
    which = lax.broadcasted_iota(jnp.int32, (1, 2 * half), 1) % half // width
    own = jnp.zeros((1, 2 * half), F32)
    for s in range(seqs):
        value = jnp.sum(jnp.where(spot == row_at * seqs + s, flags, 0.0), axis=1, keepdims=True)
        own = jnp.where(which == s, value, own)
    mask = flag_column(res_ref, column_at * length, length) * own
    mask_ref[...] = mask
    gain = gain_ref[...].reshape(1, channels)
    bias = bias_ref[...].reshape(1, channels)
    gain_out[...] = jnp.broadcast_to(gain, gain_out.shape)
    total = jnp.zeros((length, 2 * half), F32)
    for s in range(seqs):
        copies[s].wait()
        x = x_ref[s].astype(F32)
        off = x - jnp.mean(x, axis=-1, keepdims=True)
        spread = lax.rsqrt(jnp.mean(off * off, axis=-1, keepdims=True) + 1e-05)
        hat = off * spread
        hat_ref[s] = hat
        spread_ref[s] = jnp.broadcast_to(spread, spread_ref.shape[1:])
        normed = (hat * gain + bias).astype(BF16)
        total += dot_t(normed, diag[:, s * channels : (s + 1) * channels])
    out_ref[0] = (total * mask).astype(BF16)
    for copy in copies[seqs + 6 :]:
        copy.wait()


def prepare_kernel(*refs):
    sources, (loss_ref, w_ref), outs, held, (wide_w, sems) = (
        refs[:3],
        refs[3:5],
        refs[5:13],
        refs[13:16],
        refs[16:],
    )
    by_left, by_right, swap, scaled, turned, inverse_ref, row_ref, shift_out = outs
    seq_ref, res_ref, shift_ref = held
    copies = load_all(list(zip(sources, held)), sems)
    row_at, column_at = place()
    rows, length, cz = loss_ref.shape
    width = by_left.shape[0]
    span = swap.shape[0]
    deep = span // width
    wide_w[...] = w_ref[...].astype(F32)
    for n in range(width):
        by_left[:, n * cz : (n + 1) * cz] = wide_w[pl.ds(n, width, stride=width), :].astype(BF16)
        by_right[:, n * cz : (n + 1) * cz] = w_ref[n * width : (n + 1) * width, :]
    to = lax.broadcasted_iota(jnp.int32, (span, span), 0)
    at = lax.broadcasted_iota(jnp.int32, (span, span), 1)
    swap[...] = jnp.where((to // deep == at % width) & (to % deep == at // width), 1.0, 0.0).astype(BF16)
    for copy in copies:
        copy.wait()
    present = jnp.sum(flag_row(seq_ref), axis=1, keepdims=True)
    columns = flag_column(res_ref, column_at * length, length)
    inverse = jnp.broadcast_to(1.0 / jnp.maximum(present * columns, 1.0), (length, cz))
    inverse_ref[...] = inverse
    row_ref[...] = jnp.broadcast_to(flag_column(res_ref, row_at * rows, rows), (rows, cz))
    shift_out[...] = jnp.broadcast_to(shift_ref[...].reshape(1, cz), shift_out.shape)
    for i in range(rows):
        factor = jnp.where(row_ref[i : i + 1, :] > 0.0, inverse, 1.0)
        scaled[:, i * cz : (i + 1) * cz] = (loss_ref[i].astype(F32) * factor).astype(BF16)
    to = lax.broadcasted_iota(jnp.int32, (TILE * TILE, TILE * TILE), 0)
    at = lax.broadcasted_iota(jnp.int32, (TILE * TILE, TILE * TILE), 1)
    turn = jnp.where((to // TILE == at % TILE) & (to % TILE == at // TILE), 1.0, 0.0).astype(BF16)
    for i in range(0, rows, TILE):
        for j in range(0, length, 2 * TILE):
            taken = [
                jnp.concatenate(
                    [scaled[b : b + TILE, (i + k) * cz : (i + k + 1) * cz] for k in range(TILE)], axis=0
                )
                for b in (j, j + TILE)
            ]
            made = dot(turn, jnp.concatenate(taken, axis=1)).astype(BF16)
            for a in range(2):
                for k in range(TILE):
                    low = (j + a * TILE + k) * cz
                    turned[i : i + TILE, low : low + cz] = made[
                        k * TILE : (k + 1) * TILE, a * cz : (a + 1) * cz
                    ]


def stack_kernel(own, got, *refs):
    out = refs[-1]
    count = own.shape[0]
    out[:count] = own[...]
    out[count:] = got[...]


def lefts_kernel(own, got, *refs):
    out = refs[-1]
    count, _, half = out.shape
    for n in range(count // 2):
        out[n] = own[n, :, :half]
        out[count // 2 + n] = got[n, :, :half]


def select_kernel(bit, own, got, *refs):
    out = refs[-1]
    row_at, column_at = place()
    other = (row_at ^ column_at) >> bit & 1

    @pl.when(other == 1)
    def _():
        out[...] = got[...]

    @pl.when(other == 0)
    def _():
        out[...] = own[...]


def add_kernel(own, got, *refs):
    out = refs[-1]
    out[...] = (own[...].astype(F32) + got[...].astype(F32)).astype(BF16)


def spread_rows(rows, n, block, width, deep):
    length, half = block.shape
    seqs = half // width
    wide = block.astype(F32)
    for s in range(seqs):
        rows[pl.ds(n * seqs + s, length, stride=deep), :] = wide[:, s * width : (s + 1) * width]


def produce(out, rows, weight, deep):
    width = weight.shape[0]
    cz = weight.shape[1] // width
    chunk = min(2 * PRODUCED, rows.shape[0]) // deep

    def section(step, _):
        taken = rows[lanes_at(step * chunk * deep, chunk * deep), :].astype(BF16)
        for n in range(width // 2):
            made = dot(taken, weight[:, n * 2 * cz : (n + 1) * 2 * cz])
            for i in range(chunk):
                both = jnp.concatenate(
                    [made[i * deep : (i + 1) * deep, a * cz : (a + 1) * cz] for a in range(2)], axis=0
                )
                low = n * 2 * deep
                out[low : low + 2 * deep, lanes_at((step * chunk + i) * cz, cz)] = both.astype(BF16)
        return 0

    lax.fori_loop(0, rows.shape[0] // (chunk * deep), section, 0)


def v_kernel(stack, swap, weight, *refs):
    right_cols, v_ref, rows = refs[-3:]
    count, _, both = stack.shape
    width = weight.shape[0]
    deep = swap.shape[0] // width
    for n in range(count):
        spread_rows(rows, n, stack[n, :, both // 2 :], width, deep)
    right = jnp.concatenate([stack[n, :, both // 2 :] for n in range(count)], axis=1)
    right_cols[...] = dot_t(right, swap[...]).astype(BF16)
    produce(v_ref, rows, weight, deep)


def t_kernel(bit, part, own, got, weight, *refs):
    t_ref, rows = refs[-2:]
    row_at, column_at = place()
    count = own.shape[0] // 2
    width = weight.shape[0]
    deep = t_ref.shape[0] // width
    other = (row_at ^ column_at) >> bit & 1
    for n in range(count):
        k = part * count + n
        block = jnp.where(other == 1, got[k].astype(F32), own[k].astype(F32))
        spread_rows(rows, n, block, width, deep)
    produce(t_ref, rows, weight, deep)


def ungroup(out, acc, swap):
    half = out.shape[2]
    made = dot(acc.astype(BF16), swap[...]).astype(BF16)
    for k in range(out.shape[0]):
        out[k] = made[:, k * half : (k + 1) * half]


def gradient_kernel(full_ref, side, swap, *refs):
    out = refs[-1]
    span = swap.shape[0]
    size = side.shape[1] * PRODUCED // span

    def section(step, acc):
        lanes = lanes_at(step * size, size)
        return acc + dot_t(full_ref[:, lanes], side[:, lanes])

    acc = dot_t(full_ref[:, :size], side[:, :size])
    acc = lax.fori_loop(1, span // PRODUCED, section, acc)
    ungroup(out, jnp.transpose(acc), swap)


def join_kernel(part, right, own, got, out):
    row_at, column_at = place()
    mine = jnp.where(row_at == column_at, 1.0, 0.0)
    half = right.shape[2]
    count = right.shape[0]
    for n in range(count):
        k = part * count + n
        out[n, :, :half] = ((own[k].astype(F32) + got[k].astype(F32)) * mine).astype(BF16)
    out[:, :, half:] = right[...]


def halve_kernel(own, got, *refs):
    keep, send = refs[-2:]
    count = keep.shape[0]
    keep[...] = (own[:count].astype(F32) + got[:count].astype(F32)).astype(BF16)
    send[...] = (own[count:].astype(F32) + got[count:].astype(F32)).astype(BF16)


def rows_of_pass(span):
    return max(2, 8 * PRODUCED // span)


def pair_rows(out_ref, first, step, step_rows, low_cols, high_cols, t_low, t_high, shift_ref, inverse_ref, row_ref):
    cz = out_ref.shape[2]
    for n in range(step_rows // 2):
        lanes = lanes_at((first + step * step_rows + 2 * n) * cz, 2 * cz)
        made = dot(low_cols[...], t_low[:, lanes]) + dot(high_cols[...], t_high[:, lanes])
        for a in range(2):
            i = step * step_rows + 2 * n + a
            factor = jnp.where(row_ref[pl.ds(first + i, 1), :] > 0.0, inverse_ref[...], 1.0)
            out_ref[i] = ((made[:, a * cz : (a + 1) * cz] + shift_ref[:1, :]) * factor).astype(BF16)


def upper_pair_kernel(*refs):
    sources, (out_ref, done_ref) = refs[:7], refs[-2:]
    step_rows = rows_of_pass(sources[0].shape[1])
    done_ref[...] = jnp.zeros_like(done_ref)

    def section(step, _):
        pair_rows(out_ref, 0, step, step_rows, *sources)
        return 0

    lax.fori_loop(0, out_ref.shape[0] // step_rows, section, 0)


def lower_pair_kernel(*refs):
    sources, upper, (pair_ref, held, sems) = refs[:7], refs[7], refs[-3:]
    step_rows = rows_of_pass(sources[0].shape[1])
    first = upper.shape[0]
    steps = held.shape[0] // step_rows
    parts = min(PASS_COPIES, step_rows)
    size = step_rows // parts

    def copy(step, part):
        low = step * step_rows + part * size
        return pltpu.make_async_copy(
            held.at[pl.ds(low, size)], pair_ref.at[pl.ds(first + low, size)], sems.at[step * parts + part]
        )

    above = [
        pltpu.make_async_copy(src, dst, sems.at[steps * parts + n])
        for n, (src, dst) in enumerate(pieces(upper, pair_ref, PASS_COPIES))
    ]
    for part in above:
        part.start()

    def section(step, _):
        pair_rows(held, first, step, step_rows, *sources)
        for part in range(parts):
            copy(step, part).start()
        return 0

    lax.fori_loop(0, steps, section, 0)
    for part in above:
        part.wait()
    for step in range(steps):
        for part in range(parts):
            copy(step, part).wait()


def finish_kernel(own, got, mask_ref, diag, gain_ref, hat_ref, spread_ref, out_ref, held, sems):
    seqs, _, channels = hat_ref.shape
    both = ((own[0].astype(F32) + got[0].astype(F32)) * mask_ref[...]).astype(BF16)
    gain = gain_ref[:1, :]
    copies = []
    for s in range(seqs):
        hat = hat_ref[s]
        grad = dot(both, diag[:, s * channels : (s + 1) * channels]) * gain
        held[s] = (
            spread_ref[s][:, :1]
            * (
                grad
                - jnp.mean(grad, axis=-1, keepdims=True)
                - hat * jnp.mean(grad * hat, axis=-1, keepdims=True)
            )
        ).astype(BF16)
        copies.append(pltpu.make_async_copy(held.at[s], out_ref.at[s], sems.at[s]))
        copies[s].start()
    for copy in copies:
        copy.wait()


VMEM = pl.BlockSpec(memory_space=pltpu.VMEM)
HBM = pl.BlockSpec(memory_space=pltpu.HBM)


def call(kernel, name, out_shape, scratch, micros, in_specs=None, out_specs=None, limit=24, aliases=None, after=()):
    def run(*args):
        specs = [VMEM] * len(args) if in_specs is None else in_specs
        specs, args = specs + [pl.BlockSpec(memory_space=pl.ANY)] * len(after), args + tuple(after)
        outs = jax.tree.map(lambda _: VMEM, out_shape) if out_specs is None else out_specs
        return pl.pallas_call(
            kernel,
            out_shape=out_shape,
            in_specs=specs,
            out_specs=outs,
            scratch_shapes=scratch,
            input_output_aliases=aliases or {},
            compiler_params=pltpu.CompilerParams(vmem_limit_bytes=limit * 1024 * 1024),
            cost_estimate=pl.CostEstimate(flops=int(micros * 1e8), bytes_accessed=0, transcendentals=0),
            name=name,
        )(*args)

    return run


def swap_rows(x, blocks, bit):
    moves = [(z * blocks + c, (z ^ bit) * blocks + c) for z in range(blocks) for c in range(blocks)]
    return lax.ppermute(x, PLACES, moves)


def swap_columns(x, blocks, bit):
    moves = [(z * blocks + c, z * blocks + (c ^ bit)) for z in range(blocks) for c in range(blocks)]
    return lax.ppermute(x, PLACES, moves)


def per_device(
    homolog_activations,
    homolog_valid_flags,
    position_valid_flags,
    centering_factor,
    centering_shift,
    first_factor_matrix,
    second_factor_matrix,
    couple_weight_matrix,
    couple_shift_vector,
    loss_sensitivity,
):
    seqs, length, channels = homolog_activations.shape
    total_seq = homolog_valid_flags.shape[0]
    total_res = position_valid_flags.shape[0]
    width = first_factor_matrix.shape[1]
    rows, columns, cz = loss_sensitivity.shape
    blocks = lax.axis_size("cols") * lax.axis_size("sub")
    steps = blocks.bit_length() - 1
    assert blocks == 1 << steps == lax.axis_size("rows") and steps > 0
    half = seqs * width
    deep = total_seq // 2
    span = deep * width
    shape = jax.ShapeDtypeStruct

    def far(x):
        return pltpu.with_memory_space_constraint(x, pltpu.HBM)

    seq_flags, res_flags = far(homolog_valid_flags), far(position_valid_flags)

    stack, diag, mask, hat, spread, gain, loss, weights = call(
        project_kernel,
        "project",
        (
            shape((1, length, 2 * half), BF16),
            shape((2 * half, seqs * channels), BF16),
            shape((length, 2 * half), F32),
            shape((seqs, length, channels), F32),
            shape((seqs, length, cz), F32),
            shape((8, channels), F32),
            shape(loss_sensitivity.shape, BF16),
            shape(couple_weight_matrix.shape, BF16),
        ),
        [
            pltpu.VMEM((total_seq,), jnp.int32),
            pltpu.VMEM((seqs, length, channels), BF16),
            pltpu.VMEM((total_res,), jnp.int32),
            pltpu.VMEM((channels,), F32),
            pltpu.VMEM((channels,), F32),
            pltpu.VMEM((width, channels), BF16),
            pltpu.VMEM((width, channels), BF16),
            pltpu.SemaphoreType.DMA((seqs + 10 + LOSS_COPIES,)),
        ],
        2,
        in_specs=[HBM] * 9,
    )(
        seq_flags,
        far(homolog_activations),
        res_flags,
        far(centering_factor),
        far(centering_shift),
        far(first_factor_matrix.T),
        far(second_factor_matrix.T),
        far(couple_weight_matrix),
        far(loss_sensitivity),
    )

    by_left, by_right, swap, scaled, turned, inverse, row_flags, shift = call(
        prepare_kernel,
        "prepare",
        (
            shape((width, width * cz), BF16),
            shape((width, width * cz), BF16),
            shape((span, span), BF16),
            shape((columns, rows * cz), BF16),
            shape((rows, columns * cz), BF16),
            shape((columns, cz), F32),
            shape((rows, cz), F32),
            shape((8, cz), F32),
        ),
        [
            pltpu.VMEM((total_seq,), jnp.int32),
            pltpu.VMEM((total_res,), jnp.int32),
            pltpu.VMEM((cz,), F32),
            pltpu.VMEM((width * width, cz), F32),
            pltpu.SemaphoreType.DMA((3,)),
        ],
        3,
        in_specs=[HBM] * 3 + [VMEM] * 2,
    )(seq_flags, res_flags, far(couple_shift_vector), loss, weights)

    for step in range(steps):
        got = swap_rows(stack, blocks, blocks >> (step + 1))
        if step < steps - 1:
            stack = call(
                stack_kernel, "stack", shape((2 << step, length, 2 * half), BF16), [], 0.1, after=(shift,)
            )(stack, got)
    low_stack, high_stack = stack, got

    half_blocks = shape((blocks // 2, length, half), BF16)
    all_blocks = shape((blocks, length, half), BF16)
    cols_shape = shape((columns, span), BF16)
    t_limit = 16 + 2 * span * rows * cz * 2 // 2**20

    def make_v(stack, *after):
        return call(
            v_kernel,
            "expand_right",
            (cols_shape, shape((span, columns * cz), BF16)),
            [pltpu.VMEM((columns * deep, width), F32)],
            1.3,
            limit=t_limit,
            after=after,
        )(stack, swap, by_right)

    def gradient(full, side, *after):
        return call(gradient_kernel, "gradient", half_blocks, [], 1.5, limit=t_limit, after=after)(full, side, swap)

    low_cols, v_low = make_v(low_stack)
    low_sum = gradient(v_low, turned)
    lefts = call(lefts_kernel, "lefts", all_blocks, [], 0.1, after=(low_sum,))(low_stack, high_stack)
    got = swap_columns(lefts, blocks, 1)
    high_cols, v_high = make_v(high_stack, lefts)
    for step in range(1, steps):
        lefts = call(
            functools.partial(select_kernel, step - 1), "select", all_blocks, [], 0.1, after=(high_cols,)
        )(lefts, got)
        got = swap_columns(lefts, blocks, 1 << step)
    got_lefts = got
    high_sum = gradient(v_high, turned, lefts)
    sums = call(stack_kernel, "stack", all_blocks, [], 0.1)(low_sum, high_sum)

    def make_t(part, *after):
        return call(
            functools.partial(t_kernel, steps - 1, part),
            "expand_left",
            shape((span, rows * cz), BF16),
            [pltpu.VMEM((rows * deep, width), F32)],
            1.2,
            limit=t_limit,
            after=after,
        )(lefts, got_lefts, by_left)

    def make_t(part, *after):
        return call(
            functools.partial(t_kernel, steps - 1, part),
            "expand_left",
            shape((span, rows * cz), BF16),
            [pltpu.VMEM((rows * deep, width), F32)],
            1.3,
            limit=t_limit,
            after=after,
        )(lefts, got_lefts, by_left)

    for step in range(steps - 1):
        got = swap_columns(sums, blocks, 1 << step)
        sums = call(add_kernel, "add", all_blocks, [], 0.1, after=(got_lefts,))(sums, got)
    got = swap_columns(sums, blocks, 1 << (steps - 1))
    t_high = make_t(1, sums)

    def join(part, right):
        return call(
            functools.partial(join_kernel, part),
            "join",
            shape((blocks // 2, length, 2 * half), BF16),
            [],
            0.1,
        )(right, sums, got)

    send = join(1, gradient(t_high, scaled, sums))
    got_send = swap_rows(send, blocks, 1)
    t_low = make_t(0, send)
    keep = join(0, gradient(t_low, scaled, send))

    pair_sources = (low_cols, high_cols, t_low, t_high, shift, inverse, row_flags)
    upper_rows = rows // 4
    upper, paired = call(
        upper_pair_kernel,
        "pair",
        (shape((upper_rows, columns, cz), BF16), shape((8, cz), F32)),
        [],
        1,
        limit=t_limit,
        after=(keep,),
    )(*pair_sources)
    for step in range(1, steps):
        some = shape((blocks >> (step + 1), length, 2 * half), BF16)
        keep, send = call(halve_kernel, "halve", (some, some), [], 0.1, after=(paired,))(keep, got_send)
        got_send = swap_rows(send, blocks, 1 << step)
    pair = call(
        lower_pair_kernel,
        "pair",
        shape(loss_sensitivity.shape, BF16),
        [
            pltpu.VMEM((rows - upper_rows, columns, cz), BF16),
            pltpu.SemaphoreType.DMA((PASS_COPIES * (1 + (rows - upper_rows) // rows_of_pass(span)),)),
        ],
        2,
        out_specs=HBM,
        limit=t_limit,
        after=(send,),
    )(*pair_sources, upper)

    alignment = call(
        finish_kernel,
        "finish",
        shape(homolog_activations.shape, BF16),
        [pltpu.VMEM(homolog_activations.shape, BF16), pltpu.SemaphoreType.DMA((seqs,))],
        1,
        out_specs=HBM,
    )(keep, got_send, mask, diag, gain, hat, spread)
    return pair, alignment


def solution(mesh):
    split = P(("groups", "rows"), ("cols", "sub"), None)
    return jax.shard_map(
        per_device,
        mesh=mesh,
        in_specs=(split, P("groups"), P("groups"), P(), P(), P(), P(), P(), P(), split),
        out_specs=(split, split),
        check_vma=False,
    )
```

```python
import functools

import jax
import jax.numpy as jnp
from jax import lax
from jax.experimental import pallas as pl
from jax.experimental.pallas import tpu as pltpu
from jax.sharding import PartitionSpec as P

F32 = jnp.float32
BF16 = jnp.bfloat16
PLACES = ("rows", "cols", "sub")
PRODUCED = 256
TILE = 16


def dot(a, b):
    return lax.dot_general(a, b, (((1,), (0,)), ((), ())), preferred_element_type=F32)


def dot_t(a, b):
    return lax.dot_general(a, b, (((1,), (1,)), ((), ())), preferred_element_type=F32)


def place():
    column = lax.axis_index("cols") * lax.axis_size("sub") + lax.axis_index("sub")
    return lax.axis_index("rows"), column


def lanes_at(start, size):
    return pl.ds(pl.multiple_of(start, size), size)


def flag_row(flags_ref):
    return flags_ref[...].astype(F32).reshape(1, -1)


def flag_column(flags_ref, start, length):
    flags = flag_row(flags_ref)
    total = flags.shape[1]
    spot = lax.broadcasted_iota(jnp.int32, (length, total), 0) + start
    lane = lax.broadcasted_iota(jnp.int32, (length, total), 1)
    return jnp.sum(jnp.where(spot == lane, flags, 0.0), axis=1, keepdims=True)


def load_all(pairs, sems):
    copies = [pltpu.make_async_copy(src, dst, sems.at[n]) for n, (src, dst) in enumerate(pairs)]
    for copy in copies:
        copy.start()
    return copies


def project_kernel(*refs):
    sources, outs, (loss_ref, w_ref), held, sems = refs[:9], refs[9:15], refs[15:17], refs[17:24], refs[24]
    out_ref, diag, mask_ref, hat_ref, spread_ref, gain_out = outs
    copies = load_all(list(zip(sources, held + (w_ref, loss_ref))), sems)
    seq_ref, x_ref, res_ref, gain_ref, bias_ref, first_ref, second_ref = held
    row_at, column_at = place()
    seqs, length, channels = x_ref.shape
    width = first_ref.shape[0]
    half = seqs * width
    diag[...] = jnp.zeros_like(diag)
    for copy in copies[:7]:
        copy.wait()
    for s in range(seqs):
        lanes = slice(s * channels, (s + 1) * channels)
        diag[s * width : (s + 1) * width, lanes] = first_ref[...]
        diag[(seqs + s) * width : (seqs + s + 1) * width, lanes] = second_ref[...]
    flags = flag_row(seq_ref)
    spot = lax.broadcasted_iota(jnp.int32, flags.shape, 1)
    which = lax.broadcasted_iota(jnp.int32, (1, 2 * half), 1) % half // width
    own = jnp.zeros((1, 2 * half), F32)
    for s in range(seqs):
        value = jnp.sum(jnp.where(spot == row_at * seqs + s, flags, 0.0), axis=1, keepdims=True)
        own = jnp.where(which == s, value, own)
    mask = flag_column(res_ref, column_at * length, length) * own
    mask_ref[...] = mask
    gain = gain_ref[...].reshape(1, channels)
    bias = bias_ref[...].reshape(1, channels)
    gain_out[...] = jnp.broadcast_to(gain, gain_out.shape)
    total = jnp.zeros((length, 2 * half), F32)
    for s in range(seqs):
        x = x_ref[s].astype(F32)
        off = x - jnp.mean(x, axis=-1, keepdims=True)
        spread = lax.rsqrt(jnp.mean(off * off, axis=-1, keepdims=True) + 1e-05)
        hat = off * spread
        hat_ref[s] = hat
        spread_ref[s] = jnp.broadcast_to(spread, spread_ref.shape[1:])
        normed = (hat * gain + bias).astype(BF16)
        total += dot_t(normed, diag[:, s * channels : (s + 1) * channels])
    out_ref[0] = (total * mask).astype(BF16)
    for copy in copies[7:]:
        copy.wait()


def prepare_kernel(*refs):
    sources, (loss_ref, w_ref), outs, held, (wide_w, sems) = (
        refs[:3],
        refs[3:5],
        refs[5:13],
        refs[13:16],
        refs[16:],
    )
    by_left, by_right, swap, scaled, turned, inverse_ref, row_ref, shift_out = outs
    seq_ref, res_ref, shift_ref = held
    copies = load_all(list(zip(sources, held)), sems)
    row_at, column_at = place()
    rows, length, cz = loss_ref.shape
    width = by_left.shape[0]
    span = swap.shape[0]
    deep = span // width
    wide_w[...] = w_ref[...].astype(F32)
    for n in range(width):
        by_left[:, n * cz : (n + 1) * cz] = wide_w[pl.ds(n, width, stride=width), :].astype(BF16)
        by_right[:, n * cz : (n + 1) * cz] = w_ref[n * width : (n + 1) * width, :]
    to = lax.broadcasted_iota(jnp.int32, (span, span), 0)
    at = lax.broadcasted_iota(jnp.int32, (span, span), 1)
    swap[...] = jnp.where((to // deep == at % width) & (to % deep == at // width), 1.0, 0.0).astype(BF16)
    for copy in copies:
        copy.wait()
    present = jnp.sum(flag_row(seq_ref), axis=1, keepdims=True)
    columns = flag_column(res_ref, column_at * length, length)
    inverse = jnp.broadcast_to(1.0 / jnp.maximum(present * columns, 1.0), (length, cz))
    inverse_ref[...] = inverse
    row_ref[...] = jnp.broadcast_to(flag_column(res_ref, row_at * rows, rows), (rows, cz))
    shift_out[...] = jnp.broadcast_to(shift_ref[...].reshape(1, cz), shift_out.shape)
    for i in range(rows):
        factor = jnp.where(row_ref[i : i + 1, :] > 0.0, inverse, 1.0)
        scaled[:, i * cz : (i + 1) * cz] = (loss_ref[i].astype(F32) * factor).astype(BF16)
    to = lax.broadcasted_iota(jnp.int32, (TILE * TILE, TILE * TILE), 0)
    at = lax.broadcasted_iota(jnp.int32, (TILE * TILE, TILE * TILE), 1)
    turn = jnp.where((to // TILE == at % TILE) & (to % TILE == at // TILE), 1.0, 0.0).astype(BF16)
    for i in range(0, rows, TILE):
        for j in range(0, length, 2 * TILE):
            taken = [
                jnp.concatenate(
                    [scaled[b : b + TILE, (i + k) * cz : (i + k + 1) * cz] for k in range(TILE)], axis=0
                )
                for b in (j, j + TILE)
            ]
            made = dot(turn, jnp.concatenate(taken, axis=1)).astype(BF16)
            for a in range(2):
                for k in range(TILE):
                    low = (j + a * TILE + k) * cz
                    turned[i : i + TILE, low : low + cz] = made[
                        k * TILE : (k + 1) * TILE, a * cz : (a + 1) * cz
                    ]


def stack_kernel(own, got, *refs):
    out = refs[-1]
    count = own.shape[0]
    out[:count] = own[...]
    out[count:] = got[...]


def lefts_kernel(own, got, *refs):
    out = refs[-1]
    count, _, half = out.shape
    for n in range(count // 2):
        out[n] = own[n, :, :half]
        out[count // 2 + n] = got[n, :, :half]


def crossed(n, count, bit):
    if bit > 0:
        return n
    mirrored, size = 0, 1
    while size < count:
        mirrored, size = mirrored * 2 + n // size % 2, size * 2
    return mirrored


def select_kernel(bit, own, got, *refs):
    out = refs[-1]
    row_at, column_at = place()
    other = (row_at ^ column_at) >> bit & 1
    count = out.shape[0]

    @pl.when(other == 1)
    def _():
        for n in range(count):
            out[n] = got[crossed(n, count, bit)]

    @pl.when(other == 0)
    def _():
        out[...] = own[...]


def add_kernel(bit, own, got, *refs):
    out = refs[-1]
    count = out.shape[0]
    for n in range(count):
        out[n] = (own[n].astype(F32) + got[crossed(n, count, bit)].astype(F32)).astype(BF16)


def mark_kernel(*refs):
    refs[-1][...] = jnp.zeros_like(refs[-1])


def spread_rows(rows, n, block, width, deep):
    length, half = block.shape
    seqs = half // width
    wide = block.astype(F32)
    for s in range(seqs):
        rows[pl.ds(n * seqs + s, length, stride=deep), :] = wide[:, s * width : (s + 1) * width]


def produce(out, rows, weight, deep):
    width = weight.shape[0]
    cz = weight.shape[1] // width
    chunk = min(2 * PRODUCED, rows.shape[0]) // deep

    def section(step, _):
        taken = rows[lanes_at(step * chunk * deep, chunk * deep), :].astype(BF16)
        for n in range(width // 2):
            made = dot(taken, weight[:, n * 2 * cz : (n + 1) * 2 * cz])
            for i in range(chunk):
                both = jnp.concatenate(
                    [made[i * deep : (i + 1) * deep, a * cz : (a + 1) * cz] for a in range(2)], axis=0
                )
                low = n * 2 * deep
                out[low : low + 2 * deep, lanes_at((step * chunk + i) * cz, cz)] = both.astype(BF16)
        return 0

    lax.fori_loop(0, rows.shape[0] // (chunk * deep), section, 0)


def v_kernel(stack, swap, weight, *refs):
    right_cols, v_ref, rows = refs[-3:]
    count, _, both = stack.shape
    width = weight.shape[0]
    deep = swap.shape[0] // width
    for n in range(count):
        spread_rows(rows, n, stack[n, :, both // 2 :], width, deep)
    right = jnp.concatenate([stack[n, :, both // 2 :] for n in range(count)], axis=1)
    right_cols[...] = dot_t(right, swap[...]).astype(BF16)
    produce(v_ref, rows, weight, deep)


def t_kernel(bit, part, own, got, weight, *refs):
    t_ref, rows = refs[-2:]
    row_at, column_at = place()
    count = own.shape[0] // 2
    width = weight.shape[0]
    deep = t_ref.shape[0] // width
    other = (row_at ^ column_at) >> bit & 1
    for n in range(count):
        k = part * count + n
        block = jnp.where(other == 1, got[k].astype(F32), own[k].astype(F32))
        spread_rows(rows, n, block, width, deep)
    produce(t_ref, rows, weight, deep)


def ungroup(out, acc, swap):
    half = out.shape[2]
    made = dot(acc.astype(BF16), swap[...]).astype(BF16)
    for k in range(out.shape[0]):
        out[k] = made[:, k * half : (k + 1) * half]


def gradient_kernel(full_ref, side, swap, *refs):
    out = refs[-1]
    span = swap.shape[0]
    size = side.shape[1] * PRODUCED // span

    def section(step, acc):
        lanes = lanes_at(step * size, size)
        return acc + dot_t(full_ref[:, lanes], side[:, lanes])

    acc = dot_t(full_ref[:, :size], side[:, :size])
    acc = lax.fori_loop(1, span // PRODUCED, section, acc)
    ungroup(out, jnp.transpose(acc), swap)


def join_kernel(part, right, own, got, out):
    row_at, column_at = place()
    mine = jnp.where(row_at == column_at, 1.0, 0.0)
    half = right.shape[2]
    count = right.shape[0]
    for n in range(count):
        k = part * count + n
        out[n, :, :half] = ((own[k].astype(F32) + got[k].astype(F32)) * mine).astype(BF16)
    out[:, :, half:] = right[...]


def halve_kernel(own, got, *refs):
    keep, send = refs[-2:]
    count = keep.shape[0]
    keep[...] = (own[:count].astype(F32) + got[:count].astype(F32)).astype(BF16)
    send[...] = (own[count:].astype(F32) + got[count:].astype(F32)).astype(BF16)


def rows_of_pass(span):
    return max(2, 8 * PRODUCED // span)


def pair_rows(out_ref, first, step, step_rows, low_cols, high_cols, t_low, t_high, shift_ref, inverse_ref, row_ref):
    cz = out_ref.shape[2]
    for n in range(step_rows // 2):
        lanes = lanes_at((first + step * step_rows + 2 * n) * cz, 2 * cz)
        made = dot(low_cols[...], t_low[:, lanes]) + dot(high_cols[...], t_high[:, lanes])
        for a in range(2):
            i = step * step_rows + 2 * n + a
            factor = jnp.where(row_ref[pl.ds(first + i, 1), :] > 0.0, inverse_ref[...], 1.0)
            out_ref[i] = ((made[:, a * cz : (a + 1) * cz] + shift_ref[:1, :]) * factor).astype(BF16)


def upper_pair_kernel(*refs):
    sources, (out_ref, done_ref) = refs[:7], refs[-2:]
    step_rows = rows_of_pass(sources[0].shape[1])
    done_ref[...] = jnp.zeros_like(done_ref)

    def section(step, _):
        pair_rows(out_ref, 0, step, step_rows, *sources)
        return 0

    lax.fori_loop(0, out_ref.shape[0] // step_rows, section, 0)


def lower_pair_kernel(*refs):
    sources, upper, (pair_ref, held, sems) = refs[:7], refs[7], refs[-3:]
    step_rows = rows_of_pass(sources[0].shape[1])
    first = upper.shape[0]
    steps = held.shape[0] // step_rows

    def copy(step):
        spot = pl.ds(step * step_rows, step_rows)
        return pltpu.make_async_copy(
            held.at[spot], pair_ref.at[pl.ds(first + step * step_rows, step_rows)], sems.at[1 + step]
        )

    above = pltpu.make_async_copy(upper, pair_ref.at[:first], sems.at[0])
    above.start()

    def section(step, _):
        pair_rows(held, first, step, step_rows, *sources)
        copy(step).start()
        return 0

    lax.fori_loop(0, steps, section, 0)
    above.wait()
    for step in range(steps):
        copy(step).wait()


def finish_kernel(own, got, mask_ref, diag, gain_ref, hat_ref, spread_ref, out_ref, held, sems):
    seqs, _, channels = hat_ref.shape
    both = ((own[0].astype(F32) + got[0].astype(F32)) * mask_ref[...]).astype(BF16)
    gain = gain_ref[:1, :]
    copies = []
    for s in range(seqs):
        hat = hat_ref[s]
        grad = dot(both, diag[:, s * channels : (s + 1) * channels]) * gain
        held[s] = (
            spread_ref[s][:, :1]
            * (
                grad
                - jnp.mean(grad, axis=-1, keepdims=True)
                - hat * jnp.mean(grad * hat, axis=-1, keepdims=True)
            )
        ).astype(BF16)
        copies.append(pltpu.make_async_copy(held.at[s], out_ref.at[s], sems.at[s]))
        copies[s].start()
    for copy in copies:
        copy.wait()


VMEM = pl.BlockSpec(memory_space=pltpu.VMEM)
HBM = pl.BlockSpec(memory_space=pltpu.HBM)


def call(kernel, name, out_shape, scratch, micros, in_specs=None, out_specs=None, limit=24, aliases=None, after=()):
    def run(*args):
        specs = [VMEM] * len(args) if in_specs is None else in_specs
        specs, args = specs + [pl.BlockSpec(memory_space=pl.ANY)] * len(after), args + tuple(after)
        outs = jax.tree.map(lambda _: VMEM, out_shape) if out_specs is None else out_specs
        return pl.pallas_call(
            kernel,
            out_shape=out_shape,
            in_specs=specs,
            out_specs=outs,
            scratch_shapes=scratch,
            input_output_aliases=aliases or {},
            compiler_params=pltpu.CompilerParams(vmem_limit_bytes=limit * 1024 * 1024),
            cost_estimate=pl.CostEstimate(flops=int(micros * 1e8), bytes_accessed=0, transcendentals=0),
            name=name,
        )(*args)

    return run


def swap_rows(x, blocks, step):
    bits = (1 << step, blocks >> (step + 1))
    moves = [(z * blocks + c, (z ^ bits[c % 2]) * blocks + c) for z in range(blocks) for c in range(blocks)]
    return lax.ppermute(x, PLACES, moves)


def swap_columns(x, blocks, bit):
    moves = [(z * blocks + c, z * blocks + (c ^ bit)) for z in range(blocks) for c in range(blocks)]
    return lax.ppermute(x, PLACES, moves)


def per_device(
    homolog_activations,
    homolog_valid_flags,
    position_valid_flags,
    centering_factor,
    centering_shift,
    first_factor_matrix,
    second_factor_matrix,
    couple_weight_matrix,
    couple_shift_vector,
    loss_sensitivity,
):
    seqs, length, channels = homolog_activations.shape
    total_seq = homolog_valid_flags.shape[0]
    total_res = position_valid_flags.shape[0]
    width = first_factor_matrix.shape[1]
    rows, columns, cz = loss_sensitivity.shape
    blocks = lax.axis_size("cols") * lax.axis_size("sub")
    steps = blocks.bit_length() - 1
    assert blocks == 1 << steps == lax.axis_size("rows") and steps > 0
    half = seqs * width
    deep = total_seq // 2
    span = deep * width
    shape = jax.ShapeDtypeStruct

    def far(x):
        return pltpu.with_memory_space_constraint(x, pltpu.HBM)

    seq_flags, res_flags = far(homolog_valid_flags), far(position_valid_flags)

    stack, diag, mask, hat, spread, gain, loss, weights = call(
        project_kernel,
        "project",
        (
            shape((1, length, 2 * half), BF16),
            shape((2 * half, seqs * channels), BF16),
            shape((length, 2 * half), F32),
            shape((seqs, length, channels), F32),
            shape((seqs, length, cz), F32),
            shape((8, channels), F32),
            shape(loss_sensitivity.shape, BF16),
            shape(couple_weight_matrix.shape, BF16),
        ),
        [
            pltpu.VMEM((total_seq,), jnp.int32),
            pltpu.VMEM((seqs, length, channels), BF16),
            pltpu.VMEM((total_res,), jnp.int32),
            pltpu.VMEM((channels,), F32),
            pltpu.VMEM((channels,), F32),
            pltpu.VMEM((width, channels), BF16),
            pltpu.VMEM((width, channels), BF16),
            pltpu.SemaphoreType.DMA((9,)),
        ],
        2,
        in_specs=[HBM] * 9,
    )(
        seq_flags,
        far(homolog_activations),
        res_flags,
        far(centering_factor),
        far(centering_shift),
        far(first_factor_matrix.T),
        far(second_factor_matrix.T),
        far(couple_weight_matrix),
        far(loss_sensitivity),
    )

    by_left, by_right, swap, scaled, turned, inverse, row_flags, shift = call(
        prepare_kernel,
        "prepare",
        (
            shape((width, width * cz), BF16),
            shape((width, width * cz), BF16),
            shape((span, span), BF16),
            shape((columns, rows * cz), BF16),
            shape((rows, columns * cz), BF16),
            shape((columns, cz), F32),
            shape((rows, cz), F32),
            shape((8, cz), F32),
        ),
        [
            pltpu.VMEM((total_seq,), jnp.int32),
            pltpu.VMEM((total_res,), jnp.int32),
            pltpu.VMEM((cz,), F32),
            pltpu.VMEM((width * width, cz), F32),
            pltpu.SemaphoreType.DMA((3,)),
        ],
        3,
        in_specs=[HBM] * 3 + [VMEM] * 2,
    )(seq_flags, res_flags, far(couple_shift_vector), loss, weights)

    for step in range(steps):
        got = swap_rows(stack, blocks, step)
        if step < steps - 1:
            stack = call(
                stack_kernel, "stack", shape((2 << step, length, 2 * half), BF16), [], 0.1, after=(shift,)
            )(stack, got)
    low_stack, high_stack = stack, got

    half_blocks = shape((blocks // 2, length, half), BF16)
    all_blocks = shape((blocks, length, half), BF16)
    cols_shape = shape((columns, span), BF16)
    t_limit = 16 + 2 * span * rows * cz * 2 // 2**20

    def make_v(stack, *after):
        return call(
            v_kernel,
            "expand_right",
            (cols_shape, shape((span, columns * cz), BF16)),
            [pltpu.VMEM((columns * deep, width), F32)],
            1.3,
            limit=t_limit,
            after=after,
        )(stack, swap, by_right)

    def gradient(full, side, *after):
        return call(gradient_kernel, "gradient", half_blocks, [], 1.5, limit=t_limit, after=after)(full, side, swap)

    low_cols, v_low = make_v(low_stack)
    lefts = call(lefts_kernel, "lefts", all_blocks, [], 0.1, after=(low_cols,))(low_stack, high_stack)
    got = swap_columns(lefts, blocks, 1)
    high_cols, v_high = make_v(high_stack, lefts)
    for step in range(1, steps):
        lefts = call(
            functools.partial(select_kernel, step - 1), "select", all_blocks, [], 0.1, after=(high_cols,)
        )(lefts, got)
        got = swap_columns(lefts, blocks, 1 << step)
    got_lefts = got
    low_sum = gradient(v_low, turned, lefts)
    high_sum = gradient(v_high, turned, lefts)
    sums = call(stack_kernel, "stack", all_blocks, [], 0.1)(low_sum, high_sum)

    def make_t(part, *after):
        return call(
            functools.partial(t_kernel, steps - 1, part),
            "expand_left",
            shape((span, rows * cz), BF16),
            [pltpu.VMEM((rows * deep, width), F32)],
            1.2,
            limit=t_limit,
            after=after,
        )(lefts, got_lefts, by_left)

    def make_t(part, *after):
        return call(
            functools.partial(t_kernel, steps - 1, part),
            "expand_left",
            shape((span, rows * cz), BF16),
            [pltpu.VMEM((rows * deep, width), F32)],
            1.3,
            limit=t_limit,
            after=after,
        )(lefts, got_lefts, by_left)

    arrived = call(mark_kernel, "mark", shape((8, cz), F32), [], 0.1, after=(got_lefts,))()
    for step in range(steps - 1):
        got = swap_columns(sums, blocks, 1 << step)
        sums = call(functools.partial(add_kernel, step), "add", all_blocks, [], 0.1, after=(arrived,))(sums, got)
    got = swap_columns(sums, blocks, 1 << (steps - 1))
    t_high = make_t(1, sums)

    def join(part, right):
        return call(
            functools.partial(join_kernel, part),
            "join",
            shape((blocks // 2, length, 2 * half), BF16),
            [],
            0.1,
        )(right, sums, got)

    send = join(1, gradient(t_high, scaled, sums))
    got_send = swap_rows(send, blocks, steps - 1)
    t_low = make_t(0, send)
    keep = join(0, gradient(t_low, scaled, send))

    pair_sources = (low_cols, high_cols, t_low, t_high, shift, inverse, row_flags)
    upper_rows = rows // 4
    upper, paired = call(
        upper_pair_kernel,
        "pair",
        (shape((upper_rows, columns, cz), BF16), shape((8, cz), F32)),
        [],
        1,
        limit=t_limit,
        after=(keep,),
    )(*pair_sources)
    for step in range(1, steps):
        some = shape((blocks >> (step + 1), length, 2 * half), BF16)
        keep, send = call(halve_kernel, "halve", (some, some), [], 0.1, after=(paired,))(keep, got_send)
        got_send = swap_rows(send, blocks, steps - 1 - step)
    pair = call(
        lower_pair_kernel,
        "pair",
        shape(loss_sensitivity.shape, BF16),
        [
            pltpu.VMEM((rows - upper_rows, columns, cz), BF16),
            pltpu.SemaphoreType.DMA((1 + (rows - upper_rows) // rows_of_pass(span),)),
        ],
        2,
        out_specs=HBM,
        limit=t_limit,
        after=(send,),
    )(*pair_sources, upper)

    alignment = call(
        finish_kernel,
        "finish",
        shape(homolog_activations.shape, BF16),
        [pltpu.VMEM(homolog_activations.shape, BF16), pltpu.SemaphoreType.DMA((seqs,))],
        1,
        out_specs=HBM,
    )(keep, got_send, mask, diag, gain, hat, spread)
    return pair, alignment


def solution(mesh):
    split = P(("groups", "rows"), ("cols", "sub"), None)
    return jax.shard_map(
        per_device,
        mesh=mesh,
        in_specs=(split, P("groups"), P("groups"), P(), P(), P(), P(), P(), P(), split),
        out_specs=(split, split),
        check_vma=False,
    )
```

```python
import functools

import jax
import jax.numpy as jnp
from jax import lax
from jax.experimental import pallas as pl
from jax.experimental.pallas import tpu as pltpu
from jax.sharding import PartitionSpec as P

F32 = jnp.float32
BF16 = jnp.bfloat16
PLACES = ("rows", "cols", "sub")
PRODUCED = 256
TILE = 16


def dot(a, b):
    return lax.dot_general(a, b, (((1,), (0,)), ((), ())), preferred_element_type=F32)


def dot_t(a, b):
    return lax.dot_general(a, b, (((1,), (1,)), ((), ())), preferred_element_type=F32)


def place():
    column = lax.axis_index("cols") * lax.axis_size("sub") + lax.axis_index("sub")
    return lax.axis_index("rows"), column


def lanes_at(start, size):
    return pl.ds(pl.multiple_of(start, size), size)


def flag_row(flags_ref):
    return flags_ref[...].astype(F32).reshape(1, -1)


def flag_column(flags_ref, start, length):
    flags = flag_row(flags_ref)
    total = flags.shape[1]
    spot = lax.broadcasted_iota(jnp.int32, (length, total), 0) + start
    lane = lax.broadcasted_iota(jnp.int32, (length, total), 1)
    return jnp.sum(jnp.where(spot == lane, flags, 0.0), axis=1, keepdims=True)


def load_all(pairs, sems):
    copies = [pltpu.make_async_copy(src, dst, sems.at[n]) for n, (src, dst) in enumerate(pairs)]
    for copy in copies:
        copy.start()
    return copies


def project_kernel(*refs):
    sources, outs, held, sems = refs[:7], refs[7:13], refs[13:20], refs[20]
    out_ref, diag, mask_ref, hat_ref, spread_ref, gain_out = outs
    copies = load_all(list(zip(sources, held)), sems)
    seq_ref, x_ref, res_ref, gain_ref, bias_ref, first_ref, second_ref = held
    row_at, column_at = place()
    seqs, length, channels = x_ref.shape
    width = first_ref.shape[0]
    half = seqs * width
    diag[...] = jnp.zeros_like(diag)
    for copy in copies:
        copy.wait()
    for s in range(seqs):
        lanes = slice(s * channels, (s + 1) * channels)
        diag[s * width : (s + 1) * width, lanes] = first_ref[...]
        diag[(seqs + s) * width : (seqs + s + 1) * width, lanes] = second_ref[...]
    flags = flag_row(seq_ref)
    spot = lax.broadcasted_iota(jnp.int32, flags.shape, 1)
    which = lax.broadcasted_iota(jnp.int32, (1, 2 * half), 1) % half // width
    own = jnp.zeros((1, 2 * half), F32)
    for s in range(seqs):
        value = jnp.sum(jnp.where(spot == row_at * seqs + s, flags, 0.0), axis=1, keepdims=True)
        own = jnp.where(which == s, value, own)
    mask = flag_column(res_ref, column_at * length, length) * own
    mask_ref[...] = mask
    gain = gain_ref[...].reshape(1, channels)
    bias = bias_ref[...].reshape(1, channels)
    gain_out[...] = jnp.broadcast_to(gain, gain_out.shape)
    total = jnp.zeros((length, 2 * half), F32)
    for s in range(seqs):
        x = x_ref[s].astype(F32)
        off = x - jnp.mean(x, axis=-1, keepdims=True)
        spread = lax.rsqrt(jnp.mean(off * off, axis=-1, keepdims=True) + 1e-05)
        hat = off * spread
        hat_ref[s] = hat
        spread_ref[s] = jnp.broadcast_to(spread, spread_ref.shape[1:])
        normed = (hat * gain + bias).astype(BF16)
        total += dot_t(normed, diag[:, s * channels : (s + 1) * channels])
    out_ref[0] = (total * mask).astype(BF16)


def prepare_kernel(*refs):
    sources, outs, held, (wide_w, sems) = refs[:5], refs[5:13], refs[13:18], refs[18:]
    by_left, by_right, swap, scaled, turned, inverse_ref, row_ref, shift_out = outs
    w_ref, loss_ref, seq_ref, res_ref, shift_ref = held
    copies = load_all(list(zip(sources, held)), sems)
    row_at, column_at = place()
    rows, length, cz = loss_ref.shape
    width = by_left.shape[0]
    span = swap.shape[0]
    deep = span // width
    to = lax.broadcasted_iota(jnp.int32, (span, span), 0)
    at = lax.broadcasted_iota(jnp.int32, (span, span), 1)
    swap[...] = jnp.where((to // deep == at % width) & (to % deep == at // width), 1.0, 0.0).astype(BF16)
    to = lax.broadcasted_iota(jnp.int32, (TILE * TILE, TILE * TILE), 0)
    at = lax.broadcasted_iota(jnp.int32, (TILE * TILE, TILE * TILE), 1)
    turn = jnp.where((to // TILE == at % TILE) & (to % TILE == at // TILE), 1.0, 0.0).astype(BF16)
    copies[0].wait()
    wide_w[...] = w_ref[...].astype(F32)
    for n in range(width):
        by_left[:, n * cz : (n + 1) * cz] = wide_w[pl.ds(n, width, stride=width), :].astype(BF16)
        by_right[:, n * cz : (n + 1) * cz] = w_ref[n * width : (n + 1) * width, :]
    for copy in copies[1:]:
        copy.wait()
    present = jnp.sum(flag_row(seq_ref), axis=1, keepdims=True)
    columns = flag_column(res_ref, column_at * length, length)
    inverse = jnp.broadcast_to(1.0 / jnp.maximum(present * columns, 1.0), (length, cz))
    inverse_ref[...] = inverse
    row_ref[...] = jnp.broadcast_to(flag_column(res_ref, row_at * rows, rows), (rows, cz))
    shift_out[...] = jnp.broadcast_to(shift_ref[...].reshape(1, cz), shift_out.shape)
    for i in range(rows):
        factor = jnp.where(row_ref[i : i + 1, :] > 0.0, inverse, 1.0)
        scaled[:, i * cz : (i + 1) * cz] = (loss_ref[i].astype(F32) * factor).astype(BF16)
    for i in range(0, rows, TILE):
        for j in range(0, length, 2 * TILE):
            taken = [
                jnp.concatenate(
                    [scaled[b : b + TILE, (i + k) * cz : (i + k + 1) * cz] for k in range(TILE)], axis=0
                )
                for b in (j, j + TILE)
            ]
            made = dot(turn, jnp.concatenate(taken, axis=1)).astype(BF16)
            for a in range(2):
                for k in range(TILE):
                    low = (j + a * TILE + k) * cz
                    turned[i : i + TILE, low : low + cz] = made[
                        k * TILE : (k + 1) * TILE, a * cz : (a + 1) * cz
                    ]


def stack_kernel(own, got, *refs):
    out = refs[-1]
    count = own.shape[0]
    out[:count] = own[...]
    out[count:] = got[...]


def lefts_kernel(own, got, *refs):
    out = refs[-1]
    count, _, half = out.shape
    for n in range(count // 2):
        out[n] = own[n, :, :half]
        out[count // 2 + n] = got[n, :, :half]


def select_kernel(bit, own, got, *refs):
    out = refs[-1]
    row_at, column_at = place()
    other = (row_at ^ column_at) >> bit & 1

    @pl.when(other == 1)
    def _():
        out[...] = got[...]

    @pl.when(other == 0)
    def _():
        out[...] = own[...]


def add_kernel(own, got, *refs):
    out = refs[-1]
    out[...] = (own[...].astype(F32) + got[...].astype(F32)).astype(BF16)


def mark_kernel(*refs):
    refs[-1][...] = jnp.zeros_like(refs[-1])


def spread_rows(rows, n, block, width, deep):
    length, half = block.shape
    seqs = half // width
    wide = block.astype(F32)
    for s in range(seqs):
        rows[pl.ds(n * seqs + s, length, stride=deep), :] = wide[:, s * width : (s + 1) * width]


def produce(out, rows, weight, deep):
    width = weight.shape[0]
    cz = weight.shape[1] // width
    chunk = min(2 * PRODUCED, rows.shape[0]) // deep

    def section(step, _):
        taken = rows[lanes_at(step * chunk * deep, chunk * deep), :].astype(BF16)
        for n in range(width // 2):
            made = dot(taken, weight[:, n * 2 * cz : (n + 1) * 2 * cz])
            for i in range(chunk):
                both = jnp.concatenate(
                    [made[i * deep : (i + 1) * deep, a * cz : (a + 1) * cz] for a in range(2)], axis=0
                )
                low = n * 2 * deep
                out[low : low + 2 * deep, lanes_at((step * chunk + i) * cz, cz)] = both.astype(BF16)
        return 0

    lax.fori_loop(0, rows.shape[0] // (chunk * deep), section, 0)


def v_kernel(stack, swap, weight, *refs):
    right_cols, v_ref, rows = refs[-3:]
    count, _, both = stack.shape
    width = weight.shape[0]
    deep = swap.shape[0] // width
    for n in range(count):
        spread_rows(rows, n, stack[n, :, both // 2 :], width, deep)
    right = jnp.concatenate([stack[n, :, both // 2 :] for n in range(count)], axis=1)
    right_cols[...] = dot_t(right, swap[...]).astype(BF16)
    produce(v_ref, rows, weight, deep)


def t_kernel(bit, part, own, got, weight, *refs):
    t_ref, rows = refs[-2:]
    row_at, column_at = place()
    count = own.shape[0] // 2
    width = weight.shape[0]
    deep = t_ref.shape[0] // width
    other = (row_at ^ column_at) >> bit & 1
    for n in range(count):
        k = part * count + n
        block = jnp.where(other == 1, got[k].astype(F32), own[k].astype(F32))
        spread_rows(rows, n, block, width, deep)
    produce(t_ref, rows, weight, deep)


def ungroup(out, acc, swap):
    half = out.shape[2]
    made = dot(acc.astype(BF16), swap[...]).astype(BF16)
    for k in range(out.shape[0]):
        out[k] = made[:, k * half : (k + 1) * half]


def gradient_kernel(full_ref, side, swap, *refs):
    out = refs[-1]
    span = swap.shape[0]
    size = side.shape[1] * PRODUCED // span

    def section(step, acc):
        lanes = lanes_at(step * size, size)
        return acc + dot_t(full_ref[:, lanes], side[:, lanes])

    acc = dot_t(full_ref[:, :size], side[:, :size])
    acc = lax.fori_loop(1, span // PRODUCED, section, acc)
    ungroup(out, jnp.transpose(acc), swap)


def join_kernel(part, right, own, got, out):
    row_at, column_at = place()
    mine = jnp.where(row_at == column_at, 1.0, 0.0)
    half = right.shape[2]
    count = right.shape[0]
    for n in range(count):
        k = part * count + n
        out[n, :, :half] = ((own[k].astype(F32) + got[k].astype(F32)) * mine).astype(BF16)
    out[:, :, half:] = right[...]


def halve_kernel(own, got, *refs):
    keep, send = refs[-2:]
    count = keep.shape[0]
    keep[...] = (own[:count].astype(F32) + got[:count].astype(F32)).astype(BF16)
    send[...] = (own[count:].astype(F32) + got[count:].astype(F32)).astype(BF16)


def rows_of_pass(span):
    return max(2, 8 * PRODUCED // span)


def pair_rows(out_ref, first, step, step_rows, low_cols, high_cols, t_low, t_high, shift_ref, inverse_ref, row_ref):
    cz = out_ref.shape[2]
    for n in range(step_rows // 2):
        lanes = lanes_at((first + step * step_rows + 2 * n) * cz, 2 * cz)
        made = dot(low_cols[...], t_low[:, lanes]) + dot(high_cols[...], t_high[:, lanes])
        for a in range(2):
            i = step * step_rows + 2 * n + a
            factor = jnp.where(row_ref[pl.ds(first + i, 1), :] > 0.0, inverse_ref[...], 1.0)
            out_ref[i] = ((made[:, a * cz : (a + 1) * cz] + shift_ref[:1, :]) * factor).astype(BF16)


def upper_pair_kernel(*refs):
    sources, (out_ref, done_ref) = refs[:7], refs[-2:]
    step_rows = rows_of_pass(sources[0].shape[1])
    done_ref[...] = jnp.zeros_like(done_ref)

    def section(step, _):
        pair_rows(out_ref, 0, step, step_rows, *sources)
        return 0

    lax.fori_loop(0, out_ref.shape[0] // step_rows, section, 0)


def lower_pair_kernel(*refs):
    sources, upper, (pair_ref, last_ref, held, sems) = refs[:7], refs[7], refs[-4:]
    step_rows = rows_of_pass(sources[0].shape[1])
    first = upper.shape[0]
    steps = held.shape[0] // step_rows

    def copy(step):
        spot = pl.ds(step * step_rows, step_rows)
        return pltpu.make_async_copy(
            held.at[spot], pair_ref.at[pl.ds(first + step * step_rows, step_rows)], sems.at[1 + step]
        )

    above = pltpu.make_async_copy(upper, pair_ref.at[:first], sems.at[0])
    above.start()

    def section(step, _):
        pair_rows(held, first, step, step_rows, *sources)
        copy(step).start()
        return 0

    lax.fori_loop(0, steps, section, 0)
    pair_rows(last_ref, first + held.shape[0], 0, step_rows, *sources)
    above.wait()
    for step in range(steps):
        copy(step).wait()


def total_of(x, ones):
    high = x.astype(BF16)
    low = (x - high.astype(F32)).astype(BF16)
    return dot(high, ones) + dot(low, ones)


def finish_kernel(own, got, mask_ref, diag, gain_ref, hat_ref, spread_ref, last, *refs):
    pair_ref, out_ref, held, sems = refs[-4:]
    rest = pair_ref.at[pl.ds(pair_ref.shape[0] - last.shape[0], last.shape[0])]
    seqs, length, channels = hat_ref.shape
    copies = [pltpu.make_async_copy(last, rest, sems.at[seqs])]
    copies[0].start()
    both = ((own[0].astype(F32) + got[0].astype(F32)) * mask_ref[...]).astype(BF16)
    gain = gain_ref[:1, :]
    ones = jnp.ones((channels, channels), BF16)
    for s in range(seqs):
        hat = hat_ref[s]
        grad = dot(both, diag[:, s * channels : (s + 1) * channels]) * gain
        mean = total_of(grad, ones) * (1.0 / channels)
        slope = total_of(grad * hat, ones) * (1.0 / channels)
        held[s] = (spread_ref[s][:, :1] * (grad - mean - hat * slope)).astype(BF16)
        copies.append(pltpu.make_async_copy(held.at[s], out_ref.at[s], sems.at[s]))
        copies[-1].start()
    for copy in copies:
        copy.wait()


VMEM = pl.BlockSpec(memory_space=pltpu.VMEM)
HBM = pl.BlockSpec(memory_space=pltpu.HBM)


def call(kernel, name, out_shape, scratch, micros, in_specs=None, out_specs=None, limit=24, aliases=None, after=()):
    def run(*args):
        specs = [VMEM] * len(args) if in_specs is None else in_specs
        specs, args = specs + [pl.BlockSpec(memory_space=pl.ANY)] * len(after), args + tuple(after)
        outs = jax.tree.map(lambda _: VMEM, out_shape) if out_specs is None else out_specs
        return pl.pallas_call(
            kernel,
            out_shape=out_shape,
            in_specs=specs,
            out_specs=outs,
            scratch_shapes=scratch,
            input_output_aliases=aliases or {},
            compiler_params=pltpu.CompilerParams(vmem_limit_bytes=limit * 1024 * 1024),
            cost_estimate=pl.CostEstimate(flops=int(micros * 1e8), bytes_accessed=0, transcendentals=0),
            name=name,
        )(*args)

    return run


def swap_rows(x, blocks, bit):
    moves = [(z * blocks + c, (z ^ bit) * blocks + c) for z in range(blocks) for c in range(blocks)]
    return lax.ppermute(x, PLACES, moves)


def swap_columns(x, blocks, bit):
    moves = [(z * blocks + c, z * blocks + (c ^ bit)) for z in range(blocks) for c in range(blocks)]
    return lax.ppermute(x, PLACES, moves)


def per_device(
    homolog_activations,
    homolog_valid_flags,
    position_valid_flags,
    centering_factor,
    centering_shift,
    first_factor_matrix,
    second_factor_matrix,
    couple_weight_matrix,
    couple_shift_vector,
    loss_sensitivity,
):
    seqs, length, channels = homolog_activations.shape
    total_seq = homolog_valid_flags.shape[0]
    total_res = position_valid_flags.shape[0]
    width = first_factor_matrix.shape[1]
    rows, columns, cz = loss_sensitivity.shape
    blocks = lax.axis_size("cols") * lax.axis_size("sub")
    steps = blocks.bit_length() - 1
    assert blocks == 1 << steps == lax.axis_size("rows") and steps > 0
    half = seqs * width
    deep = total_seq // 2
    span = deep * width
    shape = jax.ShapeDtypeStruct

    def far(x):
        return pltpu.with_memory_space_constraint(x, pltpu.HBM)

    seq_flags, res_flags = far(homolog_valid_flags), far(position_valid_flags)

    stack, diag, mask, hat, spread, gain = call(
        project_kernel,
        "project",
        (
            shape((1, length, 2 * half), BF16),
            shape((2 * half, seqs * channels), BF16),
            shape((length, 2 * half), F32),
            shape((seqs, length, channels), F32),
            shape((seqs, length, cz), F32),
            shape((8, channels), F32),
        ),
        [
            pltpu.VMEM((total_seq,), jnp.int32),
            pltpu.VMEM((seqs, length, channels), BF16),
            pltpu.VMEM((total_res,), jnp.int32),
            pltpu.VMEM((channels,), F32),
            pltpu.VMEM((channels,), F32),
            pltpu.VMEM((width, channels), BF16),
            pltpu.VMEM((width, channels), BF16),
            pltpu.SemaphoreType.DMA((7,)),
        ],
        2,
        in_specs=[HBM] * 7,
    )(
        seq_flags,
        far(homolog_activations),
        res_flags,
        far(centering_factor),
        far(centering_shift),
        far(first_factor_matrix.T),
        far(second_factor_matrix.T),
    )

    by_left, by_right, swap, scaled, turned, inverse, row_flags, shift = call(
        prepare_kernel,
        "prepare",
        (
            shape((width, width * cz), BF16),
            shape((width, width * cz), BF16),
            shape((span, span), BF16),
            shape((columns, rows * cz), BF16),
            shape((rows, columns * cz), BF16),
            shape((columns, cz), F32),
            shape((rows, cz), F32),
            shape((8, cz), F32),
        ),
        [
            pltpu.VMEM(couple_weight_matrix.shape, BF16),
            pltpu.VMEM(loss_sensitivity.shape, BF16),
            pltpu.VMEM((total_seq,), jnp.int32),
            pltpu.VMEM((total_res,), jnp.int32),
            pltpu.VMEM((cz,), F32),
            pltpu.VMEM((width * width, cz), F32),
            pltpu.SemaphoreType.DMA((5,)),
        ],
        3,
        in_specs=[HBM] * 5,
    )(far(couple_weight_matrix), far(loss_sensitivity), seq_flags, res_flags, far(couple_shift_vector))

    for step in range(steps):
        got = swap_rows(stack, blocks, blocks >> (step + 1))
        if step < steps - 1:
            stack = call(
                stack_kernel, "stack", shape((2 << step, length, 2 * half), BF16), [], 0.1, after=(shift,)
            )(stack, got)
    low_stack, high_stack = stack, got

    half_blocks = shape((blocks // 2, length, half), BF16)
    all_blocks = shape((blocks, length, half), BF16)
    cols_shape = shape((columns, span), BF16)
    t_limit = 16 + 2 * span * rows * cz * 2 // 2**20

    def make_v(stack, *after):
        return call(
            v_kernel,
            "expand_right",
            (cols_shape, shape((span, columns * cz), BF16)),
            [pltpu.VMEM((columns * deep, width), F32)],
            1.3,
            limit=t_limit,
            after=after,
        )(stack, swap, by_right)

    def gradient(full, side, *after):
        return call(gradient_kernel, "gradient", half_blocks, [], 1.5, limit=t_limit, after=after)(full, side, swap)

    low_cols, v_low = make_v(low_stack)
    low_sum = gradient(v_low, turned)
    lefts = call(lefts_kernel, "lefts", all_blocks, [], 0.1, after=(low_sum,))(low_stack, high_stack)
    got = swap_columns(lefts, blocks, 1)
    high_cols, v_high = make_v(high_stack, lefts)
    for step in range(1, steps):
        lefts = call(
            functools.partial(select_kernel, step - 1), "select", all_blocks, [], 0.1, after=(high_cols,)
        )(lefts, got)
        got = swap_columns(lefts, blocks, 1 << step)
    got_lefts = got
    high_sum = gradient(v_high, turned, lefts)
    sums = call(stack_kernel, "stack", all_blocks, [], 0.1)(low_sum, high_sum)

    def make_t(part, *after):
        return call(
            functools.partial(t_kernel, steps - 1, part),
            "expand_left",
            shape((span, rows * cz), BF16),
            [pltpu.VMEM((rows * deep, width), F32)],
            1.2,
            limit=t_limit,
            after=after,
        )(lefts, got_lefts, by_left)

    def make_t(part, *after):
        return call(
            functools.partial(t_kernel, steps - 1, part),
            "expand_left",
            shape((span, rows * cz), BF16),
            [pltpu.VMEM((rows * deep, width), F32)],
            1.3,
            limit=t_limit,
            after=after,
        )(lefts, got_lefts, by_left)

    arrived = call(mark_kernel, "mark", shape((8, cz), F32), [], 0.1, after=(got_lefts,))()
    for step in range(steps - 1):
        got = swap_columns(sums, blocks, 1 << step)
        sums = call(add_kernel, "add", all_blocks, [], 0.1, after=(arrived,))(sums, got)
    got = swap_columns(sums, blocks, 1 << (steps - 1))
    t_high = make_t(1, sums)

    def join(part, right):
        return call(
            functools.partial(join_kernel, part),
            "join",
            shape((blocks // 2, length, 2 * half), BF16),
            [],
            0.1,
        )(right, sums, got)

    send = join(1, gradient(t_high, scaled, sums))
    got_send = swap_rows(send, blocks, 1)
    t_low = make_t(0, send)
    keep = join(0, gradient(t_low, scaled, send))

    pair_sources = (low_cols, high_cols, t_low, t_high, shift, inverse, row_flags)
    upper_rows = rows // 4
    upper, paired = call(
        upper_pair_kernel,
        "pair",
        (shape((upper_rows, columns, cz), BF16), shape((8, cz), F32)),
        [],
        1,
        limit=t_limit,
        after=(keep,),
    )(*pair_sources)
    for step in range(1, steps):
        some = shape((blocks >> (step + 1), length, 2 * half), BF16)
        keep, send = call(halve_kernel, "halve", (some, some), [], 0.1, after=(paired,))(keep, got_send)
        got_send = swap_rows(send, blocks, 1 << step)
    last_rows = rows_of_pass(span)
    held_rows = rows - upper_rows - last_rows
    pair, last = call(
        lower_pair_kernel,
        "pair",
        (shape(loss_sensitivity.shape, BF16), shape((last_rows, columns, cz), BF16)),
        [
            pltpu.VMEM((held_rows, columns, cz), BF16),
            pltpu.SemaphoreType.DMA((1 + held_rows // last_rows,)),
        ],
        2,
        out_specs=(HBM, VMEM),
        limit=t_limit,
        after=(send,),
    )(*pair_sources, upper)

    return call(
        finish_kernel,
        "finish",
        (shape(loss_sensitivity.shape, BF16), shape(homolog_activations.shape, BF16)),
        [pltpu.VMEM(homolog_activations.shape, BF16), pltpu.SemaphoreType.DMA((seqs + 1,))],
        1,
        in_specs=[VMEM] * 8 + [HBM],
        out_specs=(HBM, HBM),
        aliases={8: 0},
    )(keep, got_send, mask, diag, gain, hat, spread, last, pair)


def solution(mesh):
    split = P(("groups", "rows"), ("cols", "sub"), None)
    return jax.shard_map(
        per_device,
        mesh=mesh,
        in_specs=(split, P("groups"), P("groups"), P(), P(), P(), P(), P(), P(), split),
        out_specs=(split, split),
        check_vma=False,
    )
```

```python
import functools

import jax
import jax.numpy as jnp
from jax import lax
from jax.experimental import pallas as pl
from jax.experimental.pallas import tpu as pltpu
from jax.sharding import PartitionSpec as P

F32 = jnp.float32
BF16 = jnp.bfloat16
PLACES = ("rows", "cols", "sub")
PRODUCED = 256
TILE = 16


def dot(a, b):
    return lax.dot_general(a, b, (((1,), (0,)), ((), ())), preferred_element_type=F32)


def dot_t(a, b):
    return lax.dot_general(a, b, (((1,), (1,)), ((), ())), preferred_element_type=F32)


def place():
    column = lax.axis_index("cols") * lax.axis_size("sub") + lax.axis_index("sub")
    return lax.axis_index("rows"), column


def lanes_at(start, size):
    return pl.ds(pl.multiple_of(start, size), size)


def flag_row(flags_ref):
    return flags_ref[...].astype(F32).reshape(1, -1)


def flag_column(flags_ref, start, length):
    flags = flag_row(flags_ref)
    total = flags.shape[1]
    spot = lax.broadcasted_iota(jnp.int32, (length, total), 0) + start
    lane = lax.broadcasted_iota(jnp.int32, (length, total), 1)
    return jnp.sum(jnp.where(spot == lane, flags, 0.0), axis=1, keepdims=True)


def load_all(pairs, sems):
    copies = [pltpu.make_async_copy(src, dst, sems.at[n]) for n, (src, dst) in enumerate(pairs)]
    for copy in copies:
        copy.start()
    return copies


def project_kernel(*refs):
    sources, outs, (loss_ref, w_ref), held, sems = refs[:9], refs[9:15], refs[15:17], refs[17:24], refs[24]
    out_ref, diag, mask_ref, hat_ref, spread_ref, gain_out = outs
    copies = load_all(list(zip(sources, held + (w_ref, loss_ref))), sems)
    seq_ref, x_ref, res_ref, gain_ref, bias_ref, first_ref, second_ref = held
    row_at, column_at = place()
    seqs, length, channels = x_ref.shape
    width = first_ref.shape[0]
    half = seqs * width
    diag[...] = jnp.zeros_like(diag)
    for copy in copies[:7]:
        copy.wait()
    for s in range(seqs):
        lanes = slice(s * channels, (s + 1) * channels)
        diag[s * width : (s + 1) * width, lanes] = first_ref[...]
        diag[(seqs + s) * width : (seqs + s + 1) * width, lanes] = second_ref[...]
    flags = flag_row(seq_ref)
    spot = lax.broadcasted_iota(jnp.int32, flags.shape, 1)
    which = lax.broadcasted_iota(jnp.int32, (1, 2 * half), 1) % half // width
    own = jnp.zeros((1, 2 * half), F32)
    for s in range(seqs):
        value = jnp.sum(jnp.where(spot == row_at * seqs + s, flags, 0.0), axis=1, keepdims=True)
        own = jnp.where(which == s, value, own)
    mask = flag_column(res_ref, column_at * length, length) * own
    mask_ref[...] = mask
    gain = gain_ref[...].reshape(1, channels)
    bias = bias_ref[...].reshape(1, channels)
    gain_out[...] = jnp.broadcast_to(gain, gain_out.shape)
    total = jnp.zeros((length, 2 * half), F32)
    for s in range(seqs):
        x = x_ref[s].astype(F32)
        off = x - jnp.mean(x, axis=-1, keepdims=True)
        spread = lax.rsqrt(jnp.mean(off * off, axis=-1, keepdims=True) + 1e-05)
        hat = off * spread
        hat_ref[s] = hat
        spread_ref[s] = jnp.broadcast_to(spread, spread_ref.shape[1:])
        normed = (hat * gain + bias).astype(BF16)
        total += dot_t(normed, diag[:, s * channels : (s + 1) * channels])
    out_ref[0] = (total * mask).astype(BF16)
    for copy in copies[7:]:
        copy.wait()


def prepare_kernel(*refs):
    sources, (loss_ref, w_ref), outs, held, (wide_w, sems) = (
        refs[:3],
        refs[3:5],
        refs[5:13],
        refs[13:16],
        refs[16:],
    )
    by_left, by_right, swap, scaled, turned, inverse_ref, row_ref, shift_out = outs
    seq_ref, res_ref, shift_ref = held
    copies = load_all(list(zip(sources, held)), sems)
    row_at, column_at = place()
    rows, length, cz = loss_ref.shape
    width = by_left.shape[0]
    span = swap.shape[0]
    deep = span // width
    wide_w[...] = w_ref[...].astype(F32)
    for n in range(width):
        by_left[:, n * cz : (n + 1) * cz] = wide_w[pl.ds(n, width, stride=width), :].astype(BF16)
        by_right[:, n * cz : (n + 1) * cz] = w_ref[n * width : (n + 1) * width, :]
    to = lax.broadcasted_iota(jnp.int32, (span, span), 0)
    at = lax.broadcasted_iota(jnp.int32, (span, span), 1)
    swap[...] = jnp.where((to // deep == at % width) & (to % deep == at // width), 1.0, 0.0).astype(BF16)
    for copy in copies:
        copy.wait()
    present = jnp.sum(flag_row(seq_ref), axis=1, keepdims=True)
    columns = flag_column(res_ref, column_at * length, length)
    inverse = jnp.broadcast_to(1.0 / jnp.maximum(present * columns, 1.0), (length, cz))
    inverse_ref[...] = inverse
    row_ref[...] = jnp.broadcast_to(flag_column(res_ref, row_at * rows, rows), (rows, cz))
    shift_out[...] = jnp.broadcast_to(shift_ref[...].reshape(1, cz), shift_out.shape)
    for i in range(rows):
        factor = jnp.where(row_ref[i : i + 1, :] > 0.0, inverse, 1.0)
        scaled[:, i * cz : (i + 1) * cz] = (loss_ref[i].astype(F32) * factor).astype(BF16)
    to = lax.broadcasted_iota(jnp.int32, (TILE * TILE, TILE * TILE), 0)
    at = lax.broadcasted_iota(jnp.int32, (TILE * TILE, TILE * TILE), 1)
    turn = jnp.where((to // TILE == at % TILE) & (to % TILE == at // TILE), 1.0, 0.0).astype(BF16)
    for i in range(0, rows, TILE):
        for j in range(0, length, 2 * TILE):
            taken = [
                jnp.concatenate(
                    [scaled[b : b + TILE, (i + k) * cz : (i + k + 1) * cz] for k in range(TILE)], axis=0
                )
                for b in (j, j + TILE)
            ]
            made = dot(turn, jnp.concatenate(taken, axis=1)).astype(BF16)
            for a in range(2):
                for k in range(TILE):
                    low = (j + a * TILE + k) * cz
                    turned[i : i + TILE, low : low + cz] = made[
                        k * TILE : (k + 1) * TILE, a * cz : (a + 1) * cz
                    ]


def stack_kernel(own, got, *refs):
    out = refs[-1]
    count = own.shape[0]
    out[:count] = own[...]
    out[count:] = got[...]


def lefts_kernel(own, got, *refs):
    out = refs[-1]
    count, _, half = out.shape
    for n in range(count // 2):
        out[n] = own[n, :, :half]
        out[count // 2 + n] = got[n, :, :half]


def select_kernel(bit, own, got, *refs):
    out = refs[-1]
    row_at, column_at = place()
    other = (row_at ^ column_at) >> bit & 1

    @pl.when(other == 1)
    def _():
        out[...] = got[...]

    @pl.when(other == 0)
    def _():
        out[...] = own[...]


def add_kernel(own, got, *refs):
    out = refs[-1]
    out[...] = (own[...].astype(F32) + got[...].astype(F32)).astype(BF16)


def mark_kernel(*refs):
    refs[-1][...] = jnp.zeros_like(refs[-1])


def spread_rows(rows, n, block, width, deep):
    length, half = block.shape
    seqs = half // width
    wide = block.astype(F32)
    for s in range(seqs):
        rows[pl.ds(n * seqs + s, length, stride=deep), :] = wide[:, s * width : (s + 1) * width]


def produce(out, rows, weight, deep):
    width = weight.shape[0]
    cz = weight.shape[1] // width
    chunk = min(2 * PRODUCED, rows.shape[0]) // deep

    def section(step, _):
        taken = rows[lanes_at(step * chunk * deep, chunk * deep), :].astype(BF16)
        for n in range(width // 2):
            made = dot(taken, weight[:, n * 2 * cz : (n + 1) * 2 * cz])
            for i in range(chunk):
                both = jnp.concatenate(
                    [made[i * deep : (i + 1) * deep, a * cz : (a + 1) * cz] for a in range(2)], axis=0
                )
                low = n * 2 * deep
                out[low : low + 2 * deep, lanes_at((step * chunk + i) * cz, cz)] = both.astype(BF16)
        return 0

    lax.fori_loop(0, rows.shape[0] // (chunk * deep), section, 0)


def v_kernel(stack, swap, weight, *refs):
    right_cols, v_ref, rows = refs[-3:]
    count, _, both = stack.shape
    width = weight.shape[0]
    deep = swap.shape[0] // width
    for n in range(count):
        spread_rows(rows, n, stack[n, :, both // 2 :], width, deep)
    right = jnp.concatenate([stack[n, :, both // 2 :] for n in range(count)], axis=1)
    right_cols[...] = dot_t(right, swap[...]).astype(BF16)
    produce(v_ref, rows, weight, deep)


def t_kernel(bit, part, own, got, weight, *refs):
    t_ref, rows = refs[-2:]
    row_at, column_at = place()
    count = own.shape[0] // 2
    width = weight.shape[0]
    deep = t_ref.shape[0] // width
    other = (row_at ^ column_at) >> bit & 1
    for n in range(count):
        k = part * count + n
        block = jnp.where(other == 1, got[k].astype(F32), own[k].astype(F32))
        spread_rows(rows, n, block, width, deep)
    produce(t_ref, rows, weight, deep)


def ungroup(out, acc, swap):
    half = out.shape[2]
    made = dot(acc.astype(BF16), swap[...]).astype(BF16)
    for k in range(out.shape[0]):
        out[k] = made[:, k * half : (k + 1) * half]


def gradient_kernel(grouped, full_ref, side, swap, *refs):
    out = refs[-1]
    span = swap.shape[0]
    size = side.shape[1] * PRODUCED // span

    def section(step, acc):
        lanes = lanes_at(step * size, size)
        return acc + dot_t(full_ref[:, lanes], side[:, lanes])

    acc = dot_t(full_ref[:, :size], side[:, :size])
    acc = lax.fori_loop(1, span // PRODUCED, section, acc)
    if grouped:
        out[...] = jnp.transpose(acc).astype(BF16)
    else:
        ungroup(out, jnp.transpose(acc), swap)


def join_kernel(part, right, own, got, out):
    row_at, column_at = place()
    mine = jnp.where(row_at == column_at, 1.0, 0.0)
    count, _, both = out.shape
    half = both // 2
    for n in range(count):
        k = part * count + n
        out[n, :, :half] = ((own[k].astype(F32) + got[k].astype(F32)) * mine).astype(BF16)
        out[n, :, half:] = right[:, n * half : (n + 1) * half]


def halve_kernel(grouped, own, got, swap, *refs):
    keep, send = refs[-2:]
    count, _, both = keep.shape
    half = both // 2
    total = [(own[n].astype(F32) + got[n].astype(F32)).astype(BF16) for n in range(2 * count)]
    if grouped:
        right = dot(jnp.concatenate([part[:, half:] for part in total], axis=1), swap[...]).astype(BF16)
    for n in range(2 * count):
        out, k = (keep, n) if n < count else (send, n - count)
        out[k, :, :half] = total[n][:, :half]
        out[k, :, half:] = right[:, n * half : (n + 1) * half] if grouped else total[n][:, half:]


def rows_of_pass(span):
    return max(2, 8 * PRODUCED // span)


def pair_rows(out_ref, first, start, count, low_cols, high_cols, t_low, t_high, shift_ref, inverse_ref, row_ref):
    cz = out_ref.shape[2]
    group = min(4, count)
    for n in range(0, count, group):
        lanes = lanes_at((first + start + n) * cz, group * cz)
        made = dot(low_cols[...], t_low[:, lanes]) + dot(high_cols[...], t_high[:, lanes])
        for a in range(group):
            i = start + n + a
            factor = jnp.where(row_ref[pl.ds(first + i, 1), :] > 0.0, inverse_ref[...], 1.0)
            out_ref[i] = ((made[:, a * cz : (a + 1) * cz] + shift_ref[:1, :]) * factor).astype(BF16)


def upper_pair_kernel(*refs):
    sources, (out_ref, done_ref) = refs[:7], refs[-2:]
    step_rows = rows_of_pass(sources[0].shape[1])
    done_ref[...] = jnp.zeros_like(done_ref)

    def section(step, _):
        pair_rows(out_ref, 0, step * step_rows, step_rows, *sources)
        return 0

    lax.fori_loop(0, out_ref.shape[0] // step_rows, section, 0)


def lower_pair_kernel(*refs):
    sources, upper, (pair_ref, held, sems) = refs[:7], refs[7], refs[-3:]
    step_rows = rows_of_pass(sources[0].shape[1])
    first = upper.shape[0]
    steps = held.shape[0] // step_rows - 1
    some = step_rows // 2

    def copy(start, count, sem):
        return pltpu.make_async_copy(
            held.at[pl.ds(start, count)], pair_ref.at[pl.ds(first + start, count)], sems.at[sem]
        )

    above = pltpu.make_async_copy(upper, pair_ref.at[:first], sems.at[0])
    above.start()

    def section(step, _):
        pair_rows(held, first, step * step_rows, step_rows, *sources)
        copy(step * step_rows, step_rows, 1 + step).start()
        return 0

    lax.fori_loop(0, steps, section, 0)
    for part in range(2):
        start = steps * step_rows + part * some
        pair_rows(held, first, start, some, *sources)
        copy(start, some, 1 + steps + part).start()
    above.wait()
    for step in range(steps):
        copy(step * step_rows, step_rows, 1 + step).wait()
    for part in range(2):
        copy(steps * step_rows + part * some, some, 1 + steps + part).wait()


def finish_kernel(own, got, mask_ref, diag, gain_ref, hat_ref, spread_ref, out_ref, held, sems):
    seqs, _, channels = hat_ref.shape
    both = ((own[0].astype(F32) + got[0].astype(F32)) * mask_ref[...]).astype(BF16)
    gain = gain_ref[:1, :]
    copies = []
    for s in range(seqs):
        hat = hat_ref[s]
        grad = dot(both, diag[:, s * channels : (s + 1) * channels]) * gain
        held[s] = (
            spread_ref[s][:, :1]
            * (
                grad
                - jnp.mean(grad, axis=-1, keepdims=True)
                - hat * jnp.mean(grad * hat, axis=-1, keepdims=True)
            )
        ).astype(BF16)
        copies.append(pltpu.make_async_copy(held.at[s], out_ref.at[s], sems.at[s]))
        copies[s].start()
    for copy in copies:
        copy.wait()


VMEM = pl.BlockSpec(memory_space=pltpu.VMEM)
HBM = pl.BlockSpec(memory_space=pltpu.HBM)


def call(kernel, name, out_shape, scratch, micros, in_specs=None, out_specs=None, limit=24, aliases=None, after=()):
    def run(*args):
        specs = [VMEM] * len(args) if in_specs is None else in_specs
        specs, args = specs + [pl.BlockSpec(memory_space=pl.ANY)] * len(after), args + tuple(after)
        outs = jax.tree.map(lambda _: VMEM, out_shape) if out_specs is None else out_specs
        return pl.pallas_call(
            kernel,
            out_shape=out_shape,
            in_specs=specs,
            out_specs=outs,
            scratch_shapes=scratch,
            input_output_aliases=aliases or {},
            compiler_params=pltpu.CompilerParams(vmem_limit_bytes=limit * 1024 * 1024),
            cost_estimate=pl.CostEstimate(flops=int(micros * 1e8), bytes_accessed=0, transcendentals=0),
            name=name,
        )(*args)

    return run


def swap_rows(x, blocks, bit):
    moves = [(z * blocks + c, (z ^ bit) * blocks + c) for z in range(blocks) for c in range(blocks)]
    return lax.ppermute(x, PLACES, moves)


def swap_columns(x, blocks, bit):
    moves = [(z * blocks + c, z * blocks + (c ^ bit)) for z in range(blocks) for c in range(blocks)]
    return lax.ppermute(x, PLACES, moves)


def per_device(
    homolog_activations,
    homolog_valid_flags,
    position_valid_flags,
    centering_factor,
    centering_shift,
    first_factor_matrix,
    second_factor_matrix,
    couple_weight_matrix,
    couple_shift_vector,
    loss_sensitivity,
):
    seqs, length, channels = homolog_activations.shape
    total_seq = homolog_valid_flags.shape[0]
    total_res = position_valid_flags.shape[0]
    width = first_factor_matrix.shape[1]
    rows, columns, cz = loss_sensitivity.shape
    blocks = lax.axis_size("cols") * lax.axis_size("sub")
    steps = blocks.bit_length() - 1
    assert blocks == 1 << steps == lax.axis_size("rows") and steps > 1
    half = seqs * width
    deep = total_seq // 2
    span = deep * width
    shape = jax.ShapeDtypeStruct

    def far(x):
        return pltpu.with_memory_space_constraint(x, pltpu.HBM)

    seq_flags, res_flags = far(homolog_valid_flags), far(position_valid_flags)

    stack, diag, mask, hat, spread, gain, loss, weights = call(
        project_kernel,
        "project",
        (
            shape((1, length, 2 * half), BF16),
            shape((2 * half, seqs * channels), BF16),
            shape((length, 2 * half), F32),
            shape((seqs, length, channels), F32),
            shape((seqs, length, cz), F32),
            shape((8, channels), F32),
            shape(loss_sensitivity.shape, BF16),
            shape(couple_weight_matrix.shape, BF16),
        ),
        [
            pltpu.VMEM((total_seq,), jnp.int32),
            pltpu.VMEM((seqs, length, channels), BF16),
            pltpu.VMEM((total_res,), jnp.int32),
            pltpu.VMEM((channels,), F32),
            pltpu.VMEM((channels,), F32),
            pltpu.VMEM((width, channels), BF16),
            pltpu.VMEM((width, channels), BF16),
            pltpu.SemaphoreType.DMA((9,)),
        ],
        2,
        in_specs=[HBM] * 9,
    )(
        seq_flags,
        far(homolog_activations),
        res_flags,
        far(centering_factor),
        far(centering_shift),
        far(first_factor_matrix.T),
        far(second_factor_matrix.T),
        far(couple_weight_matrix),
        far(loss_sensitivity),
    )

    by_left, by_right, swap, scaled, turned, inverse, row_flags, shift = call(
        prepare_kernel,
        "prepare",
        (
            shape((width, width * cz), BF16),
            shape((width, width * cz), BF16),
            shape((span, span), BF16),
            shape((columns, rows * cz), BF16),
            shape((rows, columns * cz), BF16),
            shape((columns, cz), F32),
            shape((rows, cz), F32),
            shape((8, cz), F32),
        ),
        [
            pltpu.VMEM((total_seq,), jnp.int32),
            pltpu.VMEM((total_res,), jnp.int32),
            pltpu.VMEM((cz,), F32),
            pltpu.VMEM((width * width, cz), F32),
            pltpu.SemaphoreType.DMA((3,)),
        ],
        3,
        in_specs=[HBM] * 3 + [VMEM] * 2,
    )(seq_flags, res_flags, far(couple_shift_vector), loss, weights)

    for step in range(steps):
        got = swap_rows(stack, blocks, blocks >> (step + 1))
        if step < steps - 1:
            stack = call(
                stack_kernel, "stack", shape((2 << step, length, 2 * half), BF16), [], 0.1, after=(shift,)
            )(stack, got)
    low_stack, high_stack = stack, got

    half_blocks = shape((blocks // 2, length, half), BF16)
    all_blocks = shape((blocks, length, half), BF16)
    cols_shape = shape((columns, span), BF16)
    t_limit = 16 + 2 * span * rows * cz * 2 // 2**20

    def make_v(stack, *after):
        return call(
            v_kernel,
            "expand_right",
            (cols_shape, shape((span, columns * cz), BF16)),
            [pltpu.VMEM((columns * deep, width), F32)],
            1.3,
            limit=t_limit,
            after=after,
        )(stack, swap, by_right)

    def gradient(full, side, grouped, *after):
        return call(
            functools.partial(gradient_kernel, grouped),
            "gradient",
            cols_shape if grouped else half_blocks,
            [],
            1.5,
            limit=t_limit,
            after=after,
        )(full, side, swap)

    low_cols, v_low = make_v(low_stack)
    low_sum = gradient(v_low, turned, False)
    lefts = call(lefts_kernel, "lefts", all_blocks, [], 0.1, after=(low_sum,))(low_stack, high_stack)
    got = swap_columns(lefts, blocks, 1)
    high_cols, v_high = make_v(high_stack, lefts)
    for step in range(1, steps):
        lefts = call(
            functools.partial(select_kernel, step - 1), "select", all_blocks, [], 0.1, after=(high_cols,)
        )(lefts, got)
        got = swap_columns(lefts, blocks, 1 << step)
    got_lefts = got
    high_sum = gradient(v_high, turned, False, lefts)
    sums = call(stack_kernel, "stack", all_blocks, [], 0.1)(low_sum, high_sum)

    def make_t(part, *after):
        return call(
            functools.partial(t_kernel, steps - 1, part),
            "expand_left",
            shape((span, rows * cz), BF16),
            [pltpu.VMEM((rows * deep, width), F32)],
            1.2,
            limit=t_limit,
            after=after,
        )(lefts, got_lefts, by_left)

    def make_t(part, *after):
        return call(
            functools.partial(t_kernel, steps - 1, part),
            "expand_left",
            shape((span, rows * cz), BF16),
            [pltpu.VMEM((rows * deep, width), F32)],
            1.3,
            limit=t_limit,
            after=after,
        )(lefts, got_lefts, by_left)

    arrived = call(mark_kernel, "mark", shape((8, cz), F32), [], 0.1, after=(got_lefts,))()
    for step in range(steps - 1):
        got = swap_columns(sums, blocks, 1 << step)
        sums = call(add_kernel, "add", all_blocks, [], 0.1, after=(arrived,))(sums, got)
    got = swap_columns(sums, blocks, 1 << (steps - 1))
    t_high = make_t(1, sums)

    def join(part, right):
        return call(
            functools.partial(join_kernel, part),
            "join",
            shape((blocks // 2, length, 2 * half), BF16),
            [],
            0.1,
        )(right, sums, got)

    send = join(1, gradient(t_high, scaled, True, sums))
    got_send = swap_rows(send, blocks, 1)
    t_low = make_t(0, send)
    keep = join(0, gradient(t_low, scaled, True, send))

    pair_sources = (low_cols, high_cols, t_low, t_high, shift, inverse, row_flags)
    upper_rows = rows // 4
    upper, paired = call(
        upper_pair_kernel,
        "pair",
        (shape((upper_rows, columns, cz), BF16), shape((8, cz), F32)),
        [],
        1,
        limit=t_limit,
        after=(keep,),
    )(*pair_sources)
    for step in range(1, steps):
        some = shape((blocks >> (step + 1), length, 2 * half), BF16)
        keep, send = call(
            functools.partial(halve_kernel, step == 1), "halve", (some, some), [], 0.1, after=(paired,)
        )(keep, got_send, swap)
        got_send = swap_rows(send, blocks, 1 << step)
    pair = call(
        lower_pair_kernel,
        "pair",
        shape(loss_sensitivity.shape, BF16),
        [
            pltpu.VMEM((rows - upper_rows, columns, cz), BF16),
            pltpu.SemaphoreType.DMA((2 + (rows - upper_rows) // rows_of_pass(span),)),
        ],
        2,
        out_specs=HBM,
        limit=t_limit,
        after=(send,),
    )(*pair_sources, upper)

    alignment = call(
        finish_kernel,
        "finish",
        shape(homolog_activations.shape, BF16),
        [pltpu.VMEM(homolog_activations.shape, BF16), pltpu.SemaphoreType.DMA((seqs,))],
        1,
        out_specs=HBM,
    )(keep, got_send, mask, diag, gain, hat, spread)
    return pair, alignment


def solution(mesh):
    split = P(("groups", "rows"), ("cols", "sub"), None)
    return jax.shard_map(
        per_device,
        mesh=mesh,
        in_specs=(split, P("groups"), P("groups"), P(), P(), P(), P(), P(), P(), split),
        out_specs=(split, split),
        check_vma=False,
    )
```

```python
import functools

import jax
import jax.numpy as jnp
from jax import lax
from jax.experimental import pallas as pl
from jax.experimental.pallas import tpu as pltpu
from jax.sharding import PartitionSpec as P

F32 = jnp.float32
BF16 = jnp.bfloat16
PLACES = ("rows", "cols", "sub")
PRODUCED = 256
TILE = 16


def dot(a, b):
    return lax.dot_general(a, b, (((1,), (0,)), ((), ())), preferred_element_type=F32)


def dot_t(a, b):
    return lax.dot_general(a, b, (((1,), (1,)), ((), ())), preferred_element_type=F32)


def place():
    column = lax.axis_index("cols") * lax.axis_size("sub") + lax.axis_index("sub")
    return lax.axis_index("rows"), column


def lanes_at(start, size):
    return pl.ds(pl.multiple_of(start, size), size)


def flag_row(flags_ref):
    return flags_ref[...].astype(F32).reshape(1, -1)


def flag_column(flags_ref, start, length):
    flags = flag_row(flags_ref)
    total = flags.shape[1]
    spot = lax.broadcasted_iota(jnp.int32, (length, total), 0) + start
    lane = lax.broadcasted_iota(jnp.int32, (length, total), 1)
    return jnp.sum(jnp.where(spot == lane, flags, 0.0), axis=1, keepdims=True)


def load_all(pairs, sems):
    copies = [pltpu.make_async_copy(src, dst, sems.at[n]) for n, (src, dst) in enumerate(pairs)]
    for copy in copies:
        copy.start()
    return copies


def project_kernel(*refs):
    sources, outs, (loss_ref, w_ref), held, sems = refs[:9], refs[9:15], refs[15:17], refs[17:24], refs[24]
    out_ref, diag, mask_ref, hat_ref, spread_ref, gain_out = outs
    copies = load_all(list(zip(sources, held + (w_ref, loss_ref))), sems)
    seq_ref, x_ref, res_ref, gain_ref, bias_ref, first_ref, second_ref = held
    row_at, column_at = place()
    seqs, length, channels = x_ref.shape
    width = first_ref.shape[0]
    half = seqs * width
    diag[...] = jnp.zeros_like(diag)
    for copy in copies[:7]:
        copy.wait()
    for s in range(seqs):
        lanes = slice(s * channels, (s + 1) * channels)
        diag[s * width : (s + 1) * width, lanes] = first_ref[...]
        diag[(seqs + s) * width : (seqs + s + 1) * width, lanes] = second_ref[...]
    flags = flag_row(seq_ref)
    spot = lax.broadcasted_iota(jnp.int32, flags.shape, 1)
    which = lax.broadcasted_iota(jnp.int32, (1, 2 * half), 1) % half // width
    own = jnp.zeros((1, 2 * half), F32)
    for s in range(seqs):
        value = jnp.sum(jnp.where(spot == row_at * seqs + s, flags, 0.0), axis=1, keepdims=True)
        own = jnp.where(which == s, value, own)
    mask = flag_column(res_ref, column_at * length, length) * own
    mask_ref[...] = mask
    gain = gain_ref[...].reshape(1, channels)
    bias = bias_ref[...].reshape(1, channels)
    gain_out[...] = jnp.broadcast_to(gain, gain_out.shape)
    total = jnp.zeros((length, 2 * half), F32)
    for s in range(seqs):
        x = x_ref[s].astype(F32)
        off = x - jnp.mean(x, axis=-1, keepdims=True)
        spread = lax.rsqrt(jnp.mean(off * off, axis=-1, keepdims=True) + 1e-05)
        hat = off * spread
        hat_ref[s] = hat
        spread_ref[s] = jnp.broadcast_to(spread, spread_ref.shape[1:])
        normed = (hat * gain + bias).astype(BF16)
        total += dot_t(normed, diag[:, s * channels : (s + 1) * channels])
    out_ref[0] = (total * mask).astype(BF16)
    for copy in copies[7:]:
        copy.wait()


def prepare_kernel(*refs):
    sources, (loss_ref, w_ref), outs, held, (wide_w, sems) = (
        refs[:3],
        refs[3:5],
        refs[5:13],
        refs[13:16],
        refs[16:],
    )
    by_left, by_right, swap, scaled, turned, inverse_ref, row_ref, shift_out = outs
    seq_ref, res_ref, shift_ref = held
    copies = load_all(list(zip(sources, held)), sems)
    row_at, column_at = place()
    rows, length, cz = loss_ref.shape
    width = by_left.shape[0]
    span = swap.shape[0]
    deep = span // width
    wide_w[...] = w_ref[...].astype(F32)
    for n in range(width):
        by_left[:, n * cz : (n + 1) * cz] = wide_w[pl.ds(n, width, stride=width), :].astype(BF16)
        by_right[:, n * cz : (n + 1) * cz] = w_ref[n * width : (n + 1) * width, :]
    to = lax.broadcasted_iota(jnp.int32, (span, span), 0)
    at = lax.broadcasted_iota(jnp.int32, (span, span), 1)
    swap[...] = jnp.where((to // deep == at % width) & (to % deep == at // width), 1.0, 0.0).astype(BF16)
    for copy in copies:
        copy.wait()
    present = jnp.sum(flag_row(seq_ref), axis=1, keepdims=True)
    columns = flag_column(res_ref, column_at * length, length)
    inverse = jnp.broadcast_to(1.0 / jnp.maximum(present * columns, 1.0), (length, cz))
    inverse_ref[...] = inverse
    row_ref[...] = jnp.broadcast_to(flag_column(res_ref, row_at * rows, rows), (rows, cz))
    shift_out[...] = jnp.broadcast_to(shift_ref[...].reshape(1, cz), shift_out.shape)
    for i in range(rows):
        factor = jnp.where(row_ref[i : i + 1, :] > 0.0, inverse, 1.0)
        scaled[:, i * cz : (i + 1) * cz] = (loss_ref[i].astype(F32) * factor).astype(BF16)
    to = lax.broadcasted_iota(jnp.int32, (TILE * TILE, TILE * TILE), 0)
    at = lax.broadcasted_iota(jnp.int32, (TILE * TILE, TILE * TILE), 1)
    turn = jnp.where((to // TILE == at % TILE) & (to % TILE == at // TILE), 1.0, 0.0).astype(BF16)
    for i in range(0, rows, TILE):
        for j in range(0, length, 2 * TILE):
            taken = [
                jnp.concatenate(
                    [scaled[b : b + TILE, (i + k) * cz : (i + k + 1) * cz] for k in range(TILE)], axis=0
                )
                for b in (j, j + TILE)
            ]
            made = dot(turn, jnp.concatenate(taken, axis=1)).astype(BF16)
            for a in range(2):
                for k in range(TILE):
                    low = (j + a * TILE + k) * cz
                    turned[i : i + TILE, low : low + cz] = made[
                        k * TILE : (k + 1) * TILE, a * cz : (a + 1) * cz
                    ]


def stack_kernel(own, got, *refs):
    out = refs[-1]
    count = own.shape[0]
    out[:count] = own[...]
    out[count:] = got[...]


def lefts_kernel(own, got, *refs):
    out = refs[-1]
    count, _, half = out.shape
    for n in range(count // 2):
        out[n] = own[n, :, :half]
        out[count // 2 + n] = got[n, :, :half]


def select_kernel(bit, own, got, *refs):
    out = refs[-1]
    row_at, column_at = place()
    other = jnp.where((row_at ^ column_at) & (2 * bit - 1) == bit, 1, 0)

    @pl.when(other == 1)
    def _():
        out[...] = got[...]

    @pl.when(other == 0)
    def _():
        out[...] = own[...]


def add_kernel(own, got, *refs):
    out = refs[-1]
    out[...] = (own[...].astype(F32) + got[...].astype(F32)).astype(BF16)


def spread_rows(rows, n, block, width, deep):
    length, half = block.shape
    seqs = half // width
    wide = block.astype(F32)
    for s in range(seqs):
        rows[pl.ds(n * seqs + s, length, stride=deep), :] = wide[:, s * width : (s + 1) * width]


def produce(out, rows, weight, deep):
    width = weight.shape[0]
    cz = weight.shape[1] // width
    chunk = min(2 * PRODUCED, rows.shape[0]) // deep

    def section(step, _):
        taken = rows[lanes_at(step * chunk * deep, chunk * deep), :].astype(BF16)
        for n in range(width // 2):
            made = dot(taken, weight[:, n * 2 * cz : (n + 1) * 2 * cz])
            for i in range(chunk):
                both = jnp.concatenate(
                    [made[i * deep : (i + 1) * deep, a * cz : (a + 1) * cz] for a in range(2)], axis=0
                )
                low = n * 2 * deep
                out[low : low + 2 * deep, lanes_at((step * chunk + i) * cz, cz)] = both.astype(BF16)
        return 0

    lax.fori_loop(0, rows.shape[0] // (chunk * deep), section, 0)


def v_kernel(stack, swap, weight, *refs):
    right_cols, v_ref, rows = refs[-3:]
    count, _, both = stack.shape
    width = weight.shape[0]
    deep = swap.shape[0] // width
    for n in range(count):
        spread_rows(rows, n, stack[n, :, both // 2 :], width, deep)
    right = jnp.concatenate([stack[n, :, both // 2 :] for n in range(count)], axis=1)
    right_cols[...] = dot_t(right, swap[...]).astype(BF16)
    produce(v_ref, rows, weight, deep)


def t_kernel(part, own, got, weight, *refs):
    t_ref, rows = refs[-2:]
    row_at, column_at = place()
    count = own.shape[0] // 2
    width = weight.shape[0]
    deep = t_ref.shape[0] // width
    other = (row_at ^ column_at) & 1
    for n in range(count):
        k = part * count + n
        block = jnp.where(other == 1, got[k].astype(F32), own[k].astype(F32))
        spread_rows(rows, n, block, width, deep)
    produce(t_ref, rows, weight, deep)


def ungroup(out, acc, swap):
    half = out.shape[2]
    made = dot(acc.astype(BF16), swap[...]).astype(BF16)
    for k in range(out.shape[0]):
        out[k] = made[:, k * half : (k + 1) * half]


def gradient_kernel(grouped, full_ref, side, swap, *refs):
    out = refs[-1]
    span = swap.shape[0]
    size = side.shape[1] * PRODUCED // span

    def section(step, acc):
        lanes = lanes_at(step * size, size)
        return acc + dot_t(full_ref[:, lanes], side[:, lanes])

    acc = dot_t(full_ref[:, :size], side[:, :size])
    acc = lax.fori_loop(1, span // PRODUCED, section, acc)
    if grouped:
        out[...] = jnp.transpose(acc).astype(BF16)
    else:
        ungroup(out, jnp.transpose(acc), swap)


def join_kernel(part, right, own, got, out):
    row_at, column_at = place()
    mine = jnp.where(row_at == column_at, 1.0, 0.0)
    count, _, both = out.shape
    half = both // 2
    for n in range(count):
        k = part * count + n
        out[n, :, :half] = ((own[k].astype(F32) + got[k].astype(F32)) * mine).astype(BF16)
        out[n, :, half:] = right[:, n * half : (n + 1) * half]


def halve_kernel(grouped, own, got, swap, *refs):
    keep, send = refs[-2:]
    count, _, both = keep.shape
    half = both // 2
    total = [(own[n].astype(F32) + got[n].astype(F32)).astype(BF16) for n in range(2 * count)]
    if grouped:
        right = dot(jnp.concatenate([part[:, half:] for part in total], axis=1), swap[...]).astype(BF16)
    for n in range(2 * count):
        out, k = (keep, n) if n < count else (send, n - count)
        out[k, :, :half] = total[n][:, :half]
        out[k, :, half:] = right[:, n * half : (n + 1) * half] if grouped else total[n][:, half:]


def rows_of_pass(span):
    return max(2, 8 * PRODUCED // span)


def pair_rows(out_ref, first, start, count, low_cols, high_cols, t_low, t_high, shift_ref, inverse_ref, row_ref):
    cz = out_ref.shape[2]
    group = min(4, count)
    for n in range(0, count, group):
        lanes = lanes_at((first + start + n) * cz, group * cz)
        made = dot(low_cols[...], t_low[:, lanes]) + dot(high_cols[...], t_high[:, lanes])
        for a in range(group):
            i = start + n + a
            factor = jnp.where(row_ref[pl.ds(first + i, 1), :] > 0.0, inverse_ref[...], 1.0)
            out_ref[i] = ((made[:, a * cz : (a + 1) * cz] + shift_ref[:1, :]) * factor).astype(BF16)


def upper_pair_kernel(*refs):
    sources, (out_ref, done_ref) = refs[:7], refs[-2:]
    step_rows = rows_of_pass(sources[0].shape[1])
    done_ref[...] = jnp.zeros_like(done_ref)

    def section(step, _):
        pair_rows(out_ref, 0, step * step_rows, step_rows, *sources)
        return 0

    lax.fori_loop(0, out_ref.shape[0] // step_rows, section, 0)


def lower_pair_kernel(*refs):
    sources, upper, (pair_ref, held, sems) = refs[:7], refs[7], refs[-3:]
    step_rows = rows_of_pass(sources[0].shape[1])
    first = upper.shape[0]
    steps = held.shape[0] // step_rows - 1
    some = step_rows // 2

    def copy(start, count, sem):
        return pltpu.make_async_copy(
            held.at[pl.ds(start, count)], pair_ref.at[pl.ds(first + start, count)], sems.at[sem]
        )

    above = pltpu.make_async_copy(upper, pair_ref.at[:first], sems.at[0])
    above.start()

    def section(step, _):
        pair_rows(held, first, step * step_rows, step_rows, *sources)
        copy(step * step_rows, step_rows, 1 + step).start()
        return 0

    lax.fori_loop(0, steps, section, 0)
    for part in range(2):
        start = steps * step_rows + part * some
        pair_rows(held, first, start, some, *sources)
        copy(start, some, 1 + steps + part).start()
    above.wait()
    for step in range(steps):
        copy(step * step_rows, step_rows, 1 + step).wait()
    for part in range(2):
        copy(steps * step_rows + part * some, some, 1 + steps + part).wait()


def finish_kernel(own, got, mask_ref, diag, gain_ref, hat_ref, spread_ref, out_ref, held, sems):
    seqs, _, channels = hat_ref.shape
    both = ((own[0].astype(F32) + got[0].astype(F32)) * mask_ref[...]).astype(BF16)
    gain = gain_ref[:1, :]
    copies = []
    for s in range(seqs):
        hat = hat_ref[s]
        grad = dot(both, diag[:, s * channels : (s + 1) * channels]) * gain
        held[s] = (
            spread_ref[s][:, :1]
            * (
                grad
                - jnp.mean(grad, axis=-1, keepdims=True)
                - hat * jnp.mean(grad * hat, axis=-1, keepdims=True)
            )
        ).astype(BF16)
        copies.append(pltpu.make_async_copy(held.at[s], out_ref.at[s], sems.at[s]))
        copies[s].start()
    for copy in copies:
        copy.wait()


VMEM = pl.BlockSpec(memory_space=pltpu.VMEM)
HBM = pl.BlockSpec(memory_space=pltpu.HBM)


def call(kernel, name, out_shape, scratch, micros, in_specs=None, out_specs=None, limit=24, aliases=None, after=()):
    def run(*args):
        specs = [VMEM] * len(args) if in_specs is None else in_specs
        specs, args = specs + [pl.BlockSpec(memory_space=pl.ANY)] * len(after), args + tuple(after)
        outs = jax.tree.map(lambda _: VMEM, out_shape) if out_specs is None else out_specs
        return pl.pallas_call(
            kernel,
            out_shape=out_shape,
            in_specs=specs,
            out_specs=outs,
            scratch_shapes=scratch,
            input_output_aliases=aliases or {},
            compiler_params=pltpu.CompilerParams(vmem_limit_bytes=limit * 1024 * 1024),
            cost_estimate=pl.CostEstimate(flops=int(micros * 1e8), bytes_accessed=0, transcendentals=0),
            name=name,
        )(*args)

    return run


def swap_rows(x, blocks, bit):
    moves = [(z * blocks + c, (z ^ bit) * blocks + c) for z in range(blocks) for c in range(blocks)]
    return lax.ppermute(x, PLACES, moves)


def outward_columns(x, blocks, bit):
    low = 2 * bit - 1
    moves = [
        (z * blocks + c, z * blocks + (c ^ bit)) for z in range(blocks) for c in range(blocks) if (z ^ c) & low == 0
    ]
    return lax.ppermute(x, PLACES, moves)


def inward_columns(x, blocks, bit):
    low = 2 * bit - 1
    moves = [
        (z * blocks + (c ^ bit), z * blocks + c) for z in range(blocks) for c in range(blocks) if (z ^ c) & low == 0
    ]
    return lax.ppermute(x, PLACES, moves)


def per_device(
    homolog_activations,
    homolog_valid_flags,
    position_valid_flags,
    centering_factor,
    centering_shift,
    first_factor_matrix,
    second_factor_matrix,
    couple_weight_matrix,
    couple_shift_vector,
    loss_sensitivity,
):
    seqs, length, channels = homolog_activations.shape
    total_seq = homolog_valid_flags.shape[0]
    total_res = position_valid_flags.shape[0]
    width = first_factor_matrix.shape[1]
    rows, columns, cz = loss_sensitivity.shape
    blocks = lax.axis_size("cols") * lax.axis_size("sub")
    steps = blocks.bit_length() - 1
    assert blocks == 1 << steps == lax.axis_size("rows") and steps > 1
    half = seqs * width
    deep = total_seq // 2
    span = deep * width
    shape = jax.ShapeDtypeStruct

    def far(x):
        return pltpu.with_memory_space_constraint(x, pltpu.HBM)

    seq_flags, res_flags = far(homolog_valid_flags), far(position_valid_flags)

    stack, diag, mask, hat, spread, gain, loss, weights = call(
        project_kernel,
        "project",
        (
            shape((1, length, 2 * half), BF16),
            shape((2 * half, seqs * channels), BF16),
            shape((length, 2 * half), F32),
            shape((seqs, length, channels), F32),
            shape((seqs, length, cz), F32),
            shape((8, channels), F32),
            shape(loss_sensitivity.shape, BF16),
            shape(couple_weight_matrix.shape, BF16),
        ),
        [
            pltpu.VMEM((total_seq,), jnp.int32),
            pltpu.VMEM((seqs, length, channels), BF16),
            pltpu.VMEM((total_res,), jnp.int32),
            pltpu.VMEM((channels,), F32),
            pltpu.VMEM((channels,), F32),
            pltpu.VMEM((width, channels), BF16),
            pltpu.VMEM((width, channels), BF16),
            pltpu.SemaphoreType.DMA((9,)),
        ],
        2,
        in_specs=[HBM] * 9,
    )(
        seq_flags,
        far(homolog_activations),
        res_flags,
        far(centering_factor),
        far(centering_shift),
        far(first_factor_matrix.T),
        far(second_factor_matrix.T),
        far(couple_weight_matrix),
        far(loss_sensitivity),
    )

    by_left, by_right, swap, scaled, turned, inverse, row_flags, shift = call(
        prepare_kernel,
        "prepare",
        (
            shape((width, width * cz), BF16),
            shape((width, width * cz), BF16),
            shape((span, span), BF16),
            shape((columns, rows * cz), BF16),
            shape((rows, columns * cz), BF16),
            shape((columns, cz), F32),
            shape((rows, cz), F32),
            shape((8, cz), F32),
        ),
        [
            pltpu.VMEM((total_seq,), jnp.int32),
            pltpu.VMEM((total_res,), jnp.int32),
            pltpu.VMEM((cz,), F32),
            pltpu.VMEM((width * width, cz), F32),
            pltpu.SemaphoreType.DMA((3,)),
        ],
        3,
        in_specs=[HBM] * 3 + [VMEM] * 2,
    )(seq_flags, res_flags, far(couple_shift_vector), loss, weights)

    for step in range(steps):
        got = swap_rows(stack, blocks, blocks >> (step + 1))
        if step < steps - 1:
            stack = call(
                stack_kernel, "stack", shape((2 << step, length, 2 * half), BF16), [], 0.1, after=(shift,)
            )(stack, got)
    low_stack, high_stack = stack, got

    half_blocks = shape((blocks // 2, length, half), BF16)
    all_blocks = shape((blocks, length, half), BF16)
    cols_shape = shape((columns, span), BF16)
    t_limit = 16 + 2 * span * rows * cz * 2 // 2**20

    def make_v(stack, *after):
        return call(
            v_kernel,
            "expand_right",
            (cols_shape, shape((span, columns * cz), BF16)),
            [pltpu.VMEM((columns * deep, width), F32)],
            1.3,
            limit=t_limit,
            after=after,
        )(stack, swap, by_right)

    def gradient(full, side, grouped, *after):
        return call(
            functools.partial(gradient_kernel, grouped),
            "gradient",
            cols_shape if grouped else half_blocks,
            [],
            1.5,
            limit=t_limit,
            after=after,
        )(full, side, swap)

    low_cols, v_low = make_v(low_stack)
    low_sum = gradient(v_low, turned, False)
    lefts = call(lefts_kernel, "lefts", all_blocks, [], 0.1, after=(low_sum,))(low_stack, high_stack)
    got = outward_columns(lefts, blocks, blocks // 2)
    high_cols, v_high = make_v(high_stack, lefts)
    high_sum = gradient(v_high, turned, False)
    for step in range(1, steps):
        lefts = call(
            functools.partial(select_kernel, blocks >> step), "select", all_blocks, [], 0.1, after=(high_sum,)
        )(lefts, got)
        got = outward_columns(lefts, blocks, blocks >> (step + 1))
    got_lefts = got
    sums = call(stack_kernel, "stack", all_blocks, [], 0.1)(low_sum, high_sum)

    def make_t(part, *after):
        return call(
            functools.partial(t_kernel, part),
            "expand_left",
            shape((span, rows * cz), BF16),
            [pltpu.VMEM((rows * deep, width), F32)],
            1.2,
            limit=t_limit,
            after=after,
        )(lefts, got_lefts, by_left)

    def make_t(part, *after):
        return call(
            functools.partial(t_kernel, part),
            "expand_left",
            shape((span, rows * cz), BF16),
            [pltpu.VMEM((rows * deep, width), F32)],
            1.3,
            limit=t_limit,
            after=after,
        )(lefts, got_lefts, by_left)

    for step in range(steps - 1):
        got = inward_columns(sums, blocks, 1 << step)
        sums = call(add_kernel, "add", all_blocks, [], 0.1)(sums, got)
    got = inward_columns(sums, blocks, 1 << (steps - 1))
    t_high = make_t(1, sums)

    def join(part, right):
        return call(
            functools.partial(join_kernel, part),
            "join",
            shape((blocks // 2, length, 2 * half), BF16),
            [],
            0.1,
        )(right, sums, got)

    send = join(1, gradient(t_high, scaled, True, sums))
    got_send = swap_rows(send, blocks, 1)
    t_low = make_t(0, send)
    keep = join(0, gradient(t_low, scaled, True, send))

    pair_sources = (low_cols, high_cols, t_low, t_high, shift, inverse, row_flags)
    upper_rows = rows // 4
    upper, paired = call(
        upper_pair_kernel,
        "pair",
        (shape((upper_rows, columns, cz), BF16), shape((8, cz), F32)),
        [],
        1,
        limit=t_limit,
        after=(keep,),
    )(*pair_sources)
    for step in range(1, steps):
        some = shape((blocks >> (step + 1), length, 2 * half), BF16)
        keep, send = call(
            functools.partial(halve_kernel, step == 1), "halve", (some, some), [], 0.1, after=(paired,)
        )(keep, got_send, swap)
        got_send = swap_rows(send, blocks, 1 << step)
    pair = call(
        lower_pair_kernel,
        "pair",
        shape(loss_sensitivity.shape, BF16),
        [
            pltpu.VMEM((rows - upper_rows, columns, cz), BF16),
            pltpu.SemaphoreType.DMA((2 + (rows - upper_rows) // rows_of_pass(span),)),
        ],
        2,
        out_specs=HBM,
        limit=t_limit,
        after=(send,),
    )(*pair_sources, upper)

    alignment = call(
        finish_kernel,
        "finish",
        shape(homolog_activations.shape, BF16),
        [pltpu.VMEM(homolog_activations.shape, BF16), pltpu.SemaphoreType.DMA((seqs,))],
        1,
        out_specs=HBM,
    )(keep, got_send, mask, diag, gain, hat, spread)
    return pair, alignment


def solution(mesh):
    split = P(("groups", "rows"), ("cols", "sub"), None)
    return jax.shard_map(
        per_device,
        mesh=mesh,
        in_specs=(split, P("groups"), P("groups"), P(), P(), P(), P(), P(), P(), split),
        out_specs=(split, split),
        check_vma=False,
    )
```

```python
import functools

import jax
import jax.numpy as jnp
from jax import lax
from jax.experimental import pallas as pl
from jax.experimental.pallas import tpu as pltpu
from jax.sharding import PartitionSpec as P

F32 = jnp.float32
BF16 = jnp.bfloat16
PLACES = ("rows", "cols", "sub")
PRODUCED = 256
TILE = 16


def dot(a, b):
    return lax.dot_general(a, b, (((1,), (0,)), ((), ())), preferred_element_type=F32)


def dot_t(a, b):
    return lax.dot_general(a, b, (((1,), (1,)), ((), ())), preferred_element_type=F32)


def place():
    column = lax.axis_index("cols") * lax.axis_size("sub") + lax.axis_index("sub")
    return lax.axis_index("rows"), column


def lanes_at(start, size):
    return pl.ds(pl.multiple_of(start, size), size)


def flag_row(flags_ref):
    return flags_ref[...].astype(F32).reshape(1, -1)


def flag_column(flags_ref, start, length):
    flags = flag_row(flags_ref)
    total = flags.shape[1]
    spot = lax.broadcasted_iota(jnp.int32, (length, total), 0) + start
    lane = lax.broadcasted_iota(jnp.int32, (length, total), 1)
    return jnp.sum(jnp.where(spot == lane, flags, 0.0), axis=1, keepdims=True)


def load_all(pairs, sems):
    copies = [pltpu.make_async_copy(src, dst, sems.at[n]) for n, (src, dst) in enumerate(pairs)]
    for copy in copies:
        copy.start()
    return copies


def project_kernel(*refs):
    sources, outs, (loss_ref, w_ref), held, sems = refs[:9], refs[9:15], refs[15:17], refs[17:24], refs[24]
    out_ref, diag, mask_ref, hat_ref, spread_ref, gain_out = outs
    copies = load_all(list(zip(sources, held + (w_ref, loss_ref))), sems)
    seq_ref, x_ref, res_ref, gain_ref, bias_ref, first_ref, second_ref = held
    row_at, column_at = place()
    seqs, length, channels = x_ref.shape
    width = first_ref.shape[0]
    half = seqs * width
    diag[...] = jnp.zeros_like(diag)
    for copy in copies[:7]:
        copy.wait()
    for s in range(seqs):
        lanes = slice(s * channels, (s + 1) * channels)
        diag[s * width : (s + 1) * width, lanes] = first_ref[...]
        diag[(seqs + s) * width : (seqs + s + 1) * width, lanes] = second_ref[...]
    flags = flag_row(seq_ref)
    spot = lax.broadcasted_iota(jnp.int32, flags.shape, 1)
    which = lax.broadcasted_iota(jnp.int32, (1, 2 * half), 1) % half // width
    own = jnp.zeros((1, 2 * half), F32)
    for s in range(seqs):
        value = jnp.sum(jnp.where(spot == row_at * seqs + s, flags, 0.0), axis=1, keepdims=True)
        own = jnp.where(which == s, value, own)
    mask = flag_column(res_ref, column_at * length, length) * own
    mask_ref[...] = mask
    gain = gain_ref[...].reshape(1, channels)
    bias = bias_ref[...].reshape(1, channels)
    gain_out[...] = jnp.broadcast_to(gain, gain_out.shape)
    total = jnp.zeros((length, 2 * half), F32)
    for s in range(seqs):
        x = x_ref[s].astype(F32)
        off = x - jnp.mean(x, axis=-1, keepdims=True)
        spread = lax.rsqrt(jnp.mean(off * off, axis=-1, keepdims=True) + 1e-05)
        hat = off * spread
        hat_ref[s] = hat
        spread_ref[s] = jnp.broadcast_to(spread, spread_ref.shape[1:])
        normed = (hat * gain + bias).astype(BF16)
        total += dot_t(normed, diag[:, s * channels : (s + 1) * channels])
    out_ref[0] = (total * mask).astype(BF16)
    for copy in copies[7:]:
        copy.wait()


def prepare_kernel(*refs):
    sources, (loss_ref, w_ref), outs, held, (wide_w, sems) = (
        refs[:3],
        refs[3:5],
        refs[5:13],
        refs[13:16],
        refs[16:],
    )
    by_left, by_right, swap, scaled, turned, inverse_ref, row_ref, shift_out = outs
    seq_ref, res_ref, shift_ref = held
    copies = load_all(list(zip(sources, held)), sems)
    row_at, column_at = place()
    rows, length, cz = loss_ref.shape
    width = by_left.shape[0]
    span = swap.shape[0]
    deep = span // width
    wide_w[...] = w_ref[...].astype(F32)
    for n in range(width):
        by_left[:, n * cz : (n + 1) * cz] = wide_w[pl.ds(n, width, stride=width), :].astype(BF16)
        by_right[:, n * cz : (n + 1) * cz] = w_ref[n * width : (n + 1) * width, :]
    to = lax.broadcasted_iota(jnp.int32, (span, span), 0)
    at = lax.broadcasted_iota(jnp.int32, (span, span), 1)
    swap[...] = jnp.where((to // deep == at % width) & (to % deep == at // width), 1.0, 0.0).astype(BF16)
    for copy in copies:
        copy.wait()
    present = jnp.sum(flag_row(seq_ref), axis=1, keepdims=True)
    columns = flag_column(res_ref, column_at * length, length)
    inverse = jnp.broadcast_to(1.0 / jnp.maximum(present * columns, 1.0), (length, cz))
    inverse_ref[...] = inverse
    row_ref[...] = jnp.broadcast_to(flag_column(res_ref, row_at * rows, rows), (rows, cz))
    shift_out[...] = jnp.broadcast_to(shift_ref[...].reshape(1, cz), shift_out.shape)
    for i in range(rows):
        factor = jnp.where(row_ref[i : i + 1, :] > 0.0, inverse, 1.0)
        scaled[:, i * cz : (i + 1) * cz] = (loss_ref[i].astype(F32) * factor).astype(BF16)
    to = lax.broadcasted_iota(jnp.int32, (TILE * TILE, TILE * TILE), 0)
    at = lax.broadcasted_iota(jnp.int32, (TILE * TILE, TILE * TILE), 1)
    turn = jnp.where((to // TILE == at % TILE) & (to % TILE == at // TILE), 1.0, 0.0).astype(BF16)
    for i in range(0, rows, TILE):
        for j in range(0, length, 2 * TILE):
            taken = [
                jnp.concatenate(
                    [scaled[b : b + TILE, (i + k) * cz : (i + k + 1) * cz] for k in range(TILE)], axis=0
                )
                for b in (j, j + TILE)
            ]
            made = dot(turn, jnp.concatenate(taken, axis=1)).astype(BF16)
            for a in range(2):
                for k in range(TILE):
                    low = (j + a * TILE + k) * cz
                    turned[i : i + TILE, low : low + cz] = made[
                        k * TILE : (k + 1) * TILE, a * cz : (a + 1) * cz
                    ]


def stack_kernel(own, got, *refs):
    out = refs[-1]
    count = own.shape[0]
    out[:count] = own[...]
    out[count:] = got[...]


def lefts_kernel(own, got, *refs):
    out = refs[-1]
    count, _, half = out.shape
    for n in range(count // 2):
        out[n] = own[n, :, :half]
        out[count // 2 + n] = got[n, :, :half]


def select_kernel(bit, own, got, *refs):
    out = refs[-1]
    row_at, column_at = place()
    other = (row_at ^ column_at) >> bit & 1

    @pl.when(other == 1)
    def _():
        out[...] = got[...]

    @pl.when(other == 0)
    def _():
        out[...] = own[...]


def add_kernel(own, got, *refs):
    out = refs[-1]
    out[...] = (own[...].astype(F32) + got[...].astype(F32)).astype(BF16)


def mark_kernel(*refs):
    refs[-1][...] = jnp.zeros_like(refs[-1])


def spread_rows(rows, n, block, width, deep):
    length, half = block.shape
    seqs = half // width
    wide = block.astype(F32)
    for s in range(seqs):
        rows[pl.ds(n * seqs + s, length, stride=deep), :] = wide[:, s * width : (s + 1) * width]


def produce(out, rows, weight, deep):
    width = weight.shape[0]
    cz = weight.shape[1] // width
    chunk = min(2 * PRODUCED, rows.shape[0]) // deep

    def section(step, _):
        taken = rows[lanes_at(step * chunk * deep, chunk * deep), :].astype(BF16)
        for n in range(width // 2):
            made = dot(taken, weight[:, n * 2 * cz : (n + 1) * 2 * cz])
            for i in range(chunk):
                both = jnp.concatenate(
                    [made[i * deep : (i + 1) * deep, a * cz : (a + 1) * cz] for a in range(2)], axis=0
                )
                low = n * 2 * deep
                out[low : low + 2 * deep, lanes_at((step * chunk + i) * cz, cz)] = both.astype(BF16)
        return 0

    lax.fori_loop(0, rows.shape[0] // (chunk * deep), section, 0)


def v_kernel(stack, swap, weight, *refs):
    right_cols, v_ref, rows = refs[-3:]
    count, _, both = stack.shape
    width = weight.shape[0]
    deep = swap.shape[0] // width
    for n in range(count):
        spread_rows(rows, n, stack[n, :, both // 2 :], width, deep)
    right = jnp.concatenate([stack[n, :, both // 2 :] for n in range(count)], axis=1)
    right_cols[...] = dot_t(right, swap[...]).astype(BF16)
    produce(v_ref, rows, weight, deep)


def t_kernel(bit, part, own, got, weight, *refs):
    t_ref, rows = refs[-2:]
    row_at, column_at = place()
    count = own.shape[0] // 2
    width = weight.shape[0]
    deep = t_ref.shape[0] // width
    other = (row_at ^ column_at) >> bit & 1
    for n in range(count):
        k = part * count + n
        block = jnp.where(other == 1, got[k].astype(F32), own[k].astype(F32))
        spread_rows(rows, n, block, width, deep)
    produce(t_ref, rows, weight, deep)


def ungroup(out, acc, swap):
    half = out.shape[2]
    made = dot(acc.astype(BF16), swap[...]).astype(BF16)
    for k in range(out.shape[0]):
        out[k] = made[:, k * half : (k + 1) * half]


def gradient_kernel(grouped, full_ref, side, swap, *refs):
    out = refs[-1]
    span = swap.shape[0]
    size = side.shape[1] * PRODUCED // span

    def section(step, acc):
        lanes = lanes_at(step * size, size)
        return acc + dot_t(full_ref[:, lanes], side[:, lanes])

    acc = dot_t(full_ref[:, :size], side[:, :size])
    acc = lax.fori_loop(1, span // PRODUCED, section, acc)
    if grouped:
        out[...] = jnp.transpose(acc).astype(BF16)
    else:
        ungroup(out, jnp.transpose(acc), swap)


def join_kernel(part, right, own, got, out):
    row_at, column_at = place()
    mine = jnp.where(row_at == column_at, 1.0, 0.0)
    count, _, both = out.shape
    half = both // 2
    for n in range(count):
        k = part * count + n
        out[n, :, :half] = ((own[k].astype(F32) + got[k].astype(F32)) * mine).astype(BF16)
        out[n, :, half:] = right[:, n * half : (n + 1) * half]


def halve_kernel(grouped, own, got, swap, *refs):
    keep, send = refs[-2:]
    count, _, both = keep.shape
    half = both // 2
    total = [(own[n].astype(F32) + got[n].astype(F32)).astype(BF16) for n in range(2 * count)]
    if grouped:
        right = dot(jnp.concatenate([part[:, half:] for part in total], axis=1), swap[...]).astype(BF16)
    for n in range(2 * count):
        out, k = (keep, n) if n < count else (send, n - count)
        out[k, :, :half] = total[n][:, :half]
        out[k, :, half:] = right[:, n * half : (n + 1) * half] if grouped else total[n][:, half:]


def rows_of_pass(span):
    return max(2, 8 * PRODUCED // span)


def pair_rows(out_ref, first, start, count, low_cols, high_cols, t_low, t_high, shift_ref, inverse_ref, row_ref):
    cz = out_ref.shape[2]
    group = min(4, count)
    for n in range(0, count, group):
        lanes = lanes_at((first + start + n) * cz, group * cz)
        made = dot(low_cols[...], t_low[:, lanes]) + dot(high_cols[...], t_high[:, lanes])
        for a in range(group):
            i = start + n + a
            factor = jnp.where(row_ref[pl.ds(first + i, 1), :] > 0.0, inverse_ref[...], 1.0)
            out_ref[i] = ((made[:, a * cz : (a + 1) * cz] + shift_ref[:1, :]) * factor).astype(BF16)


def upper_pair_kernel(*refs):
    sources, (out_ref, done_ref) = refs[:7], refs[-2:]
    step_rows = rows_of_pass(sources[0].shape[1])
    done_ref[...] = jnp.zeros_like(done_ref)

    def section(step, _):
        pair_rows(out_ref, 0, step * step_rows, step_rows, *sources)
        return 0

    lax.fori_loop(0, out_ref.shape[0] // step_rows, section, 0)


def lower_pair_kernel(*refs):
    sources, upper, (pair_ref, last_ref, held, sems) = refs[:7], refs[7], refs[-4:]
    step_rows = rows_of_pass(sources[0].shape[1])
    first = upper.shape[0]
    steps = held.shape[0] // step_rows

    def copy(step):
        spot = pl.ds(step * step_rows, step_rows)
        return pltpu.make_async_copy(
            held.at[spot], pair_ref.at[pl.ds(first + step * step_rows, step_rows)], sems.at[1 + step]
        )

    above = pltpu.make_async_copy(upper, pair_ref.at[:first], sems.at[0])
    above.start()

    def section(step, _):
        pair_rows(held, first, step * step_rows, step_rows, *sources)
        copy(step).start()
        return 0

    lax.fori_loop(0, steps, section, 0)
    pair_rows(last_ref, first + held.shape[0], 0, step_rows, *sources)
    above.wait()
    for step in range(steps):
        copy(step).wait()


def finish_kernel(own, got, mask_ref, diag, gain_ref, hat_ref, spread_ref, last, *refs):
    pair_ref, out_ref, held, sems = refs[-4:]
    rest = pair_ref.at[pl.ds(pair_ref.shape[0] - last.shape[0], last.shape[0])]
    seqs, _, channels = hat_ref.shape
    copies = [pltpu.make_async_copy(last, rest, sems.at[seqs])]
    copies[0].start()
    both = ((own[0].astype(F32) + got[0].astype(F32)) * mask_ref[...]).astype(BF16)
    gain = gain_ref[:1, :]
    for s in range(seqs):
        hat = hat_ref[s]
        spread = jnp.concatenate([spread_ref[s]] * (channels // spread_ref.shape[2]), axis=1)
        grad = dot(both, diag[:, s * channels : (s + 1) * channels]) * gain
        held[s] = (
            spread
            * (
                grad
                - jnp.mean(grad, axis=-1, keepdims=True)
                - hat * jnp.mean(grad * hat, axis=-1, keepdims=True)
            )
        ).astype(BF16)
        copies.append(pltpu.make_async_copy(held.at[s], out_ref.at[s], sems.at[s]))
        copies[-1].start()
    for copy in copies:
        copy.wait()


VMEM = pl.BlockSpec(memory_space=pltpu.VMEM)
HBM = pl.BlockSpec(memory_space=pltpu.HBM)


def call(kernel, name, out_shape, scratch, micros, in_specs=None, out_specs=None, limit=24, aliases=None, after=()):
    def run(*args):
        specs = [VMEM] * len(args) if in_specs is None else in_specs
        specs, args = specs + [pl.BlockSpec(memory_space=pl.ANY)] * len(after), args + tuple(after)
        outs = jax.tree.map(lambda _: VMEM, out_shape) if out_specs is None else out_specs
        return pl.pallas_call(
            kernel,
            out_shape=out_shape,
            in_specs=specs,
            out_specs=outs,
            scratch_shapes=scratch,
            input_output_aliases=aliases or {},
            compiler_params=pltpu.CompilerParams(vmem_limit_bytes=limit * 1024 * 1024),
            cost_estimate=pl.CostEstimate(flops=int(micros * 1e8), bytes_accessed=0, transcendentals=0),
            name=name,
        )(*args)

    return run


def swap_rows(x, blocks, bit):
    moves = [(z * blocks + c, (z ^ bit) * blocks + c) for z in range(blocks) for c in range(blocks)]
    return lax.ppermute(x, PLACES, moves)


def swap_columns(x, blocks, bit):
    moves = [(z * blocks + c, z * blocks + (c ^ bit)) for z in range(blocks) for c in range(blocks)]
    return lax.ppermute(x, PLACES, moves)


def per_device(
    homolog_activations,
    homolog_valid_flags,
    position_valid_flags,
    centering_factor,
    centering_shift,
    first_factor_matrix,
    second_factor_matrix,
    couple_weight_matrix,
    couple_shift_vector,
    loss_sensitivity,
):
    seqs, length, channels = homolog_activations.shape
    total_seq = homolog_valid_flags.shape[0]
    total_res = position_valid_flags.shape[0]
    width = first_factor_matrix.shape[1]
    rows, columns, cz = loss_sensitivity.shape
    blocks = lax.axis_size("cols") * lax.axis_size("sub")
    steps = blocks.bit_length() - 1
    assert blocks == 1 << steps == lax.axis_size("rows") and steps > 1
    half = seqs * width
    deep = total_seq // 2
    span = deep * width
    shape = jax.ShapeDtypeStruct

    def far(x):
        return pltpu.with_memory_space_constraint(x, pltpu.HBM)

    seq_flags, res_flags = far(homolog_valid_flags), far(position_valid_flags)

    stack, diag, mask, hat, spread, gain, loss, weights = call(
        project_kernel,
        "project",
        (
            shape((1, length, 2 * half), BF16),
            shape((2 * half, seqs * channels), BF16),
            shape((length, 2 * half), F32),
            shape((seqs, length, channels), F32),
            shape((seqs, length, cz), F32),
            shape((8, channels), F32),
            shape(loss_sensitivity.shape, BF16),
            shape(couple_weight_matrix.shape, BF16),
        ),
        [
            pltpu.VMEM((total_seq,), jnp.int32),
            pltpu.VMEM((seqs, length, channels), BF16),
            pltpu.VMEM((total_res,), jnp.int32),
            pltpu.VMEM((channels,), F32),
            pltpu.VMEM((channels,), F32),
            pltpu.VMEM((width, channels), BF16),
            pltpu.VMEM((width, channels), BF16),
            pltpu.SemaphoreType.DMA((9,)),
        ],
        2,
        in_specs=[HBM] * 9,
    )(
        seq_flags,
        far(homolog_activations),
        res_flags,
        far(centering_factor),
        far(centering_shift),
        far(first_factor_matrix.T),
        far(second_factor_matrix.T),
        far(couple_weight_matrix),
        far(loss_sensitivity),
    )

    by_left, by_right, swap, scaled, turned, inverse, row_flags, shift = call(
        prepare_kernel,
        "prepare",
        (
            shape((width, width * cz), BF16),
            shape((width, width * cz), BF16),
            shape((span, span), BF16),
            shape((columns, rows * cz), BF16),
            shape((rows, columns * cz), BF16),
            shape((columns, cz), F32),
            shape((rows, cz), F32),
            shape((8, cz), F32),
        ),
        [
            pltpu.VMEM((total_seq,), jnp.int32),
            pltpu.VMEM((total_res,), jnp.int32),
            pltpu.VMEM((cz,), F32),
            pltpu.VMEM((width * width, cz), F32),
            pltpu.SemaphoreType.DMA((3,)),
        ],
        3,
        in_specs=[HBM] * 3 + [VMEM] * 2,
    )(seq_flags, res_flags, far(couple_shift_vector), loss, weights)

    for step in range(steps):
        got = swap_rows(stack, blocks, blocks >> (step + 1))
        if step < steps - 1:
            stack = call(
                stack_kernel, "stack", shape((2 << step, length, 2 * half), BF16), [], 0.1, after=(shift,)
            )(stack, got)
    low_stack, high_stack = stack, got

    half_blocks = shape((blocks // 2, length, half), BF16)
    all_blocks = shape((blocks, length, half), BF16)
    cols_shape = shape((columns, span), BF16)
    t_limit = 16 + 2 * span * rows * cz * 2 // 2**20

    def make_v(stack, *after):
        return call(
            v_kernel,
            "expand_right",
            (cols_shape, shape((span, columns * cz), BF16)),
            [pltpu.VMEM((columns * deep, width), F32)],
            1.3,
            limit=t_limit,
            after=after,
        )(stack, swap, by_right)

    def gradient(full, side, grouped, *after):
        return call(
            functools.partial(gradient_kernel, grouped),
            "gradient",
            cols_shape if grouped else half_blocks,
            [],
            1.5,
            limit=t_limit,
            after=after,
        )(full, side, swap)

    low_cols, v_low = make_v(low_stack)
    low_sum = gradient(v_low, turned, False)
    lefts = call(lefts_kernel, "lefts", all_blocks, [], 0.1, after=(low_sum,))(low_stack, high_stack)
    got = swap_columns(lefts, blocks, 1)
    high_cols, v_high = make_v(high_stack, lefts)
    for step in range(1, steps):
        lefts = call(
            functools.partial(select_kernel, step - 1), "select", all_blocks, [], 0.1, after=(high_cols,)
        )(lefts, got)
        got = swap_columns(lefts, blocks, 1 << step)
    got_lefts = got
    high_sum = gradient(v_high, turned, False, lefts)
    sums = call(stack_kernel, "stack", all_blocks, [], 0.1)(low_sum, high_sum)

    def make_t(part, *after):
        return call(
            functools.partial(t_kernel, steps - 1, part),
            "expand_left",
            shape((span, rows * cz), BF16),
            [pltpu.VMEM((rows * deep, width), F32)],
            1.2,
            limit=t_limit,
            after=after,
        )(lefts, got_lefts, by_left)

    def make_t(part, *after):
        return call(
            functools.partial(t_kernel, steps - 1, part),
            "expand_left",
            shape((span, rows * cz), BF16),
            [pltpu.VMEM((rows * deep, width), F32)],
            1.3,
            limit=t_limit,
            after=after,
        )(lefts, got_lefts, by_left)

    arrived = call(mark_kernel, "mark", shape((8, cz), F32), [], 0.1, after=(got_lefts,))()
    for step in range(steps - 1):
        got = swap_columns(sums, blocks, 1 << step)
        sums = call(add_kernel, "add", all_blocks, [], 0.1, after=(arrived,))(sums, got)
    got = swap_columns(sums, blocks, 1 << (steps - 1))
    t_high = make_t(1, sums)

    def join(part, right):
        return call(
            functools.partial(join_kernel, part),
            "join",
            shape((blocks // 2, length, 2 * half), BF16),
            [],
            0.1,
        )(right, sums, got)

    send = join(1, gradient(t_high, scaled, True, sums))
    got_send = swap_rows(send, blocks, 1)
    t_low = make_t(0, send)
    keep = join(0, gradient(t_low, scaled, True, send))

    pair_sources = (low_cols, high_cols, t_low, t_high, shift, inverse, row_flags)
    upper_rows = rows // 4
    upper, paired = call(
        upper_pair_kernel,
        "pair",
        (shape((upper_rows, columns, cz), BF16), shape((8, cz), F32)),
        [],
        1,
        limit=t_limit,
        after=(keep,),
    )(*pair_sources)
    for step in range(1, steps):
        some = shape((blocks >> (step + 1), length, 2 * half), BF16)
        keep, send = call(
            functools.partial(halve_kernel, step == 1), "halve", (some, some), [], 0.1, after=(paired,)
        )(keep, got_send, swap)
        got_send = swap_rows(send, blocks, 1 << step)
    last_rows = rows_of_pass(span)
    held_rows = rows - upper_rows - last_rows
    pair, last = call(
        lower_pair_kernel,
        "pair",
        (shape(loss_sensitivity.shape, BF16), shape((last_rows, columns, cz), BF16)),
        [
            pltpu.VMEM((held_rows, columns, cz), BF16),
            pltpu.SemaphoreType.DMA((1 + held_rows // last_rows,)),
        ],
        2,
        out_specs=(HBM, VMEM),
        limit=t_limit,
        after=(send,),
    )(*pair_sources, upper)

    return call(
        finish_kernel,
        "finish",
        (shape(loss_sensitivity.shape, BF16), shape(homolog_activations.shape, BF16)),
        [pltpu.VMEM(homolog_activations.shape, BF16), pltpu.SemaphoreType.DMA((seqs + 1,))],
        1,
        in_specs=[VMEM] * 8 + [HBM],
        out_specs=(HBM, HBM),
        aliases={8: 0},
    )(keep, got_send, mask, diag, gain, hat, spread, last, pair)


def solution(mesh):
    split = P(("groups", "rows"), ("cols", "sub"), None)
    return jax.shard_map(
        per_device,
        mesh=mesh,
        in_specs=(split, P("groups"), P("groups"), P(), P(), P(), P(), P(), P(), split),
        out_specs=(split, split),
        check_vma=False,
    )
```

```python
import functools

import jax
import jax.numpy as jnp
from jax import lax
from jax.experimental import pallas as pl
from jax.experimental.pallas import tpu as pltpu
from jax.sharding import PartitionSpec as P

F32 = jnp.float32
BF16 = jnp.bfloat16
PLACES = ("rows", "cols", "sub")
PRODUCED = 256
TILE = 16


def dot(a, b):
    return lax.dot_general(a, b, (((1,), (0,)), ((), ())), preferred_element_type=F32)


def dot_t(a, b):
    return lax.dot_general(a, b, (((1,), (1,)), ((), ())), preferred_element_type=F32)


def place():
    column = lax.axis_index("cols") * lax.axis_size("sub") + lax.axis_index("sub")
    return lax.axis_index("rows"), column


def lanes_at(start, size):
    return pl.ds(pl.multiple_of(start, size), size)


def flag_row(flags_ref):
    return flags_ref[...].astype(F32).reshape(1, -1)


def flag_column(flags_ref, start, length):
    flags = flag_row(flags_ref)
    total = flags.shape[1]
    spot = lax.broadcasted_iota(jnp.int32, (length, total), 0) + start
    lane = lax.broadcasted_iota(jnp.int32, (length, total), 1)
    return jnp.sum(jnp.where(spot == lane, flags, 0.0), axis=1, keepdims=True)


def load_all(pairs, sems):
    copies = [pltpu.make_async_copy(src, dst, sems.at[n]) for n, (src, dst) in enumerate(pairs)]
    for copy in copies:
        copy.start()
    return copies


def project_kernel(*refs):
    sources, outs, (loss_ref, w_ref), held, sems = refs[:9], refs[9:15], refs[15:17], refs[17:24], refs[24]
    out_ref, diag, mask_ref, hat_ref, spread_ref, gain_out = outs
    copies = load_all(list(zip(sources, held + (w_ref, loss_ref))), sems)
    seq_ref, x_ref, res_ref, gain_ref, bias_ref, first_ref, second_ref = held
    row_at, column_at = place()
    seqs, length, channels = x_ref.shape
    width = first_ref.shape[0]
    half = seqs * width
    diag[...] = jnp.zeros_like(diag)
    for copy in copies[:7]:
        copy.wait()
    for s in range(seqs):
        lanes = slice(s * channels, (s + 1) * channels)
        diag[s * width : (s + 1) * width, lanes] = first_ref[...]
        diag[(seqs + s) * width : (seqs + s + 1) * width, lanes] = second_ref[...]
    flags = flag_row(seq_ref)
    spot = lax.broadcasted_iota(jnp.int32, flags.shape, 1)
    which = lax.broadcasted_iota(jnp.int32, (1, 2 * half), 1) % half // width
    own = jnp.zeros((1, 2 * half), F32)
    for s in range(seqs):
        value = jnp.sum(jnp.where(spot == row_at * seqs + s, flags, 0.0), axis=1, keepdims=True)
        own = jnp.where(which == s, value, own)
    mask = flag_column(res_ref, column_at * length, length) * own
    mask_ref[...] = mask
    gain = gain_ref[...].reshape(1, channels)
    bias = bias_ref[...].reshape(1, channels)
    gain_out[...] = jnp.broadcast_to(gain, gain_out.shape)
    total = jnp.zeros((length, 2 * half), F32)
    for s in range(seqs):
        x = x_ref[s].astype(F32)
        off = x - jnp.mean(x, axis=-1, keepdims=True)
        spread = lax.rsqrt(jnp.mean(off * off, axis=-1, keepdims=True) + 1e-05)
        hat = off * spread
        hat_ref[s] = hat
        spread_ref[s] = jnp.broadcast_to(spread, spread_ref.shape[1:])
        normed = (hat * gain + bias).astype(BF16)
        total += dot_t(normed, diag[:, s * channels : (s + 1) * channels])
    out_ref[0] = (total * mask).astype(BF16)
    for copy in copies[7:]:
        copy.wait()


def prepare_kernel(*refs):
    sources, (loss_ref, w_ref), outs, held, (wide_w, sems) = (
        refs[:3],
        refs[3:5],
        refs[5:13],
        refs[13:16],
        refs[16:],
    )
    by_left, by_right, swap, scaled, turned, inverse_ref, row_ref, shift_out = outs
    seq_ref, res_ref, shift_ref = held
    copies = load_all(list(zip(sources, held)), sems)
    row_at, column_at = place()
    rows, length, cz = loss_ref.shape
    width = by_left.shape[0]
    span = swap.shape[0]
    deep = span // width
    wide_w[...] = w_ref[...].astype(F32)
    for n in range(width):
        by_left[:, n * cz : (n + 1) * cz] = wide_w[pl.ds(n, width, stride=width), :].astype(BF16)
        by_right[:, n * cz : (n + 1) * cz] = w_ref[n * width : (n + 1) * width, :]
    to = lax.broadcasted_iota(jnp.int32, (span, span), 0)
    at = lax.broadcasted_iota(jnp.int32, (span, span), 1)
    swap[...] = jnp.where((to // deep == at % width) & (to % deep == at // width), 1.0, 0.0).astype(BF16)
    for copy in copies:
        copy.wait()
    present = jnp.sum(flag_row(seq_ref), axis=1, keepdims=True)
    columns = flag_column(res_ref, column_at * length, length)
    inverse = jnp.broadcast_to(1.0 / jnp.maximum(present * columns, 1.0), (length, cz))
    inverse_ref[...] = inverse
    row_ref[...] = jnp.broadcast_to(flag_column(res_ref, row_at * rows, rows), (rows, cz))
    shift_out[...] = jnp.broadcast_to(shift_ref[...].reshape(1, cz), shift_out.shape)
    for i in range(rows):
        factor = jnp.where(row_ref[i : i + 1, :] > 0.0, inverse, 1.0)
        scaled[:, i * cz : (i + 1) * cz] = (loss_ref[i].astype(F32) * factor).astype(BF16)
    to = lax.broadcasted_iota(jnp.int32, (TILE * TILE, TILE * TILE), 0)
    at = lax.broadcasted_iota(jnp.int32, (TILE * TILE, TILE * TILE), 1)
    turn = jnp.where((to // TILE == at % TILE) & (to % TILE == at // TILE), 1.0, 0.0).astype(BF16)
    for i in range(0, rows, TILE):
        for j in range(0, length, 2 * TILE):
            taken = [
                jnp.concatenate(
                    [scaled[b : b + TILE, (i + k) * cz : (i + k + 1) * cz] for k in range(TILE)], axis=0
                )
                for b in (j, j + TILE)
            ]
            made = dot(turn, jnp.concatenate(taken, axis=1)).astype(BF16)
            for a in range(2):
                for k in range(TILE):
                    low = (j + a * TILE + k) * cz
                    turned[i : i + TILE, low : low + cz] = made[
                        k * TILE : (k + 1) * TILE, a * cz : (a + 1) * cz
                    ]


def stack_kernel(own, got, *refs):
    out = refs[-1]
    count = own.shape[0]
    out[:count] = own[...]
    out[count:] = got[...]


def lefts_kernel(own, got, *refs):
    out = refs[-1]
    count, _, half = out.shape
    for n in range(count // 2):
        out[n] = own[n, :, :half]
        out[count // 2 + n] = got[n, :, :half]


def select_kernel(bit, own, got, *refs):
    out = refs[-1]
    row_at, column_at = place()
    other = (row_at ^ column_at) >> bit & 1

    @pl.when(other == 1)
    def _():
        out[...] = got[...]

    @pl.when(other == 0)
    def _():
        out[...] = own[...]


def add_kernel(own, got, *refs):
    out = refs[-1]
    out[...] = (own[...].astype(F32) + got[...].astype(F32)).astype(BF16)


def mark_kernel(*refs):
    refs[-1][...] = jnp.zeros_like(refs[-1])


def spread_rows(rows, n, block, width, deep):
    length, half = block.shape
    seqs = half // width
    wide = block.astype(F32)
    for s in range(seqs):
        rows[pl.ds(n * seqs + s, length, stride=deep), :] = wide[:, s * width : (s + 1) * width]


def produce(out, rows, weight, deep):
    width = weight.shape[0]
    cz = weight.shape[1] // width
    chunk = min(2 * PRODUCED, rows.shape[0]) // deep

    def section(step, _):
        taken = rows[lanes_at(step * chunk * deep, chunk * deep), :].astype(BF16)
        for n in range(width // 2):
            made = dot(taken, weight[:, n * 2 * cz : (n + 1) * 2 * cz])
            for i in range(chunk):
                both = jnp.concatenate(
                    [made[i * deep : (i + 1) * deep, a * cz : (a + 1) * cz] for a in range(2)], axis=0
                )
                low = n * 2 * deep
                out[low : low + 2 * deep, lanes_at((step * chunk + i) * cz, cz)] = both.astype(BF16)
        return 0

    lax.fori_loop(0, rows.shape[0] // (chunk * deep), section, 0)


def v_kernel(stack, swap, weight, *refs):
    right_cols, v_ref, rows = refs[-3:]
    count, _, both = stack.shape
    width = weight.shape[0]
    deep = swap.shape[0] // width
    for n in range(count):
        spread_rows(rows, n, stack[n, :, both // 2 :], width, deep)
    right = jnp.concatenate([stack[n, :, both // 2 :] for n in range(count)], axis=1)
    right_cols[...] = dot_t(right, swap[...]).astype(BF16)
    produce(v_ref, rows, weight, deep)


def t_kernel(bit, part, own, got, weight, *refs):
    t_ref, rows = refs[-2:]
    row_at, column_at = place()
    count = own.shape[0] // 2
    width = weight.shape[0]
    deep = t_ref.shape[0] // width
    other = (row_at ^ column_at) >> bit & 1
    for n in range(count):
        k = part * count + n
        block = jnp.where(other == 1, got[k].astype(F32), own[k].astype(F32))
        spread_rows(rows, n, block, width, deep)
    produce(t_ref, rows, weight, deep)


def ungroup(out, acc, swap):
    half = out.shape[2]
    made = dot(acc.astype(BF16), swap[...]).astype(BF16)
    for k in range(out.shape[0]):
        out[k] = made[:, k * half : (k + 1) * half]


def gradient_kernel(grouped, full_ref, side, swap, *refs):
    out = refs[-1]
    span = swap.shape[0]
    size = side.shape[1] * PRODUCED // span

    def section(step, acc):
        lanes = lanes_at(step * size, size)
        return acc + dot_t(full_ref[:, lanes], side[:, lanes])

    acc = dot_t(full_ref[:, :size], side[:, :size])
    acc = lax.fori_loop(1, span // PRODUCED, section, acc)
    if grouped:
        out[...] = jnp.transpose(acc).astype(BF16)
    else:
        ungroup(out, jnp.transpose(acc), swap)


def join_kernel(part, right, own, got, out):
    row_at, column_at = place()
    mine = jnp.where(row_at == column_at, 1.0, 0.0)
    count, _, both = out.shape
    half = both // 2
    for n in range(count):
        k = part * count + n
        out[n, :, :half] = ((own[k].astype(F32) + got[k].astype(F32)) * mine).astype(BF16)
        out[n, :, half:] = right[:, n * half : (n + 1) * half]


def halve_kernel(grouped, own, got, swap, *refs):
    keep, send = refs[-2:]
    count, _, both = keep.shape
    half = both // 2
    total = [(own[n].astype(F32) + got[n].astype(F32)).astype(BF16) for n in range(2 * count)]
    if grouped:
        right = dot(jnp.concatenate([part[:, half:] for part in total], axis=1), swap[...]).astype(BF16)
    for n in range(2 * count):
        out, k = (keep, n) if n < count else (send, n - count)
        out[k, :, :half] = total[n][:, :half]
        out[k, :, half:] = right[:, n * half : (n + 1) * half] if grouped else total[n][:, half:]


def rows_of_pass(span):
    return max(2, 8 * PRODUCED // span)


def pair_rows(out_ref, first, start, count, low_cols, high_cols, t_low, t_high, shift_ref, inverse_ref, row_ref):
    cz = out_ref.shape[2]
    group = min(4, count)
    for n in range(0, count, group):
        lanes = lanes_at((first + start + n) * cz, group * cz)
        made = dot(low_cols[...], t_low[:, lanes]) + dot(high_cols[...], t_high[:, lanes])
        for a in range(group):
            i = start + n + a
            factor = jnp.where(row_ref[pl.ds(first + i, 1), :] > 0.0, inverse_ref[...], 1.0)
            out_ref[i] = ((made[:, a * cz : (a + 1) * cz] + shift_ref[:1, :]) * factor).astype(BF16)


def upper_pair_kernel(*refs):
    sources, (out_ref, done_ref) = refs[:7], refs[-2:]
    step_rows = rows_of_pass(sources[0].shape[1])
    done_ref[...] = jnp.zeros_like(done_ref)

    def section(step, _):
        pair_rows(out_ref, 0, step * step_rows, step_rows, *sources)
        return 0

    lax.fori_loop(0, out_ref.shape[0] // step_rows, section, 0)


def lower_pair_kernel(*refs):
    sources, upper, (pair_ref, last_ref, held, sems) = refs[:7], refs[7], refs[-4:]
    step_rows = rows_of_pass(sources[0].shape[1])
    first = upper.shape[0]
    steps = held.shape[0] // step_rows

    def copy(step):
        spot = pl.ds(step * step_rows, step_rows)
        return pltpu.make_async_copy(
            held.at[spot], pair_ref.at[pl.ds(first + step * step_rows, step_rows)], sems.at[1 + step]
        )

    above = pltpu.make_async_copy(upper, pair_ref.at[:first], sems.at[0])
    above.start()

    def section(step, _):
        pair_rows(held, first, step * step_rows, step_rows, *sources)
        copy(step).start()
        return 0

    def last_section(step, _):
        pair_rows(last_ref, first + held.shape[0], step * step_rows, step_rows, *sources)
        return 0

    lax.fori_loop(0, steps, section, 0)
    lax.fori_loop(0, last_ref.shape[0] // step_rows, last_section, 0)
    above.wait()
    for step in range(steps):
        copy(step).wait()


def finish_kernel(own, got, mask_ref, diag, gain_ref, hat_ref, spread_ref, last, *refs):
    pair_ref, out_ref, held, sems = refs[-4:]
    rest = pair_ref.at[pl.ds(pair_ref.shape[0] - last.shape[0], last.shape[0])]
    seqs, _, channels = hat_ref.shape
    copies = [pltpu.make_async_copy(last, rest, sems.at[seqs])]
    copies[0].start()
    both = ((own[0].astype(F32) + got[0].astype(F32)) * mask_ref[...]).astype(BF16)
    gain = gain_ref[:1, :]
    for s in range(seqs):
        hat = hat_ref[s]
        spread = jnp.concatenate([spread_ref[s]] * (channels // spread_ref.shape[2]), axis=1)
        grad = dot(both, diag[:, s * channels : (s + 1) * channels]) * gain
        held[s] = (
            spread
            * (
                grad
                - jnp.mean(grad, axis=-1, keepdims=True)
                - hat * jnp.mean(grad * hat, axis=-1, keepdims=True)
            )
        ).astype(BF16)
        copies.append(pltpu.make_async_copy(held.at[s], out_ref.at[s], sems.at[s]))
        copies[-1].start()
    for copy in copies:
        copy.wait()


VMEM = pl.BlockSpec(memory_space=pltpu.VMEM)
HBM = pl.BlockSpec(memory_space=pltpu.HBM)


def call(kernel, name, out_shape, scratch, micros, in_specs=None, out_specs=None, limit=24, aliases=None, after=()):
    def run(*args):
        specs = [VMEM] * len(args) if in_specs is None else in_specs
        specs, args = specs + [pl.BlockSpec(memory_space=pl.ANY)] * len(after), args + tuple(after)
        outs = jax.tree.map(lambda _: VMEM, out_shape) if out_specs is None else out_specs
        return pl.pallas_call(
            kernel,
            out_shape=out_shape,
            in_specs=specs,
            out_specs=outs,
            scratch_shapes=scratch,
            input_output_aliases=aliases or {},
            compiler_params=pltpu.CompilerParams(vmem_limit_bytes=limit * 1024 * 1024),
            cost_estimate=pl.CostEstimate(flops=int(micros * 1e8), bytes_accessed=0, transcendentals=0),
            name=name,
        )(*args)

    return run


def swap_rows(x, blocks, bit):
    moves = [(z * blocks + c, (z ^ bit) * blocks + c) for z in range(blocks) for c in range(blocks)]
    return lax.ppermute(x, PLACES, moves)


def swap_columns(x, blocks, bit):
    moves = [(z * blocks + c, z * blocks + (c ^ bit)) for z in range(blocks) for c in range(blocks)]
    return lax.ppermute(x, PLACES, moves)


def per_device(
    homolog_activations,
    homolog_valid_flags,
    position_valid_flags,
    centering_factor,
    centering_shift,
    first_factor_matrix,
    second_factor_matrix,
    couple_weight_matrix,
    couple_shift_vector,
    loss_sensitivity,
):
    seqs, length, channels = homolog_activations.shape
    total_seq = homolog_valid_flags.shape[0]
    total_res = position_valid_flags.shape[0]
    width = first_factor_matrix.shape[1]
    rows, columns, cz = loss_sensitivity.shape
    blocks = lax.axis_size("cols") * lax.axis_size("sub")
    steps = blocks.bit_length() - 1
    assert blocks == 1 << steps == lax.axis_size("rows") and steps > 1
    half = seqs * width
    deep = total_seq // 2
    span = deep * width
    shape = jax.ShapeDtypeStruct

    def far(x):
        return pltpu.with_memory_space_constraint(x, pltpu.HBM)

    seq_flags, res_flags = far(homolog_valid_flags), far(position_valid_flags)

    stack, diag, mask, hat, spread, gain, loss, weights = call(
        project_kernel,
        "project",
        (
            shape((1, length, 2 * half), BF16),
            shape((2 * half, seqs * channels), BF16),
            shape((length, 2 * half), F32),
            shape((seqs, length, channels), F32),
            shape((seqs, length, cz), F32),
            shape((8, channels), F32),
            shape(loss_sensitivity.shape, BF16),
            shape(couple_weight_matrix.shape, BF16),
        ),
        [
            pltpu.VMEM((total_seq,), jnp.int32),
            pltpu.VMEM((seqs, length, channels), BF16),
            pltpu.VMEM((total_res,), jnp.int32),
            pltpu.VMEM((channels,), F32),
            pltpu.VMEM((channels,), F32),
            pltpu.VMEM((width, channels), BF16),
            pltpu.VMEM((width, channels), BF16),
            pltpu.SemaphoreType.DMA((9,)),
        ],
        2,
        in_specs=[HBM] * 9,
    )(
        seq_flags,
        far(homolog_activations),
        res_flags,
        far(centering_factor),
        far(centering_shift),
        far(first_factor_matrix.T),
        far(second_factor_matrix.T),
        far(couple_weight_matrix),
        far(loss_sensitivity),
    )

    by_left, by_right, swap, scaled, turned, inverse, row_flags, shift = call(
        prepare_kernel,
        "prepare",
        (
            shape((width, width * cz), BF16),
            shape((width, width * cz), BF16),
            shape((span, span), BF16),
            shape((columns, rows * cz), BF16),
            shape((rows, columns * cz), BF16),
            shape((columns, cz), F32),
            shape((rows, cz), F32),
            shape((8, cz), F32),
        ),
        [
            pltpu.VMEM((total_seq,), jnp.int32),
            pltpu.VMEM((total_res,), jnp.int32),
            pltpu.VMEM((cz,), F32),
            pltpu.VMEM((width * width, cz), F32),
            pltpu.SemaphoreType.DMA((3,)),
        ],
        3,
        in_specs=[HBM] * 3 + [VMEM] * 2,
    )(seq_flags, res_flags, far(couple_shift_vector), loss, weights)

    for step in range(steps):
        got = swap_rows(stack, blocks, blocks >> (step + 1))
        if step < steps - 1:
            stack = call(
                stack_kernel, "stack", shape((2 << step, length, 2 * half), BF16), [], 0.1, after=(shift,)
            )(stack, got)
    low_stack, high_stack = stack, got

    half_blocks = shape((blocks // 2, length, half), BF16)
    all_blocks = shape((blocks, length, half), BF16)
    cols_shape = shape((columns, span), BF16)
    t_limit = 16 + 2 * span * rows * cz * 2 // 2**20

    def make_v(stack, *after):
        return call(
            v_kernel,
            "expand_right",
            (cols_shape, shape((span, columns * cz), BF16)),
            [pltpu.VMEM((columns * deep, width), F32)],
            1.3,
            limit=t_limit,
            after=after,
        )(stack, swap, by_right)

    def gradient(full, side, grouped, *after):
        return call(
            functools.partial(gradient_kernel, grouped),
            "gradient",
            cols_shape if grouped else half_blocks,
            [],
            1.5,
            limit=t_limit,
            after=after,
        )(full, side, swap)

    low_cols, v_low = make_v(low_stack)
    low_sum = gradient(v_low, turned, False)
    lefts = call(lefts_kernel, "lefts", all_blocks, [], 0.1, after=(low_sum,))(low_stack, high_stack)
    got = swap_columns(lefts, blocks, 1)
    high_cols, v_high = make_v(high_stack, lefts)
    for step in range(1, steps):
        lefts = call(
            functools.partial(select_kernel, step - 1), "select", all_blocks, [], 0.1, after=(high_cols,)
        )(lefts, got)
        got = swap_columns(lefts, blocks, 1 << step)
    got_lefts = got
    high_sum = gradient(v_high, turned, False, lefts)
    sums = call(stack_kernel, "stack", all_blocks, [], 0.1)(low_sum, high_sum)

    def make_t(part, *after):
        return call(
            functools.partial(t_kernel, steps - 1, part),
            "expand_left",
            shape((span, rows * cz), BF16),
            [pltpu.VMEM((rows * deep, width), F32)],
            1.2,
            limit=t_limit,
            after=after,
        )(lefts, got_lefts, by_left)

    def make_t(part, *after):
        return call(
            functools.partial(t_kernel, steps - 1, part),
            "expand_left",
            shape((span, rows * cz), BF16),
            [pltpu.VMEM((rows * deep, width), F32)],
            1.3,
            limit=t_limit,
            after=after,
        )(lefts, got_lefts, by_left)

    arrived = call(mark_kernel, "mark", shape((8, cz), F32), [], 0.1, after=(got_lefts,))()
    for step in range(steps - 1):
        got = swap_columns(sums, blocks, 1 << step)
        sums = call(add_kernel, "add", all_blocks, [], 0.1, after=(arrived,))(sums, got)
    got = swap_columns(sums, blocks, 1 << (steps - 1))
    t_high = make_t(1, sums)

    def join(part, right):
        return call(
            functools.partial(join_kernel, part),
            "join",
            shape((blocks // 2, length, 2 * half), BF16),
            [],
            0.1,
        )(right, sums, got)

    send = join(1, gradient(t_high, scaled, True, sums))
    got_send = swap_rows(send, blocks, 1)
    t_low = make_t(0, send)
    keep = join(0, gradient(t_low, scaled, True, send))

    pair_sources = (low_cols, high_cols, t_low, t_high, shift, inverse, row_flags)
    upper_rows = rows // 4
    upper, paired = call(
        upper_pair_kernel,
        "pair",
        (shape((upper_rows, columns, cz), BF16), shape((8, cz), F32)),
        [],
        1,
        limit=t_limit,
        after=(keep,),
    )(*pair_sources)
    for step in range(1, steps):
        some = shape((blocks >> (step + 1), length, 2 * half), BF16)
        keep, send = call(
            functools.partial(halve_kernel, step == 1), "halve", (some, some), [], 0.1, after=(paired,)
        )(keep, got_send, swap)
        got_send = swap_rows(send, blocks, 1 << step)
    last_rows = 2 * rows_of_pass(span)
    held_rows = rows - upper_rows - last_rows
    pair, last = call(
        lower_pair_kernel,
        "pair",
        (shape(loss_sensitivity.shape, BF16), shape((last_rows, columns, cz), BF16)),
        [
            pltpu.VMEM((held_rows, columns, cz), BF16),
            pltpu.SemaphoreType.DMA((1 + held_rows // rows_of_pass(span),)),
        ],
        2,
        out_specs=(HBM, VMEM),
        limit=t_limit,
        after=(send,),
    )(*pair_sources, upper)

    return call(
        finish_kernel,
        "finish",
        (shape(loss_sensitivity.shape, BF16), shape(homolog_activations.shape, BF16)),
        [pltpu.VMEM(homolog_activations.shape, BF16), pltpu.SemaphoreType.DMA((seqs + 1,))],
        1,
        in_specs=[VMEM] * 8 + [HBM],
        out_specs=(HBM, HBM),
        aliases={8: 0},
    )(keep, got_send, mask, diag, gain, hat, spread, last, pair)


def solution(mesh):
    split = P(("groups", "rows"), ("cols", "sub"), None)
    return jax.shard_map(
        per_device,
        mesh=mesh,
        in_specs=(split, P("groups"), P("groups"), P(), P(), P(), P(), P(), P(), split),
        out_specs=(split, split),
        check_vma=False,
    )
```

```python
import functools

import jax
import jax.numpy as jnp
from jax import lax
from jax.experimental import pallas as pl
from jax.experimental.pallas import tpu as pltpu
from jax.sharding import PartitionSpec as P

F32 = jnp.float32
BF16 = jnp.bfloat16
PLACES = ("rows", "cols", "sub")
PRODUCED = 256
TILE = 16


def dot(a, b):
    return lax.dot_general(a, b, (((1,), (0,)), ((), ())), preferred_element_type=F32)


def dot_t(a, b):
    return lax.dot_general(a, b, (((1,), (1,)), ((), ())), preferred_element_type=F32)


def place():
    column = lax.axis_index("cols") * lax.axis_size("sub") + lax.axis_index("sub")
    return lax.axis_index("rows"), column


def lanes_at(start, size):
    return pl.ds(pl.multiple_of(start, size), size)


def flag_row(flags_ref):
    return flags_ref[...].astype(F32).reshape(1, -1)


def flag_column(flags_ref, start, length):
    flags = flag_row(flags_ref)
    total = flags.shape[1]
    spot = lax.broadcasted_iota(jnp.int32, (length, total), 0) + start
    lane = lax.broadcasted_iota(jnp.int32, (length, total), 1)
    return jnp.sum(jnp.where(spot == lane, flags, 0.0), axis=1, keepdims=True)


def load_all(pairs, sems):
    copies = [pltpu.make_async_copy(src, dst, sems.at[n]) for n, (src, dst) in enumerate(pairs)]
    for copy in copies:
        copy.start()
    return copies


def project_kernel(*refs):
    sources, outs, (loss_ref, w_ref), held, sems = refs[:9], refs[9:15], refs[15:17], refs[17:24], refs[24]
    out_ref, factors, mask_ref, hat_ref, spread_ref, gain_out = outs
    copies = load_all(list(zip(sources, held + (w_ref, loss_ref))), sems)
    seq_ref, x_ref, res_ref, gain_ref, bias_ref, first_ref, second_ref = held
    row_at, column_at = place()
    seqs, length, channels = x_ref.shape
    width = first_ref.shape[0]
    half = seqs * width
    for copy in copies[:7]:
        copy.wait()
    for s in range(seqs):
        factors[s * width : (s + 1) * width, :] = first_ref[...]
        factors[(seqs + s) * width : (seqs + s + 1) * width, :] = second_ref[...]
    flags = flag_row(seq_ref)
    spot = lax.broadcasted_iota(jnp.int32, flags.shape, 1)
    which = lax.broadcasted_iota(jnp.int32, (1, 2 * half), 1) % half // width
    own = jnp.zeros((1, 2 * half), F32)
    for s in range(seqs):
        value = jnp.sum(jnp.where(spot == row_at * seqs + s, flags, 0.0), axis=1, keepdims=True)
        own = jnp.where(which == s, value, own)
    mask = flag_column(res_ref, column_at * length, length) * own
    mask_ref[...] = mask
    gain = gain_ref[...].reshape(1, channels)
    bias = bias_ref[...].reshape(1, channels)
    gain_out[...] = jnp.broadcast_to(gain, gain_out.shape)
    normed = []
    for s in range(seqs):
        x = x_ref[s].astype(F32)
        off = x - jnp.mean(x, axis=-1, keepdims=True)
        spread = lax.rsqrt(jnp.mean(off * off, axis=-1, keepdims=True) + 1e-05)
        hat = off * spread
        hat_ref[s] = hat
        spread_ref[s] = jnp.broadcast_to(spread, spread_ref.shape[1:])
        normed.append((hat * gain + bias).astype(BF16))
    made = dot_t(jnp.concatenate(normed, axis=0), factors[...])
    total = made[:length]
    for s in range(1, seqs):
        total = jnp.where(which == s, made[s * length : (s + 1) * length], total)
    out_ref[0] = (total * mask).astype(BF16)
    for copy in copies[7:]:
        copy.wait()


def prepare_kernel(*refs):
    sources, (loss_ref, w_ref), outs, held, (wide_w, sems) = (
        refs[:3],
        refs[3:5],
        refs[5:13],
        refs[13:16],
        refs[16:],
    )
    by_left, by_right, swap, scaled, turned, inverse_ref, row_ref, shift_out = outs
    seq_ref, res_ref, shift_ref = held
    copies = load_all(list(zip(sources, held)), sems)
    row_at, column_at = place()
    rows, length, cz = loss_ref.shape
    width = by_left.shape[0]
    span = swap.shape[0]
    deep = span // width
    wide_w[...] = w_ref[...].astype(F32)
    for n in range(width):
        by_left[:, n * cz : (n + 1) * cz] = wide_w[pl.ds(n, width, stride=width), :].astype(BF16)
        by_right[:, n * cz : (n + 1) * cz] = w_ref[n * width : (n + 1) * width, :]
    to = lax.broadcasted_iota(jnp.int32, (span, span), 0)
    at = lax.broadcasted_iota(jnp.int32, (span, span), 1)
    swap[...] = jnp.where((to // deep == at % width) & (to % deep == at // width), 1.0, 0.0).astype(BF16)
    for copy in copies:
        copy.wait()
    present = jnp.sum(flag_row(seq_ref), axis=1, keepdims=True)
    columns = flag_column(res_ref, column_at * length, length)
    inverse = jnp.broadcast_to(1.0 / jnp.maximum(present * columns, 1.0), (length, cz))
    inverse_ref[...] = inverse
    row_ref[...] = jnp.broadcast_to(flag_column(res_ref, row_at * rows, rows), (rows, cz))
    shift_out[...] = jnp.broadcast_to(shift_ref[...].reshape(1, cz), shift_out.shape)
    for i in range(rows):
        factor = jnp.where(row_ref[i : i + 1, :] > 0.0, inverse, 1.0)
        scaled[:, i * cz : (i + 1) * cz] = (loss_ref[i].astype(F32) * factor).astype(BF16)
    to = lax.broadcasted_iota(jnp.int32, (TILE * TILE, TILE * TILE), 0)
    at = lax.broadcasted_iota(jnp.int32, (TILE * TILE, TILE * TILE), 1)
    turn = jnp.where((to // TILE == at % TILE) & (to % TILE == at // TILE), 1.0, 0.0).astype(BF16)
    for i in range(0, rows, TILE):
        for j in range(0, length, 2 * TILE):
            taken = [
                jnp.concatenate(
                    [scaled[b : b + TILE, (i + k) * cz : (i + k + 1) * cz] for k in range(TILE)], axis=0
                )
                for b in (j, j + TILE)
            ]
            made = dot(turn, jnp.concatenate(taken, axis=1)).astype(BF16)
            for a in range(2):
                for k in range(TILE):
                    low = (j + a * TILE + k) * cz
                    turned[i : i + TILE, low : low + cz] = made[
                        k * TILE : (k + 1) * TILE, a * cz : (a + 1) * cz
                    ]


def stack_kernel(own, got, *refs):
    out = refs[-1]
    count = own.shape[0]
    out[:count] = own[...]
    out[count:] = got[...]


def lefts_kernel(own, got, *refs):
    out = refs[-1]
    count, _, half = out.shape
    for n in range(count // 2):
        out[n] = own[n, :, :half]
        out[count // 2 + n] = got[n, :, :half]


def select_kernel(bit, own, got, *refs):
    out = refs[-1]
    row_at, column_at = place()
    other = (row_at ^ column_at) >> bit & 1

    @pl.when(other == 1)
    def _():
        out[...] = got[...]

    @pl.when(other == 0)
    def _():
        out[...] = own[...]


def add_kernel(own, got, *refs):
    out = refs[-1]
    out[...] = (own[...].astype(F32) + got[...].astype(F32)).astype(BF16)


def mark_kernel(*refs):
    refs[-1][...] = jnp.zeros_like(refs[-1])


def spread_rows(rows, n, block, width, deep):
    length, half = block.shape
    seqs = half // width
    wide = block.astype(F32)
    for s in range(seqs):
        rows[pl.ds(n * seqs + s, length, stride=deep), :] = wide[:, s * width : (s + 1) * width]


def produce(out, rows, weight, deep):
    width = weight.shape[0]
    cz = weight.shape[1] // width
    chunk = min(2 * PRODUCED, rows.shape[0]) // deep

    def section(step, _):
        taken = rows[lanes_at(step * chunk * deep, chunk * deep), :].astype(BF16)
        for n in range(width // 2):
            made = dot(taken, weight[:, n * 2 * cz : (n + 1) * 2 * cz])
            for i in range(chunk):
                both = jnp.concatenate(
                    [made[i * deep : (i + 1) * deep, a * cz : (a + 1) * cz] for a in range(2)], axis=0
                )
                low = n * 2 * deep
                out[low : low + 2 * deep, lanes_at((step * chunk + i) * cz, cz)] = both.astype(BF16)
        return 0

    lax.fori_loop(0, rows.shape[0] // (chunk * deep), section, 0)


def v_kernel(stack, swap, weight, *refs):
    right_cols, v_ref, rows = refs[-3:]
    count, _, both = stack.shape
    width = weight.shape[0]
    deep = swap.shape[0] // width
    for n in range(count):
        spread_rows(rows, n, stack[n, :, both // 2 :], width, deep)
    right = jnp.concatenate([stack[n, :, both // 2 :] for n in range(count)], axis=1)
    right_cols[...] = dot_t(right, swap[...]).astype(BF16)
    produce(v_ref, rows, weight, deep)


def t_kernel(bit, part, own, got, weight, *refs):
    t_ref, rows = refs[-2:]
    row_at, column_at = place()
    count = own.shape[0] // 2
    width = weight.shape[0]
    deep = t_ref.shape[0] // width
    other = (row_at ^ column_at) >> bit & 1
    for n in range(count):
        k = part * count + n
        block = jnp.where(other == 1, got[k].astype(F32), own[k].astype(F32))
        spread_rows(rows, n, block, width, deep)
    produce(t_ref, rows, weight, deep)


def ungroup(out, acc, swap):
    half = out.shape[2]
    made = dot(acc.astype(BF16), swap[...]).astype(BF16)
    for k in range(out.shape[0]):
        out[k] = made[:, k * half : (k + 1) * half]


def gradient_kernel(grouped, full_ref, side, swap, *refs):
    out = refs[-1]
    span = swap.shape[0]
    size = side.shape[1] * PRODUCED // span

    def section(step, acc):
        lanes = lanes_at(step * size, size)
        return acc + dot_t(full_ref[:, lanes], side[:, lanes])

    acc = dot_t(full_ref[:, :size], side[:, :size])
    acc = lax.fori_loop(1, span // PRODUCED, section, acc)
    if grouped:
        out[...] = jnp.transpose(acc).astype(BF16)
    else:
        ungroup(out, jnp.transpose(acc), swap)


def join_kernel(part, right, own, got, out):
    row_at, column_at = place()
    mine = jnp.where(row_at == column_at, 1.0, 0.0)
    count, _, both = out.shape
    half = both // 2
    for n in range(count):
        k = part * count + n
        out[n, :, :half] = ((own[k].astype(F32) + got[k].astype(F32)) * mine).astype(BF16)
        out[n, :, half:] = right[:, n * half : (n + 1) * half]


def halve_kernel(grouped, own, got, swap, *refs):
    keep, send = refs[-2:]
    count, _, both = keep.shape
    half = both // 2
    total = [(own[n].astype(F32) + got[n].astype(F32)).astype(BF16) for n in range(2 * count)]
    if grouped:
        right = dot(jnp.concatenate([part[:, half:] for part in total], axis=1), swap[...]).astype(BF16)
    for n in range(2 * count):
        out, k = (keep, n) if n < count else (send, n - count)
        out[k, :, :half] = total[n][:, :half]
        out[k, :, half:] = right[:, n * half : (n + 1) * half] if grouped else total[n][:, half:]


def rows_of_pass(span):
    return max(2, 8 * PRODUCED // span)


def pair_rows(out_ref, first, start, count, low_cols, high_cols, t_low, t_high, shift_ref, inverse_ref, row_ref):
    cz = out_ref.shape[2]
    group = min(4, count)
    for n in range(0, count, group):
        lanes = lanes_at((first + start + n) * cz, group * cz)
        made = dot(low_cols[...], t_low[:, lanes]) + dot(high_cols[...], t_high[:, lanes])
        for a in range(group):
            i = start + n + a
            factor = jnp.where(row_ref[pl.ds(first + i, 1), :] > 0.0, inverse_ref[...], 1.0)
            out_ref[i] = ((made[:, a * cz : (a + 1) * cz] + shift_ref[:1, :]) * factor).astype(BF16)


def upper_pair_kernel(*refs):
    sources, (out_ref, done_ref) = refs[:7], refs[-2:]
    step_rows = rows_of_pass(sources[0].shape[1])
    done_ref[...] = jnp.zeros_like(done_ref)

    def section(step, _):
        pair_rows(out_ref, 0, step * step_rows, step_rows, *sources)
        return 0

    lax.fori_loop(0, out_ref.shape[0] // step_rows, section, 0)


def lower_pair_kernel(*refs):
    sources, upper, (pair_ref, last_ref, held, sems) = refs[:7], refs[7], refs[-4:]
    step_rows = rows_of_pass(sources[0].shape[1])
    first = upper.shape[0]
    steps = held.shape[0] // step_rows

    def copy(step):
        spot = pl.ds(step * step_rows, step_rows)
        return pltpu.make_async_copy(
            held.at[spot], pair_ref.at[pl.ds(first + step * step_rows, step_rows)], sems.at[1 + step]
        )

    above = pltpu.make_async_copy(upper, pair_ref.at[:first], sems.at[0])
    above.start()

    def section(step, _):
        pair_rows(held, first, step * step_rows, step_rows, *sources)
        copy(step).start()
        return 0

    def last_section(step, _):
        pair_rows(last_ref, first + held.shape[0], step * step_rows, step_rows, *sources)
        return 0

    lax.fori_loop(0, steps, section, 0)
    lax.fori_loop(0, last_ref.shape[0] // step_rows, last_section, 0)
    above.wait()
    for step in range(steps):
        copy(step).wait()


def finish_kernel(own, got, mask_ref, factors, gain_ref, hat_ref, spread_ref, last, *refs):
    pair_ref, out_ref, held, sems = refs[-4:]
    rest = pair_ref.at[pl.ds(pair_ref.shape[0] - last.shape[0], last.shape[0])]
    seqs, length, channels = hat_ref.shape
    copies = [pltpu.make_async_copy(last, rest, sems.at[seqs])]
    copies[0].start()
    both = (own[0].astype(F32) + got[0].astype(F32)) * mask_ref[...]
    half = both.shape[1] // 2
    which = lax.broadcasted_iota(jnp.int32, (1, 2 * half), 1) % half // (half // seqs)
    rows = [jnp.where(which == s, both, 0.0).astype(BF16) for s in range(seqs)]
    grads = dot(jnp.concatenate(rows, axis=0), factors[...])
    gain = gain_ref[:1, :]
    for s in range(seqs):
        hat = hat_ref[s]
        spread = jnp.concatenate([spread_ref[s]] * (channels // spread_ref.shape[2]), axis=1)
        grad = grads[s * length : (s + 1) * length] * gain
        held[s] = (
            spread
            * (
                grad
                - jnp.mean(grad, axis=-1, keepdims=True)
                - hat * jnp.mean(grad * hat, axis=-1, keepdims=True)
            )
        ).astype(BF16)
        copies.append(pltpu.make_async_copy(held.at[s], out_ref.at[s], sems.at[s]))
        copies[-1].start()
    for copy in copies:
        copy.wait()


VMEM = pl.BlockSpec(memory_space=pltpu.VMEM)
HBM = pl.BlockSpec(memory_space=pltpu.HBM)


def call(kernel, name, out_shape, scratch, micros, in_specs=None, out_specs=None, limit=24, aliases=None, after=()):
    def run(*args):
        specs = [VMEM] * len(args) if in_specs is None else in_specs
        specs, args = specs + [pl.BlockSpec(memory_space=pl.ANY)] * len(after), args + tuple(after)
        outs = jax.tree.map(lambda _: VMEM, out_shape) if out_specs is None else out_specs
        return pl.pallas_call(
            kernel,
            out_shape=out_shape,
            in_specs=specs,
            out_specs=outs,
            scratch_shapes=scratch,
            input_output_aliases=aliases or {},
            compiler_params=pltpu.CompilerParams(vmem_limit_bytes=limit * 1024 * 1024),
            cost_estimate=pl.CostEstimate(flops=int(micros * 1e8), bytes_accessed=0, transcendentals=0),
            name=name,
        )(*args)

    return run


def swap_rows(x, blocks, bit):
    moves = [(z * blocks + c, (z ^ bit) * blocks + c) for z in range(blocks) for c in range(blocks)]
    return lax.ppermute(x, PLACES, moves)


def swap_columns(x, blocks, bit):
    moves = [(z * blocks + c, z * blocks + (c ^ bit)) for z in range(blocks) for c in range(blocks)]
    return lax.ppermute(x, PLACES, moves)


def per_device(
    homolog_activations,
    homolog_valid_flags,
    position_valid_flags,
    centering_factor,
    centering_shift,
    first_factor_matrix,
    second_factor_matrix,
    couple_weight_matrix,
    couple_shift_vector,
    loss_sensitivity,
):
    seqs, length, channels = homolog_activations.shape
    total_seq = homolog_valid_flags.shape[0]
    total_res = position_valid_flags.shape[0]
    width = first_factor_matrix.shape[1]
    rows, columns, cz = loss_sensitivity.shape
    blocks = lax.axis_size("cols") * lax.axis_size("sub")
    steps = blocks.bit_length() - 1
    assert blocks == 1 << steps == lax.axis_size("rows") and steps > 1
    half = seqs * width
    deep = total_seq // 2
    span = deep * width
    shape = jax.ShapeDtypeStruct

    def far(x):
        return pltpu.with_memory_space_constraint(x, pltpu.HBM)

    seq_flags, res_flags = far(homolog_valid_flags), far(position_valid_flags)

    stack, factors, mask, hat, spread, gain, loss, weights = call(
        project_kernel,
        "project",
        (
            shape((1, length, 2 * half), BF16),
            shape((2 * half, channels), BF16),
            shape((length, 2 * half), F32),
            shape((seqs, length, channels), F32),
            shape((seqs, length, cz), F32),
            shape((8, channels), F32),
            shape(loss_sensitivity.shape, BF16),
            shape(couple_weight_matrix.shape, BF16),
        ),
        [
            pltpu.VMEM((total_seq,), jnp.int32),
            pltpu.VMEM((seqs, length, channels), BF16),
            pltpu.VMEM((total_res,), jnp.int32),
            pltpu.VMEM((channels,), F32),
            pltpu.VMEM((channels,), F32),
            pltpu.VMEM((width, channels), BF16),
            pltpu.VMEM((width, channels), BF16),
            pltpu.SemaphoreType.DMA((9,)),
        ],
        2,
        in_specs=[HBM] * 9,
    )(
        seq_flags,
        far(homolog_activations),
        res_flags,
        far(centering_factor),
        far(centering_shift),
        far(first_factor_matrix.T),
        far(second_factor_matrix.T),
        far(couple_weight_matrix),
        far(loss_sensitivity),
    )

    by_left, by_right, swap, scaled, turned, inverse, row_flags, shift = call(
        prepare_kernel,
        "prepare",
        (
            shape((width, width * cz), BF16),
            shape((width, width * cz), BF16),
            shape((span, span), BF16),
            shape((columns, rows * cz), BF16),
            shape((rows, columns * cz), BF16),
            shape((columns, cz), F32),
            shape((rows, cz), F32),
            shape((8, cz), F32),
        ),
        [
            pltpu.VMEM((total_seq,), jnp.int32),
            pltpu.VMEM((total_res,), jnp.int32),
            pltpu.VMEM((cz,), F32),
            pltpu.VMEM((width * width, cz), F32),
            pltpu.SemaphoreType.DMA((3,)),
        ],
        3,
        in_specs=[HBM] * 3 + [VMEM] * 2,
    )(seq_flags, res_flags, far(couple_shift_vector), loss, weights)

    for step in range(steps):
        got = swap_rows(stack, blocks, blocks >> (step + 1))
        if step < steps - 1:
            stack = call(
                stack_kernel, "stack", shape((2 << step, length, 2 * half), BF16), [], 0.1, after=(shift,)
            )(stack, got)
    low_stack, high_stack = stack, got

    half_blocks = shape((blocks // 2, length, half), BF16)
    all_blocks = shape((blocks, length, half), BF16)
    cols_shape = shape((columns, span), BF16)
    t_limit = 16 + 2 * span * rows * cz * 2 // 2**20

    def make_v(stack, *after):
        return call(
            v_kernel,
            "expand_right",
            (cols_shape, shape((span, columns * cz), BF16)),
            [pltpu.VMEM((columns * deep, width), F32)],
            1.3,
            limit=t_limit,
            after=after,
        )(stack, swap, by_right)

    def gradient(full, side, grouped, *after):
        return call(
            functools.partial(gradient_kernel, grouped),
            "gradient",
            cols_shape if grouped else half_blocks,
            [],
            1.5,
            limit=t_limit,
            after=after,
        )(full, side, swap)

    low_cols, v_low = make_v(low_stack)
    low_sum = gradient(v_low, turned, False)
    lefts = call(lefts_kernel, "lefts", all_blocks, [], 0.1, after=(low_sum,))(low_stack, high_stack)
    got = swap_columns(lefts, blocks, 1)
    high_cols, v_high = make_v(high_stack, lefts)
    for step in range(1, steps):
        lefts = call(
            functools.partial(select_kernel, step - 1), "select", all_blocks, [], 0.1, after=(high_cols,)
        )(lefts, got)
        got = swap_columns(lefts, blocks, 1 << step)
    got_lefts = got
    high_sum = gradient(v_high, turned, False, lefts)
    sums = call(stack_kernel, "stack", all_blocks, [], 0.1)(low_sum, high_sum)

    def make_t(part, *after):
        return call(
            functools.partial(t_kernel, steps - 1, part),
            "expand_left",
            shape((span, rows * cz), BF16),
            [pltpu.VMEM((rows * deep, width), F32)],
            1.2,
            limit=t_limit,
            after=after,
        )(lefts, got_lefts, by_left)

    def make_t(part, *after):
        return call(
            functools.partial(t_kernel, steps - 1, part),
            "expand_left",
            shape((span, rows * cz), BF16),
            [pltpu.VMEM((rows * deep, width), F32)],
            1.3,
            limit=t_limit,
            after=after,
        )(lefts, got_lefts, by_left)

    arrived = call(mark_kernel, "mark", shape((8, cz), F32), [], 0.1, after=(got_lefts,))()
    for step in range(steps - 1):
        got = swap_columns(sums, blocks, 1 << step)
        sums = call(add_kernel, "add", all_blocks, [], 0.1, after=(arrived,))(sums, got)
    got = swap_columns(sums, blocks, 1 << (steps - 1))
    t_high = make_t(1, sums)

    def join(part, right):
        return call(
            functools.partial(join_kernel, part),
            "join",
            shape((blocks // 2, length, 2 * half), BF16),
            [],
            0.1,
        )(right, sums, got)

    send = join(1, gradient(t_high, scaled, True, sums))
    got_send = swap_rows(send, blocks, 1)
    t_low = make_t(0, send)
    keep = join(0, gradient(t_low, scaled, True, send))

    pair_sources = (low_cols, high_cols, t_low, t_high, shift, inverse, row_flags)
    upper_rows = rows // 4
    upper, paired = call(
        upper_pair_kernel,
        "pair",
        (shape((upper_rows, columns, cz), BF16), shape((8, cz), F32)),
        [],
        1,
        limit=t_limit,
        after=(keep,),
    )(*pair_sources)
    for step in range(1, steps):
        some = shape((blocks >> (step + 1), length, 2 * half), BF16)
        keep, send = call(
            functools.partial(halve_kernel, step == 1), "halve", (some, some), [], 0.1, after=(paired,)
        )(keep, got_send, swap)
        got_send = swap_rows(send, blocks, 1 << step)
    last_rows = 2 * rows_of_pass(span)
    held_rows = rows - upper_rows - last_rows
    pair, last = call(
        lower_pair_kernel,
        "pair",
        (shape(loss_sensitivity.shape, BF16), shape((last_rows, columns, cz), BF16)),
        [
            pltpu.VMEM((held_rows, columns, cz), BF16),
            pltpu.SemaphoreType.DMA((1 + held_rows // rows_of_pass(span),)),
        ],
        2,
        out_specs=(HBM, VMEM),
        limit=t_limit,
        after=(send,),
    )(*pair_sources, upper)

    return call(
        finish_kernel,
        "finish",
        (shape(loss_sensitivity.shape, BF16), shape(homolog_activations.shape, BF16)),
        [pltpu.VMEM(homolog_activations.shape, BF16), pltpu.SemaphoreType.DMA((seqs + 1,))],
        1,
        in_specs=[VMEM] * 8 + [HBM],
        out_specs=(HBM, HBM),
        aliases={8: 0},
    )(keep, got_send, mask, factors, gain, hat, spread, last, pair)


def solution(mesh):
    split = P(("groups", "rows"), ("cols", "sub"), None)
    return jax.shard_map(
        per_device,
        mesh=mesh,
        in_specs=(split, P("groups"), P("groups"), P(), P(), P(), P(), P(), P(), split),
        out_specs=(split, split),
        check_vma=False,
    )
```

```python
import functools

import jax
import jax.numpy as jnp
from jax import lax
from jax.experimental import pallas as pl
from jax.experimental.pallas import tpu as pltpu
from jax.sharding import PartitionSpec as P

F32 = jnp.float32
BF16 = jnp.bfloat16
PLACES = ("rows", "cols", "sub")
PRODUCED = 256
TILE = 16


def dot(a, b):
    return lax.dot_general(a, b, (((1,), (0,)), ((), ())), preferred_element_type=F32)


def dot_t(a, b):
    return lax.dot_general(a, b, (((1,), (1,)), ((), ())), preferred_element_type=F32)


def place():
    column = lax.axis_index("cols") * lax.axis_size("sub") + lax.axis_index("sub")
    return lax.axis_index("rows"), column


def lanes_at(start, size):
    return pl.ds(pl.multiple_of(start, size), size)


def flag_row(flags_ref):
    return flags_ref[...].astype(F32).reshape(1, -1)


def flag_column(flags_ref, start, length):
    flags = flag_row(flags_ref)
    total = flags.shape[1]
    spot = lax.broadcasted_iota(jnp.int32, (length, total), 0) + start
    lane = lax.broadcasted_iota(jnp.int32, (length, total), 1)
    return jnp.sum(jnp.where(spot == lane, flags, 0.0), axis=1, keepdims=True)


def load_all(pairs, sems):
    copies = [pltpu.make_async_copy(src, dst, sems.at[n]) for n, (src, dst) in enumerate(pairs)]
    for copy in copies:
        copy.start()
    return copies


def project_kernel(*refs):
    sources, outs, (loss_ref, w_ref), held, sems = refs[:9], refs[9:15], refs[15:17], refs[17:24], refs[24]
    out_ref, factors, mask_ref, hat_ref, spread_ref, gain_out = outs
    copies = load_all(list(zip(sources, held + (w_ref, loss_ref))), sems)
    seq_ref, x_ref, res_ref, gain_ref, bias_ref, first_ref, second_ref = held
    row_at, column_at = place()
    seqs, length, channels = x_ref.shape
    width = first_ref.shape[0]
    half = seqs * width
    for copy in copies[:7]:
        copy.wait()
    for s in range(seqs):
        factors[s * width : (s + 1) * width, :] = first_ref[...]
        factors[(seqs + s) * width : (seqs + s + 1) * width, :] = second_ref[...]
    flags = flag_row(seq_ref)
    spot = lax.broadcasted_iota(jnp.int32, flags.shape, 1)
    which = lax.broadcasted_iota(jnp.int32, (1, 2 * half), 1) % half // width
    own = jnp.zeros((1, 2 * half), F32)
    for s in range(seqs):
        value = jnp.sum(jnp.where(spot == row_at * seqs + s, flags, 0.0), axis=1, keepdims=True)
        own = jnp.where(which == s, value, own)
    mask = flag_column(res_ref, column_at * length, length) * own
    mask_ref[...] = mask
    gain = gain_ref[...].reshape(1, channels)
    bias = bias_ref[...].reshape(1, channels)
    gain_out[...] = jnp.broadcast_to(gain, gain_out.shape)
    normed = []
    for s in range(seqs):
        x = x_ref[s].astype(F32)
        off = x - jnp.mean(x, axis=-1, keepdims=True)
        spread = lax.rsqrt(jnp.mean(off * off, axis=-1, keepdims=True) + 1e-05)
        hat = off * spread
        hat_ref[s] = hat
        spread_ref[s] = jnp.broadcast_to(spread, spread_ref.shape[1:])
        normed.append((hat * gain + bias).astype(BF16))
    made = dot_t(jnp.concatenate(normed, axis=0), factors[...])
    total = made[:length]
    for s in range(1, seqs):
        total = jnp.where(which == s, made[s * length : (s + 1) * length], total)
    out_ref[0] = (total * mask).astype(BF16)
    for copy in copies[7:]:
        copy.wait()


def prepare_kernel(*refs):
    sources, (loss_ref, w_ref), outs, held, (wide_w, sems) = (
        refs[:3],
        refs[3:5],
        refs[5:13],
        refs[13:16],
        refs[16:],
    )
    by_left, by_right, swap, scaled, turned, inverse_ref, row_ref, shift_out = outs
    seq_ref, res_ref, shift_ref = held
    copies = load_all(list(zip(sources, held)), sems)
    row_at, column_at = place()
    rows, length, cz = loss_ref.shape
    width = by_left.shape[0]
    span = swap.shape[0]
    deep = span // width
    wide_w[...] = w_ref[...].astype(F32)
    for n in range(width):
        by_left[:, n * cz : (n + 1) * cz] = wide_w[pl.ds(n, width, stride=width), :].astype(BF16)
        by_right[:, n * cz : (n + 1) * cz] = w_ref[n * width : (n + 1) * width, :]
    to = lax.broadcasted_iota(jnp.int32, (span, span), 0)
    at = lax.broadcasted_iota(jnp.int32, (span, span), 1)
    swap[...] = jnp.where((to // deep == at % width) & (to % deep == at // width), 1.0, 0.0).astype(BF16)
    for copy in copies:
        copy.wait()
    present = jnp.sum(flag_row(seq_ref), axis=1, keepdims=True)
    columns = flag_column(res_ref, column_at * length, length)
    inverse = jnp.broadcast_to(1.0 / jnp.maximum(present * columns, 1.0), (length, cz))
    inverse_ref[...] = inverse
    row_ref[...] = jnp.broadcast_to(flag_column(res_ref, row_at * rows, rows), (rows, cz))
    shift_out[...] = jnp.broadcast_to(shift_ref[...].reshape(1, cz), shift_out.shape)
    for i in range(rows):
        factor = jnp.where(row_ref[i : i + 1, :] > 0.0, inverse, 1.0)
        scaled[:, i * cz : (i + 1) * cz] = (loss_ref[i].astype(F32) * factor).astype(BF16)
    to = lax.broadcasted_iota(jnp.int32, (TILE * TILE, TILE * TILE), 0)
    at = lax.broadcasted_iota(jnp.int32, (TILE * TILE, TILE * TILE), 1)
    turn = jnp.where((to // TILE == at % TILE) & (to % TILE == at // TILE), 1.0, 0.0).astype(BF16)
    for i in range(0, rows, TILE):
        for j in range(0, length, 2 * TILE):
            taken = [
                jnp.concatenate(
                    [scaled[b : b + TILE, (i + k) * cz : (i + k + 1) * cz] for k in range(TILE)], axis=0
                )
                for b in (j, j + TILE)
            ]
            made = dot(turn, jnp.concatenate(taken, axis=1)).astype(BF16)
            for a in range(2):
                for k in range(TILE):
                    low = (j + a * TILE + k) * cz
                    turned[i : i + TILE, low : low + cz] = made[
                        k * TILE : (k + 1) * TILE, a * cz : (a + 1) * cz
                    ]


def stack_kernel(own, got, *refs):
    out = refs[-1]
    count = own.shape[0]
    out[:count] = own[...]
    out[count:] = got[...]


def lefts_kernel(own, got, *refs):
    out = refs[-1]
    count, _, half = out.shape
    for n in range(count // 2):
        out[n] = own[n, :, :half]
        out[count // 2 + n] = got[n, :, :half]


def select_kernel(bit, own, got, *refs):
    out = refs[-1]
    row_at, column_at = place()
    other = jnp.where((row_at ^ column_at) & (2 * bit - 1) == bit, 1, 0)

    @pl.when(other == 1)
    def _():
        out[...] = got[...]

    @pl.when(other == 0)
    def _():
        out[...] = own[...]


def add_kernel(own, got, *refs):
    out = refs[-1]
    out[...] = (own[...].astype(F32) + got[...].astype(F32)).astype(BF16)


def spread_rows(rows, n, block, width, deep):
    length, half = block.shape
    seqs = half // width
    wide = block.astype(F32)
    for s in range(seqs):
        rows[pl.ds(n * seqs + s, length, stride=deep), :] = wide[:, s * width : (s + 1) * width]


def produce(out, rows, weight, deep):
    width = weight.shape[0]
    cz = weight.shape[1] // width
    chunk = min(2 * PRODUCED, rows.shape[0]) // deep

    def section(step, _):
        taken = rows[lanes_at(step * chunk * deep, chunk * deep), :].astype(BF16)
        for n in range(width // 2):
            made = dot(taken, weight[:, n * 2 * cz : (n + 1) * 2 * cz])
            for i in range(chunk):
                both = jnp.concatenate(
                    [made[i * deep : (i + 1) * deep, a * cz : (a + 1) * cz] for a in range(2)], axis=0
                )
                low = n * 2 * deep
                out[low : low + 2 * deep, lanes_at((step * chunk + i) * cz, cz)] = both.astype(BF16)
        return 0

    lax.fori_loop(0, rows.shape[0] // (chunk * deep), section, 0)


def v_kernel(stack, swap, weight, *refs):
    right_cols, v_ref, rows = refs[-3:]
    count, _, both = stack.shape
    width = weight.shape[0]
    deep = swap.shape[0] // width
    for n in range(count):
        spread_rows(rows, n, stack[n, :, both // 2 :], width, deep)
    right = jnp.concatenate([stack[n, :, both // 2 :] for n in range(count)], axis=1)
    right_cols[...] = dot_t(right, swap[...]).astype(BF16)
    produce(v_ref, rows, weight, deep)


def t_kernel(part, own, got, weight, *refs):
    t_ref, rows = refs[-2:]
    row_at, column_at = place()
    count = own.shape[0] // 2
    width = weight.shape[0]
    deep = t_ref.shape[0] // width
    other = (row_at ^ column_at) & 1
    for n in range(count):
        k = part * count + n
        block = jnp.where(other == 1, got[k].astype(F32), own[k].astype(F32))
        spread_rows(rows, n, block, width, deep)
    produce(t_ref, rows, weight, deep)


def ungroup(out, acc, swap):
    half = out.shape[2]
    made = dot(acc.astype(BF16), swap[...]).astype(BF16)
    for k in range(out.shape[0]):
        out[k] = made[:, k * half : (k + 1) * half]


def gradient_kernel(grouped, full_ref, side, swap, *refs):
    out = refs[-1]
    span = swap.shape[0]
    size = side.shape[1] * PRODUCED // span

    def section(step, acc):
        lanes = lanes_at(step * size, size)
        return acc + dot_t(full_ref[:, lanes], side[:, lanes])

    acc = dot_t(full_ref[:, :size], side[:, :size])
    acc = lax.fori_loop(1, span // PRODUCED, section, acc)
    if grouped:
        out[...] = jnp.transpose(acc).astype(BF16)
    else:
        ungroup(out, jnp.transpose(acc), swap)


def join_kernel(part, right, own, got, out):
    row_at, column_at = place()
    mine = jnp.where(row_at == column_at, 1.0, 0.0)
    count, _, both = out.shape
    half = both // 2
    for n in range(count):
        k = part * count + n
        out[n, :, :half] = ((own[k].astype(F32) + got[k].astype(F32)) * mine).astype(BF16)
        out[n, :, half:] = right[:, n * half : (n + 1) * half]


def halve_kernel(grouped, own, got, swap, *refs):
    keep, send = refs[-2:]
    count, _, both = keep.shape
    half = both // 2
    total = [(own[n].astype(F32) + got[n].astype(F32)).astype(BF16) for n in range(2 * count)]
    if grouped:
        right = dot(jnp.concatenate([part[:, half:] for part in total], axis=1), swap[...]).astype(BF16)
    for n in range(2 * count):
        out, k = (keep, n) if n < count else (send, n - count)
        out[k, :, :half] = total[n][:, :half]
        out[k, :, half:] = right[:, n * half : (n + 1) * half] if grouped else total[n][:, half:]


def rows_of_pass(span):
    return max(2, 8 * PRODUCED // span)


def pair_rows(out_ref, first, start, count, low_cols, high_cols, t_low, t_high, shift_ref, inverse_ref, row_ref):
    cz = out_ref.shape[2]
    group = min(4, count)
    for n in range(0, count, group):
        lanes = lanes_at((first + start + n) * cz, group * cz)
        made = dot(low_cols[...], t_low[:, lanes]) + dot(high_cols[...], t_high[:, lanes])
        for a in range(group):
            i = start + n + a
            factor = jnp.where(row_ref[pl.ds(first + i, 1), :] > 0.0, inverse_ref[...], 1.0)
            out_ref[i] = ((made[:, a * cz : (a + 1) * cz] + shift_ref[:1, :]) * factor).astype(BF16)


def upper_pair_kernel(*refs):
    sources, (out_ref, done_ref) = refs[:7], refs[-2:]
    step_rows = rows_of_pass(sources[0].shape[1])
    done_ref[...] = jnp.zeros_like(done_ref)

    def section(step, _):
        pair_rows(out_ref, 0, step * step_rows, step_rows, *sources)
        return 0

    lax.fori_loop(0, out_ref.shape[0] // step_rows, section, 0)


def lower_pair_kernel(*refs):
    sources, upper, (pair_ref, last_ref, held, sems) = refs[:7], refs[7], refs[-4:]
    step_rows = rows_of_pass(sources[0].shape[1])
    first = upper.shape[0]
    steps = held.shape[0] // step_rows

    def copy(step):
        spot = pl.ds(step * step_rows, step_rows)
        return pltpu.make_async_copy(
            held.at[spot], pair_ref.at[pl.ds(first + step * step_rows, step_rows)], sems.at[1 + step]
        )

    above = pltpu.make_async_copy(upper, pair_ref.at[:first], sems.at[0])
    above.start()

    def section(step, _):
        pair_rows(held, first, step * step_rows, step_rows, *sources)
        copy(step).start()
        return 0

    def last_section(step, _):
        pair_rows(last_ref, first + held.shape[0], step * step_rows, step_rows, *sources)
        return 0

    lax.fori_loop(0, steps, section, 0)
    lax.fori_loop(0, last_ref.shape[0] // step_rows, last_section, 0)
    above.wait()
    for step in range(steps):
        copy(step).wait()


def finish_kernel(own, got, mask_ref, factors, gain_ref, hat_ref, spread_ref, last, *refs):
    pair_ref, out_ref, held, sems = refs[-4:]
    rest = pair_ref.at[pl.ds(pair_ref.shape[0] - last.shape[0], last.shape[0])]
    seqs, length, channels = hat_ref.shape
    copies = [pltpu.make_async_copy(last, rest, sems.at[seqs])]
    copies[0].start()
    both = (own[0].astype(F32) + got[0].astype(F32)) * mask_ref[...]
    half = both.shape[1] // 2
    which = lax.broadcasted_iota(jnp.int32, (1, 2 * half), 1) % half // (half // seqs)
    rows = [jnp.where(which == s, both, 0.0).astype(BF16) for s in range(seqs)]
    grads = dot(jnp.concatenate(rows, axis=0), factors[...])
    gain = gain_ref[:1, :]
    for s in range(seqs):
        hat = hat_ref[s]
        spread = jnp.concatenate([spread_ref[s]] * (channels // spread_ref.shape[2]), axis=1)
        grad = grads[s * length : (s + 1) * length] * gain
        held[s] = (
            spread
            * (
                grad
                - jnp.mean(grad, axis=-1, keepdims=True)
                - hat * jnp.mean(grad * hat, axis=-1, keepdims=True)
            )
        ).astype(BF16)
        copies.append(pltpu.make_async_copy(held.at[s], out_ref.at[s], sems.at[s]))
        copies[-1].start()
    for copy in copies:
        copy.wait()


VMEM = pl.BlockSpec(memory_space=pltpu.VMEM)
HBM = pl.BlockSpec(memory_space=pltpu.HBM)


def call(kernel, name, out_shape, scratch, micros, in_specs=None, out_specs=None, limit=24, aliases=None, after=()):
    def run(*args):
        specs = [VMEM] * len(args) if in_specs is None else in_specs
        specs, args = specs + [pl.BlockSpec(memory_space=pl.ANY)] * len(after), args + tuple(after)
        outs = jax.tree.map(lambda _: VMEM, out_shape) if out_specs is None else out_specs
        return pl.pallas_call(
            kernel,
            out_shape=out_shape,
            in_specs=specs,
            out_specs=outs,
            scratch_shapes=scratch,
            input_output_aliases=aliases or {},
            compiler_params=pltpu.CompilerParams(vmem_limit_bytes=limit * 1024 * 1024),
            cost_estimate=pl.CostEstimate(flops=int(micros * 1e8), bytes_accessed=0, transcendentals=0),
            name=name,
        )(*args)

    return run


def swap_rows(x, blocks, bit):
    moves = [(z * blocks + c, (z ^ bit) * blocks + c) for z in range(blocks) for c in range(blocks)]
    return lax.ppermute(x, PLACES, moves)


def swap_columns(x, blocks, bit):
    moves = [
        (z * blocks + c, z * blocks + (c ^ bit))
        for z in range(blocks)
        for c in range(blocks)
        if (z ^ c) & (bit - 1) == 0
    ]
    return lax.ppermute(x, PLACES, moves)


def per_device(
    homolog_activations,
    homolog_valid_flags,
    position_valid_flags,
    centering_factor,
    centering_shift,
    first_factor_matrix,
    second_factor_matrix,
    couple_weight_matrix,
    couple_shift_vector,
    loss_sensitivity,
):
    seqs, length, channels = homolog_activations.shape
    total_seq = homolog_valid_flags.shape[0]
    total_res = position_valid_flags.shape[0]
    width = first_factor_matrix.shape[1]
    rows, columns, cz = loss_sensitivity.shape
    blocks = lax.axis_size("cols") * lax.axis_size("sub")
    steps = blocks.bit_length() - 1
    assert blocks == 1 << steps == lax.axis_size("rows") and steps > 1
    half = seqs * width
    deep = total_seq // 2
    span = deep * width
    shape = jax.ShapeDtypeStruct

    def far(x):
        return pltpu.with_memory_space_constraint(x, pltpu.HBM)

    seq_flags, res_flags = far(homolog_valid_flags), far(position_valid_flags)

    stack, factors, mask, hat, spread, gain, loss, weights = call(
        project_kernel,
        "project",
        (
            shape((1, length, 2 * half), BF16),
            shape((2 * half, channels), BF16),
            shape((length, 2 * half), F32),
            shape((seqs, length, channels), F32),
            shape((seqs, length, cz), F32),
            shape((8, channels), F32),
            shape(loss_sensitivity.shape, BF16),
            shape(couple_weight_matrix.shape, BF16),
        ),
        [
            pltpu.VMEM((total_seq,), jnp.int32),
            pltpu.VMEM((seqs, length, channels), BF16),
            pltpu.VMEM((total_res,), jnp.int32),
            pltpu.VMEM((channels,), F32),
            pltpu.VMEM((channels,), F32),
            pltpu.VMEM((width, channels), BF16),
            pltpu.VMEM((width, channels), BF16),
            pltpu.SemaphoreType.DMA((9,)),
        ],
        2,
        in_specs=[HBM] * 9,
    )(
        seq_flags,
        far(homolog_activations),
        res_flags,
        far(centering_factor),
        far(centering_shift),
        far(first_factor_matrix.T),
        far(second_factor_matrix.T),
        far(couple_weight_matrix),
        far(loss_sensitivity),
    )

    by_left, by_right, swap, scaled, turned, inverse, row_flags, shift = call(
        prepare_kernel,
        "prepare",
        (
            shape((width, width * cz), BF16),
            shape((width, width * cz), BF16),
            shape((span, span), BF16),
            shape((columns, rows * cz), BF16),
            shape((rows, columns * cz), BF16),
            shape((columns, cz), F32),
            shape((rows, cz), F32),
            shape((8, cz), F32),
        ),
        [
            pltpu.VMEM((total_seq,), jnp.int32),
            pltpu.VMEM((total_res,), jnp.int32),
            pltpu.VMEM((cz,), F32),
            pltpu.VMEM((width * width, cz), F32),
            pltpu.SemaphoreType.DMA((3,)),
        ],
        3,
        in_specs=[HBM] * 3 + [VMEM] * 2,
    )(seq_flags, res_flags, far(couple_shift_vector), loss, weights)

    for step in range(steps):
        got = swap_rows(stack, blocks, blocks >> (step + 1))
        if step < steps - 1:
            stack = call(
                stack_kernel, "stack", shape((2 << step, length, 2 * half), BF16), [], 0.1, after=(shift,)
            )(stack, got)
    low_stack, high_stack = stack, got

    half_blocks = shape((blocks // 2, length, half), BF16)
    all_blocks = shape((blocks, length, half), BF16)
    cols_shape = shape((columns, span), BF16)
    t_limit = 16 + 2 * span * rows * cz * 2 // 2**20

    def make_v(stack, *after):
        return call(
            v_kernel,
            "expand_right",
            (cols_shape, shape((span, columns * cz), BF16)),
            [pltpu.VMEM((columns * deep, width), F32)],
            1.3,
            limit=t_limit,
            after=after,
        )(stack, swap, by_right)

    def gradient(full, side, grouped, *after):
        return call(
            functools.partial(gradient_kernel, grouped),
            "gradient",
            cols_shape if grouped else half_blocks,
            [],
            1.5,
            limit=t_limit,
            after=after,
        )(full, side, swap)

    low_cols, v_low = make_v(low_stack)
    low_sum = gradient(v_low, turned, False)
    lefts = call(lefts_kernel, "lefts", all_blocks, [], 0.1, after=(low_sum,))(low_stack, high_stack)
    got = swap_columns(lefts, blocks, blocks // 2)
    high_cols, v_high = make_v(high_stack, lefts)
    high_sum = gradient(v_high, turned, False)
    for step in range(1, steps):
        lefts = call(
            functools.partial(select_kernel, blocks >> step), "select", all_blocks, [], 0.1, after=(high_sum,)
        )(lefts, got)
        got = swap_columns(lefts, blocks, blocks >> (step + 1))
    got_lefts = got
    sums = call(stack_kernel, "stack", all_blocks, [], 0.1)(low_sum, high_sum)

    def make_t(part, *after):
        return call(
            functools.partial(t_kernel, part),
            "expand_left",
            shape((span, rows * cz), BF16),
            [pltpu.VMEM((rows * deep, width), F32)],
            1.2,
            limit=t_limit,
            after=after,
        )(lefts, got_lefts, by_left)

    def make_t(part, *after):
        return call(
            functools.partial(t_kernel, part),
            "expand_left",
            shape((span, rows * cz), BF16),
            [pltpu.VMEM((rows * deep, width), F32)],
            1.3,
            limit=t_limit,
            after=after,
        )(lefts, got_lefts, by_left)

    for step in range(steps - 1):
        got = swap_columns(sums, blocks, 1 << step)
        sums = call(add_kernel, "add", all_blocks, [], 0.1)(sums, got)
    got = swap_columns(sums, blocks, 1 << (steps - 1))
    t_high = make_t(1, sums)

    def join(part, right):
        return call(
            functools.partial(join_kernel, part),
            "join",
            shape((blocks // 2, length, 2 * half), BF16),
            [],
            0.1,
        )(right, sums, got)

    send = join(1, gradient(t_high, scaled, True, sums))
    got_send = swap_rows(send, blocks, 1)
    t_low = make_t(0, send)
    keep = join(0, gradient(t_low, scaled, True, send))

    pair_sources = (low_cols, high_cols, t_low, t_high, shift, inverse, row_flags)
    upper_rows = rows // 4
    upper, paired = call(
        upper_pair_kernel,
        "pair",
        (shape((upper_rows, columns, cz), BF16), shape((8, cz), F32)),
        [],
        1,
        limit=t_limit,
        after=(keep,),
    )(*pair_sources)
    for step in range(1, steps):
        some = shape((blocks >> (step + 1), length, 2 * half), BF16)
        keep, send = call(
            functools.partial(halve_kernel, step == 1), "halve", (some, some), [], 0.1, after=(paired,)
        )(keep, got_send, swap)
        got_send = swap_rows(send, blocks, 1 << step)
    last_rows = 2 * rows_of_pass(span)
    held_rows = rows - upper_rows - last_rows
    pair, last = call(
        lower_pair_kernel,
        "pair",
        (shape(loss_sensitivity.shape, BF16), shape((last_rows, columns, cz), BF16)),
        [
            pltpu.VMEM((held_rows, columns, cz), BF16),
            pltpu.SemaphoreType.DMA((1 + held_rows // rows_of_pass(span),)),
        ],
        2,
        out_specs=(HBM, VMEM),
        limit=t_limit,
        after=(send,),
    )(*pair_sources, upper)

    return call(
        finish_kernel,
        "finish",
        (shape(loss_sensitivity.shape, BF16), shape(homolog_activations.shape, BF16)),
        [pltpu.VMEM(homolog_activations.shape, BF16), pltpu.SemaphoreType.DMA((seqs + 1,))],
        1,
        in_specs=[VMEM] * 8 + [HBM],
        out_specs=(HBM, HBM),
        aliases={8: 0},
    )(keep, got_send, mask, factors, gain, hat, spread, last, pair)


def solution(mesh):
    split = P(("groups", "rows"), ("cols", "sub"), None)
    return jax.shard_map(
        per_device,
        mesh=mesh,
        in_specs=(split, P("groups"), P("groups"), P(), P(), P(), P(), P(), P(), split),
        out_specs=(split, split),
        check_vma=False,
    )
```

```python
import functools

import jax
import jax.numpy as jnp
from jax import lax
from jax.experimental import pallas as pl
from jax.experimental.pallas import tpu as pltpu
from jax.sharding import PartitionSpec as P

F32 = jnp.float32
BF16 = jnp.bfloat16
PLACES = ("rows", "cols", "sub")
PRODUCED = 256
TILE = 16


def dot(a, b):
    return lax.dot_general(a, b, (((1,), (0,)), ((), ())), preferred_element_type=F32)


def dot_t(a, b):
    return lax.dot_general(a, b, (((1,), (1,)), ((), ())), preferred_element_type=F32)


def place():
    column = lax.axis_index("cols") * lax.axis_size("sub") + lax.axis_index("sub")
    return lax.axis_index("rows"), column


def lanes_at(start, size):
    return pl.ds(pl.multiple_of(start, size), size)


def flag_row(flags_ref):
    return flags_ref[...].astype(F32).reshape(1, -1)


def flag_column(flags_ref, start, length):
    flags = flag_row(flags_ref)
    total = flags.shape[1]
    spot = lax.broadcasted_iota(jnp.int32, (length, total), 0) + start
    lane = lax.broadcasted_iota(jnp.int32, (length, total), 1)
    return jnp.sum(jnp.where(spot == lane, flags, 0.0), axis=1, keepdims=True)


def load_all(pairs, sems):
    copies = [pltpu.make_async_copy(src, dst, sems.at[n]) for n, (src, dst) in enumerate(pairs)]
    for copy in copies:
        copy.start()
    return copies


def project_kernel(*refs):
    sources, outs, (loss_ref, w_ref), held, sems = refs[:9], refs[9:15], refs[15:17], refs[17:24], refs[24]
    out_ref, factors, mask_ref, hat_ref, spread_ref, gain_out = outs
    copies = load_all(list(zip(sources, held + (w_ref, loss_ref))), sems)
    seq_ref, x_ref, res_ref, gain_ref, bias_ref, first_ref, second_ref = held
    row_at, column_at = place()
    seqs, length, channels = x_ref.shape
    width = first_ref.shape[0]
    half = seqs * width
    for copy in copies[:7]:
        copy.wait()
    for s in range(seqs):
        factors[s * width : (s + 1) * width, :] = first_ref[...]
        factors[(seqs + s) * width : (seqs + s + 1) * width, :] = second_ref[...]
    flags = flag_row(seq_ref)
    spot = lax.broadcasted_iota(jnp.int32, flags.shape, 1)
    which = lax.broadcasted_iota(jnp.int32, (1, 2 * half), 1) % half // width
    own = jnp.zeros((1, 2 * half), F32)
    for s in range(seqs):
        value = jnp.sum(jnp.where(spot == row_at * seqs + s, flags, 0.0), axis=1, keepdims=True)
        own = jnp.where(which == s, value, own)
    mask = flag_column(res_ref, column_at * length, length) * own
    mask_ref[...] = mask
    gain = gain_ref[...].reshape(1, channels)
    bias = bias_ref[...].reshape(1, channels)
    gain_out[...] = jnp.broadcast_to(gain, gain_out.shape)
    normed = []
    for s in range(seqs):
        x = x_ref[s].astype(F32)
        off = x - jnp.mean(x, axis=-1, keepdims=True)
        spread = lax.rsqrt(jnp.mean(off * off, axis=-1, keepdims=True) + 1e-05)
        hat = off * spread
        hat_ref[s] = hat
        spread_ref[s] = jnp.broadcast_to(spread, spread_ref.shape[1:])
        normed.append((hat * gain + bias).astype(BF16))
    made = dot_t(jnp.concatenate(normed, axis=0), factors[...])
    total = made[:length]
    for s in range(1, seqs):
        total = jnp.where(which == s, made[s * length : (s + 1) * length], total)
    out_ref[0] = (total * mask).astype(BF16)
    for copy in copies[7:]:
        copy.wait()


def prepare_kernel(*refs):
    sources, (loss_ref, w_ref), outs, held, (wide_w, sems) = (
        refs[:3],
        refs[3:5],
        refs[5:13],
        refs[13:16],
        refs[16:],
    )
    by_left, by_right, swap, scaled, turned, inverse_ref, row_ref, shift_out = outs
    seq_ref, res_ref, shift_ref = held
    copies = load_all(list(zip(sources, held)), sems)
    row_at, column_at = place()
    rows, length, cz = loss_ref.shape
    width = by_left.shape[0]
    span = swap.shape[0]
    deep = span // width
    wide_w[...] = w_ref[...].astype(F32)
    for n in range(width):
        by_left[:, n * cz : (n + 1) * cz] = wide_w[pl.ds(n, width, stride=width), :].astype(BF16)
        by_right[:, n * cz : (n + 1) * cz] = w_ref[n * width : (n + 1) * width, :]
    to = lax.broadcasted_iota(jnp.int32, (span, span), 0)
    at = lax.broadcasted_iota(jnp.int32, (span, span), 1)
    swap[...] = jnp.where((to // deep == at % width) & (to % deep == at // width), 1.0, 0.0).astype(BF16)
    for copy in copies:
        copy.wait()
    present = jnp.sum(flag_row(seq_ref), axis=1, keepdims=True)
    columns = flag_column(res_ref, column_at * length, length)
    inverse = jnp.broadcast_to(1.0 / jnp.maximum(present * columns, 1.0), (length, cz))
    inverse_ref[...] = inverse
    row_ref[...] = jnp.broadcast_to(flag_column(res_ref, row_at * rows, rows), (rows, cz))
    shift_out[...] = jnp.broadcast_to(shift_ref[...].reshape(1, cz), shift_out.shape)
    for i in range(rows):
        factor = jnp.where(row_ref[i : i + 1, :] > 0.0, inverse, 1.0)
        scaled[:, i * cz : (i + 1) * cz] = (loss_ref[i].astype(F32) * factor).astype(BF16)
    to = lax.broadcasted_iota(jnp.int32, (TILE * TILE, TILE * TILE), 0)
    at = lax.broadcasted_iota(jnp.int32, (TILE * TILE, TILE * TILE), 1)
    turn = jnp.where((to // TILE == at % TILE) & (to % TILE == at // TILE), 1.0, 0.0).astype(BF16)
    for i in range(0, rows, TILE):
        for j in range(0, length, 2 * TILE):
            taken = [
                jnp.concatenate(
                    [scaled[b : b + TILE, (i + k) * cz : (i + k + 1) * cz] for k in range(TILE)], axis=0
                )
                for b in (j, j + TILE)
            ]
            made = dot(turn, jnp.concatenate(taken, axis=1)).astype(BF16)
            for a in range(2):
                for k in range(TILE):
                    low = (j + a * TILE + k) * cz
                    turned[i : i + TILE, low : low + cz] = made[
                        k * TILE : (k + 1) * TILE, a * cz : (a + 1) * cz
                    ]


def stack_kernel(own, got, *refs):
    out = refs[-1]
    count = own.shape[0]
    out[:count] = own[...]
    out[count:] = got[...]


def lefts_kernel(own, got, *refs):
    out = refs[-1]
    count, _, half = out.shape
    for n in range(count // 2):
        out[n] = own[n, :, :half]
        out[count // 2 + n] = got[n, :, :half]


def select_kernel(bit, own, got, *refs):
    out = refs[-1]
    row_at, column_at = place()
    other = jnp.where((row_at ^ column_at) & (2 * bit - 1) == bit, 1, 0)

    @pl.when(other == 1)
    def _():
        out[...] = got[...]

    @pl.when(other == 0)
    def _():
        out[...] = own[...]


def add_kernel(own, got, *refs):
    out = refs[-1]
    out[...] = (own[...].astype(F32) + got[...].astype(F32)).astype(BF16)


def spread_rows(rows, n, block, width, deep):
    length, half = block.shape
    seqs = half // width
    wide = block.astype(F32)
    for s in range(seqs):
        rows[pl.ds(n * seqs + s, length, stride=deep), :] = wide[:, s * width : (s + 1) * width]


def produce(out, rows, weight, deep):
    width = weight.shape[0]
    cz = weight.shape[1] // width
    chunk = min(2 * PRODUCED, rows.shape[0]) // deep

    def section(step, _):
        taken = rows[lanes_at(step * chunk * deep, chunk * deep), :].astype(BF16)
        for n in range(width // 2):
            made = dot(taken, weight[:, n * 2 * cz : (n + 1) * 2 * cz])
            for i in range(chunk):
                both = jnp.concatenate(
                    [made[i * deep : (i + 1) * deep, a * cz : (a + 1) * cz] for a in range(2)], axis=0
                )
                low = n * 2 * deep
                out[low : low + 2 * deep, lanes_at((step * chunk + i) * cz, cz)] = both.astype(BF16)
        return 0

    lax.fori_loop(0, rows.shape[0] // (chunk * deep), section, 0)


def v_kernel(stack, swap, weight, *refs):
    right_cols, v_ref, rows = refs[-3:]
    count, _, both = stack.shape
    width = weight.shape[0]
    deep = swap.shape[0] // width
    for n in range(count):
        spread_rows(rows, n, stack[n, :, both // 2 :], width, deep)
    right = jnp.concatenate([stack[n, :, both // 2 :] for n in range(count)], axis=1)
    right_cols[...] = dot_t(right, swap[...]).astype(BF16)
    produce(v_ref, rows, weight, deep)


def t_kernel(part, own, got, weight, *refs):
    t_ref, rows = refs[-2:]
    row_at, column_at = place()
    count = own.shape[0] // 2
    width = weight.shape[0]
    deep = t_ref.shape[0] // width
    other = (row_at ^ column_at) & 1
    for n in range(count):
        k = part * count + n
        block = jnp.where(other == 1, got[k].astype(F32), own[k].astype(F32))
        spread_rows(rows, n, block, width, deep)
    produce(t_ref, rows, weight, deep)


def ungroup(out, acc, swap):
    half = out.shape[2]
    made = dot(acc.astype(BF16), swap[...]).astype(BF16)
    for k in range(out.shape[0]):
        out[k] = made[:, k * half : (k + 1) * half]


def gradient_kernel(grouped, full_ref, side, swap, *refs):
    out = refs[-1]
    span = swap.shape[0]
    size = side.shape[1] * PRODUCED // span

    def section(step, acc):
        lanes = lanes_at(step * size, size)
        return acc + dot_t(full_ref[:, lanes], side[:, lanes])

    acc = dot_t(full_ref[:, :size], side[:, :size])
    acc = lax.fori_loop(1, span // PRODUCED, section, acc)
    if grouped:
        out[...] = jnp.transpose(acc).astype(BF16)
    else:
        ungroup(out, jnp.transpose(acc), swap)


def join_kernel(part, right, own, got, out):
    row_at, column_at = place()
    mine = jnp.where(row_at == column_at, 1.0, 0.0)
    count, _, both = out.shape
    half = both // 2
    for n in range(count):
        k = part * count + n
        out[n, :, :half] = ((own[k].astype(F32) + got[k].astype(F32)) * mine).astype(BF16)
        out[n, :, half:] = right[:, n * half : (n + 1) * half]


def halve_kernel(grouped, own, got, swap, *refs):
    keep, send = refs[-2:]
    count, _, both = keep.shape
    half = both // 2
    total = [(own[n].astype(F32) + got[n].astype(F32)).astype(BF16) for n in range(2 * count)]
    if grouped:
        right = dot(jnp.concatenate([part[:, half:] for part in total], axis=1), swap[...]).astype(BF16)
    for n in range(2 * count):
        out, k = (keep, n) if n < count else (send, n - count)
        out[k, :, :half] = total[n][:, :half]
        out[k, :, half:] = right[:, n * half : (n + 1) * half] if grouped else total[n][:, half:]


def rows_of_pass(span):
    return max(2, 8 * PRODUCED // span)


def pair_rows(out_ref, first, start, count, low_cols, high_cols, t_low, t_high, shift_ref, inverse_ref, row_ref):
    cz = out_ref.shape[2]
    group = min(4, count)
    for n in range(0, count, group):
        lanes = lanes_at((first + start + n) * cz, group * cz)
        made = dot(low_cols[...], t_low[:, lanes]) + dot(high_cols[...], t_high[:, lanes])
        for a in range(group):
            i = start + n + a
            factor = jnp.where(row_ref[pl.ds(first + i, 1), :] > 0.0, inverse_ref[...], 1.0)
            out_ref[i] = ((made[:, a * cz : (a + 1) * cz] + shift_ref[:1, :]) * factor).astype(BF16)


def upper_pair_kernel(*refs):
    sources, (out_ref, done_ref) = refs[:7], refs[-2:]
    step_rows = rows_of_pass(sources[0].shape[1])
    done_ref[...] = jnp.zeros_like(done_ref)

    def section(step, _):
        pair_rows(out_ref, 0, step * step_rows, step_rows, *sources)
        return 0

    lax.fori_loop(0, out_ref.shape[0] // step_rows, section, 0)


def lower_pair_kernel(*refs):
    sources, upper, (pair_ref, last_ref, held, sems) = refs[:7], refs[7], refs[-4:]
    step_rows = rows_of_pass(sources[0].shape[1])
    first = upper.shape[0]
    steps = held.shape[0] // step_rows

    def copy(step):
        spot = pl.ds(step * step_rows, step_rows)
        return pltpu.make_async_copy(
            held.at[spot], pair_ref.at[pl.ds(first + step * step_rows, step_rows)], sems.at[1 + step]
        )

    above = pltpu.make_async_copy(upper, pair_ref.at[:first], sems.at[0])
    above.start()

    def section(step, _):
        pair_rows(held, first, step * step_rows, step_rows, *sources)
        copy(step).start()
        return 0

    def last_section(step, _):
        pair_rows(last_ref, first + held.shape[0], step * step_rows, step_rows, *sources)
        return 0

    lax.fori_loop(0, steps, section, 0)
    lax.fori_loop(0, last_ref.shape[0] // step_rows, last_section, 0)
    above.wait()
    for step in range(steps):
        copy(step).wait()


def finish_kernel(own, got, mask_ref, factors, gain_ref, hat_ref, spread_ref, last, *refs):
    pair_ref, out_ref, held, sems = refs[-4:]
    rest = pair_ref.at[pl.ds(pair_ref.shape[0] - last.shape[0], last.shape[0])]
    seqs, length, channels = hat_ref.shape
    copies = [pltpu.make_async_copy(last, rest, sems.at[seqs])]
    copies[0].start()
    both = (own[0].astype(F32) + got[0].astype(F32)) * mask_ref[...]
    half = both.shape[1] // 2
    which = lax.broadcasted_iota(jnp.int32, (1, 2 * half), 1) % half // (half // seqs)
    rows = [jnp.where(which == s, both, 0.0).astype(BF16) for s in range(seqs)]
    grads = dot(jnp.concatenate(rows, axis=0), factors[...])
    gain = gain_ref[:1, :]
    for s in range(seqs):
        hat = hat_ref[s]
        spread = jnp.concatenate([spread_ref[s]] * (channels // spread_ref.shape[2]), axis=1)
        grad = grads[s * length : (s + 1) * length] * gain
        held[s] = (
            spread
            * (
                grad
                - jnp.mean(grad, axis=-1, keepdims=True)
                - hat * jnp.mean(grad * hat, axis=-1, keepdims=True)
            )
        ).astype(BF16)
        copies.append(pltpu.make_async_copy(held.at[s], out_ref.at[s], sems.at[s]))
        copies[-1].start()
    for copy in copies:
        copy.wait()


VMEM = pl.BlockSpec(memory_space=pltpu.VMEM)
HBM = pl.BlockSpec(memory_space=pltpu.HBM)


def call(kernel, name, out_shape, scratch, micros, in_specs=None, out_specs=None, limit=24, aliases=None, after=()):
    def run(*args):
        specs = [VMEM] * len(args) if in_specs is None else in_specs
        specs, args = specs + [pl.BlockSpec(memory_space=pl.ANY)] * len(after), args + tuple(after)
        outs = jax.tree.map(lambda _: VMEM, out_shape) if out_specs is None else out_specs
        return pl.pallas_call(
            kernel,
            out_shape=out_shape,
            in_specs=specs,
            out_specs=outs,
            scratch_shapes=scratch,
            input_output_aliases=aliases or {},
            compiler_params=pltpu.CompilerParams(vmem_limit_bytes=limit * 1024 * 1024),
            cost_estimate=pl.CostEstimate(flops=int(micros * 1e8), bytes_accessed=0, transcendentals=0),
            name=name,
        )(*args)

    return run


def swap_rows(x, blocks, bit):
    moves = [(z * blocks + c, (z ^ bit) * blocks + c) for z in range(blocks) for c in range(blocks)]
    return lax.ppermute(x, PLACES, moves)


def swap_columns(x, blocks, bit):
    moves = [
        (z * blocks + c, z * blocks + (c if (z ^ c) & (bit - 1) else c ^ bit))
        for z in range(blocks)
        for c in range(blocks)
    ]
    return lax.ppermute(x, PLACES, moves)


def per_device(
    homolog_activations,
    homolog_valid_flags,
    position_valid_flags,
    centering_factor,
    centering_shift,
    first_factor_matrix,
    second_factor_matrix,
    couple_weight_matrix,
    couple_shift_vector,
    loss_sensitivity,
):
    seqs, length, channels = homolog_activations.shape
    total_seq = homolog_valid_flags.shape[0]
    total_res = position_valid_flags.shape[0]
    width = first_factor_matrix.shape[1]
    rows, columns, cz = loss_sensitivity.shape
    blocks = lax.axis_size("cols") * lax.axis_size("sub")
    steps = blocks.bit_length() - 1
    assert blocks == 1 << steps == lax.axis_size("rows") and steps > 1
    half = seqs * width
    deep = total_seq // 2
    span = deep * width
    shape = jax.ShapeDtypeStruct

    def far(x):
        return pltpu.with_memory_space_constraint(x, pltpu.HBM)

    seq_flags, res_flags = far(homolog_valid_flags), far(position_valid_flags)

    stack, factors, mask, hat, spread, gain, loss, weights = call(
        project_kernel,
        "project",
        (
            shape((1, length, 2 * half), BF16),
            shape((2 * half, channels), BF16),
            shape((length, 2 * half), F32),
            shape((seqs, length, channels), F32),
            shape((seqs, length, cz), F32),
            shape((8, channels), F32),
            shape(loss_sensitivity.shape, BF16),
            shape(couple_weight_matrix.shape, BF16),
        ),
        [
            pltpu.VMEM((total_seq,), jnp.int32),
            pltpu.VMEM((seqs, length, channels), BF16),
            pltpu.VMEM((total_res,), jnp.int32),
            pltpu.VMEM((channels,), F32),
            pltpu.VMEM((channels,), F32),
            pltpu.VMEM((width, channels), BF16),
            pltpu.VMEM((width, channels), BF16),
            pltpu.SemaphoreType.DMA((9,)),
        ],
        2,
        in_specs=[HBM] * 9,
    )(
        seq_flags,
        far(homolog_activations),
        res_flags,
        far(centering_factor),
        far(centering_shift),
        far(first_factor_matrix.T),
        far(second_factor_matrix.T),
        far(couple_weight_matrix),
        far(loss_sensitivity),
    )

    by_left, by_right, swap, scaled, turned, inverse, row_flags, shift = call(
        prepare_kernel,
        "prepare",
        (
            shape((width, width * cz), BF16),
            shape((width, width * cz), BF16),
            shape((span, span), BF16),
            shape((columns, rows * cz), BF16),
            shape((rows, columns * cz), BF16),
            shape((columns, cz), F32),
            shape((rows, cz), F32),
            shape((8, cz), F32),
        ),
        [
            pltpu.VMEM((total_seq,), jnp.int32),
            pltpu.VMEM((total_res,), jnp.int32),
            pltpu.VMEM((cz,), F32),
            pltpu.VMEM((width * width, cz), F32),
            pltpu.SemaphoreType.DMA((3,)),
        ],
        3,
        in_specs=[HBM] * 3 + [VMEM] * 2,
    )(seq_flags, res_flags, far(couple_shift_vector), loss, weights)

    for step in range(steps):
        got = swap_rows(stack, blocks, blocks >> (step + 1))
        if step < steps - 1:
            stack = call(
                stack_kernel, "stack", shape((2 << step, length, 2 * half), BF16), [], 0.1, after=(shift,)
            )(stack, got)
    low_stack, high_stack = stack, got

    half_blocks = shape((blocks // 2, length, half), BF16)
    all_blocks = shape((blocks, length, half), BF16)
    cols_shape = shape((columns, span), BF16)
    t_limit = 16 + 2 * span * rows * cz * 2 // 2**20

    def make_v(stack, *after):
        return call(
            v_kernel,
            "expand_right",
            (cols_shape, shape((span, columns * cz), BF16)),
            [pltpu.VMEM((columns * deep, width), F32)],
            1.3,
            limit=t_limit,
            after=after,
        )(stack, swap, by_right)

    def gradient(full, side, grouped, *after):
        return call(
            functools.partial(gradient_kernel, grouped),
            "gradient",
            cols_shape if grouped else half_blocks,
            [],
            1.5,
            limit=t_limit,
            after=after,
        )(full, side, swap)

    low_cols, v_low = make_v(low_stack)
    low_sum = gradient(v_low, turned, False)
    lefts = call(lefts_kernel, "lefts", all_blocks, [], 0.1, after=(low_sum,))(low_stack, high_stack)
    got = swap_columns(lefts, blocks, blocks // 2)
    high_cols, v_high = make_v(high_stack, lefts)
    high_sum = gradient(v_high, turned, False)
    for step in range(1, steps):
        lefts = call(
            functools.partial(select_kernel, blocks >> step), "select", all_blocks, [], 0.1, after=(high_sum,)
        )(lefts, got)
        got = swap_columns(lefts, blocks, blocks >> (step + 1))
    got_lefts = got
    sums = call(stack_kernel, "stack", all_blocks, [], 0.1)(low_sum, high_sum)

    def make_t(part, *after):
        return call(
            functools.partial(t_kernel, part),
            "expand_left",
            shape((span, rows * cz), BF16),
            [pltpu.VMEM((rows * deep, width), F32)],
            1.2,
            limit=t_limit,
            after=after,
        )(lefts, got_lefts, by_left)

    def make_t(part, *after):
        return call(
            functools.partial(t_kernel, part),
            "expand_left",
            shape((span, rows * cz), BF16),
            [pltpu.VMEM((rows * deep, width), F32)],
            1.3,
            limit=t_limit,
            after=after,
        )(lefts, got_lefts, by_left)

    for step in range(steps - 1):
        got = swap_columns(sums, blocks, 1 << step)
        sums = call(add_kernel, "add", all_blocks, [], 0.1)(sums, got)
    got = swap_columns(sums, blocks, 1 << (steps - 1))
    t_high = make_t(1, sums)

    def join(part, right):
        return call(
            functools.partial(join_kernel, part),
            "join",
            shape((blocks // 2, length, 2 * half), BF16),
            [],
            0.1,
        )(right, sums, got)

    send = join(1, gradient(t_high, scaled, True, sums))
    got_send = swap_rows(send, blocks, 1)
    t_low = make_t(0, send)
    keep = join(0, gradient(t_low, scaled, True, send))

    pair_sources = (low_cols, high_cols, t_low, t_high, shift, inverse, row_flags)
    upper_rows = rows // 4
    upper, paired = call(
        upper_pair_kernel,
        "pair",
        (shape((upper_rows, columns, cz), BF16), shape((8, cz), F32)),
        [],
        1,
        limit=t_limit,
        after=(keep,),
    )(*pair_sources)
    for step in range(1, steps):
        some = shape((blocks >> (step + 1), length, 2 * half), BF16)
        keep, send = call(
            functools.partial(halve_kernel, step == 1), "halve", (some, some), [], 0.1, after=(paired,)
        )(keep, got_send, swap)
        got_send = swap_rows(send, blocks, 1 << step)
    last_rows = 2 * rows_of_pass(span)
    held_rows = rows - upper_rows - last_rows
    pair, last = call(
        lower_pair_kernel,
        "pair",
        (shape(loss_sensitivity.shape, BF16), shape((last_rows, columns, cz), BF16)),
        [
            pltpu.VMEM((held_rows, columns, cz), BF16),
            pltpu.SemaphoreType.DMA((1 + held_rows // rows_of_pass(span),)),
        ],
        2,
        out_specs=(HBM, VMEM),
        limit=t_limit,
        after=(send,),
    )(*pair_sources, upper)

    return call(
        finish_kernel,
        "finish",
        (shape(loss_sensitivity.shape, BF16), shape(homolog_activations.shape, BF16)),
        [pltpu.VMEM(homolog_activations.shape, BF16), pltpu.SemaphoreType.DMA((seqs + 1,))],
        1,
        in_specs=[VMEM] * 8 + [HBM],
        out_specs=(HBM, HBM),
        aliases={8: 0},
    )(keep, got_send, mask, factors, gain, hat, spread, last, pair)


def solution(mesh):
    split = P(("groups", "rows"), ("cols", "sub"), None)
    return jax.shard_map(
        per_device,
        mesh=mesh,
        in_specs=(split, P("groups"), P("groups"), P(), P(), P(), P(), P(), P(), split),
        out_specs=(split, split),
        check_vma=False,
    )
```

```python
import functools

import jax
import jax.numpy as jnp
from jax import lax
from jax.experimental import pallas as pl
from jax.experimental.pallas import tpu as pltpu
from jax.sharding import PartitionSpec as P

F32 = jnp.float32
BF16 = jnp.bfloat16
PLACES = ("rows", "cols", "sub")
PRODUCED = 256
TILE = 16


def dot(a, b):
    return lax.dot_general(a, b, (((1,), (0,)), ((), ())), preferred_element_type=F32)


def dot_t(a, b):
    return lax.dot_general(a, b, (((1,), (1,)), ((), ())), preferred_element_type=F32)


def place():
    column = lax.axis_index("cols") * lax.axis_size("sub") + lax.axis_index("sub")
    return lax.axis_index("rows"), column


def lanes_at(start, size):
    return pl.ds(pl.multiple_of(start, size), size)


def flag_row(flags_ref):
    return flags_ref[...].astype(F32).reshape(1, -1)


def flag_column(flags_ref, start, length):
    flags = flag_row(flags_ref)
    total = flags.shape[1]
    spot = lax.broadcasted_iota(jnp.int32, (length, total), 0) + start
    lane = lax.broadcasted_iota(jnp.int32, (length, total), 1)
    return jnp.sum(jnp.where(spot == lane, flags, 0.0), axis=1, keepdims=True)


def load_all(pairs, sems):
    copies = [pltpu.make_async_copy(src, dst, sems.at[n]) for n, (src, dst) in enumerate(pairs)]
    for copy in copies:
        copy.start()
    return copies


def project_kernel(*refs):
    sources, outs, (loss_ref, w_ref), held, sems = refs[:9], refs[9:15], refs[15:17], refs[17:24], refs[24]
    out_ref, factors, mask_ref, hat_ref, spread_ref, gain_out = outs
    copies = load_all(list(zip(sources, held + (w_ref, loss_ref))), sems)
    seq_ref, x_ref, res_ref, gain_ref, bias_ref, first_ref, second_ref = held
    row_at, column_at = place()
    seqs, length, channels = x_ref.shape
    width = first_ref.shape[0]
    half = seqs * width
    for copy in copies[:7]:
        copy.wait()
    for s in range(seqs):
        factors[s * width : (s + 1) * width, :] = first_ref[...]
        factors[(seqs + s) * width : (seqs + s + 1) * width, :] = second_ref[...]
    flags = flag_row(seq_ref)
    spot = lax.broadcasted_iota(jnp.int32, flags.shape, 1)
    which = lax.broadcasted_iota(jnp.int32, (1, 2 * half), 1) % half // width
    own = jnp.zeros((1, 2 * half), F32)
    for s in range(seqs):
        value = jnp.sum(jnp.where(spot == row_at * seqs + s, flags, 0.0), axis=1, keepdims=True)
        own = jnp.where(which == s, value, own)
    mask = flag_column(res_ref, column_at * length, length) * own
    mask_ref[...] = mask
    gain = gain_ref[...].reshape(1, channels)
    bias = bias_ref[...].reshape(1, channels)
    gain_out[...] = jnp.broadcast_to(gain, gain_out.shape)
    normed = []
    for s in range(seqs):
        x = x_ref[s].astype(F32)
        off = x - jnp.mean(x, axis=-1, keepdims=True)
        spread = lax.rsqrt(jnp.mean(off * off, axis=-1, keepdims=True) + 1e-05)
        hat = off * spread
        hat_ref[s] = hat
        spread_ref[s] = jnp.broadcast_to(spread, spread_ref.shape[1:])
        normed.append((hat * gain + bias).astype(BF16))
    made = dot_t(jnp.concatenate(normed, axis=0), factors[...])
    total = made[:length]
    for s in range(1, seqs):
        total = jnp.where(which == s, made[s * length : (s + 1) * length], total)
    out_ref[0] = (total * mask).astype(BF16)
    for copy in copies[7:]:
        copy.wait()


def prepare_kernel(*refs):
    sources, (loss_ref, w_ref), outs, held, (wide_w, sems) = (
        refs[:3],
        refs[3:5],
        refs[5:13],
        refs[13:16],
        refs[16:],
    )
    by_left, by_right, swap, scaled, turned, inverse_ref, row_ref, shift_out = outs
    seq_ref, res_ref, shift_ref = held
    copies = load_all(list(zip(sources, held)), sems)
    row_at, column_at = place()
    rows, length, cz = loss_ref.shape
    width = by_left.shape[0]
    span = swap.shape[0]
    deep = span // width
    wide_w[...] = w_ref[...].astype(F32)
    for n in range(width):
        by_left[:, n * cz : (n + 1) * cz] = wide_w[pl.ds(n, width, stride=width), :].astype(BF16)
        by_right[:, n * cz : (n + 1) * cz] = w_ref[n * width : (n + 1) * width, :]
    to = lax.broadcasted_iota(jnp.int32, (span, span), 0)
    at = lax.broadcasted_iota(jnp.int32, (span, span), 1)
    swap[...] = jnp.where((to // deep == at % width) & (to % deep == at // width), 1.0, 0.0).astype(BF16)
    for copy in copies:
        copy.wait()
    present = jnp.sum(flag_row(seq_ref), axis=1, keepdims=True)
    columns = flag_column(res_ref, column_at * length, length)
    inverse = jnp.broadcast_to(1.0 / jnp.maximum(present * columns, 1.0), (length, cz))
    inverse_ref[...] = inverse
    row_ref[...] = jnp.broadcast_to(flag_column(res_ref, row_at * rows, rows), (rows, cz))
    shift_out[...] = jnp.broadcast_to(shift_ref[...].reshape(1, cz), shift_out.shape)
    for i in range(rows):
        factor = jnp.where(row_ref[i : i + 1, :] > 0.0, inverse, 1.0)
        scaled[:, i * cz : (i + 1) * cz] = (loss_ref[i].astype(F32) * factor).astype(BF16)
    to = lax.broadcasted_iota(jnp.int32, (TILE * TILE, TILE * TILE), 0)
    at = lax.broadcasted_iota(jnp.int32, (TILE * TILE, TILE * TILE), 1)
    turn = jnp.where((to // TILE == at % TILE) & (to % TILE == at // TILE), 1.0, 0.0).astype(BF16)
    for i in range(0, rows, TILE):
        for j in range(0, length, 2 * TILE):
            taken = [
                jnp.concatenate(
                    [scaled[b : b + TILE, (i + k) * cz : (i + k + 1) * cz] for k in range(TILE)], axis=0
                )
                for b in (j, j + TILE)
            ]
            made = dot(turn, jnp.concatenate(taken, axis=1)).astype(BF16)
            for a in range(2):
                for k in range(TILE):
                    low = (j + a * TILE + k) * cz
                    turned[i : i + TILE, low : low + cz] = made[
                        k * TILE : (k + 1) * TILE, a * cz : (a + 1) * cz
                    ]


def stack_kernel(own, got, *refs):
    out = refs[-1]
    count = own.shape[0]
    out[:count] = own[...]
    out[count:] = got[...]


def lefts_kernel(own, got, *refs):
    out = refs[-1]
    count, _, half = out.shape
    for n in range(count // 2):
        out[n] = own[n, :, :half]
        out[count // 2 + n] = got[n, :, :half]


def select_kernel(bit, own, got, *refs):
    out = refs[-1]
    row_at, column_at = place()
    other = jnp.where((row_at ^ column_at) & bit == 0, 0, 1)

    @pl.when(other == 1)
    def _():
        out[...] = got[...]

    @pl.when(other == 0)
    def _():
        out[...] = own[...]


def add_kernel(own, got, *refs):
    out = refs[-1]
    out[...] = (own[...].astype(F32) + got[...].astype(F32)).astype(BF16)


def spread_rows(rows, n, block, width, deep):
    length, half = block.shape
    seqs = half // width
    wide = block.astype(F32)
    for s in range(seqs):
        rows[pl.ds(n * seqs + s, length, stride=deep), :] = wide[:, s * width : (s + 1) * width]


def produce(out, rows, weight, deep):
    width = weight.shape[0]
    cz = weight.shape[1] // width
    chunk = min(2 * PRODUCED, rows.shape[0]) // deep

    def section(step, _):
        taken = rows[lanes_at(step * chunk * deep, chunk * deep), :].astype(BF16)
        for n in range(width // 2):
            made = dot(taken, weight[:, n * 2 * cz : (n + 1) * 2 * cz])
            for i in range(chunk):
                both = jnp.concatenate(
                    [made[i * deep : (i + 1) * deep, a * cz : (a + 1) * cz] for a in range(2)], axis=0
                )
                low = n * 2 * deep
                out[low : low + 2 * deep, lanes_at((step * chunk + i) * cz, cz)] = both.astype(BF16)
        return 0

    lax.fori_loop(0, rows.shape[0] // (chunk * deep), section, 0)


def v_kernel(stack, swap, weight, *refs):
    right_cols, v_ref, rows = refs[-3:]
    count, _, both = stack.shape
    width = weight.shape[0]
    deep = swap.shape[0] // width
    for n in range(count):
        spread_rows(rows, n, stack[n, :, both // 2 :], width, deep)
    right = jnp.concatenate([stack[n, :, both // 2 :] for n in range(count)], axis=1)
    right_cols[...] = dot_t(right, swap[...]).astype(BF16)
    produce(v_ref, rows, weight, deep)


def t_kernel(part, own, got, weight, *refs):
    t_ref, rows = refs[-2:]
    row_at, column_at = place()
    count = own.shape[0] // 2
    width = weight.shape[0]
    deep = t_ref.shape[0] // width
    other = (row_at ^ column_at) & 1
    for n in range(count):
        k = part * count + n
        block = jnp.where(other == 1, got[k].astype(F32), own[k].astype(F32))
        spread_rows(rows, n, block, width, deep)
    produce(t_ref, rows, weight, deep)


def ungroup(out, acc, swap):
    half = out.shape[2]
    made = dot(acc.astype(BF16), swap[...]).astype(BF16)
    for k in range(out.shape[0]):
        out[k] = made[:, k * half : (k + 1) * half]


def gradient_kernel(grouped, full_ref, side, swap, *refs):
    out = refs[-1]
    span = swap.shape[0]
    size = side.shape[1] * PRODUCED // span

    def section(step, acc):
        lanes = lanes_at(step * size, size)
        return acc + dot_t(full_ref[:, lanes], side[:, lanes])

    acc = dot_t(full_ref[:, :size], side[:, :size])
    acc = lax.fori_loop(1, span // PRODUCED, section, acc)
    if grouped:
        out[...] = jnp.transpose(acc).astype(BF16)
    else:
        ungroup(out, jnp.transpose(acc), swap)


def join_kernel(part, right, own, got, out):
    row_at, column_at = place()
    mine = jnp.where(row_at == column_at, 1.0, 0.0)
    count, _, both = out.shape
    half = both // 2
    for n in range(count):
        k = part * count + n
        out[n, :, :half] = ((own[k].astype(F32) + got[k].astype(F32)) * mine).astype(BF16)
        out[n, :, half:] = right[:, n * half : (n + 1) * half]


def halve_kernel(grouped, own, got, swap, *refs):
    keep, send = refs[-2:]
    count, _, both = keep.shape
    half = both // 2
    total = [(own[n].astype(F32) + got[n].astype(F32)).astype(BF16) for n in range(2 * count)]
    if grouped:
        right = dot(jnp.concatenate([part[:, half:] for part in total], axis=1), swap[...]).astype(BF16)
    for n in range(2 * count):
        out, k = (keep, n) if n < count else (send, n - count)
        out[k, :, :half] = total[n][:, :half]
        out[k, :, half:] = right[:, n * half : (n + 1) * half] if grouped else total[n][:, half:]


def rows_of_pass(span):
    return max(2, 8 * PRODUCED // span)


def pair_rows(out_ref, first, start, count, low_cols, high_cols, t_low, t_high, shift_ref, inverse_ref, row_ref):
    cz = out_ref.shape[2]
    group = min(4, count)
    for n in range(0, count, group):
        lanes = lanes_at((first + start + n) * cz, group * cz)
        made = dot(low_cols[...], t_low[:, lanes]) + dot(high_cols[...], t_high[:, lanes])
        for a in range(group):
            i = start + n + a
            factor = jnp.where(row_ref[pl.ds(first + i, 1), :] > 0.0, inverse_ref[...], 1.0)
            out_ref[i] = ((made[:, a * cz : (a + 1) * cz] + shift_ref[:1, :]) * factor).astype(BF16)


def upper_pair_kernel(*refs):
    sources, (out_ref, done_ref) = refs[:7], refs[-2:]
    step_rows = rows_of_pass(sources[0].shape[1])
    done_ref[...] = jnp.zeros_like(done_ref)

    def section(step, _):
        pair_rows(out_ref, 0, step * step_rows, step_rows, *sources)
        return 0

    lax.fori_loop(0, out_ref.shape[0] // step_rows, section, 0)


def lower_pair_kernel(*refs):
    sources, upper, (pair_ref, last_ref, held, sems) = refs[:7], refs[7], refs[-4:]
    step_rows = rows_of_pass(sources[0].shape[1])
    first = upper.shape[0]
    steps = held.shape[0] // step_rows

    def copy(step):
        spot = pl.ds(step * step_rows, step_rows)
        return pltpu.make_async_copy(
            held.at[spot], pair_ref.at[pl.ds(first + step * step_rows, step_rows)], sems.at[1 + step]
        )

    above = pltpu.make_async_copy(upper, pair_ref.at[:first], sems.at[0])
    above.start()

    def section(step, _):
        pair_rows(held, first, step * step_rows, step_rows, *sources)
        copy(step).start()
        return 0

    def last_section(step, _):
        pair_rows(last_ref, first + held.shape[0], step * step_rows, step_rows, *sources)
        return 0

    lax.fori_loop(0, steps, section, 0)
    lax.fori_loop(0, last_ref.shape[0] // step_rows, last_section, 0)
    above.wait()
    for step in range(steps):
        copy(step).wait()


def finish_kernel(own, got, mask_ref, factors, gain_ref, hat_ref, spread_ref, last, *refs):
    pair_ref, out_ref, held, sems = refs[-4:]
    rest = pair_ref.at[pl.ds(pair_ref.shape[0] - last.shape[0], last.shape[0])]
    seqs, length, channels = hat_ref.shape
    copies = [pltpu.make_async_copy(last, rest, sems.at[seqs])]
    copies[0].start()
    both = (own[0].astype(F32) + got[0].astype(F32)) * mask_ref[...]
    half = both.shape[1] // 2
    which = lax.broadcasted_iota(jnp.int32, (1, 2 * half), 1) % half // (half // seqs)
    rows = [jnp.where(which == s, both, 0.0).astype(BF16) for s in range(seqs)]
    grads = dot(jnp.concatenate(rows, axis=0), factors[...])
    gain = gain_ref[:1, :]
    for s in range(seqs):
        hat = hat_ref[s]
        spread = jnp.concatenate([spread_ref[s]] * (channels // spread_ref.shape[2]), axis=1)
        grad = grads[s * length : (s + 1) * length] * gain
        held[s] = (
            spread
            * (
                grad
                - jnp.mean(grad, axis=-1, keepdims=True)
                - hat * jnp.mean(grad * hat, axis=-1, keepdims=True)
            )
        ).astype(BF16)
        copies.append(pltpu.make_async_copy(held.at[s], out_ref.at[s], sems.at[s]))
        copies[-1].start()
    for copy in copies:
        copy.wait()


VMEM = pl.BlockSpec(memory_space=pltpu.VMEM)
HBM = pl.BlockSpec(memory_space=pltpu.HBM)


def call(kernel, name, out_shape, scratch, micros, in_specs=None, out_specs=None, limit=24, aliases=None, after=()):
    def run(*args):
        specs = [VMEM] * len(args) if in_specs is None else in_specs
        specs, args = specs + [pl.BlockSpec(memory_space=pl.ANY)] * len(after), args + tuple(after)
        outs = jax.tree.map(lambda _: VMEM, out_shape) if out_specs is None else out_specs
        return pl.pallas_call(
            kernel,
            out_shape=out_shape,
            in_specs=specs,
            out_specs=outs,
            scratch_shapes=scratch,
            input_output_aliases=aliases or {},
            compiler_params=pltpu.CompilerParams(vmem_limit_bytes=limit * 1024 * 1024),
            cost_estimate=pl.CostEstimate(flops=int(micros * 1e8), bytes_accessed=0, transcendentals=0),
            name=name,
        )(*args)

    return run


def swap_rows(x, blocks, bit):
    moves = [(z * blocks + c, (z ^ bit) * blocks + c) for z in range(blocks) for c in range(blocks)]
    return lax.ppermute(x, PLACES, moves)


def swap_columns(x, blocks, bit):
    moves = [(z * blocks + c, z * blocks + (c ^ bit)) for z in range(blocks) for c in range(blocks)]
    return lax.ppermute(x, PLACES, moves)


def per_device(
    homolog_activations,
    homolog_valid_flags,
    position_valid_flags,
    centering_factor,
    centering_shift,
    first_factor_matrix,
    second_factor_matrix,
    couple_weight_matrix,
    couple_shift_vector,
    loss_sensitivity,
):
    seqs, length, channels = homolog_activations.shape
    total_seq = homolog_valid_flags.shape[0]
    total_res = position_valid_flags.shape[0]
    width = first_factor_matrix.shape[1]
    rows, columns, cz = loss_sensitivity.shape
    blocks = lax.axis_size("cols") * lax.axis_size("sub")
    steps = blocks.bit_length() - 1
    assert blocks == 1 << steps == lax.axis_size("rows") and steps > 1
    half = seqs * width
    deep = total_seq // 2
    span = deep * width
    shape = jax.ShapeDtypeStruct

    def far(x):
        return pltpu.with_memory_space_constraint(x, pltpu.HBM)

    seq_flags, res_flags = far(homolog_valid_flags), far(position_valid_flags)

    stack, factors, mask, hat, spread, gain, loss, weights = call(
        project_kernel,
        "project",
        (
            shape((1, length, 2 * half), BF16),
            shape((2 * half, channels), BF16),
            shape((length, 2 * half), F32),
            shape((seqs, length, channels), F32),
            shape((seqs, length, cz), F32),
            shape((8, channels), F32),
            shape(loss_sensitivity.shape, BF16),
            shape(couple_weight_matrix.shape, BF16),
        ),
        [
            pltpu.VMEM((total_seq,), jnp.int32),
            pltpu.VMEM((seqs, length, channels), BF16),
            pltpu.VMEM((total_res,), jnp.int32),
            pltpu.VMEM((channels,), F32),
            pltpu.VMEM((channels,), F32),
            pltpu.VMEM((width, channels), BF16),
            pltpu.VMEM((width, channels), BF16),
            pltpu.SemaphoreType.DMA((9,)),
        ],
        2,
        in_specs=[HBM] * 9,
    )(
        seq_flags,
        far(homolog_activations),
        res_flags,
        far(centering_factor),
        far(centering_shift),
        far(first_factor_matrix.T),
        far(second_factor_matrix.T),
        far(couple_weight_matrix),
        far(loss_sensitivity),
    )

    by_left, by_right, swap, scaled, turned, inverse, row_flags, shift = call(
        prepare_kernel,
        "prepare",
        (
            shape((width, width * cz), BF16),
            shape((width, width * cz), BF16),
            shape((span, span), BF16),
            shape((columns, rows * cz), BF16),
            shape((rows, columns * cz), BF16),
            shape((columns, cz), F32),
            shape((rows, cz), F32),
            shape((8, cz), F32),
        ),
        [
            pltpu.VMEM((total_seq,), jnp.int32),
            pltpu.VMEM((total_res,), jnp.int32),
            pltpu.VMEM((cz,), F32),
            pltpu.VMEM((width * width, cz), F32),
            pltpu.SemaphoreType.DMA((3,)),
        ],
        3,
        in_specs=[HBM] * 3 + [VMEM] * 2,
    )(seq_flags, res_flags, far(couple_shift_vector), loss, weights)

    for step in range(steps):
        got = swap_rows(stack, blocks, blocks >> (step + 1))
        if step < steps - 1:
            stack = call(
                stack_kernel, "stack", shape((2 << step, length, 2 * half), BF16), [], 0.1, after=(shift,)
            )(stack, got)
    low_stack, high_stack = stack, got

    half_blocks = shape((blocks // 2, length, half), BF16)
    all_blocks = shape((blocks, length, half), BF16)
    cols_shape = shape((columns, span), BF16)
    t_limit = 16 + 2 * span * rows * cz * 2 // 2**20

    def make_v(stack, *after):
        return call(
            v_kernel,
            "expand_right",
            (cols_shape, shape((span, columns * cz), BF16)),
            [pltpu.VMEM((columns * deep, width), F32)],
            1.3,
            limit=t_limit,
            after=after,
        )(stack, swap, by_right)

    def gradient(full, side, grouped, *after):
        return call(
            functools.partial(gradient_kernel, grouped),
            "gradient",
            cols_shape if grouped else half_blocks,
            [],
            1.5,
            limit=t_limit,
            after=after,
        )(full, side, swap)

    low_cols, v_low = make_v(low_stack)
    low_sum = gradient(v_low, turned, False)
    lefts = call(lefts_kernel, "lefts", all_blocks, [], 0.1, after=(low_sum,))(low_stack, high_stack)
    got = swap_columns(lefts, blocks, blocks // 2)
    high_cols, v_high = make_v(high_stack, lefts)
    high_sum = gradient(v_high, turned, False)
    for step in range(1, steps):
        lefts = call(
            functools.partial(select_kernel, blocks >> step), "select", all_blocks, [], 0.1, after=(high_sum,)
        )(lefts, got)
        got = swap_columns(lefts, blocks, blocks >> (step + 1))
    got_lefts = got
    sums = call(stack_kernel, "stack", all_blocks, [], 0.1)(low_sum, high_sum)

    def make_t(part, *after):
        return call(
            functools.partial(t_kernel, part),
            "expand_left",
            shape((span, rows * cz), BF16),
            [pltpu.VMEM((rows * deep, width), F32)],
            1.2,
            limit=t_limit,
            after=after,
        )(lefts, got_lefts, by_left)

    def make_t(part, *after):
        return call(
            functools.partial(t_kernel, part),
            "expand_left",
            shape((span, rows * cz), BF16),
            [pltpu.VMEM((rows * deep, width), F32)],
            1.3,
            limit=t_limit,
            after=after,
        )(lefts, got_lefts, by_left)

    for step in range(steps - 1):
        got = swap_columns(sums, blocks, 1 << step)
        sums = call(add_kernel, "add", all_blocks, [], 0.1)(sums, got)
    got = swap_columns(sums, blocks, 1 << (steps - 1))
    t_high = make_t(1, sums)

    def join(part, right):
        return call(
            functools.partial(join_kernel, part),
            "join",
            shape((blocks // 2, length, 2 * half), BF16),
            [],
            0.1,
        )(right, sums, got)

    send = join(1, gradient(t_high, scaled, True, sums))
    got_send = swap_rows(send, blocks, 1)
    t_low = make_t(0, send)
    keep = join(0, gradient(t_low, scaled, True, send))

    pair_sources = (low_cols, high_cols, t_low, t_high, shift, inverse, row_flags)
    upper_rows = rows // 4
    upper, paired = call(
        upper_pair_kernel,
        "pair",
        (shape((upper_rows, columns, cz), BF16), shape((8, cz), F32)),
        [],
        1,
        limit=t_limit,
        after=(keep,),
    )(*pair_sources)
    for step in range(1, steps):
        some = shape((blocks >> (step + 1), length, 2 * half), BF16)
        keep, send = call(
            functools.partial(halve_kernel, step == 1), "halve", (some, some), [], 0.1, after=(paired,)
        )(keep, got_send, swap)
        got_send = swap_rows(send, blocks, 1 << step)
    last_rows = 2 * rows_of_pass(span)
    held_rows = rows - upper_rows - last_rows
    pair, last = call(
        lower_pair_kernel,
        "pair",
        (shape(loss_sensitivity.shape, BF16), shape((last_rows, columns, cz), BF16)),
        [
            pltpu.VMEM((held_rows, columns, cz), BF16),
            pltpu.SemaphoreType.DMA((1 + held_rows // rows_of_pass(span),)),
        ],
        2,
        out_specs=(HBM, VMEM),
        limit=t_limit,
        after=(send,),
    )(*pair_sources, upper)

    return call(
        finish_kernel,
        "finish",
        (shape(loss_sensitivity.shape, BF16), shape(homolog_activations.shape, BF16)),
        [pltpu.VMEM(homolog_activations.shape, BF16), pltpu.SemaphoreType.DMA((seqs + 1,))],
        1,
        in_specs=[VMEM] * 8 + [HBM],
        out_specs=(HBM, HBM),
        aliases={8: 0},
    )(keep, got_send, mask, factors, gain, hat, spread, last, pair)


def solution(mesh):
    split = P(("groups", "rows"), ("cols", "sub"), None)
    return jax.shard_map(
        per_device,
        mesh=mesh,
        in_specs=(split, P("groups"), P("groups"), P(), P(), P(), P(), P(), P(), split),
        out_specs=(split, split),
        check_vma=False,
    )
```

```python
import functools

import jax
import jax.numpy as jnp
from jax import lax
from jax.experimental import pallas as pl
from jax.experimental.pallas import tpu as pltpu
from jax.sharding import PartitionSpec as P

F32 = jnp.float32
BF16 = jnp.bfloat16
PLACES = ("rows", "cols", "sub")
PRODUCED = 256
TILE = 16


def dot(a, b):
    return lax.dot_general(a, b, (((1,), (0,)), ((), ())), preferred_element_type=F32)


def dot_t(a, b):
    return lax.dot_general(a, b, (((1,), (1,)), ((), ())), preferred_element_type=F32)


def place():
    column = lax.axis_index("cols") * lax.axis_size("sub") + lax.axis_index("sub")
    return lax.axis_index("rows"), column


def lanes_at(start, size):
    return pl.ds(pl.multiple_of(start, size), size)


def flag_row(flags_ref):
    return flags_ref[...].astype(F32).reshape(1, -1)


def flag_column(flags_ref, start, length):
    flags = flag_row(flags_ref)
    total = flags.shape[1]
    spot = lax.broadcasted_iota(jnp.int32, (length, total), 0) + start
    lane = lax.broadcasted_iota(jnp.int32, (length, total), 1)
    return jnp.sum(jnp.where(spot == lane, flags, 0.0), axis=1, keepdims=True)


def load_all(pairs, sems):
    copies = [pltpu.make_async_copy(src, dst, sems.at[n]) for n, (src, dst) in enumerate(pairs)]
    for copy in copies:
        copy.start()
    return copies


def project_kernel(*refs):
    sources, outs, w_ref, held, sems = refs[:8], refs[8:14], refs[14], refs[15:22], refs[22]
    out_ref, factors, mask_ref, hat_ref, spread_ref, gain_out = outs
    copies = load_all(list(zip(sources, held + (w_ref,))), sems)
    seq_ref, x_ref, res_ref, gain_ref, bias_ref, first_ref, second_ref = held
    row_at, column_at = place()
    seqs, length, channels = x_ref.shape
    width = first_ref.shape[0]
    half = seqs * width
    for copy in copies[:7]:
        copy.wait()
    for s in range(seqs):
        factors[s * width : (s + 1) * width, :] = first_ref[...]
        factors[(seqs + s) * width : (seqs + s + 1) * width, :] = second_ref[...]
    flags = flag_row(seq_ref)
    spot = lax.broadcasted_iota(jnp.int32, flags.shape, 1)
    which = lax.broadcasted_iota(jnp.int32, (1, 2 * half), 1) % half // width
    own = jnp.zeros((1, 2 * half), F32)
    for s in range(seqs):
        value = jnp.sum(jnp.where(spot == row_at * seqs + s, flags, 0.0), axis=1, keepdims=True)
        own = jnp.where(which == s, value, own)
    mask = flag_column(res_ref, column_at * length, length) * own
    mask_ref[...] = mask
    gain = gain_ref[...].reshape(1, channels)
    bias = bias_ref[...].reshape(1, channels)
    gain_out[...] = jnp.broadcast_to(gain, gain_out.shape)
    normed = []
    for s in range(seqs):
        x = x_ref[s].astype(F32)
        off = x - jnp.mean(x, axis=-1, keepdims=True)
        spread = lax.rsqrt(jnp.mean(off * off, axis=-1, keepdims=True) + 1e-05)
        hat = off * spread
        hat_ref[s] = hat
        spread_ref[s] = jnp.broadcast_to(spread, spread_ref.shape[1:])
        normed.append((hat * gain + bias).astype(BF16))
    made = dot_t(jnp.concatenate(normed, axis=0), factors[...])
    total = made[:length]
    for s in range(1, seqs):
        total = jnp.where(which == s, made[s * length : (s + 1) * length], total)
    out_ref[0] = (total * mask).astype(BF16)
    for copy in copies[7:]:
        copy.wait()


def prepare_kernel(*refs):
    sources, w_ref, outs, held, (wide_w, sems) = refs[:4], refs[4], refs[5:13], refs[13:17], refs[17:]
    by_left, by_right, swap, scaled, turned, inverse_ref, row_ref, shift_out = outs
    loss_ref, seq_ref, res_ref, shift_ref = held
    copies = load_all(list(zip(sources, held)), sems)
    row_at, column_at = place()
    rows, length, cz = loss_ref.shape
    width = by_left.shape[0]
    span = swap.shape[0]
    deep = span // width
    wide_w[...] = w_ref[...].astype(F32)
    for n in range(width):
        by_left[:, n * cz : (n + 1) * cz] = wide_w[pl.ds(n, width, stride=width), :].astype(BF16)
        by_right[:, n * cz : (n + 1) * cz] = w_ref[n * width : (n + 1) * width, :]
    to = lax.broadcasted_iota(jnp.int32, (span, span), 0)
    at = lax.broadcasted_iota(jnp.int32, (span, span), 1)
    swap[...] = jnp.where((to // deep == at % width) & (to % deep == at // width), 1.0, 0.0).astype(BF16)
    for copy in copies:
        copy.wait()
    present = jnp.sum(flag_row(seq_ref), axis=1, keepdims=True)
    columns = flag_column(res_ref, column_at * length, length)
    inverse = jnp.broadcast_to(1.0 / jnp.maximum(present * columns, 1.0), (length, cz))
    inverse_ref[...] = inverse
    row_ref[...] = jnp.broadcast_to(flag_column(res_ref, row_at * rows, rows), (rows, cz))
    shift_out[...] = jnp.broadcast_to(shift_ref[...].reshape(1, cz), shift_out.shape)
    for i in range(rows):
        factor = jnp.where(row_ref[i : i + 1, :] > 0.0, inverse, 1.0)
        scaled[:, i * cz : (i + 1) * cz] = (loss_ref[i].astype(F32) * factor).astype(BF16)
    to = lax.broadcasted_iota(jnp.int32, (TILE * TILE, TILE * TILE), 0)
    at = lax.broadcasted_iota(jnp.int32, (TILE * TILE, TILE * TILE), 1)
    turn = jnp.where((to // TILE == at % TILE) & (to % TILE == at // TILE), 1.0, 0.0).astype(BF16)
    for i in range(0, rows, TILE):
        for j in range(0, length, 2 * TILE):
            taken = [
                jnp.concatenate(
                    [scaled[b : b + TILE, (i + k) * cz : (i + k + 1) * cz] for k in range(TILE)], axis=0
                )
                for b in (j, j + TILE)
            ]
            made = dot(turn, jnp.concatenate(taken, axis=1)).astype(BF16)
            for a in range(2):
                for k in range(TILE):
                    low = (j + a * TILE + k) * cz
                    turned[i : i + TILE, low : low + cz] = made[
                        k * TILE : (k + 1) * TILE, a * cz : (a + 1) * cz
                    ]


def stack_kernel(own, got, *refs):
    out = refs[-1]
    count = own.shape[0]
    out[:count] = own[...]
    out[count:] = got[...]


def lefts_kernel(own, got, *refs):
    out = refs[-1]
    count, _, half = out.shape
    for n in range(count // 2):
        out[n] = own[n, :, :half]
        out[count // 2 + n] = got[n, :, :half]


def select_kernel(bit, own, got, *refs):
    out = refs[-1]
    row_at, column_at = place()
    other = jnp.where((row_at ^ column_at) & bit == 0, 0, 1)

    @pl.when(other == 1)
    def _():
        out[...] = got[...]

    @pl.when(other == 0)
    def _():
        out[...] = own[...]


def add_kernel(own, got, *refs):
    out = refs[-1]
    out[...] = (own[...].astype(F32) + got[...].astype(F32)).astype(BF16)


def spread_rows(rows, n, block, width, deep):
    length, half = block.shape
    seqs = half // width
    wide = block.astype(F32)
    for s in range(seqs):
        rows[pl.ds(n * seqs + s, length, stride=deep), :] = wide[:, s * width : (s + 1) * width]


def produce(out, rows, weight, deep):
    width = weight.shape[0]
    cz = weight.shape[1] // width
    chunk = min(2 * PRODUCED, rows.shape[0]) // deep

    def section(step, _):
        taken = rows[lanes_at(step * chunk * deep, chunk * deep), :].astype(BF16)
        for n in range(width // 2):
            made = dot(taken, weight[:, n * 2 * cz : (n + 1) * 2 * cz])
            for i in range(chunk):
                both = jnp.concatenate(
                    [made[i * deep : (i + 1) * deep, a * cz : (a + 1) * cz] for a in range(2)], axis=0
                )
                low = n * 2 * deep
                out[low : low + 2 * deep, lanes_at((step * chunk + i) * cz, cz)] = both.astype(BF16)
        return 0

    lax.fori_loop(0, rows.shape[0] // (chunk * deep), section, 0)


def v_kernel(stack, swap, weight, *refs):
    right_cols, v_ref, rows = refs[-3:]
    count, _, both = stack.shape
    width = weight.shape[0]
    deep = swap.shape[0] // width
    for n in range(count):
        spread_rows(rows, n, stack[n, :, both // 2 :], width, deep)
    right = jnp.concatenate([stack[n, :, both // 2 :] for n in range(count)], axis=1)
    right_cols[...] = dot_t(right, swap[...]).astype(BF16)
    produce(v_ref, rows, weight, deep)


def t_kernel(part, own, got, weight, *refs):
    t_ref, rows = refs[-2:]
    row_at, column_at = place()
    count = own.shape[0] // 2
    width = weight.shape[0]
    deep = t_ref.shape[0] // width
    other = (row_at ^ column_at) & 1
    for n in range(count):
        k = part * count + n
        block = jnp.where(other == 1, got[k].astype(F32), own[k].astype(F32))
        spread_rows(rows, n, block, width, deep)
    produce(t_ref, rows, weight, deep)


def ungroup(out, acc, swap):
    half = out.shape[2]
    made = dot(acc.astype(BF16), swap[...]).astype(BF16)
    for k in range(out.shape[0]):
        out[k] = made[:, k * half : (k + 1) * half]


def gradient_kernel(grouped, full_ref, side, swap, *refs):
    out = refs[-1]
    span = swap.shape[0]
    size = side.shape[1] * PRODUCED // span

    def section(step, acc):
        lanes = lanes_at(step * size, size)
        return acc + dot_t(full_ref[:, lanes], side[:, lanes])

    acc = dot_t(full_ref[:, :size], side[:, :size])
    acc = lax.fori_loop(1, span // PRODUCED, section, acc)
    if grouped:
        out[...] = jnp.transpose(acc).astype(BF16)
    else:
        ungroup(out, jnp.transpose(acc), swap)


def join_kernel(part, right, own, got, out):
    row_at, column_at = place()
    mine = jnp.where(row_at == column_at, 1.0, 0.0)
    count, _, both = out.shape
    half = both // 2
    for n in range(count):
        k = part * count + n
        out[n, :, :half] = ((own[k].astype(F32) + got[k].astype(F32)) * mine).astype(BF16)
        out[n, :, half:] = right[:, n * half : (n + 1) * half]


def halve_kernel(grouped, own, got, swap, *refs):
    keep, send = refs[-2:]
    count, _, both = keep.shape
    half = both // 2
    total = [(own[n].astype(F32) + got[n].astype(F32)).astype(BF16) for n in range(2 * count)]
    if grouped:
        right = dot(jnp.concatenate([part[:, half:] for part in total], axis=1), swap[...]).astype(BF16)
    for n in range(2 * count):
        out, k = (keep, n) if n < count else (send, n - count)
        out[k, :, :half] = total[n][:, :half]
        out[k, :, half:] = right[:, n * half : (n + 1) * half] if grouped else total[n][:, half:]


def rows_of_pass(span):
    return max(2, 8 * PRODUCED // span)


def pair_rows(out_ref, first, start, count, low_cols, high_cols, t_low, t_high, shift_ref, inverse_ref, row_ref):
    cz = out_ref.shape[2]
    group = min(4, count)
    for n in range(0, count, group):
        lanes = lanes_at((first + start + n) * cz, group * cz)
        made = dot(low_cols[...], t_low[:, lanes]) + dot(high_cols[...], t_high[:, lanes])
        for a in range(group):
            i = start + n + a
            factor = jnp.where(row_ref[pl.ds(first + i, 1), :] > 0.0, inverse_ref[...], 1.0)
            out_ref[i] = ((made[:, a * cz : (a + 1) * cz] + shift_ref[:1, :]) * factor).astype(BF16)


def upper_pair_kernel(*refs):
    sources, (out_ref, done_ref) = refs[:7], refs[-2:]
    step_rows = rows_of_pass(sources[0].shape[1])
    done_ref[...] = jnp.zeros_like(done_ref)

    def section(step, _):
        pair_rows(out_ref, 0, step * step_rows, step_rows, *sources)
        return 0

    lax.fori_loop(0, out_ref.shape[0] // step_rows, section, 0)


def lower_pair_kernel(*refs):
    sources, upper, (pair_ref, last_ref, held, sems) = refs[:7], refs[7], refs[-4:]
    step_rows = rows_of_pass(sources[0].shape[1])
    first = upper.shape[0]
    steps = held.shape[0] // step_rows

    def copy(step):
        spot = pl.ds(step * step_rows, step_rows)
        return pltpu.make_async_copy(
            held.at[spot], pair_ref.at[pl.ds(first + step * step_rows, step_rows)], sems.at[1 + step]
        )

    above = pltpu.make_async_copy(upper, pair_ref.at[:first], sems.at[0])
    above.start()

    def section(step, _):
        pair_rows(held, first, step * step_rows, step_rows, *sources)
        copy(step).start()
        return 0

    def last_section(step, _):
        pair_rows(last_ref, first + held.shape[0], step * step_rows, step_rows, *sources)
        return 0

    lax.fori_loop(0, steps, section, 0)
    lax.fori_loop(0, last_ref.shape[0] // step_rows, last_section, 0)
    above.wait()
    for step in range(steps):
        copy(step).wait()


def finish_kernel(own, got, mask_ref, factors, gain_ref, hat_ref, spread_ref, last, *refs):
    pair_ref, out_ref, held, sems = refs[-4:]
    rest = pair_ref.at[pl.ds(pair_ref.shape[0] - last.shape[0], last.shape[0])]
    seqs, length, channels = hat_ref.shape
    copies = [pltpu.make_async_copy(last, rest, sems.at[seqs])]
    copies[0].start()
    both = (own[0].astype(F32) + got[0].astype(F32)) * mask_ref[...]
    half = both.shape[1] // 2
    which = lax.broadcasted_iota(jnp.int32, (1, 2 * half), 1) % half // (half // seqs)
    rows = [jnp.where(which == s, both, 0.0).astype(BF16) for s in range(seqs)]
    grads = dot(jnp.concatenate(rows, axis=0), factors[...])
    gain = gain_ref[:1, :]
    for s in range(seqs):
        hat = hat_ref[s]
        spread = jnp.concatenate([spread_ref[s]] * (channels // spread_ref.shape[2]), axis=1)
        grad = grads[s * length : (s + 1) * length] * gain
        held[s] = (
            spread
            * (
                grad
                - jnp.mean(grad, axis=-1, keepdims=True)
                - hat * jnp.mean(grad * hat, axis=-1, keepdims=True)
            )
        ).astype(BF16)
        copies.append(pltpu.make_async_copy(held.at[s], out_ref.at[s], sems.at[s]))
        copies[-1].start()
    for copy in copies:
        copy.wait()


VMEM = pl.BlockSpec(memory_space=pltpu.VMEM)
HBM = pl.BlockSpec(memory_space=pltpu.HBM)


def call(kernel, name, out_shape, scratch, micros, in_specs=None, out_specs=None, limit=24, aliases=None, after=()):
    def run(*args):
        specs = [VMEM] * len(args) if in_specs is None else in_specs
        specs, args = specs + [pl.BlockSpec(memory_space=pl.ANY)] * len(after), args + tuple(after)
        outs = jax.tree.map(lambda _: VMEM, out_shape) if out_specs is None else out_specs
        return pl.pallas_call(
            kernel,
            out_shape=out_shape,
            in_specs=specs,
            out_specs=outs,
            scratch_shapes=scratch,
            input_output_aliases=aliases or {},
            compiler_params=pltpu.CompilerParams(vmem_limit_bytes=limit * 1024 * 1024),
            cost_estimate=pl.CostEstimate(flops=int(micros * 1e8), bytes_accessed=0, transcendentals=0),
            name=name,
        )(*args)

    return run


def swap_rows(x, blocks, bit):
    moves = [(z * blocks + c, (z ^ bit) * blocks + c) for z in range(blocks) for c in range(blocks)]
    return lax.ppermute(x, PLACES, moves)


def swap_columns(x, blocks, bit):
    moves = [(z * blocks + c, z * blocks + (c ^ bit)) for z in range(blocks) for c in range(blocks)]
    return lax.ppermute(x, PLACES, moves)


def per_device(
    homolog_activations,
    homolog_valid_flags,
    position_valid_flags,
    centering_factor,
    centering_shift,
    first_factor_matrix,
    second_factor_matrix,
    couple_weight_matrix,
    couple_shift_vector,
    loss_sensitivity,
):
    seqs, length, channels = homolog_activations.shape
    total_seq = homolog_valid_flags.shape[0]
    total_res = position_valid_flags.shape[0]
    width = first_factor_matrix.shape[1]
    rows, columns, cz = loss_sensitivity.shape
    blocks = lax.axis_size("cols") * lax.axis_size("sub")
    steps = blocks.bit_length() - 1
    assert blocks == 1 << steps == lax.axis_size("rows") and steps > 1
    half = seqs * width
    deep = total_seq // 2
    span = deep * width
    shape = jax.ShapeDtypeStruct

    def far(x):
        return pltpu.with_memory_space_constraint(x, pltpu.HBM)

    seq_flags, res_flags = far(homolog_valid_flags), far(position_valid_flags)

    stack, factors, mask, hat, spread, gain, weights = call(
        project_kernel,
        "project",
        (
            shape((1, length, 2 * half), BF16),
            shape((2 * half, channels), BF16),
            shape((length, 2 * half), F32),
            shape((seqs, length, channels), F32),
            shape((seqs, length, cz), F32),
            shape((8, channels), F32),
            shape(couple_weight_matrix.shape, BF16),
        ),
        [
            pltpu.VMEM((total_seq,), jnp.int32),
            pltpu.VMEM((seqs, length, channels), BF16),
            pltpu.VMEM((total_res,), jnp.int32),
            pltpu.VMEM((channels,), F32),
            pltpu.VMEM((channels,), F32),
            pltpu.VMEM((width, channels), BF16),
            pltpu.VMEM((width, channels), BF16),
            pltpu.SemaphoreType.DMA((8,)),
        ],
        2,
        in_specs=[HBM] * 8,
    )(
        seq_flags,
        far(homolog_activations),
        res_flags,
        far(centering_factor),
        far(centering_shift),
        far(first_factor_matrix.T),
        far(second_factor_matrix.T),
        far(couple_weight_matrix),
    )

    by_left, by_right, swap, scaled, turned, inverse, row_flags, shift = call(
        prepare_kernel,
        "prepare",
        (
            shape((width, width * cz), BF16),
            shape((width, width * cz), BF16),
            shape((span, span), BF16),
            shape((columns, rows * cz), BF16),
            shape((rows, columns * cz), BF16),
            shape((columns, cz), F32),
            shape((rows, cz), F32),
            shape((8, cz), F32),
        ),
        [
            pltpu.VMEM(loss_sensitivity.shape, BF16),
            pltpu.VMEM((total_seq,), jnp.int32),
            pltpu.VMEM((total_res,), jnp.int32),
            pltpu.VMEM((cz,), F32),
            pltpu.VMEM((width * width, cz), F32),
            pltpu.SemaphoreType.DMA((4,)),
        ],
        3,
        in_specs=[HBM] * 4 + [VMEM],
    )(far(loss_sensitivity), seq_flags, res_flags, far(couple_shift_vector), weights)

    for step in range(steps):
        got = swap_rows(stack, blocks, blocks >> (step + 1))
        if step < steps - 1:
            stack = call(
                stack_kernel, "stack", shape((2 << step, length, 2 * half), BF16), [], 0.1, after=(shift,)
            )(stack, got)
    low_stack, high_stack = stack, got

    half_blocks = shape((blocks // 2, length, half), BF16)
    all_blocks = shape((blocks, length, half), BF16)
    cols_shape = shape((columns, span), BF16)
    t_limit = 16 + 2 * span * rows * cz * 2 // 2**20

    def make_v(stack, *after):
        return call(
            v_kernel,
            "expand_right",
            (cols_shape, shape((span, columns * cz), BF16)),
            [pltpu.VMEM((columns * deep, width), F32)],
            1.3,
            limit=t_limit,
            after=after,
        )(stack, swap, by_right)

    def gradient(full, side, grouped, *after):
        return call(
            functools.partial(gradient_kernel, grouped),
            "gradient",
            cols_shape if grouped else half_blocks,
            [],
            1.5,
            limit=t_limit,
            after=after,
        )(full, side, swap)

    low_cols, v_low = make_v(low_stack)
    low_sum = gradient(v_low, turned, False)
    lefts = call(lefts_kernel, "lefts", all_blocks, [], 0.1, after=(low_sum,))(low_stack, high_stack)
    got = swap_columns(lefts, blocks, blocks // 2)
    high_cols, v_high = make_v(high_stack, lefts)
    high_sum = gradient(v_high, turned, False)
    for step in range(1, steps):
        lefts = call(
            functools.partial(select_kernel, blocks >> step), "select", all_blocks, [], 0.1, after=(high_sum,)
        )(lefts, got)
        got = swap_columns(lefts, blocks, blocks >> (step + 1))
    got_lefts = got
    sums = call(stack_kernel, "stack", all_blocks, [], 0.1)(low_sum, high_sum)

    def make_t(part, *after):
        return call(
            functools.partial(t_kernel, part),
            "expand_left",
            shape((span, rows * cz), BF16),
            [pltpu.VMEM((rows * deep, width), F32)],
            1.2,
            limit=t_limit,
            after=after,
        )(lefts, got_lefts, by_left)

    def make_t(part, *after):
        return call(
            functools.partial(t_kernel, part),
            "expand_left",
            shape((span, rows * cz), BF16),
            [pltpu.VMEM((rows * deep, width), F32)],
            1.3,
            limit=t_limit,
            after=after,
        )(lefts, got_lefts, by_left)

    for step in range(steps - 1):
        got = swap_columns(sums, blocks, 1 << step)
        sums = call(add_kernel, "add", all_blocks, [], 0.1)(sums, got)
    got = swap_columns(sums, blocks, 1 << (steps - 1))
    t_high = make_t(1, sums)

    def join(part, right):
        return call(
            functools.partial(join_kernel, part),
            "join",
            shape((blocks // 2, length, 2 * half), BF16),
            [],
            0.1,
        )(right, sums, got)

    send = join(1, gradient(t_high, scaled, True, sums))
    got_send = swap_rows(send, blocks, 1)
    t_low = make_t(0, send)
    keep = join(0, gradient(t_low, scaled, True, send))

    pair_sources = (low_cols, high_cols, t_low, t_high, shift, inverse, row_flags)
    upper_rows = rows // 4
    upper, paired = call(
        upper_pair_kernel,
        "pair",
        (shape((upper_rows, columns, cz), BF16), shape((8, cz), F32)),
        [],
        1,
        limit=t_limit,
        after=(keep,),
    )(*pair_sources)
    for step in range(1, steps):
        some = shape((blocks >> (step + 1), length, 2 * half), BF16)
        keep, send = call(
            functools.partial(halve_kernel, step == 1), "halve", (some, some), [], 0.1, after=(paired,)
        )(keep, got_send, swap)
        got_send = swap_rows(send, blocks, 1 << step)
    last_rows = 2 * rows_of_pass(span)
    held_rows = rows - upper_rows - last_rows
    pair, last = call(
        lower_pair_kernel,
        "pair",
        (shape(loss_sensitivity.shape, BF16), shape((last_rows, columns, cz), BF16)),
        [
            pltpu.VMEM((held_rows, columns, cz), BF16),
            pltpu.SemaphoreType.DMA((1 + held_rows // rows_of_pass(span),)),
        ],
        2,
        out_specs=(HBM, VMEM),
        limit=t_limit,
        after=(send,),
    )(*pair_sources, upper)

    return call(
        finish_kernel,
        "finish",
        (shape(loss_sensitivity.shape, BF16), shape(homolog_activations.shape, BF16)),
        [pltpu.VMEM(homolog_activations.shape, BF16), pltpu.SemaphoreType.DMA((seqs + 1,))],
        1,
        in_specs=[VMEM] * 8 + [HBM],
        out_specs=(HBM, HBM),
        aliases={8: 0},
    )(keep, got_send, mask, factors, gain, hat, spread, last, pair)


def solution(mesh):
    split = P(("groups", "rows"), ("cols", "sub"), None)
    return jax.shard_map(
        per_device,
        mesh=mesh,
        in_specs=(split, P("groups"), P("groups"), P(), P(), P(), P(), P(), P(), split),
        out_specs=(split, split),
        check_vma=False,
    )
```
